32 devices in a mesh: gx: 4 (over y, core), gy: 4 (over z), gz: 2 (over x).
Axes of the slice: x: 2, y: 2, z: 4, core: 2. Of those that a mesh axis runs over, the one named last changes fastest.
Arguments:
- positions: float32 [3, 4096], P(None, ('gx', 'gy', 'gz')), may hold values from -8 to 8
- atom_features: float32 [4096, 128], P(('gx', 'gy', 'gz')), may hold values from -6 to 6
- send_face: int32 [32, 6, 32], P(('gx', 'gy', 'gz')), may hold values from 0 to 127
- send_edge: int32 [32, 12, 8], P(('gx', 'gy', 'gz')), may hold values from 0 to 127
- send_corner: int32 [32, 8, 2], P(('gx', 'gy', 'gz')), may hold values from 0 to 127
- centre: int32 [196608], P(('gx', 'gy', 'gz')), may hold values from 0 to 127
- other: int32 [196608], P(('gx', 'gy', 'gz')), may hold values from 0 to 431
- edge_count: int32 [32], P(('gx', 'gy', 'gz')), may hold values from 1536 to 6144, as said below
- w_proj_a: float32 [128, 128], replicated, may hold values from -0.5 to 0.5
- w_proj_b: float32 [128, 128], replicated, may hold values from -0.5 to 0.5
- w_radial: float32 [8, 128], replicated, may hold values from -2 to 2
- w_first: bfloat16 [128, 128], replicated, may hold values from -0.5 to 0.5
- w_env: bfloat16 [128, 128], replicated, may hold values from -0.5 to 0.5
- w_value: bfloat16 [128, 128], replicated, may hold values from -0.5 to 0.5
- w_second: bfloat16 [256, 128], replicated, may hold values from -0.375 to 0.375
- w_out: bfloat16 [128], replicated, may hold values from -0.5 to 0.5
Outputs:
- forces: float32 [3, 4096], P(None, ('gx', 'gy', 'gz'))
- atom_energy: float32 [4096], P(('gx', 'gy', 'gz'))
- feature_grad: float32 [4096, 128], P(('gx', 'gy', 'gz'))
The draws below stay inside these ranges and needn't reach their ends.
Inputs may be any that keep to these rules, and one draw needn't show every extreme that they name: `edge_count`: some domain has exactly 6144 live edges in every draw.
All inputs are finite; a program needn't handle non-finite values.
Results may differ from the reference program's by a relative error of at most 0.035.
Values sent between devices are 32-bit elements; how exact they have to be, the bound alone decides.
No kernel may reach another device: no remote copies, remote signals or barrier semaphores. Data moves between devices by JAX's collectives and lax.ppermute only.
A program may use at most 192 MiB of HBM per device.

```python
import math
import jax
import jax.numpy as jnp
import numpy as np
from jax import lax

C = 128
NB = 8
A_DEV = 128
GHOST = 32
GHOST_EDGE = 8
GHOST_CORNER = 2
E_DEV = 6144
TABLE = 432
ATOMS = 4096
EDGES = 196608
N_GX = 4
N_GY = 4
N_GZ = 2


def draw_edge_count(key, part):
    key = jax.random.fold_in(key, 7)
    first_key, second_key = jax.random.split(key)
    domains = N_GX * N_GY * N_GZ
    counts = jax.random.randint(first_key, (domains,), E_DEV // 4, E_DEV + 1)
    fullest = jax.random.randint(second_key, (), 0, domains)
    return jnp.where(jnp.arange(domains) == fullest, E_DEV, counts).astype(jnp.int32)


def touch_ends(result, rng, least, high):
    place = [jax.random.randint(jax.random.fold_in(rng, axis), (), 0, length) for axis, length in enumerate(result.shape)]
    main_axis = result.shape.index(max(result.shape))
    neighbour = place[:main_axis] + [(place[main_axis] + 1) % result.shape[main_axis]] + place[main_axis + 1:]
    return result.at[tuple(place)].set(least).at[tuple(neighbour)].set(high)


def block_levels(rng, dims, cuts, smallest, largest):
    def one(position, blocks):
        heights = jax.random.uniform(jax.random.fold_in(jax.random.fold_in(rng, 6), position), (blocks,), jnp.float32, smallest / len(cuts), largest / len(cuts))
        return jnp.repeat(jnp.exp(heights), dims[position] // blocks).reshape((-1,) + (1,) * (len(dims) - position - 1))

    loudness = one(*cuts[0])
    for cut in cuts[1:]:
        loudness = loudness * one(*cut)
    return loudness


def centred(own_key, extent, width, limit, cuts=(), held_as=jnp.bfloat16):
    result = width * jax.random.normal(own_key, extent, jnp.float32)
    if cuts:
        result = result * block_levels(own_key, extent, cuts, -0.22, 0.18)
    return jnp.clip(result, -limit, limit).astype(held_as)


def setup_inputs(seed: int = 0) -> dict:
    seeds = jax.random.split(jax.random.key(seed), 17)
    return {
        "positions": centred(seeds[0], (3, ATOMS), 1.5, 8.0, ((1, 32),), jnp.float32),
        "atom_features": centred(seeds[1], (ATOMS, C), 1.0, 6.0, ((0, 32),), jnp.float32),
        "send_face": touch_ends(jax.random.randint(seeds[2], (N_GX * N_GY * N_GZ, 6, GHOST), 0, A_DEV), jax.random.fold_in(seeds[2], 1), 0, A_DEV - 1).astype(jnp.int32),
        "send_edge": touch_ends(jax.random.randint(seeds[3], (N_GX * N_GY * N_GZ, 12, GHOST_EDGE), 0, A_DEV), jax.random.fold_in(seeds[3], 1), 0, A_DEV - 1).astype(jnp.int32),
        "send_corner": touch_ends(jax.random.randint(seeds[4], (N_GX * N_GY * N_GZ, 8, GHOST_CORNER), 0, A_DEV), jax.random.fold_in(seeds[4], 1), 0, A_DEV - 1).astype(jnp.int32),
        "centre": touch_ends(jax.random.randint(seeds[5], (EDGES,), 0, A_DEV), jax.random.fold_in(seeds[5], 1), 0, A_DEV - 1).astype(jnp.int32),
        "other": touch_ends(jax.random.randint(seeds[6], (EDGES,), 0, TABLE), jax.random.fold_in(seeds[6], 1), 0, TABLE - 1).astype(jnp.int32),
        "edge_count": draw_edge_count(jax.random.fold_in(seeds[16], 71), 0),
        "w_proj_a": centred(seeds[8], (C, C), C ** -0.5, 0.5, (), jnp.float32),
        "w_proj_b": centred(seeds[9], (C, C), C ** -0.5, 0.5, (), jnp.float32),
        "w_radial": centred(seeds[10], (NB, C), NB ** -0.5, 2.0, (), jnp.float32),
        "w_first": centred(seeds[11], (C, C), C ** -0.5, 0.5),
        "w_env": centred(seeds[12], (C, C), C ** -0.5, 0.5),
        "w_value": centred(seeds[13], (C, C), C ** -0.5, 0.5),
        "w_second": centred(seeds[14], (2 * C, C), (2 * C) ** -0.5, 0.375),
        "w_out": centred(seeds[15], (C,), C ** -0.5, 0.5),
    }


def offsets_table():
    rows = []
    for a in (-1, 0, 1):
        for b in (-1, 0, 1):
            for c in (-1, 0, 1):
                if a != 0 or b != 0 or c != 0:
                    rows.append((a, b, c))
    return np.array(rows, dtype=np.int32)

def class_keys():
    groups = [[], [], []]
    index = 0
    for a in (-1, 0, 1):
        for b in (-1, 0, 1):
            for c in (-1, 0, 1):
                if a != 0 or b != 0 or c != 0:
                    groups[abs(a) + abs(b) + abs(c) - 1].append(index)
                    index = index + 1
    return [np.array(group, dtype=np.int32) for group in groups]

def harmonics(unit):
    ux, uy, uz = (unit[0], unit[1], unit[2])
    return [jnp.ones_like(ux), ux, uy, uz, 1.732 * ux * uy, 1.732 * uy * uz, 1.732 * ux * uz, 0.866 * (ux * ux - uy * uy), 0.5 * (3.0 * uz * uz - 1.0)]

def local_energy(pos_tab, proj_a, proj_b, centre, other, valid, w_radial, w_first, w_env, w_value, w_second, w_out):
    n_own = proj_a.shape[0]
    disp = jnp.take(pos_tab, other, axis=1) - jnp.take(pos_tab, centre, axis=1)
    dist = jnp.sqrt(lax.optimization_barrier(jnp.sum(disp * disp, axis=0)) + 0.01)
    unit = disp / dist[None, :]
    envelope = 1.0 / (1.0 + (dist / 2.0) ** 2) ** 2
    orders = jnp.arange(1, w_radial.shape[0] + 1).astype(jnp.float32)
    basis = jnp.sin(orders[None, :] * (math.pi / 2.0) * dist[:, None]) / dist[:, None] * envelope[:, None]
    radial = jnp.dot(basis, w_radial, precision=lax.Precision.HIGHEST)
    mixed = (jnp.take(proj_a, centre, axis=0) + jnp.take(proj_b, other, axis=0) + radial).astype(jnp.bfloat16)
    first = jax.nn.silu(jnp.dot(mixed, w_first, preferred_element_type=jnp.float32)).astype(jnp.bfloat16)
    env_weight = jnp.dot(first, w_env, preferred_element_type=jnp.float32) * (envelope * valid)[:, None]
    value = jnp.dot(first, w_value, preferred_element_type=jnp.float32)
    total = jnp.zeros(value.shape, jnp.float32)
    for comp in harmonics(unit):
        env_m = jax.ops.segment_sum(env_weight * comp[:, None], centre, num_segments=n_own)
        total = total + comp[:, None] * jnp.take(env_m, centre, axis=0)
    scalar = (0.2 * value * total).astype(jnp.bfloat16)
    joined = jnp.concatenate([first, scalar], axis=1)
    second = jax.nn.silu(jnp.dot(joined, w_second, preferred_element_type=jnp.float32)).astype(jnp.bfloat16)
    edge_energy = jnp.dot(second, w_out, preferred_element_type=jnp.float32) * envelope * valid
    atom_energy = jax.ops.segment_sum(edge_energy, centre, num_segments=n_own)
    return (jnp.sum(edge_energy), atom_energy)

def reference(positions, atom_features, send_face, send_edge, send_corner, centre, other, edge_count, w_proj_a, w_proj_b, w_radial, w_first, w_env, w_value, w_second, w_out):
    n_dev = N_GX * N_GY * N_GZ
    high = lax.Precision.HIGHEST
    proj_a = jnp.dot(atom_features, w_proj_a, precision=high)
    proj_b = jnp.dot(atom_features, w_proj_b, precision=high)
    offs_np = offsets_table()
    dev = jnp.arange(n_dev).astype(jnp.int32)
    cx = dev // (N_GY * N_GZ)
    cy = dev // N_GZ % N_GY
    cz = dev % N_GZ
    own_idx = dev[:, None] * A_DEV + jnp.arange(A_DEV).astype(jnp.int32)[None, :]
    pieces = [own_idx]
    for keys, lists in zip(class_keys(), (send_face, send_edge, send_corner)):
        offs = jnp.asarray(offs_np[keys])
        src = ((cx[:, None] - offs[None, :, 0]) % N_GX * N_GY + (cy[:, None] - offs[None, :, 1]) % N_GY) * N_GZ + (cz[:, None] - offs[None, :, 2]) % N_GZ
        kidx = jnp.arange(keys.shape[0]).astype(jnp.int32)
        ghost_idx = src[:, :, None] * A_DEV + lists[src, kidx[None, :], :]
        pieces.append(ghost_idx.reshape(n_dev, -1))
    tables = jnp.concatenate(pieces, axis=1).astype(jnp.int32)

    def one(d):
        tab = tables[d]
        pos_tab = jnp.take(positions, tab, axis=1)
        pa = lax.dynamic_slice_in_dim(proj_a, (d * A_DEV).astype(jnp.int32), A_DEV, 0)
        pb = jnp.take(proj_b, tab, axis=0)
        ce = lax.dynamic_slice_in_dim(centre, (d * E_DEV).astype(jnp.int32), E_DEV, 0)
        ot = lax.dynamic_slice_in_dim(other, (d * E_DEV).astype(jnp.int32), E_DEV, 0)
        valid = (jnp.arange(E_DEV) < edge_count[d]).astype(jnp.float32)

        def energy(p, a, b):
            return local_energy(p, a, b, ce, ot, valid, w_radial, w_first, w_env, w_value, w_second, w_out)
        total, pullback, atom_e = jax.vjp(energy, pos_tab, pa, pb, has_aux=True)
        gp, ga, gb = pullback(jnp.ones((), jnp.float32))
        return (gp, ga, gb, atom_e)
    gp, ga, gb, atom_e = lax.map(one, dev)
    flat = tables.reshape(-1)
    grad_pos = jax.ops.segment_sum(jnp.transpose(gp, (0, 2, 1)).reshape(-1, 3), flat, num_segments=ATOMS)
    grad_b = jax.ops.segment_sum(gb.reshape(-1, gb.shape[2]), flat, num_segments=ATOMS)
    grad_a = ga.reshape(ATOMS, ga.shape[2])
    feature_grad = jnp.dot(grad_a, w_proj_a.T, precision=high) + jnp.dot(grad_b, w_proj_b.T, precision=high)
    return (-grad_pos.T, atom_e.reshape(ATOMS), feature_grad)
```

```python
import math

import jax
import jax.numpy as jnp
from jax import lax
from jax.experimental import pallas as pl
from jax.experimental.pallas import tpu as pltpu
from jax.sharding import PartitionSpec as P

F32 = jnp.float32
BF16 = jnp.bfloat16
HIGH = lax.Precision.HIGHEST
AXES = ("gx", "gy", "gz")
CHUNK = 1024
SUB = 256
WIN = 16
OTHER_BITS = 9
OTHER_MASK = (1 << OTHER_BITS) - 1
LANES = 128
ROOT3 = 1.732


def dot_nn(a, b, precision=None):
    return lax.dot_general(
        a, b, (((1,), (0,)), ((), ())), preferred_element_type=F32, precision=precision
    )


def dot_nt(a, b, precision=None):
    return lax.dot_general(
        a, b, (((1,), (1,)), ((), ())), preferred_element_type=F32, precision=precision
    )


def dot_tn(a, b, precision=None):
    return lax.dot_general(
        a, b, (((0,), (0,)), ((), ())), preferred_element_type=F32, precision=precision
    )


def offset_classes():
    classes = [[], [], []]
    for a in (-1, 0, 1):
        for b in (-1, 0, 1):
            for c in (-1, 0, 1):
                if (a, b, c) != (0, 0, 0):
                    classes[abs(a) + abs(b) + abs(c) - 1].append((a, b, c))
    return classes


CLASSES = offset_classes()


def kind(off):
    return abs(off[0]) + abs(off[1]) + abs(off[2]) - 1


def z_blocks(s):
    blocks = []
    for t in (1, -1):
        blocks += [(0, t, s), (-1, t, s), (1, t, s)]
    return blocks + [(0, 0, s), (-1, 0, s), (1, 0, s)]


def y_own(s):
    return [(0, s, 0), (-1, s, 0), (1, s, 0)]


def y_blocks(s):
    blocks = y_own(s)
    for t in (1, -1):
        blocks += [(0, s, t), (-1, s, t), (1, s, t)]
    return blocks


def x_own(s):
    return [(s, 0, 0)]


def x_blocks(s):
    blocks = x_own(s)
    for t in (1, -1):
        blocks += [(s, t, 0), (s, t, 1), (s, t, -1)]
    return blocks + [(s, 0, 1), (s, 0, -1)]


SEND_GROUPS = [z_blocks(1), z_blocks(-1), y_own(1), y_own(-1), x_own(1), x_own(-1)]


class Plan:
    def __init__(self, widths):
        self.widths = widths

    def live(self, off):
        return self.widths[kind(off)]

    def rows(self, off):
        return -(-self.live(off) // 8) * 8

    def total(self, blocks):
        return sum(self.rows(off) for off in blocks)

    def start(self, blocks, off):
        at = 0
        for other in blocks:
            if other == off:
                return at
            at += self.rows(other)
        raise KeyError(off)

    def find(self, off):
        if off[0] != 0:
            return "x", off[0], self.start(x_blocks(off[0]), off)
        if off[1] != 0:
            return "y", off[1], self.start(y_blocks(off[1]), off)
        return "z", off[2], self.start(z_blocks(off[2]), off)

    def piece(self, messages, off, axis):
        if axis == "x" and off[1] != 0:
            axis, sign, at = "y", off[1], self.start(y_blocks(off[1]), off)
        else:
            axis, sign, at = "z", off[2], self.start(z_blocks(off[2]), off)
        return lax.slice_in_dim(messages[axis, sign], at, at + self.rows(off), axis=0)


def swap(plus, minus, axis, size, back=False):
    up = [(i, (i + 1) % size) for i in range(size)]
    down = [((i + 1) % size, i) for i in range(size)]
    if back:
        up, down = down, up
    if size <= 2:
        both = lax.ppermute(jnp.concatenate([plus, minus], axis=0), axis, up)
        rows = plus.shape[0]
        return both[:rows], both[rows:]
    return lax.ppermute(plus, axis, up), lax.ppermute(minus, axis, down)


def prep_kernel(plan, pos_ref, feat_ref, wa_ref, wb_ref, face_ref, edge_ref, corner_ref, *outs):
    pa_ref, pb_ref, sel_ref = outs[:3]
    sends = outs[3:9]
    own = feat_ref.shape[0]
    feat = feat_ref[...]
    pa_ref[...] = dot_nn(feat, wa_ref[...], HIGH)
    pb_ref[:, 0:LANES] = dot_nn(feat, wb_ref[...], HIGH)
    pos = jnp.concatenate([pos_ref[...], jnp.zeros((LANES - 3, own), F32)], axis=0)
    pb_ref[:, LANES:] = pos.T
    lists = (face_ref, edge_ref, corner_ref)
    lane = lax.broadcasted_iota(jnp.int32, (1, own), 1)
    sel_ref[...] = jnp.zeros_like(sel_ref)
    at = 0
    for blocks in SEND_GROUPS:
        for off in blocks:
            ref = lists[kind(off)]
            key = CLASSES[kind(off)].index(off)
            for j in range(plan.live(off)):
                row = ref[0, key, j]
                sel_ref[at + j : at + j + 1, :] = (lane == row).astype(F32)
            at += plan.rows(off)
    packed = dot_nn(sel_ref[...], pb_ref[...], HIGH)
    at = 0
    for blocks, send in zip(SEND_GROUPS, sends):
        rows = plan.total(blocks)
        send[...] = packed[at : at + rows, :]
        at += rows


def harmonics(ux, uy, uz):
    return [
        ux,
        uy,
        uz,
        ROOT3 * ux * uy,
        ROOT3 * uy * uz,
        ROOT3 * ux * uz,
        0.866 * (ux * ux - uy * uy),
        0.5 * (3.0 * uz * uz - 1.0),
    ]


def trig(half):
    turns = jnp.round(half)
    x = math.pi * (half - turns)
    odd = turns - 2.0 * jnp.floor(0.5 * turns)
    sign = 1.0 - 2.0 * odd
    x2 = x * x
    s = jnp.full_like(x, -1.0 / 39916800)
    for coef in (1.0 / 362880, -1.0 / 5040, 1.0 / 120, -1.0 / 6, 1.0):
        s = s * x2 + coef
    c = jnp.full_like(x, 1.0 / 479001600)
    for coef in (-1.0 / 3628800, 1.0 / 40320, -1.0 / 720, 1.0 / 24, -0.5, 1.0):
        c = c * x2 + coef
    return sign * x * s, sign * c


def waves(half, count):
    s1, c1 = trig(half)
    sins, coss = [s1], [c1]
    s0, c0 = jnp.zeros_like(s1), jnp.ones_like(c1)
    for _ in range(count - 1):
        sn = 2.0 * c1 * sins[-1] - s0
        cn = 2.0 * c1 * coss[-1] - c0
        s0, c0 = sins[-1], coss[-1]
        sins.append(sn)
        coss.append(cn)
    return sins, coss


def look_up(table_row, index):
    low = index & (LANES - 1)
    high = index >> 7
    result = jnp.zeros(index.shape, F32)
    for block in range(table_row.shape[1] // LANES):
        part = jnp.broadcast_to(table_row[:, block * LANES : (block + 1) * LANES], index.shape)
        got = jnp.take_along_axis(part, low, axis=1)
        result = jnp.where(high == block, got, result)
    return result


def in_lanes(tile):
    return jnp.concatenate([tile[r : r + 1, :] for r in range(tile.shape[0])], axis=1)


def one_hot(row, base, count):
    near = jnp.clip(row - base, -1, LANES).astype(BF16)
    iota = lax.broadcasted_iota(jnp.int32, (count, row.shape[1]), 0).astype(BF16)
    return jnp.where(iota == near, jnp.ones((), BF16), jnp.zeros((), BF16))


def split(x):
    high = x.astype(BF16).astype(F32)
    return high, x - high


def main_kernel(plan, *refs):
    (
        count_ref,
        skey_ref,
        key_ref,
        pa_ref,
        pb_ref,
        zp_ref,
        zm_ref,
        yp_ref,
        ym_ref,
        xp_ref,
        xm_ref,
        wa_ref,
        wb_ref,
        wrad_ref,
        w1_ref,
        wenv_ref,
        wval_ref,
        w2_ref,
        wout_ref,
        energy_ref,
        fg_ref,
        force_ref,
        rxp_ref,
        rxm_ref,
        ryp_ref,
        rym_ref,
        rzp_ref,
        rzm_ref,
        tab_ref,
        table_ref,
        w1t_ref,
        wevt_ref,
        w2t_ref,
        wev_ref,
        wradb_ref,
        wcol_ref,
        y_ref,
        basis_ref,
        geo_ref,
        first_ref,
        dsilu_ref,
        ew_ref,
        val_ref,
        a_ref,
        env_ref,
        denv_ref,
        big_ref,
        dt_ref,
        dv_ref,
        dfa_ref,
        dmix_env_ref,
        ae_ref,
        dy_ref,
        db_ref,
        dr_ref,
        acc_ref,
    ) = refs
    own, chans = pa_ref.shape
    n_basis = wrad_ref.shape[0]
    rows_all = key_ref.shape[0]
    per = CHUNK // LANES
    subs = CHUNK // SUB
    sub_rows = SUB // LANES
    messages = {
        ("z", 1): zp_ref,
        ("z", -1): zm_ref,
        ("y", 1): yp_ref,
        ("y", -1): ym_ref,
        ("x", 1): xp_ref,
        ("x", -1): xm_ref,
    }
    n_ghost = sum(len(c) * w for c, w in zip(CLASSES, plan.widths))
    n_tab = own + n_ghost
    n_sel = own + n_tab

    tab_ref[...] = jnp.zeros_like(tab_ref)
    tab_ref[0:own, 0:chans] = pa_ref[...]
    tab_ref[own : 2 * own, :] = pb_ref[...]
    at = 2 * own
    for group in CLASSES:
        for off in group:
            axis, sign, begin = plan.find(off)
            live = plan.live(off)
            tab_ref[at : at + live, :] = messages[axis, sign][begin : begin + live, :]
            at += live
    pos_t = tab_ref[own : own + 4 * LANES, LANES:].T
    rad = wrad_ref[...]
    rad_hi, rad_lo = split(rad)
    pad_at = n_sel
    tab_ref[pad_at : pad_at + n_basis, 0:chans] = rad_hi
    tab_ref[pad_at + n_basis : pad_at + 2 * n_basis, 0:chans] = rad_hi
    tab_ref[pad_at + 2 * n_basis : pad_at + 3 * n_basis, 0:chans] = rad_lo
    table_ref[...] = tab_ref[0 : table_ref.shape[1], 0:chans].T.astype(BF16)

    def flip(w):
        return w.astype(F32).T.astype(BF16)

    w1t_ref[...] = flip(w1_ref[...])
    wevt_ref[0:chans, :] = flip(wenv_ref[...])
    wevt_ref[chans:, :] = flip(wval_ref[...])
    w2t_ref[:, 0:chans] = flip(w2_ref[0:chans, :])
    w2t_ref[:, chans:] = flip(w2_ref[chans:, :])
    wev_ref[:, 0:chans] = wenv_ref[...]
    wev_ref[:, chans:] = wval_ref[...]
    wradb_ref[...] = jnp.concatenate([rad, jnp.zeros_like(rad)], axis=0).astype(BF16)
    wcol_ref[...] = jnp.broadcast_to(wout_ref[...].astype(F32), (chans, LANES)).T

    keys = key_ref[...]
    centre = keys >> OTHER_BITS
    other = keys & OTHER_MASK
    valid = (keys != (own - 1) * (OTHER_MASK + 1) + OTHER_MASK).astype(F32)
    r = [
        look_up(pos_t[a : a + 1, :], other) - look_up(pos_t[a : a + 1, 0:LANES], centre)
        for a in range(3)
    ]
    d2 = r[0] * r[0] + r[1] * r[1] + r[2] * r[2] + 0.01
    dist = jnp.sqrt(d2)
    inv = 1.0 / dist
    q = 1.0 / (1.0 + 0.25 * d2)
    envelope = q * q
    unit = [x * inv for x in r]
    for m, comp in enumerate(harmonics(*unit)):
        y_ref[pl.ds(m, rows_all, stride=8), :] = comp
    sins, _ = waves(0.5 * dist, n_basis)
    scale = envelope * inv
    for n in range(n_basis):
        basis_ref[pl.ds(n, rows_all, stride=n_basis), :] = sins[n] * scale
    for i, plane in enumerate((unit[0], unit[1], unit[2], dist, inv, q, envelope * valid, valid)):
        geo_ref[i] = plane

    env_ref[...] = jnp.zeros_like(env_ref)
    denv_ref[...] = jnp.zeros_like(denv_ref)
    ae_ref[...] = jnp.zeros_like(ae_ref)
    acc_ref[...] = jnp.zeros_like(acc_ref)
    dr_ref[...] = jnp.zeros_like(dr_ref)

    n_chunks = lax.div(count_ref[0] + (CHUNK - 1), jnp.int32(CHUNK))

    def window(k, s):
        row = k * per + s * sub_rows
        low = skey_ref[row, 0] >> OTHER_BITS
        high = skey_ref[row + sub_rows - 1, LANES - 1] >> OTHER_BITS
        start = pl.multiple_of((low >> 3) << 3, 8)
        more = lax.div(high - start, jnp.int32(WIN))
        return start, more

    def any_more(k):
        most = window(k, 0)[1]
        for s in range(1, subs):
            most = jnp.maximum(most, window(k, s)[1])
        return most > 0

    def select(k, s, start):
        row = k * per + s * sub_rows
        crow = in_lanes(key_ref[pl.ds(row, sub_rows), :] >> OTHER_BITS) - start
        hot = lax.broadcasted_iota(jnp.int32, (WIN, SUB), 0) == crow
        tiles = [
            y_ref[pl.ds(pl.multiple_of((row + j) * 8, 8), 8), :] for j in range(sub_rows)
        ]
        ys = jnp.concatenate(tiles, axis=1)
        parts = [hot.astype(F32)]
        for m in range(8):
            parts.append(jnp.where(hot, ys[m : m + 1, :], 0.0))
        return jnp.concatenate(parts, axis=0).astype(BF16)

    def load_window(ref, start):
        return jnp.concatenate(
            [ref[m, pl.ds(start, WIN), :] for m in range(9)], axis=0
        ).astype(BF16)

    def add_window(ref, start, rows):
        for m in range(9):
            ref[m, pl.ds(start, WIN), :] += rows[m * WIN : (m + 1) * WIN, :]

    def sub_lanes(s):
        return slice(s * SUB, (s + 1) * SUB)

    def more_windows(k, body):
        @pl.when(any_more(k))
        def _():
            for s in range(subs):
                start, more = window(k, s)

                def step(t, carry, s=s, start=start):
                    body(s, pl.multiple_of(start + t * WIN, 8))
                    return carry

                lax.fori_loop(1, more + 1, step, 0)

    def row_of(plane, k):
        return in_lanes(geo_ref[plane, pl.ds(pl.multiple_of(k * per, 8), per), :])

    def phase_a(k, carry):
        kt = key_ref[pl.ds(pl.multiple_of(k * per, 8), per), :]
        crow = in_lanes(kt >> OTHER_BITS)
        orow = in_lanes(kt & OTHER_MASK)
        hots = [one_hot(crow, 0, own)]
        for base in range(0, n_tab, LANES):
            hots.append(one_hot(orow, base, min(LANES, n_tab - base)))
        tiles = [
            basis_ref[pl.ds(pl.multiple_of((k * per + j) * n_basis, 8), n_basis), :]
            for j in range(per)
        ]
        basis = jnp.concatenate(tiles, axis=1)
        b_hi, b_lo = split(basis)
        hots.append(jnp.concatenate([b_hi, b_lo], axis=0).astype(BF16))
        hots.append(jnp.concatenate([b_hi, jnp.zeros_like(b_hi)], axis=0).astype(BF16))
        mixed = dot_nn(table_ref[...], jnp.concatenate(hots, axis=0)).astype(BF16)
        z1 = dot_nn(w1t_ref[...], mixed)
        sg = 0.5 + 0.5 * jnp.tanh(0.5 * z1)
        first = z1 * sg
        dsilu_ref[k] = (sg + first * (1.0 - sg)).astype(BF16)
        first = first.astype(BF16)
        first_ref[k] = first
        both = dot_nn(wevt_ref[...], first)
        ew = (both[0:chans] * row_of(6, k)).astype(BF16)
        ew_ref[k] = ew
        val_ref[k] = both[chans:].astype(BF16)
        for s in range(subs):
            start, _ = window(k, s)
            a = select(k, s, start)
            a_ref[k * subs + s] = a
            add_window(env_ref, start, dot_nt(a, ew[:, sub_lanes(s)]))

        def again(s, start):
            a = select(k, s, start)
            add_window(env_ref, start, dot_nt(a, ew_ref[k, :, sub_lanes(s)]))

        more_windows(k, again)
        return carry

    lax.fori_loop(0, n_chunks, phase_a, 0)

    def phase_b(k, carry):
        for s in range(subs):
            start, _ = window(k, s)
            big_ref[:, sub_lanes(s)] = dot_tn(load_window(env_ref, start), a_ref[k * subs + s])

        def again_total(s, start):
            big_ref[:, sub_lanes(s)] += dot_tn(load_window(env_ref, start), select(k, s, start))

        more_windows(k, again_total)
        total = 0.2 * big_ref[...]
        value = val_ref[k].astype(F32)
        scalar = (value * total).astype(BF16)
        z2 = dot_nn(w2t_ref[...], jnp.concatenate([first_ref[k], scalar], axis=0))
        sg = 0.5 + 0.5 * jnp.tanh(0.5 * z2)
        second = z2 * sg
        wcol = jnp.concatenate([wcol_ref[...]] * per, axis=1)
        ee = jnp.sum(second.astype(BF16).astype(F32) * wcol, axis=0, keepdims=True)
        envv = row_of(6, k)
        dy_ref[9, :, :] = jnp.zeros((per, LANES), F32)
        live = ee * row_of(7, k)
        for j in range(per):
            dmix_env_ref[k, j : j + 1, :] = live[:, j * LANES : (j + 1) * LANES]
        energy = ee * envv
        dz2 = ((wcol * envv) * (sg + second * (1.0 - sg))).astype(BF16)
        dj = dot_nn(w2_ref[...], dz2)
        dfa_ref[k] = dj[0:chans].astype(BF16)
        dscalar = dj[chans:]
        dt = (0.2 * value * dscalar).astype(BF16)
        dt_ref[k] = dt
        dv_ref[k] = (total * dscalar).astype(BF16)

        def add_energy(s, start):
            row = k * per + s * sub_rows
            crow = in_lanes(key_ref[pl.ds(row, sub_rows), :] >> OTHER_BITS) - start
            hot = lax.broadcasted_iota(jnp.int32, (WIN, SUB), 0) == crow
            part = jnp.where(hot, energy[:, sub_lanes(s)], 0.0)
            half = part[:, 0:LANES]
            for j in range(1, sub_rows):
                half = half + part[:, j * LANES : (j + 1) * LANES]
            ae_ref[pl.ds(start, WIN), :] += half

        for s in range(subs):
            start, _ = window(k, s)
            add_window(denv_ref, start, dot_nt(a_ref[k * subs + s], dt[:, sub_lanes(s)]))
            add_energy(s, start)

        def again(s, start):
            add_window(
                denv_ref, start, dot_nt(select(k, s, start), dt_ref[k, :, sub_lanes(s)])
            )
            add_energy(s, start)

        more_windows(k, again)
        return carry

    lax.fori_loop(0, n_chunks, phase_b, 0)

    def phase_c(k, carry):
        def env_terms(s, start, a, fresh):
            e_win = load_window(env_ref, start)
            d_win = load_window(denv_ref, start)
            dew = dot_tn(d_win, a)
            pair = jnp.concatenate(
                [dt_ref[k, :, sub_lanes(s)], ew_ref[k, :, sub_lanes(s)]], axis=0
            )
            prods = dot_nn(jnp.concatenate([e_win, d_win], axis=1), pair)
            hot = a[0:WIN].astype(F32)
            if fresh:
                big_ref[:, sub_lanes(s)] = dew
            else:
                big_ref[:, sub_lanes(s)] += dew
            for m in range(1, 9):
                row = jnp.sum(prods[m * WIN : (m + 1) * WIN] * hot, axis=0, keepdims=True)
                for j in range(sub_rows):
                    at = s * sub_rows + j
                    piece = row[:, j * LANES : (j + 1) * LANES]
                    if fresh:
                        dy_ref[m, at : at + 1, :] = piece
                    else:
                        dy_ref[m, at : at + 1, :] += piece

        for s in range(subs):
            start, _ = window(k, s)
            env_terms(s, start, a_ref[k * subs + s], True)
        more_windows(k, lambda s, start: env_terms(s, start, select(k, s, start), False))
        dew = big_ref[...]
        dpre = (dew * row_of(6, k)).astype(BF16)
        denv_row = jnp.sum(dew * ew_ref[k].astype(F32), axis=0, keepdims=True)
        for j in range(per):
            dy_ref[0, j : j + 1, :] = denv_row[:, j * LANES : (j + 1) * LANES]
        dfirst = dfa_ref[k].astype(F32) + dot_nn(
            wev_ref[...], jnp.concatenate([dpre, dv_ref[k]], axis=0)
        )
        dz1 = (dfirst * dsilu_ref[k].astype(F32)).astype(BF16)
        dmixed = dot_nn(w1_ref[...], dz1).astype(BF16)
        dbasis = dot_nn(wradb_ref[...], dmixed)
        for j in range(per):
            db_ref[j * n_basis : (j + 1) * n_basis, :] = dbasis[
                0:n_basis, j * LANES : (j + 1) * LANES
            ]
        tile = pl.ds(pl.multiple_of(k * per, 8), per)
        ux, uy, uz, dist, inv, q = [geo_ref[i, tile, :] for i in range(6)]
        envelope = q * q
        g = envelope * inv
        denvelope = -(q * envelope) * dist
        dg = (denvelope - g) * inv
        sins, coss = waves(0.5 * dist, n_basis)
        denv_direct = dmix_env_ref[k] + dy_ref[0] / envelope
        ddist = denv_direct * denvelope
        for n in range(n_basis):
            db = db_ref[pl.ds(n, per, stride=n_basis), :]
            ddist = ddist + db * (coss[n] * ((n + 1) * math.pi / 2.0) * g + sins[n] * dg)
        y = [dy_ref[m] for m in range(9)]
        gx = y[1] + ROOT3 * (uy * y[4] + uz * y[6]) + (2.0 * 0.866) * ux * y[7]
        gy = y[2] + ROOT3 * (ux * y[4] + uz * y[5]) - (2.0 * 0.866) * uy * y[7]
        gz = y[3] + ROOT3 * (uy * y[5] + ux * y[6]) + 3.0 * uz * y[8]
        along = ddist - inv * (gx * ux + gy * uy + gz * uz)
        for i, (gu, u) in enumerate(((gx, ux), (gy, uy), (gz, uz))):
            hi, lo = split(inv * gu + along * u)
            dr_ref[pl.ds(i, per, stride=16), :] = hi
            dr_ref[pl.ds(3 + i, per, stride=16), :] = lo
        dr = jnp.concatenate([dr_ref[j * 16 : (j + 1) * 16, :] for j in range(per)], axis=1)
        kt = key_ref[tile, :]
        crow = in_lanes(kt >> OTHER_BITS)
        orow = in_lanes(kt & OTHER_MASK)
        hots = [one_hot(crow, 0, own)]
        for base in range(0, n_tab, LANES):
            hots.append(one_hot(orow, base, min(LANES, n_tab - base)))
        sums = dot_nt(
            jnp.concatenate(hots, axis=0),
            jnp.concatenate([dmixed, dr.astype(BF16)], axis=0),
        )
        acc_ref[:, 0:chans] += sums[:, 0:chans]
        acc_ref[:, chans : chans + 16] += sums[:, chans:]
        return carry

    lax.fori_loop(0, n_chunks, phase_c, 0)

    energy_ref[...] = jnp.sum(ae_ref[0:own, :].T, axis=0, keepdims=True)
    fg_ref[...] = dot_nt(acc_ref[0:own, 0:chans], wa_ref[...], HIGH) + dot_nt(
        acc_ref[own : 2 * own, 0:chans], wb_ref[...], HIGH
    )
    force_ref[...] = acc_ref[own : 2 * own, LANES:] - acc_ref[0:own, LANES:]
    returns = [
        (rxp_ref, x_blocks(1)),
        (rxm_ref, x_blocks(-1)),
        (ryp_ref, y_blocks(1)),
        (rym_ref, y_blocks(-1)),
        (rzp_ref, z_blocks(1)),
        (rzm_ref, z_blocks(-1)),
    ]
    place = {}
    at = 2 * own
    for group in CLASSES:
        for off in group:
            place[off] = at
            at += plan.live(off)
    for (axis, sign), (ref, blocks) in zip(
        (("x", 1), ("x", -1), ("y", 1), ("y", -1), ("z", 1), ("z", -1)), returns
    ):
        row = 0
        for off in blocks:
            if plan.find(off)[:2] != (axis, sign):
                continue
            live = plan.live(off)
            if plan.rows(off) != live:
                ref[row : row + plan.rows(off), :] = jnp.zeros((plan.rows(off), 2 * LANES), F32)
            ref[row : row + live, :] = acc_ref[place[off] : place[off] + live, :]
            row += plan.rows(off)


def last_kernel(sel_ref, fg_ref, force_ref, wb_ref, *refs):
    returned = refs[:6]
    out_force_ref, out_fg_ref = refs[6:8]
    ret = jnp.concatenate([ref[...] for ref in returned], axis=0)
    sums = dot_tn(sel_ref[...], ret, HIGH)
    out_fg_ref[...] = fg_ref[...] + dot_nt(sums[:, 0:LANES], wb_ref[...], HIGH)
    total = (force_ref[...] + sums[:, LANES:]).T
    out_force_ref[...] = -(total[0:3, :] + total[3:6, :])


VMEM = pl.BlockSpec(memory_space=pltpu.VMEM)
SMEM = pl.BlockSpec(memory_space=pltpu.SMEM)
PARAMS = pltpu.CompilerParams(vmem_limit_bytes=52 * 2**20)


def shape(*dims, dtype=F32):
    return jax.ShapeDtypeStruct(dims, dtype)


def local(
    positions,
    atom_features,
    send_face,
    send_edge,
    send_corner,
    centre,
    other,
    edge_count,
    w_proj_a,
    w_proj_b,
    w_radial,
    w_first,
    w_env,
    w_value,
    w_second,
    w_out,
):
    own, chans = atom_features.shape
    edges = centre.shape[0]
    n_basis = w_radial.shape[0]
    plan = Plan([send_face.shape[2], send_edge.shape[2], send_corner.shape[2]])
    sizes = {axis: lax.axis_size(axis) for axis in AXES}
    wide = 2 * LANES
    n_ghost = sum(len(c) * w for c, w in zip(CLASSES, plan.widths))
    n_sel = 2 * own + n_ghost
    n_send = sum(plan.total(blocks) for blocks in SEND_GROUPS)

    dead = (own - 1) * (OTHER_MASK + 1) + OTHER_MASK
    key = jnp.where(
        jnp.arange(edges) < edge_count[0], centre * (OTHER_MASK + 1) + other, dead
    ).astype(jnp.int32)
    key = lax.sort(key, is_stable=False)
    edges_up = -(-edges // CHUNK) * CHUNK
    if edges_up != edges:
        key = jnp.concatenate([key, jnp.full((edges_up - edges,), dead, jnp.int32)])
    key = key.reshape(edges_up // LANES, LANES)

    with jax.named_scope("prep"):
        pa, pb, sel, *sends = pl.pallas_call(
            lambda *refs: prep_kernel(plan, *refs),
            out_shape=[shape(own, chans), shape(own, wide), shape(n_send, own)]
            + [shape(plan.total(blocks), wide) for blocks in SEND_GROUPS],
            in_specs=[VMEM] * 4 + [SMEM] * 3,
            out_specs=[VMEM] * 9,
            compiler_params=PARAMS,
        )(positions, atom_features, w_proj_a, w_proj_b, send_face, send_edge, send_corner)

    with jax.named_scope("halo"):
        got = {}
        got["z", 1], got["z", -1] = swap(sends[0], sends[1], "gz", sizes["gz"])

        def gather_message(own_part, blocks, axis):
            return jnp.concatenate(
                [own_part] + [plan.piece(got, off, axis) for off in blocks], axis=0
            )

        got["y", 1], got["y", -1] = swap(
            gather_message(sends[2], y_blocks(1)[3:], "y"),
            gather_message(sends[3], y_blocks(-1)[3:], "y"),
            "gy",
            sizes["gy"],
        )
        got["x", 1], got["x", -1] = swap(
            gather_message(sends[4], x_blocks(1)[1:], "x"),
            gather_message(sends[5], x_blocks(-1)[1:], "x"),
            "gx",
            sizes["gx"],
        )

    held = {}
    for axis, blocks in (("x", x_blocks), ("y", y_blocks), ("z", z_blocks)):
        for sign in (1, -1):
            held[axis, sign] = [
                off for off in blocks(sign) if plan.find(off)[:2] == (axis, sign)
            ]
    order = (("x", 1), ("x", -1), ("y", 1), ("y", -1), ("z", 1), ("z", -1))
    n_rows = edges_up // LANES
    n_chunks = edges_up // CHUNK
    n_table = n_sel + 4 * n_basis
    planes = (n_chunks, chans, CHUNK)
    scratch = [
        pltpu.VMEM((max(n_table, own + 4 * LANES), wide), F32),
        pltpu.VMEM((chans, n_table), BF16),
        pltpu.VMEM((chans, chans), BF16),
        pltpu.VMEM((2 * chans, chans), BF16),
        pltpu.VMEM((chans, 2 * chans), BF16),
        pltpu.VMEM((chans, 2 * chans), BF16),
        pltpu.VMEM((2 * n_basis, chans), BF16),
        pltpu.VMEM((chans, LANES), F32),
        pltpu.VMEM((n_rows * 8, LANES), F32),
        pltpu.VMEM((n_rows * n_basis, LANES), F32),
        pltpu.VMEM((8, n_rows, LANES), F32),
        pltpu.VMEM(planes, BF16),
        pltpu.VMEM(planes, BF16),
        pltpu.VMEM(planes, BF16),
        pltpu.VMEM(planes, BF16),
        pltpu.VMEM((edges_up // SUB, 9 * WIN, SUB), BF16),
        pltpu.VMEM((9, own + WIN, chans), F32),
        pltpu.VMEM((9, own + WIN, chans), F32),
        pltpu.VMEM((chans, CHUNK), F32),
        pltpu.VMEM(planes, BF16),
        pltpu.VMEM(planes, BF16),
        pltpu.VMEM(planes, BF16),
        pltpu.VMEM((n_chunks, CHUNK // LANES, LANES), F32),
        pltpu.VMEM((own + WIN, LANES), F32),
        pltpu.VMEM((10, CHUNK // LANES, LANES), F32),
        pltpu.VMEM((CHUNK // LANES * n_basis, LANES), F32),
        pltpu.VMEM((CHUNK // LANES * 16, LANES), F32),
        pltpu.VMEM((n_sel, wide), F32),
    ]
    with jax.named_scope("layer"):
        energy, fg, force, *back = pl.pallas_call(
            lambda *refs: main_kernel(plan, *refs),
            out_shape=[shape(1, own), shape(own, chans), shape(own, LANES)]
            + [shape(plan.total(held[side]), wide) for side in order],
            in_specs=[SMEM, SMEM] + [VMEM] * 17,
            out_specs=[VMEM] * 9,
            scratch_shapes=scratch,
            compiler_params=PARAMS,
        )(
            edge_count,
            key,
            key,
            pa,
            pb,
            got["z", 1],
            got["z", -1],
            got["y", 1],
            got["y", -1],
            got["x", 1],
            got["x", -1],
            w_proj_a,
            w_proj_b,
            w_radial,
            w_first,
            w_env,
            w_value,
            w_second,
            w_out.reshape(1, -1),
        )

    with jax.named_scope("halo_back"):
        mine = dict(zip(order, back))
        home = {}

        def put(blocks, parts, sign):
            at = 0
            for off in blocks:
                home[off] = lax.slice_in_dim(parts, at, at + plan.rows(off), axis=0)
                at += plan.rows(off)

        def message(axis, sign, blocks):
            pieces = []
            at = 0
            for off in blocks:
                if off in held[axis, sign]:
                    pieces.append(
                        lax.slice_in_dim(mine[axis, sign], at, at + plan.rows(off), axis=0)
                    )
                    at += plan.rows(off)
                else:
                    pieces.append(home[off])
            return jnp.concatenate(pieces, axis=0)

        for axis, name, blocks in (
            ("x", "gx", x_blocks),
            ("y", "gy", y_blocks),
            ("z", "gz", z_blocks),
        ):
            plus = message(axis, 1, blocks(1))
            minus = message(axis, -1, blocks(-1))
            plus, minus = swap(plus, minus, name, sizes[name], back=True)
            put(blocks(1), plus, 1)
            put(blocks(-1), minus, -1)
        returned = [
            jnp.concatenate([home[off] for off in blocks], axis=0) for blocks in SEND_GROUPS
        ]

    with jax.named_scope("owner_sums"):
        forces, feature_grad = pl.pallas_call(
            last_kernel,
            out_shape=[shape(3, own), shape(own, chans)],
            in_specs=[VMEM] * 10,
            out_specs=[VMEM] * 2,
            compiler_params=PARAMS,
        )(sel, fg, force, w_proj_b, *returned)
    return forces, energy.reshape(own), feature_grad


def solution(mesh):
    shard = P(AXES)
    return jax.shard_map(
        local,
        mesh=mesh,
        in_specs=(
            P(None, AXES),
            P(AXES, None),
            P(AXES, None, None),
            P(AXES, None, None),
            P(AXES, None, None),
            shard,
            shard,
            shard,
        )
        + (P(),) * 8,
        out_specs=(P(None, AXES), shard, P(AXES, None)),
        check_vma=False,
    )
```

```python
import math

import jax
import jax.numpy as jnp
from jax import lax
from jax.experimental import pallas as pl
from jax.experimental.pallas import tpu as pltpu
from jax.sharding import PartitionSpec as P

F32 = jnp.float32
BF16 = jnp.bfloat16
HIGH = lax.Precision.HIGHEST
AXES = ("gx", "gy", "gz")
CHUNK = 1024
SUB = 256
WIN = 16
OTHER_BITS = 9
OTHER_MASK = (1 << OTHER_BITS) - 1
LANES = 128
ROOT3 = 1.732


def dot_nn(a, b, precision=None):
    return lax.dot_general(
        a, b, (((1,), (0,)), ((), ())), preferred_element_type=F32, precision=precision
    )


def dot_nt(a, b, precision=None):
    return lax.dot_general(
        a, b, (((1,), (1,)), ((), ())), preferred_element_type=F32, precision=precision
    )


def dot_tn(a, b, precision=None):
    return lax.dot_general(
        a, b, (((0,), (0,)), ((), ())), preferred_element_type=F32, precision=precision
    )


def offset_classes():
    classes = [[], [], []]
    for a in (-1, 0, 1):
        for b in (-1, 0, 1):
            for c in (-1, 0, 1):
                if (a, b, c) != (0, 0, 0):
                    classes[abs(a) + abs(b) + abs(c) - 1].append((a, b, c))
    return classes


CLASSES = offset_classes()


def kind(off):
    return abs(off[0]) + abs(off[1]) + abs(off[2]) - 1


def z_blocks(s):
    blocks = []
    for t in (1, -1):
        blocks += [(0, t, s), (-1, t, s), (1, t, s)]
    return blocks + [(0, 0, s), (-1, 0, s), (1, 0, s)]


def y_own(s):
    return [(0, s, 0), (-1, s, 0), (1, s, 0)]


def y_blocks(s):
    blocks = y_own(s)
    for t in (1, -1):
        blocks += [(0, s, t), (-1, s, t), (1, s, t)]
    return blocks


def x_own(s):
    return [(s, 0, 0)]


def x_blocks(s):
    blocks = x_own(s)
    for t in (1, -1):
        blocks += [(s, t, 0), (s, t, 1), (s, t, -1)]
    return blocks + [(s, 0, 1), (s, 0, -1)]


SIDES = (("x", 1), ("x", -1), ("y", 1), ("y", -1), ("z", 1), ("z", -1))
BLOCKS = {"x": x_blocks, "y": y_blocks, "z": z_blocks}


def held_blocks(side):
    axis, sign = side
    first = {"x": 0, "y": 1, "z": 2}[axis]
    return [off for off in BLOCKS[axis](sign) if all(o == 0 for o in off[:first])]


SEND_GROUPS = [z_blocks(1), z_blocks(-1), y_own(1), y_own(-1), x_own(1), x_own(-1)]


class Plan:
    def __init__(self, widths):
        self.widths = widths

    def live(self, off):
        return self.widths[kind(off)]

    def rows(self, off):
        return self.live(off) + 1

    def total(self, blocks):
        return sum(self.rows(off) for off in blocks)

    def spans(self, blocks):
        at = 0
        for off in blocks:
            yield off, at
            at += self.rows(off)

    def start(self, blocks, off):
        return dict(self.spans(blocks))[off]

    def find(self, off):
        if off[0] != 0:
            return "x", off[0], self.start(x_blocks(off[0]), off)
        if off[1] != 0:
            return "y", off[1], self.start(y_blocks(off[1]), off)
        return "z", off[2], self.start(z_blocks(off[2]), off)

    def piece(self, messages, off, axis):
        if axis == "x" and off[1] != 0:
            axis, sign, at = "y", off[1], self.start(y_blocks(off[1]), off)
        else:
            axis, sign, at = "z", off[2], self.start(z_blocks(off[2]), off)
        return lax.slice_in_dim(messages[axis, sign], at, at + self.rows(off), axis=0)


def swap(plus, minus, axis, size, back=False):
    up = [(i, (i + 1) % size) for i in range(size)]
    down = [((i + 1) % size, i) for i in range(size)]
    if back:
        up, down = down, up
    if size <= 2:
        both = lax.ppermute(jnp.concatenate([plus, minus], axis=0), axis, up)
        rows = plus.shape[0]
        return both[:rows], both[rows:]
    return lax.ppermute(plus, axis, up), lax.ppermute(minus, axis, down)


GROUP = 32


def group_rows(count):
    row = lax.broadcasted_iota(jnp.int32, (count, LANES), 0)
    group = lax.broadcasted_iota(jnp.int32, (count, LANES), 1) // GROUP
    return (row == group).astype(F32) * (group < 3).astype(F32)


def diagonal(x):
    row = lax.broadcasted_iota(jnp.int32, x.shape, 0)
    lane = lax.broadcasted_iota(jnp.int32, x.shape, 1)
    return jnp.where((lane & (GROUP - 1)) == row, x, 0.0)


def spread(row, live):
    return diagonal(jnp.broadcast_to(row, (live, LANES)))


def prep_kernel(plan, *refs):
    inputs, outs = refs[:7], refs[7:16]
    held, sem = refs[16:23], refs[23]
    copies = [
        pltpu.make_async_copy(src, dst, sem.at[i])
        for i, (src, dst) in enumerate(zip(inputs, held))
    ]
    for copy in copies:
        copy.start()
    for copy in copies:
        copy.wait()
    pos_ref, feat_ref, wa_ref, wb_ref, face_ref, edge_ref, corner_ref = held
    pa_ref, pb_ref, sel_ref = outs[:3]
    sends = outs[3:9]
    own = feat_ref.shape[0]
    lists = (face_ref, edge_ref, corner_ref)
    lane = lax.broadcasted_iota(jnp.int32, (1, own), 1)
    sel_ref[...] = jnp.zeros_like(sel_ref)
    at = 0
    for blocks in SEND_GROUPS:
        for off in blocks:
            key = CLASSES[kind(off)].index(off)
            live = plan.live(off)
            column = lists[kind(off)][0, :, key : key + 1]
            sel_ref[at : at + live, :] = (column == lane).astype(F32)
            at += plan.rows(off)
    feat = feat_ref[...]
    pb = dot_nn(feat, wb_ref[...], HIGH)
    pb_ref[...] = pb
    pos = dot_tn(pos_ref[...], group_rows(3), HIGH)
    sel = sel_ref[...]
    rows = dot_nn(sel, pb, HIGH)
    places = dot_nn(sel, pos, HIGH)
    at = 0
    for blocks, send in zip(SEND_GROUPS, sends):
        count = plan.total(blocks)
        send[...] = rows[at : at + count, :]
        for off, begin in plan.spans(blocks):
            live = plan.live(off)
            block = places[at + begin : at + begin + live, :]
            send[begin + live : begin + live + 1, :] = jnp.sum(
                diagonal(block), axis=0, keepdims=True
            )
        at += count
    pa_ref[...] = dot_nn(feat, wa_ref[...], HIGH)


def weight_kernel(
    wrad_ref,
    w1_ref,
    wenv_ref,
    wval_ref,
    w2_ref,
    wout_ref,
    w1t_ref,
    wevt_ref,
    w2t_ref,
    wev_ref,
    wradb_ref,
    wcol_ref,
):
    chans = w1_ref.shape[0]

    def flip(w):
        return w.astype(F32).T.astype(BF16)

    w1t_ref[...] = flip(w1_ref[...])
    wevt_ref[0:chans, :] = flip(wenv_ref[...])
    wevt_ref[chans:, :] = flip(wval_ref[...])
    w2t_ref[:, 0:chans] = flip(w2_ref[0:chans, :])
    w2t_ref[:, chans:] = flip(w2_ref[chans:, :])
    wev_ref[:, 0:chans] = wenv_ref[...]
    wev_ref[:, chans:] = wval_ref[...]
    rad = wrad_ref[...]
    wradb_ref[...] = jnp.concatenate([rad, jnp.zeros_like(rad)], axis=0).astype(BF16)
    wcol_ref[...] = jnp.broadcast_to(wout_ref[...].astype(F32), (LANES, chans)).T


def harmonics(ux, uy, uz):
    return [
        ux,
        uy,
        uz,
        ROOT3 * ux * uy,
        ROOT3 * uy * uz,
        ROOT3 * ux * uz,
        0.866 * (ux * ux - uy * uy),
        0.5 * (3.0 * uz * uz - 1.0),
    ]


def trig(half):
    turns = jnp.round(half)
    x = math.pi * (half - turns)
    odd = turns - 2.0 * jnp.floor(0.5 * turns)
    sign = 1.0 - 2.0 * odd
    x2 = x * x
    s = jnp.full_like(x, -1.0 / 39916800)
    for coef in (1.0 / 362880, -1.0 / 5040, 1.0 / 120, -1.0 / 6, 1.0):
        s = s * x2 + coef
    c = jnp.full_like(x, 1.0 / 479001600)
    for coef in (-1.0 / 3628800, 1.0 / 40320, -1.0 / 720, 1.0 / 24, -0.5, 1.0):
        c = c * x2 + coef
    return sign * x * s, sign * c


def waves(half, count):
    s1, c1 = trig(half)
    sins, coss = [s1], [c1]
    s0, c0 = jnp.zeros_like(s1), jnp.ones_like(c1)
    for _ in range(count - 1):
        sn = 2.0 * c1 * sins[-1] - s0
        cn = 2.0 * c1 * coss[-1] - c0
        s0, c0 = sins[-1], coss[-1]
        sins.append(sn)
        coss.append(cn)
    return sins, coss


def look_up(table_row, index):
    low = index & (LANES - 1)
    high = index >> 7
    result = jnp.zeros(index.shape, F32)
    for block in range(table_row.shape[1] // LANES):
        part = jnp.broadcast_to(table_row[:, block * LANES : (block + 1) * LANES], index.shape)
        got = jnp.take_along_axis(part, low, axis=1)
        result = jnp.where(high == block, got, result)
    return result


def in_lanes(tile):
    return jnp.concatenate([tile[r : r + 1, :] for r in range(tile.shape[0])], axis=1)


def one_hot(row, base, count):
    near = jnp.clip(row - base, -1, LANES).astype(BF16)
    iota = lax.broadcasted_iota(jnp.int32, (count, row.shape[1]), 0).astype(BF16)
    return jnp.where(iota == near, jnp.ones((), BF16), jnp.zeros((), BF16))


def split(x):
    high = x.astype(BF16).astype(F32)
    return high, x - high


def main_kernel(plan, *refs):
    (
        count_ref,
        bound_ref,
        key_ref,
        pos_ref,
        pa_ref,
        pb_ref,
        zp_ref,
        zm_ref,
        yp_ref,
        ym_ref,
        xp_ref,
        xm_ref,
        wrad_ref,
        w1_ref,
        w2_ref,
        w1t_ref,
        wevt_ref,
        w2t_ref,
        wev_ref,
        wradb_ref,
        wcol_ref,
        ae_ref,
        own_ref,
        rxp_ref,
        rxm_ref,
        ryp_ref,
        rym_ref,
        rzp_ref,
        rzm_ref,
        tab_ref,
        place_ref,
        table_ref,
        y_ref,
        basis_ref,
        geo_ref,
        first_ref,
        dsilu_ref,
        ew_ref,
        val_ref,
        a_ref,
        env_ref,
        denv_ref,
        big_ref,
        dt_ref,
        dv_ref,
        dfa_ref,
        live_ref,
        dy_ref,
        db_ref,
        dr_ref,
        acc_ref,
    ) = refs
    own, chans = pa_ref.shape
    n_basis = wrad_ref.shape[0]
    rows_all = key_ref.shape[0]
    per = CHUNK // LANES
    subs = CHUNK // SUB
    sub_rows = SUB // LANES
    messages = {
        ("z", 1): zp_ref,
        ("z", -1): zm_ref,
        ("y", 1): yp_ref,
        ("y", -1): ym_ref,
        ("x", 1): xp_ref,
        ("x", -1): xm_ref,
    }
    n_ghost = sum(len(c) * w for c, w in zip(CLASSES, plan.widths))
    n_tab = own + n_ghost
    n_sel = own + n_tab

    tab_ref[0:own, :] = pa_ref[...]
    tab_ref[own : 2 * own, :] = pb_ref[...]
    place_ref[...] = jnp.zeros_like(place_ref)
    at = 2 * own
    for group in CLASSES:
        for off in group:
            axis, sign, begin = plan.find(off)
            live = plan.live(off)
            message = messages[axis, sign]
            tab_ref[at : at + live, :] = message[begin : begin + live, :]
            place_ref[at - 2 * own : at - 2 * own + live, :] = spread(
                message[begin + live : begin + live + 1, :], live
            )
            at += live
    ghost_pos = dot_nt(group_rows(8), place_ref[...], HIGH)
    pos_t = jnp.concatenate([pos_ref[...], ghost_pos[0:3, :]], axis=1)
    rad_hi, rad_lo = split(wrad_ref[...])
    tab_ref[n_sel : n_sel + 4 * n_basis, :] = jnp.concatenate(
        [rad_hi, rad_hi, rad_lo, jnp.zeros_like(rad_lo)], axis=0
    )
    table_ref[...] = tab_ref[...].T.astype(BF16)

    keys = key_ref[...]
    centre = keys >> OTHER_BITS
    other = keys & OTHER_MASK
    valid = (keys != (own - 1) * (OTHER_MASK + 1) + OTHER_MASK).astype(F32)
    r = [
        look_up(pos_t[a : a + 1, :], other) - look_up(pos_t[a : a + 1, 0:LANES], centre)
        for a in range(3)
    ]
    d2 = r[0] * r[0] + r[1] * r[1] + r[2] * r[2] + 0.01
    dist = jnp.sqrt(d2)
    inv = 1.0 / dist
    q = 1.0 / (1.0 + 0.25 * d2)
    envelope = q * q
    unit = [x * inv for x in r]
    for m, comp in enumerate(harmonics(*unit)):
        y_ref[pl.ds(m, rows_all, stride=8), :] = comp
    sins, _ = waves(0.5 * dist, n_basis)
    scale = envelope * inv
    for n in range(n_basis):
        basis_ref[pl.ds(n, rows_all, stride=n_basis), :] = sins[n] * scale
    for i, plane in enumerate((unit[0], unit[1], unit[2], dist, inv, q, envelope * valid, valid)):
        geo_ref[i] = plane

    env_ref[...] = jnp.zeros_like(env_ref)
    denv_ref[...] = jnp.zeros_like(denv_ref)
    ae_ref[...] = jnp.zeros_like(ae_ref)
    acc_ref[...] = jnp.zeros_like(acc_ref)
    dr_ref[...] = jnp.zeros_like(dr_ref)

    n_chunks = lax.div(count_ref[0] + (CHUNK - 1), jnp.int32(CHUNK))

    def window(k, s):
        low = bound_ref[0, k * subs + s]
        high = bound_ref[1, k * subs + s]
        start = pl.multiple_of((low >> 3) << 3, 8)
        more = lax.div(high - start, jnp.int32(WIN))
        return start, more

    def any_more(k):
        most = window(k, 0)[1]
        for s in range(1, subs):
            most = jnp.maximum(most, window(k, s)[1])
        return most > 0

    def select(k, s, start):
        row = k * per + s * sub_rows
        crow = in_lanes(key_ref[pl.ds(row, sub_rows), :] >> OTHER_BITS) - start
        hot = lax.broadcasted_iota(jnp.int32, (WIN, SUB), 0) == crow
        tiles = [
            y_ref[pl.ds(pl.multiple_of((row + j) * 8, 8), 8), :] for j in range(sub_rows)
        ]
        ys = jnp.concatenate(tiles, axis=1)
        parts = [hot.astype(F32)]
        for m in range(8):
            parts.append(jnp.where(hot, ys[m : m + 1, :], 0.0))
        return jnp.concatenate(parts, axis=0).astype(BF16)

    def load_window(ref, start):
        return jnp.concatenate(
            [ref[m, pl.ds(start, WIN), :] for m in range(9)], axis=0
        ).astype(BF16)

    def add_window(ref, start, rows):
        for m in range(9):
            ref[m, pl.ds(start, WIN), :] += rows[m * WIN : (m + 1) * WIN, :]

    def sub_lanes(s):
        return slice(s * SUB, (s + 1) * SUB)

    def more_windows(k, body):
        @pl.when(any_more(k))
        def _():
            for s in range(subs):
                start, more = window(k, s)

                def step(t, carry, s=s, start=start):
                    body(s, pl.multiple_of(start + t * WIN, 8))
                    return carry

                lax.fori_loop(1, more + 1, step, 0)

    def row_of(plane, k):
        return in_lanes(geo_ref[plane, pl.ds(pl.multiple_of(k * per, 8), per), :])

    def phase_a(k, carry):
        kt = key_ref[pl.ds(pl.multiple_of(k * per, 8), per), :]
        crow = in_lanes(kt >> OTHER_BITS)
        orow = in_lanes(kt & OTHER_MASK)
        hots = [one_hot(crow, 0, own)]
        for base in range(0, n_tab, LANES):
            hots.append(one_hot(orow, base, min(LANES, n_tab - base)))
        tiles = [
            basis_ref[pl.ds(pl.multiple_of((k * per + j) * n_basis, 8), n_basis), :]
            for j in range(per)
        ]
        basis = jnp.concatenate(tiles, axis=1)
        b_hi, b_lo = split(basis)
        hots.append(jnp.concatenate([b_hi, b_lo], axis=0).astype(BF16))
        hots.append(jnp.concatenate([b_hi, jnp.zeros_like(b_hi)], axis=0).astype(BF16))
        mixed = dot_nn(table_ref[...], jnp.concatenate(hots, axis=0)).astype(BF16)
        z1 = dot_nn(w1t_ref[...], mixed)
        sg = 0.5 + 0.5 * jnp.tanh(0.5 * z1)
        first = z1 * sg
        dsilu_ref[k] = (sg + first * (1.0 - sg)).astype(BF16)
        first = first.astype(BF16)
        first_ref[k] = first
        both = dot_nn(wevt_ref[...], first)
        ew = (both[0:chans] * row_of(6, k)).astype(BF16)
        ew_ref[k] = ew
        val_ref[k] = both[chans:].astype(BF16)
        for s in range(subs):
            start, _ = window(k, s)
            a = select(k, s, start)
            a_ref[k * subs + s] = a
            add_window(env_ref, start, dot_nt(a, ew[:, sub_lanes(s)]))

        def again(s, start):
            a = select(k, s, start)
            add_window(env_ref, start, dot_nt(a, ew_ref[k, :, sub_lanes(s)]))

        more_windows(k, again)
        return carry

    lax.fori_loop(0, n_chunks, phase_a, 0)

    def phase_b(k, carry):
        for s in range(subs):
            start, _ = window(k, s)
            big_ref[:, sub_lanes(s)] = dot_tn(load_window(env_ref, start), a_ref[k * subs + s])

        def again_total(s, start):
            big_ref[:, sub_lanes(s)] += dot_tn(load_window(env_ref, start), select(k, s, start))

        more_windows(k, again_total)
        total = 0.2 * big_ref[...]
        value = val_ref[k].astype(F32)
        scalar = (value * total).astype(BF16)
        z2 = dot_nn(w2t_ref[...], jnp.concatenate([first_ref[k], scalar], axis=0))
        sg = 0.5 + 0.5 * jnp.tanh(0.5 * z2)
        second = z2 * sg
        wcol = jnp.concatenate([wcol_ref[...]] * per, axis=1)
        ee = jnp.sum(second.astype(BF16).astype(F32) * wcol, axis=0, keepdims=True)
        envv = row_of(6, k)
        dy_ref[9, :, :] = jnp.zeros((per, LANES), F32)
        live = ee * row_of(7, k)
        for j in range(per):
            live_ref[k, j : j + 1, :] = live[:, j * LANES : (j + 1) * LANES]
        energy = ee * envv
        dz2 = ((wcol * envv) * (sg + second * (1.0 - sg))).astype(BF16)
        dj = dot_nn(w2_ref[...], dz2)
        dfa_ref[k] = dj[0:chans].astype(BF16)
        dscalar = dj[chans:]
        dt = (0.2 * value * dscalar).astype(BF16)
        dt_ref[k] = dt
        dv_ref[k] = (total * dscalar).astype(BF16)

        def add_energy(s, start):
            row = k * per + s * sub_rows
            crow = in_lanes(key_ref[pl.ds(row, sub_rows), :] >> OTHER_BITS) - start
            hot = lax.broadcasted_iota(jnp.int32, (WIN, SUB), 0) == crow
            part = jnp.where(hot, energy[:, sub_lanes(s)], 0.0)
            half = part[:, 0:LANES]
            for j in range(1, sub_rows):
                half = half + part[:, j * LANES : (j + 1) * LANES]
            ae_ref[pl.ds(start, WIN), :] += half

        for s in range(subs):
            start, _ = window(k, s)
            add_window(denv_ref, start, dot_nt(a_ref[k * subs + s], dt[:, sub_lanes(s)]))
            add_energy(s, start)

        def again(s, start):
            add_window(
                denv_ref, start, dot_nt(select(k, s, start), dt_ref[k, :, sub_lanes(s)])
            )
            add_energy(s, start)

        more_windows(k, again)
        return carry

    lax.fori_loop(0, n_chunks, phase_b, 0)

    def phase_c(k, carry):
        def env_terms(s, start, a, fresh):
            e_win = load_window(env_ref, start)
            d_win = load_window(denv_ref, start)
            dew = dot_tn(d_win, a)
            pair = jnp.concatenate(
                [dt_ref[k, :, sub_lanes(s)], ew_ref[k, :, sub_lanes(s)]], axis=0
            )
            prods = dot_nn(jnp.concatenate([e_win, d_win], axis=1), pair)
            hot = a[0:WIN].astype(F32)
            if fresh:
                big_ref[:, sub_lanes(s)] = dew
            else:
                big_ref[:, sub_lanes(s)] += dew
            for m in range(1, 9):
                row = jnp.sum(prods[m * WIN : (m + 1) * WIN] * hot, axis=0, keepdims=True)
                for j in range(sub_rows):
                    at = s * sub_rows + j
                    piece = row[:, j * LANES : (j + 1) * LANES]
                    if fresh:
                        dy_ref[m, at : at + 1, :] = piece
                    else:
                        dy_ref[m, at : at + 1, :] += piece

        for s in range(subs):
            start, _ = window(k, s)
            env_terms(s, start, a_ref[k * subs + s], True)
        more_windows(k, lambda s, start: env_terms(s, start, select(k, s, start), False))
        dew = big_ref[...]
        dpre = (dew * row_of(6, k)).astype(BF16)
        denv_row = jnp.sum(dew * ew_ref[k].astype(F32), axis=0, keepdims=True)
        for j in range(per):
            dy_ref[0, j : j + 1, :] = denv_row[:, j * LANES : (j + 1) * LANES]
        dfirst = dfa_ref[k].astype(F32) + dot_nn(
            wev_ref[...], jnp.concatenate([dpre, dv_ref[k]], axis=0)
        )
        dz1 = (dfirst * dsilu_ref[k].astype(F32)).astype(BF16)
        dmixed = dot_nn(w1_ref[...], dz1).astype(BF16)
        dbasis = dot_nn(wradb_ref[...], dmixed)
        for j in range(per):
            db_ref[j * n_basis : (j + 1) * n_basis, :] = dbasis[
                0:n_basis, j * LANES : (j + 1) * LANES
            ]
        tile = pl.ds(pl.multiple_of(k * per, 8), per)
        ux, uy, uz, dist, inv, q = [geo_ref[i, tile, :] for i in range(6)]
        envelope = q * q
        g = envelope * inv
        denvelope = -(q * envelope) * dist
        dg = (denvelope - g) * inv
        sins, coss = waves(0.5 * dist, n_basis)
        denv_direct = live_ref[k] + dy_ref[0] / envelope
        ddist = denv_direct * denvelope
        for n in range(n_basis):
            db = db_ref[pl.ds(n, per, stride=n_basis), :]
            ddist = ddist + db * (coss[n] * ((n + 1) * math.pi / 2.0) * g + sins[n] * dg)
        y = [dy_ref[m] for m in range(9)]
        gx = y[1] + ROOT3 * (uy * y[4] + uz * y[6]) + (2.0 * 0.866) * ux * y[7]
        gy = y[2] + ROOT3 * (ux * y[4] + uz * y[5]) - (2.0 * 0.866) * uy * y[7]
        gz = y[3] + ROOT3 * (uy * y[5] + ux * y[6]) + 3.0 * uz * y[8]
        along = ddist - inv * (gx * ux + gy * uy + gz * uz)
        for i, (gu, u) in enumerate(((gx, ux), (gy, uy), (gz, uz))):
            hi, lo = split(inv * gu + along * u)
            dr_ref[pl.ds(i, per, stride=16), :] = hi
            dr_ref[pl.ds(3 + i, per, stride=16), :] = lo
        dr = jnp.concatenate([dr_ref[j * 16 : (j + 1) * 16, :] for j in range(per)], axis=1)
        kt = key_ref[tile, :]
        crow = in_lanes(kt >> OTHER_BITS)
        orow = in_lanes(kt & OTHER_MASK)
        hots = [one_hot(crow, 0, own)]
        for base in range(0, n_tab, LANES):
            hots.append(one_hot(orow, base, min(LANES, n_tab - base)))
        sums = dot_nt(
            jnp.concatenate(hots, axis=0),
            jnp.concatenate([dmixed, dr.astype(BF16)], axis=0),
        )
        acc_ref[:, 0:chans] += sums[:, 0:chans]
        acc_ref[:, chans : chans + 16] += sums[:, chans:]
        return carry

    lax.fori_loop(0, n_chunks, phase_c, 0)

    own_ref[...] = acc_ref[0 : 2 * own, :]
    row = lax.broadcasted_iota(jnp.int32, (LANES, LANES), 0)
    group = lax.broadcasted_iota(jnp.int32, (LANES, LANES), 1) // GROUP
    both = ((group < 3) & ((row == group) | (row == group + 3))).astype(F32)
    places = dot_nn(acc_ref[2 * own :, LANES:], both, HIGH)
    found = {}
    at = 2 * own
    for group in CLASSES:
        for off in group:
            found[off] = at
            at += plan.live(off)
    for side, ref in zip(SIDES, (rxp_ref, rxm_ref, ryp_ref, rym_ref, rzp_ref, rzm_ref)):
        for off, row in plan.spans(held_blocks(side)):
            live = plan.live(off)
            at = found[off]
            ref[row : row + live, :] = acc_ref[at : at + live, 0:chans]
            block = places[at - 2 * own : at - 2 * own + live, :]
            ref[row + live : row + live + 1, :] = jnp.sum(diagonal(block), axis=0, keepdims=True)


def own_kernel(ae_ref, own_ref, wa_ref, wb_ref, energy_ref, fg_ref, force_ref):
    chans = wa_ref.shape[1]
    own = force_ref.shape[1]
    energy_ref[...] = jnp.sum(ae_ref[0:own, :].T, axis=0, keepdims=True)
    fg_ref[...] = dot_nt(own_ref[0:own, 0:chans], wa_ref[...], HIGH) + dot_nt(
        own_ref[own:, 0:chans], wb_ref[...], HIGH
    )
    force = (own_ref[own:, LANES:] - own_ref[0:own, LANES:]).T
    force_ref[...] = force[0:3, :] + force[3:6, :]


def last_kernel(plan, sel_ref, fg_ref, force_ref, wb_ref, *refs):
    returned = refs[:6]
    out_force_ref, out_fg_ref, place_ref = refs[6:9]
    ret = jnp.concatenate([ref[...] for ref in returned], axis=0)
    place_ref[...] = jnp.zeros_like(place_ref)
    at = 0
    for blocks, ref in zip(SEND_GROUPS, returned):
        for off, row in plan.spans(blocks):
            live = plan.live(off)
            place_ref[at + row : at + row + live, :] = spread(
                ref[row + live : row + live + 1, :], live
            )
        at += plan.total(blocks)
    sel = sel_ref[...]
    sums = dot_tn(sel, ret, HIGH)
    places = dot_tn(sel, place_ref[...], HIGH)
    out_fg_ref[...] = fg_ref[...] + dot_nt(sums, wb_ref[...], HIGH)
    total = dot_nt(group_rows(8), places, HIGH)
    out_force_ref[...] = -(force_ref[...] + total[0:3, :])


VMEM = pl.BlockSpec(memory_space=pltpu.VMEM)
HBM = pl.BlockSpec(memory_space=pltpu.HBM)
SMEM = pl.BlockSpec(memory_space=pltpu.SMEM)
PARAMS = pltpu.CompilerParams(vmem_limit_bytes=52 * 2**20)


def shape(*dims, dtype=F32):
    return jax.ShapeDtypeStruct(dims, dtype)


def local(
    positions,
    atom_features,
    send_face,
    send_edge,
    send_corner,
    centre,
    other,
    edge_count,
    w_proj_a,
    w_proj_b,
    w_radial,
    w_first,
    w_env,
    w_value,
    w_second,
    w_out,
):
    own, chans = atom_features.shape
    edges = centre.shape[0]
    n_basis = w_radial.shape[0]
    plan = Plan([send_face.shape[2], send_edge.shape[2], send_corner.shape[2]])
    sizes = {axis: lax.axis_size(axis) for axis in AXES}
    n_ghost = sum(len(c) * w for c, w in zip(CLASSES, plan.widths))
    n_sel = 2 * own + n_ghost
    n_send = sum(plan.total(blocks) for blocks in SEND_GROUPS)
    n_table = n_sel + 4 * n_basis

    dead = (own - 1) * (OTHER_MASK + 1) + OTHER_MASK
    key = jnp.where(
        jnp.arange(edges) < edge_count[0], centre * (OTHER_MASK + 1) + other, dead
    ).astype(jnp.int32)
    key = lax.sort(key, is_stable=False)
    edges_up = -(-edges // CHUNK) * CHUNK
    if edges_up != edges:
        key = jnp.concatenate([key, jnp.full((edges_up - edges,), dead, jnp.int32)])
    windows = (key >> OTHER_BITS).reshape(edges_up // SUB, SUB)
    bounds = jnp.stack([windows[:, 0], windows[:, SUB - 1]])
    key = key.reshape(edges_up // LANES, LANES)

    with jax.named_scope("prep"):
        given = (positions, atom_features, w_proj_a, w_proj_b) + tuple(
            jnp.transpose(lists, (0, 2, 1)) for lists in (send_face, send_edge, send_corner)
        )
        pa, pb, sel, *sends = pl.pallas_call(
            lambda *refs: prep_kernel(plan, *refs),
            out_shape=[shape(own, chans), shape(own, chans), shape(n_send, own)]
            + [shape(plan.total(blocks), chans) for blocks in SEND_GROUPS],
            in_specs=[HBM] * len(given),
            out_specs=[VMEM] * 9,
            scratch_shapes=[pltpu.VMEM(x.shape, x.dtype) for x in given]
            + [pltpu.SemaphoreType.DMA((len(given),))],
            compiler_params=PARAMS,
        )(*given)

    with jax.named_scope("weights"):
        weights = pl.pallas_call(
            weight_kernel,
            out_shape=[
                shape(chans, chans, dtype=BF16),
                shape(2 * chans, chans, dtype=BF16),
                shape(chans, 2 * chans, dtype=BF16),
                shape(chans, 2 * chans, dtype=BF16),
                shape(2 * n_basis, chans, dtype=BF16),
                shape(chans, LANES),
            ],
            in_specs=[VMEM] * 6,
            out_specs=[VMEM] * 6,
            compiler_params=PARAMS,
        )(w_radial, w_first, w_env, w_value, w_second, w_out.reshape(1, -1))

    with jax.named_scope("halo"):
        got = {}
        got["z", 1], got["z", -1] = swap(sends[0], sends[1], "gz", sizes["gz"])

        def gather_message(own_part, blocks, axis):
            return jnp.concatenate(
                [own_part] + [plan.piece(got, off, axis) for off in blocks], axis=0
            )

        got["y", 1], got["y", -1] = swap(
            gather_message(sends[2], y_blocks(1)[3:], "y"),
            gather_message(sends[3], y_blocks(-1)[3:], "y"),
            "gy",
            sizes["gy"],
        )
        got["x", 1], got["x", -1] = swap(
            gather_message(sends[4], x_blocks(1)[1:], "x"),
            gather_message(sends[5], x_blocks(-1)[1:], "x"),
            "gx",
            sizes["gx"],
        )

    n_rows = edges_up // LANES
    n_chunks = edges_up // CHUNK
    planes = (n_chunks, chans, CHUNK)
    scratch = [
        pltpu.VMEM((n_table, chans), F32),
        pltpu.VMEM((-(-n_ghost // LANES) * LANES, LANES), F32),
        pltpu.VMEM((chans, n_table), BF16),
        pltpu.VMEM((n_rows * 8, LANES), F32),
        pltpu.VMEM((n_rows * n_basis, LANES), F32),
        pltpu.VMEM((8, n_rows, LANES), F32),
        pltpu.VMEM(planes, BF16),
        pltpu.VMEM(planes, BF16),
        pltpu.VMEM(planes, BF16),
        pltpu.VMEM(planes, BF16),
        pltpu.VMEM((edges_up // SUB, 9 * WIN, SUB), BF16),
        pltpu.VMEM((9, own + WIN, chans), F32),
        pltpu.VMEM((9, own + WIN, chans), F32),
        pltpu.VMEM((chans, CHUNK), F32),
        pltpu.VMEM(planes, BF16),
        pltpu.VMEM(planes, BF16),
        pltpu.VMEM(planes, BF16),
        pltpu.VMEM((n_chunks, CHUNK // LANES, LANES), F32),
        pltpu.VMEM((10, CHUNK // LANES, LANES), F32),
        pltpu.VMEM((CHUNK // LANES * n_basis, LANES), F32),
        pltpu.VMEM((CHUNK // LANES * 16, LANES), F32),
        pltpu.VMEM((n_sel, 2 * LANES), F32),
    ]
    with jax.named_scope("layer"):
        atom_sums, own_sums, *back = pl.pallas_call(
            lambda *refs: main_kernel(plan, *refs),
            out_shape=[shape(own + WIN, LANES), shape(2 * own, 2 * LANES)]
            + [shape(plan.total(held_blocks(side)), chans) for side in SIDES],
            in_specs=[SMEM, SMEM] + [VMEM] * 19,
            out_specs=[VMEM] * 8,
            scratch_shapes=scratch,
            compiler_params=PARAMS,
        )(
            edge_count,
            bounds,
            key,
            positions,
            pa,
            pb,
            got["z", 1],
            got["z", -1],
            got["y", 1],
            got["y", -1],
            got["x", 1],
            got["x", -1],
            w_radial,
            w_first,
            w_second,
            *weights,
        )

    with jax.named_scope("own_part"):
        energy, fg, force = pl.pallas_call(
            own_kernel,
            out_shape=[shape(1, own), shape(own, chans), shape(3, own)],
            in_specs=[VMEM] * 4,
            out_specs=[VMEM] * 3,
            compiler_params=PARAMS,
        )(atom_sums, own_sums, w_proj_a, w_proj_b)

    with jax.named_scope("halo_back"):
        mine = dict(zip(SIDES, back))
        home = {}

        def message(side):
            at = dict(plan.spans(held_blocks(side)))
            pieces = []
            for off in BLOCKS[side[0]](side[1]):
                if off in at:
                    begin = at[off]
                    pieces.append(
                        lax.slice_in_dim(mine[side], begin, begin + plan.rows(off), axis=0)
                    )
                else:
                    pieces.append(home[off])
            return jnp.concatenate(pieces, axis=0)

        for axis, name in (("x", "gx"), ("y", "gy"), ("z", "gz")):
            sides = ((axis, 1), (axis, -1))
            pair = swap(*(message(side) for side in sides), name, sizes[name], back=True)
            for (_, sign), got_back in zip(sides, pair):
                for off, at in plan.spans(BLOCKS[axis](sign)):
                    home[off] = lax.slice_in_dim(got_back, at, at + plan.rows(off), axis=0)
        returned = [
            jnp.concatenate([home[off] for off in blocks], axis=0) for blocks in SEND_GROUPS
        ]

    with jax.named_scope("owner_sums"):
        forces, feature_grad = pl.pallas_call(
            lambda *refs: last_kernel(plan, *refs),
            out_shape=[shape(3, own), shape(own, chans)],
            in_specs=[VMEM] * 10,
            out_specs=[VMEM] * 2,
            scratch_shapes=[pltpu.VMEM((n_send, LANES), F32)],
            compiler_params=PARAMS,
        )(sel, fg, force, w_proj_b, *returned)
    return forces, energy.reshape(own), feature_grad


def solution(mesh):
    shard = P(AXES)
    return jax.shard_map(
        local,
        mesh=mesh,
        in_specs=(
            P(None, AXES),
            P(AXES, None),
            P(AXES, None, None),
            P(AXES, None, None),
            P(AXES, None, None),
            shard,
            shard,
            shard,
        )
        + (P(),) * 8,
        out_specs=(P(None, AXES), shard, P(AXES, None)),
        check_vma=False,
    )
```

```python
import math

import jax
import jax.numpy as jnp
from jax import lax
from jax.experimental import pallas as pl
from jax.experimental.pallas import tpu as pltpu
from jax.sharding import PartitionSpec as P

F32 = jnp.float32
BF16 = jnp.bfloat16
HIGH = lax.Precision.HIGHEST
AXES = ("gx", "gy", "gz")
CHUNK = 512
SUB = 256
WIN = 16
OTHER_BITS = 9
OTHER_MASK = (1 << OTHER_BITS) - 1
LANES = 128
ROOT3 = 1.732


def dot_nn(a, b, precision=None):
    return lax.dot_general(
        a, b, (((1,), (0,)), ((), ())), preferred_element_type=F32, precision=precision
    )


def dot_nt(a, b, precision=None):
    return lax.dot_general(
        a, b, (((1,), (1,)), ((), ())), preferred_element_type=F32, precision=precision
    )


def dot_tn(a, b, precision=None):
    return lax.dot_general(
        a, b, (((0,), (0,)), ((), ())), preferred_element_type=F32, precision=precision
    )


def offset_classes():
    classes = [[], [], []]
    for a in (-1, 0, 1):
        for b in (-1, 0, 1):
            for c in (-1, 0, 1):
                if (a, b, c) != (0, 0, 0):
                    classes[abs(a) + abs(b) + abs(c) - 1].append((a, b, c))
    return classes


CLASSES = offset_classes()


OFFSETS = [off for group in CLASSES for off in group]


def kind(off):
    return abs(off[0]) + abs(off[1]) + abs(off[2]) - 1


class Plan:
    def __init__(self, widths, sizes):
        self.widths = widths
        self.sizes = sizes
        self.x_groups = self.group([off for off in OFFSETS if off[0] != 0], (0,))
        self.p_groups = self.group([off for off in OFFSETS if off[1:] != (0, 0)], (1, 2))
        self.own_plane = [off for g in self.p_groups for off in g if off[0] == 0]
        self.x_faces = [off for off in OFFSETS if off[1:] == (0, 0)]

    def group(self, offs, axes):
        groups = {}
        for off in offs:
            groups.setdefault(tuple(off[a] % self.sizes[a] for a in axes), []).append(off)
        return list(groups.values())

    def live(self, off):
        return self.widths[kind(off)]

    def rows(self, off):
        return self.live(off) + 1

    def total(self, blocks):
        return sum(self.rows(off) for off in blocks)

    def spans(self, blocks):
        at = 0
        for off in blocks:
            yield off, at
            at += self.rows(off)

    def place(self, groups, off):
        for g, blocks in enumerate(groups):
            if off in blocks:
                return g, dict(self.spans(blocks))[off]
        raise KeyError(off)

    def send_x(self, messages, back=False):
        n = self.sizes[0]
        got = []
        for blocks, message in zip(self.x_groups, messages):
            step = -blocks[0][0] if back else blocks[0][0]
            got.append(lax.ppermute(message, "gx", [(i, (i + step) % n) for i in range(n)]))
        return got

    def send_plane(self, messages, back=False):
        ny, nz = self.sizes[1:]
        got = []
        for blocks, message in zip(self.p_groups, messages):
            sy, sz = [-o if back else o for o in blocks[0][1:]]
            pairs = [
                (y * nz + z, (y + sy) % ny * nz + (z + sz) % nz)
                for y in range(ny)
                for z in range(nz)
            ]
            got.append(lax.ppermute(message, ("gy", "gz"), pairs))
        return got


GROUP = 32


def group_rows(count):
    row = lax.broadcasted_iota(jnp.int32, (count, LANES), 0)
    group = lax.broadcasted_iota(jnp.int32, (count, LANES), 1) // GROUP
    return (row == group).astype(F32) * (group < 3).astype(F32)


def diagonal(x):
    row = lax.broadcasted_iota(jnp.int32, x.shape, 0)
    lane = lax.broadcasted_iota(jnp.int32, x.shape, 1)
    return jnp.where((lane & (GROUP - 1)) == row, x, 0.0)


def spread(row, live):
    return diagonal(jnp.broadcast_to(row, (live, LANES)))


def split(x):
    high = x.astype(BF16).astype(F32)
    return high, x - high


def dot_exact(hot, x, dims):
    high, low = split(x)
    both = jnp.concatenate([high, low], axis=1).astype(BF16)
    out = lax.dot_general(hot, both, (dims, ((), ())), preferred_element_type=F32)
    return out[:, 0 : x.shape[1]] + out[:, x.shape[1] :]


def prep_kernel(plan, pos_ref, feat_ref, face_ref, edge_ref, corner_ref, *outs):
    n_x = len(plan.x_groups)
    sends, plane_ref, sel_ref = outs[:n_x], outs[n_x], outs[n_x + 1]
    list_ref = outs[n_x + 2]
    own = feat_ref.shape[0]
    lane = lax.broadcasted_iota(jnp.int32, (1, own), 1)
    list_ref[...] = jnp.zeros_like(list_ref)
    for key in range(face_ref.shape[0]):
        list_ref[key : key + 1, 0 : face_ref.shape[2]] = face_ref[key]
    faces = list_ref[...].T
    columns = (faces, edge_ref[0], corner_ref[0])
    sel_ref[...] = jnp.zeros_like(sel_ref)
    messages = plan.x_groups + [plan.own_plane]
    at = 0
    for blocks in messages:
        for off, begin in plan.spans(blocks):
            key = CLASSES[kind(off)].index(off)
            live = plan.live(off)
            column = columns[kind(off)][0:live, key : key + 1]
            sel_ref[at + begin : at + begin + live, :] = (column == lane).astype(F32)
        at += plan.total(blocks)
    pos = dot_tn(pos_ref[...], group_rows(3), HIGH)
    sel = sel_ref[...]
    rows = dot_nn(sel, feat_ref[...], HIGH)
    places = dot_nn(sel, pos, HIGH)
    at = 0
    for blocks, send in zip(messages, tuple(sends) + (plane_ref,)):
        count = plan.total(blocks)
        send[...] = rows[at : at + count, :]
        for off, begin in plan.spans(blocks):
            live = plan.live(off)
            block = places[at + begin : at + begin + live, :]
            send[begin + live : begin + live + 1, :] = jnp.sum(
                diagonal(block), axis=0, keepdims=True
            )
        at += count


def plane_kernel(plan, *refs):
    n_x = len(plan.x_groups)
    own_ref, came, outs = refs[0], refs[1 : 1 + n_x], refs[1 + n_x :]
    own_at = dict(plan.spans(plan.own_plane))
    for blocks, out in zip(plan.p_groups, outs):
        for off, row in plan.spans(blocks):
            if off[0] == 0:
                src, begin = own_ref, own_at[off]
            else:
                g, begin = plan.place(plan.x_groups, off)
                src = came[g]
            out[row : row + plan.rows(off), :] = src[begin : begin + plan.rows(off), :]


def back_kernel(plan, *refs):
    n_p = len(plan.p_groups)
    face_ref, came, outs = refs[0], refs[1 : 1 + n_p], refs[1 + n_p :]
    face_at = dict(plan.spans(plan.x_faces))
    for blocks, out in zip(plan.x_groups, outs):
        for off, row in plan.spans(blocks):
            if off in face_at:
                src, begin = face_ref, face_at[off]
            else:
                g, begin = plan.place(plan.p_groups, off)
                src = came[g]
            out[row : row + plan.rows(off), :] = src[begin : begin + plan.rows(off), :]


def sort_kernel(dead, count_ref, centre_ref, other_ref, key_ref, bound_ref, turn_ref):
    rows = centre_ref.shape[0]
    regs = turn_ref.shape[0] // 16
    group = regs * 8
    row = lax.broadcasted_iota(jnp.int32, (rows, LANES), 0)
    lane = lax.broadcasted_iota(jnp.int32, (rows, LANES), 1)
    key = jnp.where(
        row * LANES + lane < count_ref[0], (centre_ref[...] << OTHER_BITS) + other_ref[...], dead
    ).astype(F32)
    x = [key[8 * v : 8 * v + 8, :] for v in range(rows // 8)]
    x += [jnp.full((8, LANES), float(dead), F32)] * (regs - len(x))
    s = lax.broadcasted_iota(jnp.int32, (8, LANES), 0)
    ln = lax.broadcasted_iota(jnp.int32, (8, LANES), 1)
    base = ln * group + s * regs

    def sign(k, v):
        return jnp.where(((base + v) & k) == 0, 1.0, -1.0).astype(F32)

    last = [jnp.ones((8, LANES), F32)] * regs
    total = group * LANES
    k = 2
    while k <= total:
        signs = [sign(k, v) for v in range(regs)] if k < total else [1.0] * regs
        x = [x[v] * (last[v] * signs[v]) for v in range(regs)]
        last = signs
        j = k // 2
        while j >= 1:
            if j < regs:
                for v in range(regs):
                    if v & j == 0:
                        a, b = x[v], x[v | j]
                        x[v], x[v | j] = jnp.minimum(a, b), jnp.maximum(a, b)
            else:
                axis, step, size, ids = (
                    (0, j // regs, 8, s) if j < group else (1, j // group, LANES, ln)
                )
                low = (ids & step) == 0
                for v in range(regs):
                    up = pltpu.roll(x[v], size - step, axis)
                    if 2 * step == size:
                        mate = up
                    else:
                        mate = jnp.where(low, up, pltpu.roll(x[v], step, axis))
                    x[v] = jnp.where(low, jnp.minimum(x[v], mate), jnp.maximum(x[v], mate))
            j //= 2
        k *= 2
    least = x[0]
    most = jnp.where(x[0] == float(dead), -1.0, x[0])
    for v in range(1, regs):
        least = jnp.minimum(least, x[v])
        most = jnp.maximum(most, jnp.where(x[v] == float(dead), -1.0, x[v]))
    bound_ref[0:1, :] = jnp.min(least, axis=0, keepdims=True).astype(jnp.int32) >> OTHER_BITS
    bound_ref[1:2, :] = jnp.max(most, axis=0, keepdims=True).astype(jnp.int32) >> OTHER_BITS
    turned = jnp.concatenate(x + [jnp.zeros((LANES - group, LANES), F32)], axis=0).T
    turn_ref[...] = turned
    ratio = LANES // group
    parts = [
        turn_ref[pl.ds(i, rows, stride=ratio), 0:group] for i in range(ratio)
    ]
    done = jnp.concatenate(parts, axis=1).astype(jnp.int32)
    per = key_ref.shape[1]
    for c in range(key_ref.shape[0]):
        key_ref[c] = done[c * per : (c + 1) * per, :]


def weight_kernel(
    feat_ref,
    wa_ref,
    wb_ref,
    wrad_ref,
    w1_ref,
    wenv_ref,
    wval_ref,
    w2_ref,
    wout_ref,
    tab_ref,
    w1t_ref,
    wevt_ref,
    w2t_ref,
    wev_ref,
    wradb_ref,
    wcol_ref,
):
    own, chans = feat_ref.shape

    def flip(w):
        return w.astype(F32).T.astype(BF16)

    w1t_ref[...] = flip(w1_ref[...])
    wevt_ref[0:chans, :] = flip(wenv_ref[...])
    wevt_ref[chans:, :] = flip(wval_ref[...])
    w2t_ref[:, 0:chans] = flip(w2_ref[0:chans, :])
    w2t_ref[:, chans:] = flip(w2_ref[chans:, :])
    wev_ref[:, 0:chans] = wenv_ref[...]
    wev_ref[:, chans:] = wval_ref[...]
    rad = wrad_ref[...]
    wradb_ref[...] = jnp.concatenate([rad, jnp.zeros_like(rad)], axis=0).astype(BF16)
    wcol_ref[...] = jnp.broadcast_to(wout_ref[...].astype(F32), (LANES, chans)).T
    feat = feat_ref[...]
    tab_ref[0:own, :] = dot_nn(feat, wa_ref[...], HIGH)
    tab_ref[own : 2 * own, :] = dot_nn(feat, wb_ref[...], HIGH)
    rad_hi, rad_lo = split(rad)
    tab_ref[2 * own :, :] = jnp.concatenate([rad_hi, rad_hi, rad_lo, jnp.zeros_like(rad)], axis=0)


def harmonics(ux, uy, uz):
    return [
        ux,
        uy,
        uz,
        ROOT3 * ux * uy,
        ROOT3 * uy * uz,
        ROOT3 * ux * uz,
        0.866 * (ux * ux - uy * uy),
        0.5 * (3.0 * uz * uz - 1.0),
    ]


def trig(half):
    turns = jnp.round(half)
    x = math.pi * (half - turns)
    odd = turns - 2.0 * jnp.floor(0.5 * turns)
    sign = 1.0 - 2.0 * odd
    x2 = x * x
    s = jnp.full_like(x, -1.0 / 39916800)
    for coef in (1.0 / 362880, -1.0 / 5040, 1.0 / 120, -1.0 / 6, 1.0):
        s = s * x2 + coef
    c = jnp.full_like(x, 1.0 / 479001600)
    for coef in (-1.0 / 3628800, 1.0 / 40320, -1.0 / 720, 1.0 / 24, -0.5, 1.0):
        c = c * x2 + coef
    return sign * x * s, sign * c


def waves(half, count):
    s1, c1 = trig(half)
    sins, coss = [s1], [c1]
    s0, c0 = jnp.zeros_like(s1), jnp.ones_like(c1)
    for _ in range(count - 1):
        sn = 2.0 * c1 * sins[-1] - s0
        cn = 2.0 * c1 * coss[-1] - c0
        s0, c0 = sins[-1], coss[-1]
        sins.append(sn)
        coss.append(cn)
    return sins, coss


def look_up(table_row, index):
    low = index & (LANES - 1)
    high = index >> 7
    result = jnp.zeros(index.shape, F32)
    for block in range(table_row.shape[1] // LANES):
        part = jnp.broadcast_to(table_row[:, block * LANES : (block + 1) * LANES], index.shape)
        got = jnp.take_along_axis(part, low, axis=1)
        result = jnp.where(high == block, got, result)
    return result


def in_lanes(tile):
    return jnp.concatenate([tile[r : r + 1, :] for r in range(tile.shape[0])], axis=1)


def one_hot(row, base, count):
    near = jnp.clip(row - base, -1, LANES).astype(BF16)
    iota = lax.broadcasted_iota(jnp.int32, (count, row.shape[1]), 0).astype(BF16)
    return jnp.where(iota == near, jnp.ones((), BF16), jnp.zeros((), BF16))


def sorted_size(edges):
    return 1 << (edges - 1).bit_length()


def main_kernel(plan, *refs):
    count_ref, bound_ref, key_ref, pos_ref, wb_ref = refs[:5]
    n_x, n_p = len(plan.x_groups), len(plan.p_groups)
    refs = refs[5:]
    x_refs, p_refs, refs = refs[:n_x], refs[n_x : n_x + n_p], refs[n_x + n_p :]
    w1_ref, w2_ref, half_ref, w1t_ref, wevt_ref, w2t_ref, wev_ref, wradb_ref, wcol_ref = refs[:9]
    ae_ref, own_ref = refs[9:11]
    back_refs, face_ref = refs[11 : 11 + n_p], refs[11 + n_p]
    (
        tab_ref,
        ghost_ref,
        place_ref,
        table_ref,
        y_ref,
        basis_ref,
        geo_ref,
        first_ref,
        dsilu_ref,
        ew_ref,
        val_ref,
        a_ref,
        env_ref,
        denv_ref,
        big_ref,
        dt_ref,
        dv_ref,
        dfa_ref,
        live_ref,
        dy_ref,
        db_ref,
        dr_ref,
        acc_ref,
    ) = refs[12 + n_p :]
    own = pos_ref.shape[1]
    chans = w1_ref.shape[0]
    n_basis = wradb_ref.shape[0] // 2
    rows_all = key_ref.shape[0] * key_ref.shape[1]
    per = CHUNK // LANES
    subs = CHUNK // SUB
    sub_rows = SUB // LANES
    n_ghost = sum(len(c) * w for c, w in zip(CLASSES, plan.widths))
    n_tab = own + n_ghost
    n_sel = own + n_tab

    place_ref[...] = jnp.zeros_like(place_ref)
    at = 0
    for off in OFFSETS:
        live = plan.live(off)
        if off in plan.x_faces:
            g, begin = plan.place(plan.x_groups, off)
            message = x_refs[g]
        else:
            g, begin = plan.place(plan.p_groups, off)
            message = p_refs[g]
        ghost_ref[at : at + live, :] = message[begin : begin + live, :]
        place_ref[at : at + live, :] = spread(message[begin + live : begin + live + 1, :], live)
        at += live
    ghost_pos = dot_nt(group_rows(8), place_ref[...], HIGH)
    pos_t = jnp.concatenate([pos_ref[...], ghost_pos[0:3, :]], axis=1)
    f_hi, f_lo = split(ghost_ref[...])
    w_hi, w_lo = split(wb_ref[...])
    tab_ref[0 : 2 * own, :] = half_ref[0 : 2 * own, :]
    tab_ref[2 * own : n_sel, :] = dot_nn(
        jnp.concatenate([f_hi, f_lo, f_hi], axis=1).astype(BF16),
        jnp.concatenate([w_hi, w_hi, w_lo], axis=0).astype(BF16),
    )
    tab_ref[n_sel:, :] = half_ref[2 * own :, :]
    table_ref[...] = tab_ref[...].T.astype(BF16)

    keys = key_ref[...].reshape(rows_all, LANES)
    centre = keys >> OTHER_BITS
    other = keys & OTHER_MASK
    valid = (keys != (own - 1) * (OTHER_MASK + 1) + OTHER_MASK).astype(F32)
    r = [
        look_up(pos_t[a : a + 1, :], other) - look_up(pos_t[a : a + 1, 0:LANES], centre)
        for a in range(3)
    ]
    d2 = r[0] * r[0] + r[1] * r[1] + r[2] * r[2] + 0.01
    dist = jnp.sqrt(d2)
    inv = 1.0 / dist
    q = 1.0 / (1.0 + 0.25 * d2)
    envelope = q * q
    unit = [x * inv for x in r]
    for m, comp in enumerate(harmonics(*unit)):
        y_ref[pl.ds(m, rows_all, stride=8), :] = comp
    sins, _ = waves(0.5 * dist, n_basis)
    scale = envelope * inv
    for n in range(n_basis):
        basis_ref[pl.ds(n, rows_all, stride=n_basis), :] = sins[n] * scale
    for i, plane in enumerate((unit[0], unit[1], unit[2], dist, inv, q, envelope * valid, valid)):
        geo_ref[i] = plane.reshape(geo_ref.shape[1:])

    env_ref[...] = jnp.zeros_like(env_ref)
    denv_ref[...] = jnp.zeros_like(denv_ref)
    ae_ref[...] = jnp.zeros_like(ae_ref)
    acc_ref[...] = jnp.zeros_like(acc_ref)
    dr_ref[...] = jnp.zeros_like(dr_ref)

    bound_total = sorted_size(rows_all * LANES)
    n_chunks = lax.div(count_ref[0] + (CHUNK - 1), jnp.int32(CHUNK))

    def window(k, s):
        groups = bound_ref.shape[1] * SUB // bound_total
        first = (k * subs + s) * groups
        low = bound_ref[0, first]
        high = low
        for g in range(groups):
            high = jnp.maximum(high, bound_ref[1, first + g])
        start = pl.multiple_of((low >> 3) << 3, 8)
        more = lax.div(high - start, jnp.int32(WIN))
        return start, more

    def any_more(k):
        most = window(k, 0)[1]
        for s in range(1, subs):
            most = jnp.maximum(most, window(k, s)[1])
        return most > 0

    def window_hot(k, s, start):
        rows = key_ref[k, s * sub_rows : (s + 1) * sub_rows, :]
        crow = in_lanes(rows >> OTHER_BITS) - start
        return lax.broadcasted_iota(jnp.int32, (WIN, SUB), 0) == crow

    def select(k, s, start):
        row = k * per + s * sub_rows
        hot = window_hot(k, s, start)
        tiles = [
            y_ref[pl.ds(pl.multiple_of((row + j) * 8, 8), 8), :] for j in range(sub_rows)
        ]
        ys = jnp.concatenate(tiles, axis=1)
        parts = [hot.astype(F32)]
        for m in range(8):
            parts.append(jnp.where(hot, ys[m : m + 1, :], 0.0))
        return jnp.concatenate(parts, axis=0).astype(BF16)

    def load_window(ref, start):
        return jnp.concatenate(
            [ref[m, pl.ds(start, WIN), :] for m in range(9)], axis=0
        ).astype(BF16)

    def add_window(ref, start, rows):
        for m in range(9):
            ref[m, pl.ds(start, WIN), :] += rows[m * WIN : (m + 1) * WIN, :]

    def sub_lanes(s):
        return slice(s * SUB, (s + 1) * SUB)

    def more_windows(k, body):
        @pl.when(any_more(k))
        def _():
            for s in range(subs):
                start, more = window(k, s)

                def step(t, carry, s=s, start=start):
                    body(s, pl.multiple_of(start + t * WIN, 8))
                    return carry

                lax.fori_loop(1, more + 1, step, 0)

    def row_of(plane, k):
        return in_lanes(geo_ref[plane, k])

    def phase_a(k, carry):
        kt = key_ref[k]
        crow = in_lanes(kt >> OTHER_BITS)
        orow = in_lanes(kt & OTHER_MASK)
        hots = [one_hot(crow, 0, own)]
        for base in range(0, n_tab, LANES):
            hots.append(one_hot(orow, base, min(LANES, n_tab - base)))
        tiles = [
            basis_ref[pl.ds(pl.multiple_of((k * per + j) * n_basis, 8), n_basis), :]
            for j in range(per)
        ]
        basis = jnp.concatenate(tiles, axis=1)
        b_hi, b_lo = split(basis)
        hots.append(jnp.concatenate([b_hi, b_lo], axis=0).astype(BF16))
        hots.append(jnp.concatenate([b_hi, jnp.zeros_like(b_hi)], axis=0).astype(BF16))
        mixed = dot_nn(table_ref[...], jnp.concatenate(hots, axis=0)).astype(BF16)
        z1 = dot_nn(w1t_ref[...], mixed)
        sg = 0.5 + 0.5 * jnp.tanh(0.5 * z1)
        first = z1 * sg
        dsilu_ref[k] = (sg + first * (1.0 - sg)).astype(BF16)
        first = first.astype(BF16)
        first_ref[k] = first
        both = dot_nn(wevt_ref[...], first)
        ew = (both[0:chans] * row_of(6, k)).astype(BF16)
        ew_ref[k] = ew
        val_ref[k] = both[chans:].astype(BF16)
        for s in range(subs):
            start, _ = window(k, s)
            a = select(k, s, start)
            a_ref[k * subs + s] = a
            add_window(env_ref, start, dot_nt(a, ew[:, sub_lanes(s)]))

        def again(s, start):
            a = select(k, s, start)
            add_window(env_ref, start, dot_nt(a, ew_ref[k, :, sub_lanes(s)]))

        more_windows(k, again)
        return carry

    lax.fori_loop(0, n_chunks, phase_a, 0)

    def phase_b(k, carry):
        for s in range(subs):
            start, _ = window(k, s)
            big_ref[:, sub_lanes(s)] = dot_tn(load_window(env_ref, start), a_ref[k * subs + s])

        def again_total(s, start):
            big_ref[:, sub_lanes(s)] += dot_tn(load_window(env_ref, start), select(k, s, start))

        more_windows(k, again_total)
        total = 0.2 * big_ref[...]
        value = val_ref[k].astype(F32)
        scalar = (value * total).astype(BF16)
        z2 = dot_nn(w2t_ref[...], jnp.concatenate([first_ref[k], scalar], axis=0))
        sg = 0.5 + 0.5 * jnp.tanh(0.5 * z2)
        second = z2 * sg
        wcol = jnp.concatenate([wcol_ref[...]] * per, axis=1)
        ee = jnp.sum(second.astype(BF16).astype(F32) * wcol, axis=0, keepdims=True)
        envv = row_of(6, k)
        dy_ref[9, :, :] = jnp.zeros((per, LANES), F32)
        live = ee * row_of(7, k)
        for j in range(per):
            live_ref[k, j : j + 1, :] = live[:, j * LANES : (j + 1) * LANES]
        energy = ee * envv
        dz2 = ((wcol * envv) * (sg + second * (1.0 - sg))).astype(BF16)
        dj = dot_nn(w2_ref[...], dz2)
        dfa_ref[k] = dj[0:chans].astype(BF16)
        dscalar = dj[chans:]
        dt = (0.2 * value * dscalar).astype(BF16)
        dt_ref[k] = dt
        dv_ref[k] = (total * dscalar).astype(BF16)

        def add_energy(s, start):
            hot = window_hot(k, s, start)
            part = jnp.where(hot, energy[:, sub_lanes(s)], 0.0)
            half = part[:, 0:LANES]
            for j in range(1, sub_rows):
                half = half + part[:, j * LANES : (j + 1) * LANES]
            ae_ref[pl.ds(start, WIN), :] += half

        for s in range(subs):
            start, _ = window(k, s)
            add_window(denv_ref, start, dot_nt(a_ref[k * subs + s], dt[:, sub_lanes(s)]))
            add_energy(s, start)

        def again(s, start):
            add_window(
                denv_ref, start, dot_nt(select(k, s, start), dt_ref[k, :, sub_lanes(s)])
            )
            add_energy(s, start)

        more_windows(k, again)
        return carry

    lax.fori_loop(0, n_chunks, phase_b, 0)

    def phase_c(k, carry):
        def env_terms(s, start, a, fresh):
            e_win = load_window(env_ref, start)
            d_win = load_window(denv_ref, start)
            dew = dot_tn(d_win, a)
            pair = jnp.concatenate(
                [dt_ref[k, :, sub_lanes(s)], ew_ref[k, :, sub_lanes(s)]], axis=0
            )
            prods = dot_nn(jnp.concatenate([e_win, d_win], axis=1), pair)
            hot = a[0:WIN].astype(F32)
            if fresh:
                big_ref[:, sub_lanes(s)] = dew
            else:
                big_ref[:, sub_lanes(s)] += dew
            for m in range(1, 9):
                row = jnp.sum(prods[m * WIN : (m + 1) * WIN] * hot, axis=0, keepdims=True)
                for j in range(sub_rows):
                    at = s * sub_rows + j
                    piece = row[:, j * LANES : (j + 1) * LANES]
                    if fresh:
                        dy_ref[m, at : at + 1, :] = piece
                    else:
                        dy_ref[m, at : at + 1, :] += piece

        for s in range(subs):
            start, _ = window(k, s)
            env_terms(s, start, a_ref[k * subs + s], True)
        more_windows(k, lambda s, start: env_terms(s, start, select(k, s, start), False))
        dew = big_ref[...]
        dpre = (dew * row_of(6, k)).astype(BF16)
        denv_row = jnp.sum(dew * ew_ref[k].astype(F32), axis=0, keepdims=True)
        for j in range(per):
            dy_ref[0, j : j + 1, :] = denv_row[:, j * LANES : (j + 1) * LANES]
        dfirst = dfa_ref[k].astype(F32) + dot_nn(
            wev_ref[...], jnp.concatenate([dpre, dv_ref[k]], axis=0)
        )
        dz1 = (dfirst * dsilu_ref[k].astype(F32)).astype(BF16)
        dmixed = dot_nn(w1_ref[...], dz1).astype(BF16)
        dbasis = dot_nn(wradb_ref[...], dmixed)
        for j in range(per):
            db_ref[j * n_basis : (j + 1) * n_basis, :] = dbasis[
                0:n_basis, j * LANES : (j + 1) * LANES
            ]
        ux, uy, uz, dist, inv, q = [geo_ref[i, k] for i in range(6)]
        envelope = q * q
        g = envelope * inv
        denvelope = -(q * envelope) * dist
        dg = (denvelope - g) * inv
        sins, coss = waves(0.5 * dist, n_basis)
        denv_direct = live_ref[k] + dy_ref[0] / envelope
        ddist = denv_direct * denvelope
        for n in range(n_basis):
            db = db_ref[pl.ds(n, per, stride=n_basis), :]
            ddist = ddist + db * (coss[n] * ((n + 1) * math.pi / 2.0) * g + sins[n] * dg)
        y = [dy_ref[m] for m in range(9)]
        gx = y[1] + ROOT3 * (uy * y[4] + uz * y[6]) + (2.0 * 0.866) * ux * y[7]
        gy = y[2] + ROOT3 * (ux * y[4] + uz * y[5]) - (2.0 * 0.866) * uy * y[7]
        gz = y[3] + ROOT3 * (uy * y[5] + ux * y[6]) + 3.0 * uz * y[8]
        along = ddist - inv * (gx * ux + gy * uy + gz * uz)
        for i, (gu, u) in enumerate(((gx, ux), (gy, uy), (gz, uz))):
            hi, lo = split(inv * gu + along * u)
            dr_ref[pl.ds(i, per, stride=16), :] = hi
            dr_ref[pl.ds(3 + i, per, stride=16), :] = lo
        dr = jnp.concatenate([dr_ref[j * 16 : (j + 1) * 16, :] for j in range(per)], axis=1)
        kt = key_ref[k]
        crow = in_lanes(kt >> OTHER_BITS)
        orow = in_lanes(kt & OTHER_MASK)
        hots = [one_hot(crow, 0, own)]
        for base in range(0, n_tab, LANES):
            hots.append(one_hot(orow, base, min(LANES, n_tab - base)))
        sums = dot_nt(
            jnp.concatenate(hots, axis=0),
            jnp.concatenate([dmixed, dr.astype(BF16)], axis=0),
        )
        acc_ref[:, 0:chans] += sums[:, 0:chans]
        acc_ref[:, chans : chans + 16] += sums[:, chans:]
        return carry

    lax.fori_loop(0, n_chunks, phase_c, 0)

    own_ref[...] = acc_ref[0 : 2 * own, :]
    row = lax.broadcasted_iota(jnp.int32, (LANES, LANES), 0)
    group = lax.broadcasted_iota(jnp.int32, (LANES, LANES), 1) // GROUP
    both = ((group < 3) & ((row == group) | (row == group + 3))).astype(F32)
    places = dot_nn(acc_ref[2 * own :, LANES:], both, HIGH)
    found = {}
    at = 2 * own
    for off in OFFSETS:
        found[off] = at
        at += plan.live(off)
    for blocks, ref in zip(plan.p_groups + [plan.x_faces], tuple(back_refs) + (face_ref,)):
        for off, row in plan.spans(blocks):
            live = plan.live(off)
            at = found[off]
            ref[row : row + live, :] = acc_ref[at : at + live, 0:chans]
            block = places[at - 2 * own : at - 2 * own + live, :]
            ref[row + live : row + live + 1, :] = jnp.sum(diagonal(block), axis=0, keepdims=True)


def own_kernel(ae_ref, own_ref, wa_ref, wb_ref, energy_ref, fg_ref, force_ref):
    chans = wa_ref.shape[1]
    own = force_ref.shape[1]
    energy_ref[...] = jnp.sum(ae_ref[0:own, :].T, axis=0, keepdims=True)
    fg_ref[...] = dot_nt(own_ref[0:own, 0:chans], wa_ref[...], HIGH) + dot_nt(
        own_ref[own:, 0:chans], wb_ref[...], HIGH
    )
    force = (own_ref[own:, LANES:] - own_ref[0:own, LANES:]).T
    force_ref[...] = force[0:3, :] + force[3:6, :]


def last_kernel(plan, sel_ref, fg_ref, force_ref, wb_ref, *refs):
    n_x, n_p = len(plan.x_groups), len(plan.p_groups)
    x_refs, p_refs = refs[:n_x], refs[n_x : n_x + n_p]
    out_force_ref, out_fg_ref, both_ref = refs[n_x + n_p :]
    both_ref[...] = jnp.zeros_like(both_ref)
    chans = fg_ref.shape[1]
    at = 0
    for blocks in plan.x_groups + [plan.own_plane]:
        for off, row in plan.spans(blocks):
            live = plan.live(off)
            if off[0] != 0:
                g, begin = plan.place(plan.x_groups, off)
                src = x_refs[g]
            else:
                g, begin = plan.place(plan.p_groups, off)
                src = p_refs[g]
            here = slice(at + row, at + row + live)
            both_ref[here, 0:chans] = src[begin : begin + live, :]
            both_ref[here, chans:] = spread(src[begin + live : begin + live + 1, :], live)
        at += plan.total(blocks)
    sums = dot_exact(sel_ref[...].astype(BF16), both_ref[...], ((0,), (0,)))
    out_fg_ref[...] = fg_ref[...] + dot_nt(sums[:, 0:chans], wb_ref[...], HIGH)
    total = dot_nt(group_rows(8), sums[:, chans:], HIGH)
    out_force_ref[...] = -(force_ref[...] + total[0:3, :])


VMEM = pl.BlockSpec(memory_space=pltpu.VMEM)
SMEM = pl.BlockSpec(memory_space=pltpu.SMEM)
PARAMS = pltpu.CompilerParams(vmem_limit_bytes=52 * 2**20)


def shape(*dims, dtype=F32):
    return jax.ShapeDtypeStruct(dims, dtype)


def local(
    positions,
    atom_features,
    send_face,
    send_edge,
    send_corner,
    centre,
    other,
    edge_count,
    w_proj_a,
    w_proj_b,
    w_radial,
    w_first,
    w_env,
    w_value,
    w_second,
    w_out,
):
    own, chans = atom_features.shape
    edges = centre.shape[0]
    n_basis = w_radial.shape[0]
    plan = Plan(
        [send_face.shape[2], send_edge.shape[2], send_corner.shape[2]],
        [lax.axis_size(axis) for axis in AXES],
    )
    n_ghost = sum(len(c) * w for c, w in zip(CLASSES, plan.widths))
    n_sel = 2 * own + n_ghost
    n_send = sum(plan.total(blocks) for blocks in plan.x_groups) + plan.total(plan.own_plane)
    n_table = n_sel + 4 * n_basis
    edges_up = -(-edges // CHUNK) * CHUNK
    n_rows = edges_up // LANES
    n_chunks = edges_up // CHUNK

    with jax.named_scope("prep"):
        *sends, own_rows, sel = pl.pallas_call(
            lambda *refs: prep_kernel(plan, *refs),
            out_shape=[shape(plan.total(blocks), chans) for blocks in plan.x_groups]
            + [shape(plan.total(plan.own_plane), chans), shape(n_send, own)],
            in_specs=[VMEM] * 5,
            out_specs=[VMEM] * (len(plan.x_groups) + 2),
            scratch_shapes=[pltpu.VMEM((LANES, LANES), jnp.int32)],
            compiler_params=PARAMS,
        )(
            positions,
            atom_features,
            jnp.transpose(send_face, (1, 0, 2)),
            jnp.transpose(send_edge, (0, 2, 1)),
            jnp.transpose(send_corner, (0, 2, 1)),
        )

    with jax.named_scope("halo_x"):
        came_x = plan.send_x(sends)

    with jax.named_scope("group_edges"):
        dead = (own - 1) * (OTHER_MASK + 1) + OTHER_MASK
        pad = [(0, edges_up - edges)]
        regs = max(sorted_size(edges_up) // (8 * LANES), 1)
        key, bounds = pl.pallas_call(
            lambda *refs: sort_kernel(dead, *refs),
            out_shape=[
                shape(n_chunks, CHUNK // LANES, LANES, dtype=jnp.int32),
                shape(2, LANES, dtype=jnp.int32),
            ],
            in_specs=[SMEM, VMEM, VMEM],
            out_specs=[VMEM] * 2,
            scratch_shapes=[pltpu.VMEM((16 * regs, LANES), F32)],
            compiler_params=PARAMS,
        )(
            edge_count,
            jnp.pad(centre, pad).reshape(n_rows, LANES),
            jnp.pad(other, pad).reshape(n_rows, LANES),
        )

    with jax.named_scope("weights"):
        half, *weights = pl.pallas_call(
            weight_kernel,
            out_shape=[
                shape(2 * own + 4 * n_basis, chans),
                shape(chans, chans, dtype=BF16),
                shape(2 * chans, chans, dtype=BF16),
                shape(chans, 2 * chans, dtype=BF16),
                shape(chans, 2 * chans, dtype=BF16),
                shape(2 * n_basis, chans, dtype=BF16),
                shape(chans, LANES),
            ],
            in_specs=[VMEM] * 9,
            out_specs=[VMEM] * 7,
            compiler_params=PARAMS,
        )(
            atom_features,
            w_proj_a,
            w_proj_b,
            w_radial,
            w_first,
            w_env,
            w_value,
            w_second,
            w_out.reshape(1, -1),
        )

    with jax.named_scope("plane_messages"):
        sends = pl.pallas_call(
            lambda *refs: plane_kernel(plan, *refs),
            out_shape=[shape(plan.total(blocks), chans) for blocks in plan.p_groups],
            in_specs=[VMEM] * (1 + len(came_x)),
            out_specs=[VMEM] * len(plan.p_groups),
            compiler_params=PARAMS,
        )(own_rows, *came_x)

    with jax.named_scope("halo_plane"):
        came_p = plan.send_plane(sends)

    planes = (n_chunks, chans, CHUNK)
    scratch = [
        pltpu.VMEM((n_table, chans), F32),
        pltpu.VMEM((n_ghost, chans), F32),
        pltpu.VMEM((-(-n_ghost // LANES) * LANES, LANES), F32),
        pltpu.VMEM((chans, n_table), BF16),
        pltpu.VMEM((n_rows * 8, LANES), F32),
        pltpu.VMEM((n_rows * n_basis, LANES), F32),
        pltpu.VMEM((8, n_chunks, CHUNK // LANES, LANES), F32),
        pltpu.VMEM(planes, BF16),
        pltpu.VMEM(planes, BF16),
        pltpu.VMEM(planes, BF16),
        pltpu.VMEM(planes, BF16),
        pltpu.VMEM((edges_up // SUB, 9 * WIN, SUB), BF16),
        pltpu.VMEM((9, own + WIN, chans), F32),
        pltpu.VMEM((9, own + WIN, chans), F32),
        pltpu.VMEM((chans, CHUNK), F32),
        pltpu.VMEM(planes, BF16),
        pltpu.VMEM(planes, BF16),
        pltpu.VMEM(planes, BF16),
        pltpu.VMEM((n_chunks, CHUNK // LANES, LANES), F32),
        pltpu.VMEM((10, CHUNK // LANES, LANES), F32),
        pltpu.VMEM((CHUNK // LANES * n_basis, LANES), F32),
        pltpu.VMEM((CHUNK // LANES * 16, LANES), F32),
        pltpu.VMEM((n_sel, 2 * LANES), F32),
    ]
    with jax.named_scope("layer"):
        atom_sums, own_sums, *back, x_back = pl.pallas_call(
            lambda *refs: main_kernel(plan, *refs),
            out_shape=[shape(own + WIN, LANES), shape(2 * own, 2 * LANES)]
            + [shape(plan.total(blocks), chans) for blocks in plan.p_groups + [plan.x_faces]],
            in_specs=[SMEM, SMEM] + [VMEM] * (12 + len(came_x) + len(came_p)),
            out_specs=[VMEM] * (3 + len(plan.p_groups)),
            scratch_shapes=scratch,
            compiler_params=PARAMS,
        )(
            edge_count,
            bounds,
            key,
            positions,
            w_proj_b,
            *came_x,
            *came_p,
            w_first,
            w_second,
            half,
            *weights,
        )

    with jax.named_scope("halo_plane_back"):
        back_p = plan.send_plane(back, back=True)

    with jax.named_scope("own_part"):
        energy, fg, force = pl.pallas_call(
            own_kernel,
            out_shape=[shape(1, own), shape(own, chans), shape(3, own)],
            in_specs=[VMEM] * 4,
            out_specs=[VMEM] * 3,
            compiler_params=PARAMS,
        )(atom_sums, own_sums, w_proj_a, w_proj_b)

    with jax.named_scope("x_messages"):
        sends = pl.pallas_call(
            lambda *refs: back_kernel(plan, *refs),
            out_shape=[shape(plan.total(blocks), chans) for blocks in plan.x_groups],
            in_specs=[VMEM] * (1 + len(back_p)),
            out_specs=[VMEM] * len(plan.x_groups),
            compiler_params=PARAMS,
        )(x_back, *back_p)

    with jax.named_scope("halo_x_back"):
        back_x = plan.send_x(sends, back=True)

    with jax.named_scope("owner_sums"):
        forces, feature_grad = pl.pallas_call(
            lambda *refs: last_kernel(plan, *refs),
            out_shape=[shape(3, own), shape(own, chans)],
            in_specs=[VMEM] * (4 + len(back_x) + len(back_p)),
            out_specs=[VMEM] * 2,
            scratch_shapes=[pltpu.VMEM((n_send, chans + LANES), F32)],
            compiler_params=PARAMS,
        )(sel, fg, force, w_proj_b, *back_x, *back_p)
    return forces, energy.reshape(own), feature_grad


def solution(mesh):
    shard = P(AXES)
    return jax.shard_map(
        local,
        mesh=mesh,
        in_specs=(
            P(None, AXES),
            P(AXES, None),
            P(AXES, None, None),
            P(AXES, None, None),
            P(AXES, None, None),
            shard,
            shard,
            shard,
        )
        + (P(),) * 8,
        out_specs=(P(None, AXES), shard, P(AXES, None)),
        check_vma=False,
    )
```

```python
import math

import jax
import jax.numpy as jnp
from jax import lax
from jax.experimental import pallas as pl
from jax.experimental.pallas import tpu as pltpu
from jax.sharding import PartitionSpec as P

F32 = jnp.float32
BF16 = jnp.bfloat16
HIGH = lax.Precision.HIGHEST
AXES = ("gx", "gy", "gz")
CHUNK = 2048
SUB = 256
WIN = 16
OTHER_BITS = 9
OTHER_MASK = (1 << OTHER_BITS) - 1
LANES = 128
ROOT3 = 1.732


VMEM = pl.BlockSpec(memory_space=pltpu.VMEM)
SMEM = pl.BlockSpec(memory_space=pltpu.SMEM)
PARAMS = pltpu.CompilerParams(vmem_limit_bytes=52 * 2**20)


def shape(*dims, dtype=F32):
    return jax.ShapeDtypeStruct(dims, dtype)


def dot_nn(a, b, precision=None):
    return lax.dot_general(
        a, b, (((1,), (0,)), ((), ())), preferred_element_type=F32, precision=precision
    )


def dot_nt(a, b, precision=None):
    return lax.dot_general(
        a, b, (((1,), (1,)), ((), ())), preferred_element_type=F32, precision=precision
    )


def dot_tn(a, b, precision=None):
    return lax.dot_general(
        a, b, (((0,), (0,)), ((), ())), preferred_element_type=F32, precision=precision
    )


def offset_classes():
    classes = [[], [], []]
    for a in (-1, 0, 1):
        for b in (-1, 0, 1):
            for c in (-1, 0, 1):
                if (a, b, c) != (0, 0, 0):
                    classes[abs(a) + abs(b) + abs(c) - 1].append((a, b, c))
    return classes


CLASSES = offset_classes()


OFFSETS = [off for group in CLASSES for off in group]


def kind(off):
    return abs(off[0]) + abs(off[1]) + abs(off[2]) - 1


class Plan:
    def __init__(self, widths, sizes):
        self.widths = widths
        self.sizes = sizes
        self.groups = [self.group(a) for a in range(3)]
        self.own_rest = [off for off in OFFSETS if off[2] == 0]
        self.held_rest = [off for off in OFFSETS if off[0] == 0]

    def group(self, a):
        groups = {}
        for off in OFFSETS:
            if off[a] != 0:
                groups.setdefault(off[a] % self.sizes[a], []).append(off)
        return list(groups.values())

    def live(self, off):
        return self.widths[kind(off)]

    def rows(self, off):
        return self.live(off) + 1

    def total(self, blocks):
        return sum(self.rows(off) for off in blocks)

    def spans(self, blocks):
        at = 0
        for off in blocks:
            yield off, at
            at += self.rows(off)

    def place(self, a, off):
        for g, blocks in enumerate(self.groups[a]):
            if off in blocks:
                return g, dict(self.spans(blocks))[off]
        raise KeyError(off)

    def find(self, came, axes, rest_ref, rest, off):
        for a in axes:
            if off[a] != 0:
                g, begin = self.place(a, off)
                return came[a][g], begin
        return rest_ref, dict(self.spans(rest))[off]

    def cut(self, refs, *axes):
        came = {}
        for a in axes:
            n = len(self.groups[a])
            came[a], refs = refs[:n], refs[n:]
        return came, refs

    def shapes(self, a, chans):
        return [shape(self.total(blocks), chans) for blocks in self.groups[a]]

    def send(self, a, messages, back=False):
        n = self.sizes[a]
        got = []
        for blocks, message in zip(self.groups[a], messages):
            step = -blocks[0][a] if back else blocks[0][a]
            got.append(lax.ppermute(message, AXES[a], [(i, (i + step) % n) for i in range(n)]))
        return got


GROUP = 32


def group_rows(count):
    row = lax.broadcasted_iota(jnp.int32, (count, LANES), 0)
    group = lax.broadcasted_iota(jnp.int32, (count, LANES), 1) // GROUP
    return (row == group).astype(F32) * (group < 3).astype(F32)


def diagonal(x):
    row = lax.broadcasted_iota(jnp.int32, x.shape, 0)
    lane = lax.broadcasted_iota(jnp.int32, x.shape, 1)
    return jnp.where((lane & (GROUP - 1)) == row, x, 0.0)


def spread(row, live):
    return diagonal(jnp.broadcast_to(row, (live, LANES)))


def split(x):
    high = x.astype(BF16).astype(F32)
    return high, x - high


def dot_exact(hot, x, dims):
    high, low = split(x)
    both = jnp.concatenate([high, low], axis=1).astype(BF16)
    out = lax.dot_general(hot, both, (dims, ((), ())), preferred_element_type=F32)
    return out[:, 0 : x.shape[1]] + out[:, x.shape[1] :]


def prep_kernel(plan, rows_ref, list_ref, *outs):
    n_z = len(plan.groups[2])
    sends, rest_ref, sel_ref, turn_ref = outs[:n_z], outs[n_z], outs[n_z + 1], outs[n_z + 2]
    own = sel_ref.shape[1]
    lane = lax.broadcasted_iota(jnp.int32, (1, own), 1)
    turn_ref[...] = jnp.zeros_like(turn_ref)
    turn_ref[0 : list_ref.shape[0], 0 : list_ref.shape[1]] = list_ref[...]
    columns = turn_ref[...].T
    sel_ref[...] = jnp.zeros_like(sel_ref)
    messages = plan.groups[2] + [plan.own_rest]
    at = 0
    for blocks in messages:
        for off, begin in plan.spans(blocks):
            key = OFFSETS.index(off)
            live = plan.live(off)
            column = columns[0:live, key : key + 1]
            sel_ref[at + begin : at + begin + live, :] = (column == lane).astype(F32)
        at += plan.total(blocks)
    pos = dot_tn(rows_ref[own : own + 3, :], group_rows(3), HIGH)
    sel = sel_ref[...]
    rows = dot_nn(sel, rows_ref[0:own, :], HIGH)
    places = dot_nn(sel, pos, HIGH)
    at = 0
    for blocks, send in zip(messages, tuple(sends) + (rest_ref,)):
        count = plan.total(blocks)
        send[...] = rows[at : at + count, :]
        for off, begin in plan.spans(blocks):
            live = plan.live(off)
            block = places[at + begin : at + begin + live, :]
            send[begin + live : begin + live + 1, :] = jnp.sum(
                diagonal(block), axis=0, keepdims=True
            )
        at += count


def glue_kernel(plan, a, axes, rest, *refs):
    rest_ref = refs[0]
    came, outs = plan.cut(refs[1:], *axes)
    for blocks, out in zip(plan.groups[a], outs):
        for off, row in plan.spans(blocks):
            src, begin = plan.find(came, axes, rest_ref, rest, off)
            out[row : row + plan.rows(off), :] = src[begin : begin + plan.rows(off), :]


def glue(plan, a, axes, rest, rest_rows, came):
    given = [rest_rows] + [message for axis in axes for message in came[axis]]
    outs = plan.shapes(a, rest_rows.shape[1])
    return pl.pallas_call(
        lambda *refs: glue_kernel(plan, a, axes, rest, *refs),
        out_shape=outs,
        in_specs=[VMEM] * len(given),
        out_specs=[VMEM] * len(outs),
        compiler_params=PARAMS,
    )(*given)


def sort_kernel(dead, count_ref, centre_ref, other_ref, key_ref, bound_ref, turn_ref):
    rows = centre_ref.shape[0]
    regs = turn_ref.shape[0] // 16
    group = regs * 8
    row = lax.broadcasted_iota(jnp.int32, (rows, LANES), 0)
    lane = lax.broadcasted_iota(jnp.int32, (rows, LANES), 1)
    key = jnp.where(
        row * LANES + lane < count_ref[0], (centre_ref[...] << OTHER_BITS) + other_ref[...], dead
    ).astype(F32)
    x = [key[8 * v : 8 * v + 8, :] for v in range(rows // 8)]
    x += [jnp.full((8, LANES), float(dead), F32)] * (regs - len(x))
    s = lax.broadcasted_iota(jnp.int32, (8, LANES), 0)
    ln = lax.broadcasted_iota(jnp.int32, (8, LANES), 1)
    base = ln * group + s * regs

    def sign(k, v):
        return jnp.where(((base + v) & k) == 0, 1.0, -1.0).astype(F32)

    last = [jnp.ones((8, LANES), F32)] * regs
    total = group * LANES
    k = 2
    while k <= total:
        signs = [sign(k, v) for v in range(regs)] if k < total else [1.0] * regs
        x = [x[v] * (last[v] * signs[v]) for v in range(regs)]
        last = signs
        j = k // 2
        while j >= 1:
            if j < regs:
                for v in range(regs):
                    if v & j == 0:
                        a, b = x[v], x[v | j]
                        x[v], x[v | j] = jnp.minimum(a, b), jnp.maximum(a, b)
            else:
                axis, step, size, ids = (
                    (0, j // regs, 8, s) if j < group else (1, j // group, LANES, ln)
                )
                low = (ids & step) == 0
                for v in range(regs):
                    up = pltpu.roll(x[v], size - step, axis)
                    if 2 * step == size:
                        mate = up
                    else:
                        mate = jnp.where(low, up, pltpu.roll(x[v], step, axis))
                    x[v] = jnp.where(low, jnp.minimum(x[v], mate), jnp.maximum(x[v], mate))
            j //= 2
        k *= 2
    least = x[0]
    most = jnp.where(x[0] == float(dead), -1.0, x[0])
    for v in range(1, regs):
        least = jnp.minimum(least, x[v])
        most = jnp.maximum(most, jnp.where(x[v] == float(dead), -1.0, x[v]))
    bound_ref[0:1, :] = jnp.min(least, axis=0, keepdims=True).astype(jnp.int32) >> OTHER_BITS
    bound_ref[1:2, :] = jnp.max(most, axis=0, keepdims=True).astype(jnp.int32) >> OTHER_BITS
    turned = jnp.concatenate(x + [jnp.zeros((LANES - group, LANES), F32)], axis=0).T
    turn_ref[...] = turned
    ratio = LANES // group
    parts = [
        turn_ref[pl.ds(i, rows, stride=ratio), 0:group] for i in range(ratio)
    ]
    done = jnp.concatenate(parts, axis=1).astype(jnp.int32)
    per = key_ref.shape[1]
    for c in range(key_ref.shape[0]):
        key_ref[c] = done[c * per : (c + 1) * per, :]


def weight_kernel(
    rows_ref,
    wide_ref,
    half_ref,
    tab_ref,
    w1t_ref,
    wevt_ref,
    w2t_ref,
    w1_ref,
    wev_ref,
    w2_ref,
    wradb_ref,
    wcol_ref,
):
    chans = wide_ref.shape[1]
    own = rows_ref.shape[0] - 3
    wa, wb, rad = wide_ref[0:chans, :], wide_ref[chans : 2 * chans, :], wide_ref[2 * chans :, :]
    w1, wenv, wval = [half_ref[i * chans : (i + 1) * chans, :] for i in range(3)]
    w2 = half_ref[3 * chans : 5 * chans, :]

    def flip(w):
        return w.astype(F32).T.astype(BF16)

    w1_ref[...] = w1
    w2_ref[...] = w2
    w1t_ref[...] = flip(w1)
    wevt_ref[0:chans, :] = flip(wenv)
    wevt_ref[chans:, :] = flip(wval)
    w2t_ref[:, 0:chans] = flip(w2[0:chans, :])
    w2t_ref[:, chans:] = flip(w2[chans:, :])
    wev_ref[:, 0:chans] = wenv
    wev_ref[:, chans:] = wval
    wradb_ref[...] = jnp.concatenate([rad, jnp.zeros_like(rad)], axis=0).astype(BF16)
    wout = half_ref[5 * chans : 5 * chans + 1, :].astype(F32)
    wcol_ref[...] = jnp.broadcast_to(wout, (LANES, chans)).T
    feat = rows_ref[0:own, :]
    tab_ref[0:own, :] = dot_nn(feat, wa, HIGH)
    tab_ref[own : 2 * own, :] = dot_nn(feat, wb, HIGH)
    rad_hi, rad_lo = split(rad)
    tab_ref[2 * own :, :] = jnp.concatenate([rad_hi, rad_hi, rad_lo, jnp.zeros_like(rad)], axis=0)


def harmonics(ux, uy, uz):
    return [
        ux,
        uy,
        uz,
        ROOT3 * ux * uy,
        ROOT3 * uy * uz,
        ROOT3 * ux * uz,
        0.866 * (ux * ux - uy * uy),
        0.5 * (3.0 * uz * uz - 1.0),
    ]


def trig(half):
    turns = jnp.round(half)
    x = math.pi * (half - turns)
    odd = turns - 2.0 * jnp.floor(0.5 * turns)
    sign = 1.0 - 2.0 * odd
    x2 = x * x
    s = jnp.full_like(x, -1.0 / 39916800)
    for coef in (1.0 / 362880, -1.0 / 5040, 1.0 / 120, -1.0 / 6, 1.0):
        s = s * x2 + coef
    c = jnp.full_like(x, 1.0 / 479001600)
    for coef in (-1.0 / 3628800, 1.0 / 40320, -1.0 / 720, 1.0 / 24, -0.5, 1.0):
        c = c * x2 + coef
    return sign * x * s, sign * c


def waves(half, count):
    s1, c1 = trig(half)
    sins, coss = [s1], [c1]
    s0, c0 = jnp.zeros_like(s1), jnp.ones_like(c1)
    for _ in range(count - 1):
        sn = 2.0 * c1 * sins[-1] - s0
        cn = 2.0 * c1 * coss[-1] - c0
        s0, c0 = sins[-1], coss[-1]
        sins.append(sn)
        coss.append(cn)
    return sins, coss


def look_up(table_row, index):
    low = index & (LANES - 1)
    high = index >> 7
    result = jnp.zeros(index.shape, F32)
    for block in range(table_row.shape[1] // LANES):
        part = jnp.broadcast_to(table_row[:, block * LANES : (block + 1) * LANES], index.shape)
        got = jnp.take_along_axis(part, low, axis=1)
        result = jnp.where(high == block, got, result)
    return result


def in_lanes(tile):
    return jnp.concatenate([tile[r : r + 1, :] for r in range(tile.shape[0])], axis=1)


def one_hot(row, base, count):
    near = jnp.clip(row - base, -1, LANES).astype(BF16)
    iota = lax.broadcasted_iota(jnp.int32, (count, row.shape[1]), 0).astype(BF16)
    return jnp.where(iota == near, jnp.ones((), BF16), jnp.zeros((), BF16))


def sorted_size(edges):
    return 1 << (edges - 1).bit_length()


def main_kernel(plan, *refs):
    count_ref, bound_ref, key_ref, pos_ref, wb_ref = refs[:5]
    came, refs = plan.cut(refs[5:], 0, 1, 2)
    half_ref, w1t_ref, wevt_ref, w2t_ref, w1_ref, wev_ref, w2_ref, wradb_ref, wcol_ref = refs[:9]
    ae_ref, own_ref = refs[9:11]
    n_x = len(plan.groups[0])
    back_refs, rest_ref = refs[11 : 11 + n_x], refs[11 + n_x]
    (
        tab_ref,
        ghost_ref,
        place_ref,
        table_ref,
        y_ref,
        basis_ref,
        geo_ref,
        first_ref,
        dsilu_ref,
        ew_ref,
        val_ref,
        a_ref,
        env_ref,
        denv_ref,
        big_ref,
        dt_ref,
        dv_ref,
        dfa_ref,
        live_ref,
        dy_ref,
        db_ref,
        dr_ref,
        acc_ref,
    ) = refs[12 + n_x :]
    own = pos_ref.shape[1]
    chans = w1_ref.shape[0]
    n_basis = wradb_ref.shape[0] // 2
    rows_all = key_ref.shape[0] * key_ref.shape[1]
    per = CHUNK // LANES
    subs = CHUNK // SUB
    sub_rows = SUB // LANES
    n_ghost = sum(len(c) * w for c, w in zip(CLASSES, plan.widths))
    n_tab = own + n_ghost
    n_sel = own + n_tab

    place_ref[...] = jnp.zeros_like(place_ref)
    at = 0
    for off in OFFSETS:
        live = plan.live(off)
        message, begin = plan.find(came, (0, 1, 2), None, [], off)
        ghost_ref[at : at + live, :] = message[begin : begin + live, :]
        place_ref[at : at + live, :] = spread(message[begin + live : begin + live + 1, :], live)
        at += live
    ghost_pos = dot_nt(group_rows(8), place_ref[...], HIGH)
    pos_t = jnp.concatenate([pos_ref[...], ghost_pos[0:3, :]], axis=1)
    f_hi, f_lo = split(ghost_ref[...])
    w_hi, w_lo = split(wb_ref[...])
    tab_ref[0 : 2 * own, :] = half_ref[0 : 2 * own, :]
    tab_ref[2 * own : n_sel, :] = dot_nn(
        jnp.concatenate([f_hi, f_lo, f_hi], axis=1).astype(BF16),
        jnp.concatenate([w_hi, w_hi, w_lo], axis=0).astype(BF16),
    )
    tab_ref[n_sel:, :] = half_ref[2 * own :, :]
    table_ref[...] = tab_ref[...].T.astype(BF16)

    keys = key_ref[...].reshape(rows_all, LANES)
    centre = keys >> OTHER_BITS
    other = keys & OTHER_MASK
    valid = (keys != (own - 1) * (OTHER_MASK + 1) + OTHER_MASK).astype(F32)
    r = [
        look_up(pos_t[a : a + 1, :], other) - look_up(pos_t[a : a + 1, 0:LANES], centre)
        for a in range(3)
    ]
    d2 = r[0] * r[0] + r[1] * r[1] + r[2] * r[2] + 0.01
    dist = jnp.sqrt(d2)
    inv = 1.0 / dist
    q = 1.0 / (1.0 + 0.25 * d2)
    envelope = q * q
    unit = [x * inv for x in r]
    for m, comp in enumerate(harmonics(*unit)):
        y_ref[pl.ds(m, rows_all, stride=8), :] = comp
    sins, _ = waves(0.5 * dist, n_basis)
    scale = envelope * inv
    for n in range(n_basis):
        basis_ref[pl.ds(n, rows_all, stride=n_basis), :] = sins[n] * scale
    for i, plane in enumerate((unit[0], unit[1], unit[2], dist, inv, q, envelope * valid, valid)):
        geo_ref[i] = plane.reshape(geo_ref.shape[1:])

    env_ref[...] = jnp.zeros_like(env_ref)
    denv_ref[...] = jnp.zeros_like(denv_ref)
    ae_ref[...] = jnp.zeros_like(ae_ref)
    acc_ref[...] = jnp.zeros_like(acc_ref)
    dr_ref[...] = jnp.zeros_like(dr_ref)

    bound_total = sorted_size(rows_all * LANES)
    n_chunks = lax.div(count_ref[0] + (CHUNK - 1), jnp.int32(CHUNK))

    def window(k, s):
        groups = bound_ref.shape[1] * SUB // bound_total
        first = (k * subs + s) * groups
        low = bound_ref[0, first]
        high = low
        for g in range(groups):
            high = jnp.maximum(high, bound_ref[1, first + g])
        start = pl.multiple_of((low >> 3) << 3, 8)
        more = lax.div(high - start, jnp.int32(WIN))
        return start, more

    def any_more(k):
        most = window(k, 0)[1]
        for s in range(1, subs):
            most = jnp.maximum(most, window(k, s)[1])
        return most > 0

    def window_hot(k, s, start):
        rows = key_ref[k, s * sub_rows : (s + 1) * sub_rows, :]
        crow = in_lanes(rows >> OTHER_BITS) - start
        return lax.broadcasted_iota(jnp.int32, (WIN, SUB), 0) == crow

    def select(k, s, start):
        row = k * per + s * sub_rows
        hot = window_hot(k, s, start)
        tiles = [
            y_ref[pl.ds(pl.multiple_of((row + j) * 8, 8), 8), :] for j in range(sub_rows)
        ]
        ys = jnp.concatenate(tiles, axis=1)
        parts = [hot.astype(F32)]
        for m in range(8):
            parts.append(jnp.where(hot, ys[m : m + 1, :], 0.0))
        return jnp.concatenate(parts, axis=0).astype(BF16)

    def load_window(ref, start):
        return jnp.concatenate(
            [ref[m, pl.ds(start, WIN), :] for m in range(9)], axis=0
        ).astype(BF16)

    def add_window(ref, start, rows):
        for m in range(9):
            ref[m, pl.ds(start, WIN), :] += rows[m * WIN : (m + 1) * WIN, :]

    def sub_lanes(s):
        return slice(s * SUB, (s + 1) * SUB)

    def more_windows(k, body):
        @pl.when(any_more(k))
        def _():
            for s in range(subs):
                start, more = window(k, s)

                def step(t, carry, s=s, start=start):
                    body(s, pl.multiple_of(start + t * WIN, 8))
                    return carry

                lax.fori_loop(1, more + 1, step, 0)

    def row_of(plane, k):
        return in_lanes(geo_ref[plane, k])

    def phase_a(k, carry):
        kt = key_ref[k]
        crow = in_lanes(kt >> OTHER_BITS)
        orow = in_lanes(kt & OTHER_MASK)
        hots = [one_hot(crow, 0, own)]
        for base in range(0, n_tab, LANES):
            hots.append(one_hot(orow, base, min(LANES, n_tab - base)))
        tiles = [
            basis_ref[pl.ds(pl.multiple_of((k * per + j) * n_basis, 8), n_basis), :]
            for j in range(per)
        ]
        basis = jnp.concatenate(tiles, axis=1)
        b_hi, b_lo = split(basis)
        hots.append(jnp.concatenate([b_hi, b_lo], axis=0).astype(BF16))
        hots.append(jnp.concatenate([b_hi, jnp.zeros_like(b_hi)], axis=0).astype(BF16))
        mixed = dot_nn(table_ref[...], jnp.concatenate(hots, axis=0)).astype(BF16)
        z1 = dot_nn(w1t_ref[...], mixed)
        sg = 0.5 + 0.5 * jnp.tanh(0.5 * z1)
        first = z1 * sg
        dsilu_ref[k] = (sg + first * (1.0 - sg)).astype(BF16)
        first = first.astype(BF16)
        first_ref[k] = first
        both = dot_nn(wevt_ref[...], first)
        ew = (both[0:chans] * row_of(6, k)).astype(BF16)
        ew_ref[k] = ew
        val_ref[k] = both[chans:].astype(BF16)
        for s in range(subs):
            start, _ = window(k, s)
            a = select(k, s, start)
            a_ref[k * subs + s] = a
            add_window(env_ref, start, dot_nt(a, ew[:, sub_lanes(s)]))

        def again(s, start):
            a = select(k, s, start)
            add_window(env_ref, start, dot_nt(a, ew_ref[k, :, sub_lanes(s)]))

        more_windows(k, again)
        return carry

    lax.fori_loop(0, n_chunks, phase_a, 0)

    def phase_b(k, carry):
        for s in range(subs):
            start, _ = window(k, s)
            big_ref[:, sub_lanes(s)] = dot_tn(load_window(env_ref, start), a_ref[k * subs + s])

        def again_total(s, start):
            big_ref[:, sub_lanes(s)] += dot_tn(load_window(env_ref, start), select(k, s, start))

        more_windows(k, again_total)
        total = 0.2 * big_ref[...]
        value = val_ref[k].astype(F32)
        scalar = (value * total).astype(BF16)
        z2 = dot_nn(w2t_ref[...], jnp.concatenate([first_ref[k], scalar], axis=0))
        sg = 0.5 + 0.5 * jnp.tanh(0.5 * z2)
        second = z2 * sg
        wcol = jnp.concatenate([wcol_ref[...]] * per, axis=1)
        ee = jnp.sum(second.astype(BF16).astype(F32) * wcol, axis=0, keepdims=True)
        envv = row_of(6, k)
        dy_ref[9, :, :] = jnp.zeros((per, LANES), F32)
        live = ee * row_of(7, k)
        for j in range(per):
            live_ref[k, j : j + 1, :] = live[:, j * LANES : (j + 1) * LANES]
        energy = ee * envv
        dz2 = ((wcol * envv) * (sg + second * (1.0 - sg))).astype(BF16)
        dj = dot_nn(w2_ref[...], dz2)
        dfa_ref[k] = dj[0:chans].astype(BF16)
        dscalar = dj[chans:]
        dt = (0.2 * value * dscalar).astype(BF16)
        dt_ref[k] = dt
        dv_ref[k] = (total * dscalar).astype(BF16)

        def add_energy(s, start):
            hot = window_hot(k, s, start)
            part = jnp.where(hot, energy[:, sub_lanes(s)], 0.0)
            half = part[:, 0:LANES]
            for j in range(1, sub_rows):
                half = half + part[:, j * LANES : (j + 1) * LANES]
            ae_ref[pl.ds(start, WIN), :] += half

        for s in range(subs):
            start, _ = window(k, s)
            add_window(denv_ref, start, dot_nt(a_ref[k * subs + s], dt[:, sub_lanes(s)]))
            add_energy(s, start)

        def again(s, start):
            add_window(
                denv_ref, start, dot_nt(select(k, s, start), dt_ref[k, :, sub_lanes(s)])
            )
            add_energy(s, start)

        more_windows(k, again)
        return carry

    lax.fori_loop(0, n_chunks, phase_b, 0)

    def phase_c(k, carry):
        def env_terms(s, start, a, fresh):
            e_win = load_window(env_ref, start)
            d_win = load_window(denv_ref, start)
            dew = dot_tn(d_win, a)
            pair = jnp.concatenate(
                [dt_ref[k, :, sub_lanes(s)], ew_ref[k, :, sub_lanes(s)]], axis=0
            )
            prods = dot_nn(jnp.concatenate([e_win, d_win], axis=1), pair)
            hot = a[0:WIN].astype(F32)
            if fresh:
                big_ref[:, sub_lanes(s)] = dew
            else:
                big_ref[:, sub_lanes(s)] += dew
            for m in range(1, 9):
                row = jnp.sum(prods[m * WIN : (m + 1) * WIN] * hot, axis=0, keepdims=True)
                for j in range(sub_rows):
                    at = s * sub_rows + j
                    piece = row[:, j * LANES : (j + 1) * LANES]
                    if fresh:
                        dy_ref[m, at : at + 1, :] = piece
                    else:
                        dy_ref[m, at : at + 1, :] += piece

        for s in range(subs):
            start, _ = window(k, s)
            env_terms(s, start, a_ref[k * subs + s], True)
        more_windows(k, lambda s, start: env_terms(s, start, select(k, s, start), False))
        dew = big_ref[...]
        dpre = (dew * row_of(6, k)).astype(BF16)
        denv_row = jnp.sum(dew * ew_ref[k].astype(F32), axis=0, keepdims=True)
        for j in range(per):
            dy_ref[0, j : j + 1, :] = denv_row[:, j * LANES : (j + 1) * LANES]
        dfirst = dfa_ref[k].astype(F32) + dot_nn(
            wev_ref[...], jnp.concatenate([dpre, dv_ref[k]], axis=0)
        )
        dz1 = (dfirst * dsilu_ref[k].astype(F32)).astype(BF16)
        dmixed = dot_nn(w1_ref[...], dz1).astype(BF16)
        dbasis = dot_nn(wradb_ref[...], dmixed)
        for j in range(per):
            db_ref[j * n_basis : (j + 1) * n_basis, :] = dbasis[
                0:n_basis, j * LANES : (j + 1) * LANES
            ]
        ux, uy, uz, dist, inv, q = [geo_ref[i, k] for i in range(6)]
        envelope = q * q
        g = envelope * inv
        denvelope = -(q * envelope) * dist
        dg = (denvelope - g) * inv
        sins, coss = waves(0.5 * dist, n_basis)
        denv_direct = live_ref[k] + dy_ref[0] / envelope
        ddist = denv_direct * denvelope
        for n in range(n_basis):
            db = db_ref[pl.ds(n, per, stride=n_basis), :]
            ddist = ddist + db * (coss[n] * ((n + 1) * math.pi / 2.0) * g + sins[n] * dg)
        y = [dy_ref[m] for m in range(9)]
        gx = y[1] + ROOT3 * (uy * y[4] + uz * y[6]) + (2.0 * 0.866) * ux * y[7]
        gy = y[2] + ROOT3 * (ux * y[4] + uz * y[5]) - (2.0 * 0.866) * uy * y[7]
        gz = y[3] + ROOT3 * (uy * y[5] + ux * y[6]) + 3.0 * uz * y[8]
        along = ddist - inv * (gx * ux + gy * uy + gz * uz)
        for i, (gu, u) in enumerate(((gx, ux), (gy, uy), (gz, uz))):
            hi, lo = split(inv * gu + along * u)
            dr_ref[pl.ds(i, per, stride=16), :] = hi
            dr_ref[pl.ds(3 + i, per, stride=16), :] = lo
        dr = jnp.concatenate([dr_ref[j * 16 : (j + 1) * 16, :] for j in range(per)], axis=1)
        kt = key_ref[k]
        crow = in_lanes(kt >> OTHER_BITS)
        orow = in_lanes(kt & OTHER_MASK)
        hots = [one_hot(crow, 0, own)]
        for base in range(0, n_tab, LANES):
            hots.append(one_hot(orow, base, min(LANES, n_tab - base)))
        sums = dot_nt(
            jnp.concatenate(hots, axis=0),
            jnp.concatenate([dmixed, dr.astype(BF16)], axis=0),
        )
        acc_ref[:, 0:chans] += sums[:, 0:chans]
        acc_ref[:, chans : chans + 16] += sums[:, chans:]
        return carry

    lax.fori_loop(0, n_chunks, phase_c, 0)

    own_ref[...] = acc_ref[0 : 2 * own, :]
    row = lax.broadcasted_iota(jnp.int32, (LANES, LANES), 0)
    group = lax.broadcasted_iota(jnp.int32, (LANES, LANES), 1) // GROUP
    both = ((group < 3) & ((row == group) | (row == group + 3))).astype(F32)
    places = dot_nn(acc_ref[2 * own :, LANES:], both, HIGH)
    found = {}
    at = 2 * own
    for off in OFFSETS:
        found[off] = at
        at += plan.live(off)
    for blocks, ref in zip(
        plan.groups[0] + [plan.held_rest], tuple(back_refs) + (rest_ref,)
    ):
        for off, row in plan.spans(blocks):
            live = plan.live(off)
            at = found[off]
            ref[row : row + live, :] = acc_ref[at : at + live, 0:chans]
            block = places[at - 2 * own : at - 2 * own + live, :]
            ref[row + live : row + live + 1, :] = jnp.sum(diagonal(block), axis=0, keepdims=True)


def own_kernel(ae_ref, own_ref, wa_ref, wb_ref, energy_ref, fg_ref, force_ref):
    chans = wa_ref.shape[1]
    own = force_ref.shape[1]
    energy_ref[...] = jnp.sum(ae_ref[0:own, :].T, axis=0, keepdims=True)
    fg_ref[...] = dot_nt(own_ref[0:own, 0:chans], wa_ref[...], HIGH) + dot_nt(
        own_ref[own:, 0:chans], wb_ref[...], HIGH
    )
    force = (own_ref[own:, LANES:] - own_ref[0:own, LANES:]).T
    force_ref[...] = force[0:3, :] + force[3:6, :]


def last_kernel(plan, sel_ref, fg_ref, force_ref, wb_ref, *refs):
    came, refs = plan.cut(refs, 0, 1, 2)
    out_force_ref, out_fg_ref, both_ref = refs
    both_ref[...] = jnp.zeros_like(both_ref)
    chans = fg_ref.shape[1]
    at = 0
    for blocks in plan.groups[2] + [plan.own_rest]:
        for off, row in plan.spans(blocks):
            live = plan.live(off)
            src, begin = plan.find(came, (2, 1, 0), None, [], off)
            here = slice(at + row, at + row + live)
            both_ref[here, 0:chans] = src[begin : begin + live, :]
            both_ref[here, chans:] = spread(src[begin + live : begin + live + 1, :], live)
        at += plan.total(blocks)
    sums = dot_exact(sel_ref[...].astype(BF16), both_ref[...], ((0,), (0,)))
    out_fg_ref[...] = fg_ref[...] + dot_nt(sums[:, 0:chans], wb_ref[...], HIGH)
    total = dot_nt(group_rows(8), sums[:, chans:], HIGH)
    out_force_ref[...] = -(force_ref[...] + total[0:3, :])


def local(
    positions,
    atom_features,
    send_face,
    send_edge,
    send_corner,
    centre,
    other,
    edge_count,
    w_proj_a,
    w_proj_b,
    w_radial,
    w_first,
    w_env,
    w_value,
    w_second,
    w_out,
):
    own, chans = atom_features.shape
    edges = centre.shape[0]
    n_basis = w_radial.shape[0]
    plan = Plan(
        [send_face.shape[2], send_edge.shape[2], send_corner.shape[2]],
        [lax.axis_size(axis) for axis in AXES],
    )
    n_ghost = sum(len(c) * w for c, w in zip(CLASSES, plan.widths))
    n_sel = 2 * own + n_ghost
    n_send = sum(plan.total(blocks) for blocks in plan.groups[2]) + plan.total(plan.own_rest)
    n_table = n_sel + 4 * n_basis
    edges_up = -(-edges // CHUNK) * CHUNK
    n_rows = edges_up // LANES
    n_chunks = edges_up // CHUNK

    with jax.named_scope("prep"):
        rows = jnp.concatenate([atom_features, positions], axis=0)
        widest = max(plan.widths)
        lists = jnp.concatenate(
            [
                jnp.pad(x[0], ((0, 0), (0, widest - x.shape[2])))
                for x in (send_face, send_edge, send_corner)
            ],
            axis=0,
        )
        *sends, own_rows, sel = pl.pallas_call(
            lambda *refs: prep_kernel(plan, *refs),
            out_shape=plan.shapes(2, chans)
            + [shape(plan.total(plan.own_rest), chans), shape(n_send, own)],
            in_specs=[VMEM] * 2,
            out_specs=[VMEM] * (len(plan.groups[2]) + 2),
            scratch_shapes=[pltpu.VMEM((LANES, LANES), jnp.int32)],
            compiler_params=PARAMS,
        )(rows, lists)

    came = {}
    with jax.named_scope("halo_z"):
        came[2] = plan.send(2, sends)

    with jax.named_scope("group_edges"):
        dead = (own - 1) * (OTHER_MASK + 1) + OTHER_MASK
        pad = [(0, edges_up - edges)]
        regs = max(sorted_size(edges_up) // (8 * LANES), 1)
        key, bounds = pl.pallas_call(
            lambda *refs: sort_kernel(dead, *refs),
            out_shape=[
                shape(n_chunks, CHUNK // LANES, LANES, dtype=jnp.int32),
                shape(2, LANES, dtype=jnp.int32),
            ],
            in_specs=[SMEM, VMEM, VMEM],
            out_specs=[VMEM] * 2,
            scratch_shapes=[pltpu.VMEM((16 * regs, LANES), F32)],
            compiler_params=PARAMS,
        )(
            edge_count,
            jnp.pad(centre, pad).reshape(n_rows, LANES),
            jnp.pad(other, pad).reshape(n_rows, LANES),
        )

    with jax.named_scope("halo_y"):
        came[2], key, bounds = lax.optimization_barrier((came[2], key, bounds))
        came[1] = plan.send(1, glue(plan, 1, (2,), plan.own_rest, own_rows, came))

    with jax.named_scope("weights"):
        wide = jnp.concatenate([w_proj_a, w_proj_b, w_radial], axis=0)
        narrow = jnp.concatenate([w_first, w_env, w_value, w_second, w_out[None, :]], axis=0)
        half, *weights = pl.pallas_call(
            weight_kernel,
            out_shape=[
                shape(2 * own + 4 * n_basis, chans),
                shape(chans, chans, dtype=BF16),
                shape(2 * chans, chans, dtype=BF16),
                shape(chans, 2 * chans, dtype=BF16),
                shape(chans, chans, dtype=BF16),
                shape(chans, 2 * chans, dtype=BF16),
                shape(2 * chans, chans, dtype=BF16),
                shape(2 * n_basis, chans, dtype=BF16),
                shape(chans, LANES),
            ],
            in_specs=[VMEM] * 3,
            out_specs=[VMEM] * 9,
            compiler_params=PARAMS,
        )(rows, wide, narrow)

    with jax.named_scope("halo_x"):
        came[1], half, weights = lax.optimization_barrier((came[1], half, weights))
        came[0] = plan.send(0, glue(plan, 0, (1, 2), plan.own_rest, own_rows, came))

    planes = (n_chunks, chans, CHUNK)
    scratch = [
        pltpu.VMEM((n_table, chans), F32),
        pltpu.VMEM((n_ghost, chans), F32),
        pltpu.VMEM((-(-n_ghost // LANES) * LANES, LANES), F32),
        pltpu.VMEM((chans, n_table), BF16),
        pltpu.VMEM((n_rows * 8, LANES), F32),
        pltpu.VMEM((n_rows * n_basis, LANES), F32),
        pltpu.VMEM((8, n_chunks, CHUNK // LANES, LANES), F32),
        pltpu.VMEM(planes, BF16),
        pltpu.VMEM(planes, BF16),
        pltpu.VMEM(planes, BF16),
        pltpu.VMEM(planes, BF16),
        pltpu.VMEM((edges_up // SUB, 9 * WIN, SUB), BF16),
        pltpu.VMEM((9, own + WIN, chans), F32),
        pltpu.VMEM((9, own + WIN, chans), F32),
        pltpu.VMEM((chans, CHUNK), F32),
        pltpu.VMEM(planes, BF16),
        pltpu.VMEM(planes, BF16),
        pltpu.VMEM(planes, BF16),
        pltpu.VMEM((n_chunks, CHUNK // LANES, LANES), F32),
        pltpu.VMEM((10, CHUNK // LANES, LANES), F32),
        pltpu.VMEM((CHUNK // LANES * n_basis, LANES), F32),
        pltpu.VMEM((CHUNK // LANES * 16, LANES), F32),
        pltpu.VMEM((n_sel, 2 * LANES), F32),
    ]
    with jax.named_scope("layer"):
        given = [edge_count, bounds, key, positions, w_proj_b]
        given += [*came[0], *came[1], *came[2], half, *weights]
        atom_sums, own_sums, *back, held = pl.pallas_call(
            lambda *refs: main_kernel(plan, *refs),
            out_shape=[shape(own + WIN, LANES), shape(2 * own, 2 * LANES)]
            + plan.shapes(0, chans)
            + [shape(plan.total(plan.held_rest), chans)],
            in_specs=[SMEM, SMEM] + [VMEM] * (len(given) - 2),
            out_specs=[VMEM] * (3 + len(plan.groups[0])),
            scratch_shapes=scratch,
            compiler_params=PARAMS,
        )(*given)

    with jax.named_scope("halo_back"):
        home = {0: plan.send(0, back, back=True)}
        home[1] = plan.send(1, glue(plan, 1, (0,), plan.held_rest, held, home), back=True)
        home[2] = plan.send(2, glue(plan, 2, (1, 0), plan.held_rest, held, home), back=True)

    with jax.named_scope("own_part"):
        energy, fg, force = pl.pallas_call(
            own_kernel,
            out_shape=[shape(1, own), shape(own, chans), shape(3, own)],
            in_specs=[VMEM] * 4,
            out_specs=[VMEM] * 3,
            compiler_params=PARAMS,
        )(atom_sums, own_sums, w_proj_a, w_proj_b)

    with jax.named_scope("owner_sums"):
        given = [sel, fg, force, w_proj_b, *home[0], *home[1], *home[2]]
        forces, feature_grad = pl.pallas_call(
            lambda *refs: last_kernel(plan, *refs),
            out_shape=[shape(3, own), shape(own, chans)],
            in_specs=[VMEM] * len(given),
            out_specs=[VMEM] * 2,
            scratch_shapes=[pltpu.VMEM((n_send, chans + LANES), F32)],
            compiler_params=PARAMS,
        )(*given)
    return forces, energy.reshape(own), feature_grad


def solution(mesh):
    shard = P(AXES)
    return jax.shard_map(
        local,
        mesh=mesh,
        in_specs=(
            P(None, AXES),
            P(AXES, None),
            P(AXES, None, None),
            P(AXES, None, None),
            P(AXES, None, None),
            shard,
            shard,
            shard,
        )
        + (P(),) * 8,
        out_specs=(P(None, AXES), shard, P(AXES, None)),
        check_vma=False,
    )
```

```python
import math

import jax
import jax.numpy as jnp
from jax import lax
from jax.experimental import pallas as pl
from jax.experimental.pallas import tpu as pltpu
from jax.sharding import PartitionSpec as P

F32 = jnp.float32
BF16 = jnp.bfloat16
HIGH = lax.Precision.HIGHEST
AXES = ("gx", "gy", "gz")
CHUNK = 6144
SUB = 256
WIN = 16
OTHER_BITS = 9
OTHER_MASK = (1 << OTHER_BITS) - 1
LANES = 128
ROOT3 = 1.732


VMEM = pl.BlockSpec(memory_space=pltpu.VMEM)
SMEM = pl.BlockSpec(memory_space=pltpu.SMEM)
PARAMS = pltpu.CompilerParams(vmem_limit_bytes=52 * 2**20)


def shape(*dims, dtype=F32):
    return jax.ShapeDtypeStruct(dims, dtype)


def dot_nn(a, b, precision=None):
    return lax.dot_general(
        a, b, (((1,), (0,)), ((), ())), preferred_element_type=F32, precision=precision
    )


def dot_nt(a, b, precision=None):
    return lax.dot_general(
        a, b, (((1,), (1,)), ((), ())), preferred_element_type=F32, precision=precision
    )


def dot_tn(a, b, precision=None):
    return lax.dot_general(
        a, b, (((0,), (0,)), ((), ())), preferred_element_type=F32, precision=precision
    )


def offset_classes():
    classes = [[], [], []]
    for a in (-1, 0, 1):
        for b in (-1, 0, 1):
            for c in (-1, 0, 1):
                if (a, b, c) != (0, 0, 0):
                    classes[abs(a) + abs(b) + abs(c) - 1].append((a, b, c))
    return classes


CLASSES = offset_classes()


OFFSETS = [off for group in CLASSES for off in group]


def kind(off):
    return abs(off[0]) + abs(off[1]) + abs(off[2]) - 1


class Plan:
    def __init__(self, widths, sizes):
        self.widths = widths
        self.sizes = sizes
        self.groups = [self.group(a) for a in range(3)]
        self.own_rest = [off for off in OFFSETS if off[2] == 0]
        self.held_rest = [off for off in OFFSETS if off[0] == 0]

    def group(self, a):
        groups = {}
        for off in OFFSETS:
            if off[a] != 0:
                groups.setdefault(off[a] % self.sizes[a], []).append(off)
        return list(groups.values())

    def live(self, off):
        return self.widths[kind(off)]

    def rows(self, off):
        return self.live(off) + 1

    def total(self, blocks):
        return sum(self.rows(off) for off in blocks)

    def spans(self, blocks):
        at = 0
        for off in blocks:
            yield off, at
            at += self.rows(off)

    def place(self, a, off):
        for g, blocks in enumerate(self.groups[a]):
            if off in blocks:
                return g, dict(self.spans(blocks))[off]
        raise KeyError(off)

    def find(self, came, axes, rest_ref, rest, off):
        for a in axes:
            if off[a] != 0:
                g, begin = self.place(a, off)
                return came[a][g], begin
        return rest_ref, dict(self.spans(rest))[off]

    def cut(self, refs, *axes):
        came = {}
        for a in axes:
            n = len(self.groups[a])
            came[a], refs = refs[:n], refs[n:]
        return came, refs

    def shapes(self, a, chans):
        return [shape(self.total(blocks), chans) for blocks in self.groups[a]]

    def send(self, a, messages, back=False):
        n = self.sizes[a]
        got = []
        for blocks, message in zip(self.groups[a], messages):
            step = -blocks[0][a] if back else blocks[0][a]
            got.append(lax.ppermute(message, AXES[a], [(i, (i + step) % n) for i in range(n)]))
        return got


GROUP = 32


def group_rows(count):
    row = lax.broadcasted_iota(jnp.int32, (count, LANES), 0)
    group = lax.broadcasted_iota(jnp.int32, (count, LANES), 1) // GROUP
    return (row == group).astype(F32) * (group < 3).astype(F32)


def diagonal(x):
    row = lax.broadcasted_iota(jnp.int32, x.shape, 0)
    lane = lax.broadcasted_iota(jnp.int32, x.shape, 1)
    return jnp.where((lane & (GROUP - 1)) == row, x, 0.0)


def spread(row, live):
    return diagonal(jnp.broadcast_to(row, (live, LANES)))


def split(x):
    high = x.astype(BF16).astype(F32)
    return high, x - high


def dot_exact(hot, x, dims):
    high, low = split(x)
    both = jnp.concatenate([high, low], axis=1).astype(BF16)
    out = lax.dot_general(hot, both, (dims, ((), ())), preferred_element_type=F32)
    return out[:, 0 : x.shape[1]] + out[:, x.shape[1] :]


def prep_kernel(plan, rows_ref, *outs):
    n_z = len(plan.groups[2])
    sends, rest_ref, sel_ref, turn_ref = outs[:n_z], outs[n_z], outs[n_z + 1], outs[n_z + 2]
    own = sel_ref.shape[1]
    lane = lax.broadcasted_iota(jnp.int32, (1, own), 1).astype(F32)
    n_faces = len(CLASSES[0])
    turn_ref[...] = jnp.zeros_like(turn_ref)
    turn_ref[0:n_faces, :] = rows_ref[own + 8 : own + 8 + n_faces, :]
    columns = [turn_ref[...].T]
    at = own + 16
    for width in plan.widths[1:]:
        columns.append(rows_ref[at : at + width, :])
        at += -(-width // 8) * 8
    sel_ref[...] = jnp.zeros_like(sel_ref)
    messages = plan.groups[2] + [plan.own_rest]
    at = 0
    for blocks in messages:
        for off, begin in plan.spans(blocks):
            key = CLASSES[kind(off)].index(off)
            live = plan.live(off)
            column = columns[kind(off)][0:live, key : key + 1]
            sel_ref[at + begin : at + begin + live, :] = (column == lane).astype(F32)
        at += plan.total(blocks)
    pos = dot_tn(rows_ref[own : own + 3, :], group_rows(3), HIGH)
    sel = sel_ref[...]
    rows = dot_nn(sel, rows_ref[0:own, :], HIGH)
    places = dot_nn(sel, pos, HIGH)
    at = 0
    for blocks, send in zip(messages, tuple(sends) + (rest_ref,)):
        count = plan.total(blocks)
        send[...] = rows[at : at + count, :]
        for off, begin in plan.spans(blocks):
            live = plan.live(off)
            block = places[at + begin : at + begin + live, :]
            send[begin + live : begin + live + 1, :] = jnp.sum(
                diagonal(block), axis=0, keepdims=True
            )
        at += count


def glue_kernel(plan, a, axes, rest, *refs):
    rest_ref = refs[0]
    came, outs = plan.cut(refs[1:], *axes)
    for blocks, out in zip(plan.groups[a], outs):
        for off, row in plan.spans(blocks):
            src, begin = plan.find(came, axes, rest_ref, rest, off)
            out[row : row + plan.rows(off), :] = src[begin : begin + plan.rows(off), :]


def glue(plan, a, axes, rest, rest_rows, came):
    given = [rest_rows] + [message for axis in axes for message in came[axis]]
    outs = plan.shapes(a, rest_rows.shape[1])
    return pl.pallas_call(
        lambda *refs: glue_kernel(plan, a, axes, rest, *refs),
        out_shape=outs,
        in_specs=[VMEM] * len(given),
        out_specs=[VMEM] * len(outs),
        compiler_params=PARAMS,
    )(*given)


def sort_kernel(dead, count_ref, centre_ref, other_ref, key_ref, bound_ref, turn_ref):
    rows = centre_ref.shape[0]
    regs = turn_ref.shape[0] // 16
    group = regs * 8
    row = lax.broadcasted_iota(jnp.int32, (rows, LANES), 0)
    lane = lax.broadcasted_iota(jnp.int32, (rows, LANES), 1)
    key = jnp.where(
        row * LANES + lane < count_ref[0], (centre_ref[...] << OTHER_BITS) + other_ref[...], dead
    ).astype(F32)
    x = [key[8 * v : 8 * v + 8, :] for v in range(rows // 8)]
    x += [jnp.full((8, LANES), float(dead), F32)] * (regs - len(x))
    s = lax.broadcasted_iota(jnp.int32, (8, LANES), 0)
    ln = lax.broadcasted_iota(jnp.int32, (8, LANES), 1)
    base = ln * group + s * regs

    def sign(k, v):
        return jnp.where(((base + v) & k) == 0, 1.0, -1.0).astype(F32)

    last = [jnp.ones((8, LANES), F32)] * regs
    total = group * LANES
    k = 2
    while k <= total:
        signs = [sign(k, v) for v in range(regs)] if k < total else [1.0] * regs
        x = [x[v] * (last[v] * signs[v]) for v in range(regs)]
        last = signs
        j = k // 2
        while j >= 1:
            if j < regs:
                for v in range(regs):
                    if v & j == 0:
                        a, b = x[v], x[v | j]
                        x[v], x[v | j] = jnp.minimum(a, b), jnp.maximum(a, b)
            else:
                axis, step, size, ids = (
                    (0, j // regs, 8, s) if j < group else (1, j // group, LANES, ln)
                )
                low = (ids & step) == 0
                for v in range(regs):
                    up = pltpu.roll(x[v], size - step, axis)
                    if 2 * step == size:
                        mate = up
                    else:
                        mate = jnp.where(low, up, pltpu.roll(x[v], step, axis))
                    x[v] = jnp.where(low, jnp.minimum(x[v], mate), jnp.maximum(x[v], mate))
            j //= 2
        k *= 2
    least = x[0]
    most = jnp.where(x[0] == float(dead), -1.0, x[0])
    for v in range(1, regs):
        least = jnp.minimum(least, x[v])
        most = jnp.maximum(most, jnp.where(x[v] == float(dead), -1.0, x[v]))
    bound_ref[0:1, :] = jnp.min(least, axis=0, keepdims=True).astype(jnp.int32) >> OTHER_BITS
    bound_ref[1:2, :] = jnp.max(most, axis=0, keepdims=True).astype(jnp.int32) >> OTHER_BITS
    turned = jnp.concatenate(x + [jnp.zeros((LANES - group, LANES), F32)], axis=0).T
    turn_ref[...] = turned
    ratio = LANES // group
    parts = [
        turn_ref[pl.ds(i, rows, stride=ratio), 0:group] for i in range(ratio)
    ]
    done = jnp.concatenate(parts, axis=1).astype(jnp.int32)
    per = key_ref.shape[1]
    for c in range(key_ref.shape[0]):
        key_ref[c] = done[c * per : (c + 1) * per, :]


def weight_kernel(
    rows_ref,
    wide_ref,
    half_ref,
    tab_ref,
    w1t_ref,
    wevt_ref,
    w2t_ref,
    w1_ref,
    wev_ref,
    w2_ref,
    wcol_ref,
):
    chans = wide_ref.shape[1]
    rad_rows = wide_ref.shape[0] - 2 * chans
    own = (tab_ref.shape[0] - 4 * rad_rows) // 2
    wa, wb, rad = wide_ref[0:chans, :], wide_ref[chans : 2 * chans, :], wide_ref[2 * chans :, :]
    w1, wenv, wval = [half_ref[i * chans : (i + 1) * chans, :] for i in range(3)]
    w2 = half_ref[3 * chans : 5 * chans, :]

    def flip(w):
        return w.astype(F32).T.astype(BF16)

    down = dot_nn(rad, w1.astype(F32), HIGH)
    w1_ref[0:chans, :] = w1
    w1_ref[chans:, :] = jnp.concatenate([down, jnp.zeros_like(down)], axis=0).astype(BF16)
    w2_ref[...] = w2
    w1t_ref[...] = flip(w1)
    wevt_ref[0:chans, :] = flip(wenv)
    wevt_ref[chans:, :] = flip(wval)
    w2t_ref[:, 0:chans] = flip(w2[0:chans, :])
    w2t_ref[:, chans:] = flip(w2[chans:, :])
    wev_ref[:, 0:chans] = wenv
    wev_ref[:, chans:] = wval
    wout = half_ref[5 * chans : 5 * chans + 1, :].astype(F32)
    wcol_ref[...] = jnp.broadcast_to(wout, (LANES, chans)).T
    feat = rows_ref[0:own, :]
    tab_ref[0:own, :] = dot_nn(feat, wa, HIGH)
    tab_ref[own : 2 * own, :] = dot_nn(feat, wb, HIGH)
    rad_hi, rad_lo = split(rad)
    tab_ref[2 * own :, :] = jnp.concatenate([rad_hi, rad_hi, rad_lo, jnp.zeros_like(rad)], axis=0)


def harmonics(ux, uy, uz):
    return [
        ux,
        uy,
        uz,
        ROOT3 * ux * uy,
        ROOT3 * uy * uz,
        ROOT3 * ux * uz,
        0.866 * (ux * ux - uy * uy),
        0.5 * (3.0 * uz * uz - 1.0),
    ]


def trig(half):
    turns = jnp.round(half)
    x = math.pi * (half - turns)
    odd = turns - 2.0 * jnp.floor(0.5 * turns)
    sign = 1.0 - 2.0 * odd
    x2 = x * x
    s = jnp.full_like(x, -1.0 / 39916800)
    for coef in (1.0 / 362880, -1.0 / 5040, 1.0 / 120, -1.0 / 6, 1.0):
        s = s * x2 + coef
    c = jnp.full_like(x, 1.0 / 479001600)
    for coef in (-1.0 / 3628800, 1.0 / 40320, -1.0 / 720, 1.0 / 24, -0.5, 1.0):
        c = c * x2 + coef
    return sign * x * s, sign * c


def waves(half, count):
    s1, c1 = trig(half)
    sins, coss = [s1], [c1]
    s0, c0 = jnp.zeros_like(s1), jnp.ones_like(c1)
    for _ in range(count - 1):
        sn = 2.0 * c1 * sins[-1] - s0
        cn = 2.0 * c1 * coss[-1] - c0
        s0, c0 = sins[-1], coss[-1]
        sins.append(sn)
        coss.append(cn)
    return sins, coss


def look_up(table_row, index):
    low = index & (LANES - 1)
    high = index >> 7
    result = jnp.zeros(index.shape, F32)
    for block in range(table_row.shape[1] // LANES):
        part = jnp.broadcast_to(table_row[:, block * LANES : (block + 1) * LANES], index.shape)
        got = jnp.take_along_axis(part, low, axis=1)
        result = jnp.where(high == block, got, result)
    return result


def in_lanes(tile):
    return jnp.concatenate([tile[r : r + 1, :] for r in range(tile.shape[0])], axis=1)


def one_hot(row, base, count):
    near = jnp.clip(row - base, -1, LANES).astype(BF16)
    iota = lax.broadcasted_iota(jnp.int32, (count, row.shape[1]), 0).astype(BF16)
    return jnp.where(iota == near, jnp.ones((), BF16), jnp.zeros((), BF16))


def sorted_size(edges):
    return 1 << (edges - 1).bit_length()


def main_kernel(plan, *refs):
    count_ref, bound_ref, key_ref, pos_ref, wb_ref = refs[:5]
    came, refs = plan.cut(refs[5:], 0, 1, 2)
    half_ref, w1t_ref, wevt_ref, w2t_ref, w1_ref, wev_ref, w2_ref, wcol_ref = refs[:8]
    ae_ref, own_ref = refs[8:10]
    n_x = len(plan.groups[0])
    back_refs, rest_ref = refs[10 : 10 + n_x], refs[10 + n_x]
    (
        tab_ref,
        ghost_ref,
        place_ref,
        table_ref,
        y_ref,
        basis_ref,
        geo_ref,
        first_ref,
        dsilu_ref,
        ew_ref,
        val_ref,
        a_ref,
        env_ref,
        denv_ref,
        big_ref,
        dt_ref,
        dv_ref,
        dfa_ref,
        live_ref,
        energy_ref,
        dy_ref,
        db_ref,
        dr_ref,
        acc_ref,
    ) = refs[11 + n_x :]
    own = pos_ref.shape[1]
    chans = w1_ref.shape[1]
    n_basis = (w1_ref.shape[0] - chans) // 2
    rows_all = key_ref.shape[0] * key_ref.shape[1]
    per = CHUNK // LANES
    subs = CHUNK // SUB
    sub_rows = SUB // LANES
    n_ghost = sum(len(c) * w for c, w in zip(CLASSES, plan.widths))
    n_tab = own + n_ghost
    n_sel = own + n_tab

    place_ref[...] = jnp.zeros_like(place_ref)
    at = 0
    for off in OFFSETS:
        live = plan.live(off)
        message, begin = plan.find(came, (0, 1, 2), None, [], off)
        ghost_ref[at : at + live, :] = message[begin : begin + live, :]
        place_ref[at : at + live, :] = spread(message[begin + live : begin + live + 1, :], live)
        at += live
    ghost_pos = dot_nt(group_rows(8), place_ref[...], HIGH)
    pos_t = jnp.concatenate([pos_ref[...], ghost_pos[0:3, :]], axis=1)
    f_hi, f_lo = split(ghost_ref[...])
    w_hi, w_lo = split(wb_ref[...])
    tab_ref[0 : 2 * own, :] = half_ref[0 : 2 * own, :]
    tab_ref[2 * own : n_sel, :] = dot_nn(
        jnp.concatenate([f_hi, f_lo, f_hi], axis=1).astype(BF16),
        jnp.concatenate([w_hi, w_hi, w_lo], axis=0).astype(BF16),
    )
    tab_ref[n_sel:, :] = half_ref[2 * own :, :]
    table_ref[...] = tab_ref[...].T.astype(BF16)

    keys = key_ref[...].reshape(rows_all, LANES)
    centre = keys >> OTHER_BITS
    other = keys & OTHER_MASK
    valid = (keys != (own - 1) * (OTHER_MASK + 1) + OTHER_MASK).astype(F32)
    r = [
        look_up(pos_t[a : a + 1, :], other) - look_up(pos_t[a : a + 1, 0:LANES], centre)
        for a in range(3)
    ]
    d2 = r[0] * r[0] + r[1] * r[1] + r[2] * r[2] + 0.01
    dist = jnp.sqrt(d2)
    inv = 1.0 / dist
    q = 1.0 / (1.0 + 0.25 * d2)
    envelope = q * q
    unit = [x * inv for x in r]
    for m, comp in enumerate(harmonics(*unit)):
        y_ref[pl.ds(m, rows_all, stride=8), :] = comp
    sins, _ = waves(0.5 * dist, n_basis)
    scale = envelope * inv
    for n in range(n_basis):
        basis_ref[pl.ds(n, rows_all, stride=n_basis), :] = sins[n] * scale
    for i, plane in enumerate((unit[0], unit[1], unit[2], dist, inv, q, envelope * valid, valid)):
        geo_ref[i] = plane.reshape(geo_ref.shape[1:])

    env_ref[...] = jnp.zeros_like(env_ref)
    denv_ref[...] = jnp.zeros_like(denv_ref)
    ae_ref[...] = jnp.zeros_like(ae_ref)
    acc_ref[...] = jnp.zeros_like(acc_ref)
    dr_ref[...] = jnp.zeros_like(dr_ref)

    bound_total = sorted_size(rows_all * LANES)
    n_chunks = lax.div(count_ref[0] + (CHUNK - 1), jnp.int32(CHUNK))

    def window(k, s):
        groups = bound_ref.shape[1] * SUB // bound_total
        first = (k * subs + s) * groups
        low = bound_ref[0, first]
        high = low
        for g in range(groups):
            high = jnp.maximum(high, bound_ref[1, first + g])
        start = pl.multiple_of((low >> 3) << 3, 8)
        more = lax.div(high - start, jnp.int32(WIN))
        return start, more

    most = jnp.int32(0)
    for s in range(rows_all // sub_rows):
        most = jnp.maximum(most, window(s // subs, s % subs)[1])

    def window_hot(k, s, start):
        rows = [key_ref[k, pl.ds(s * sub_rows + j, 1), :] for j in range(sub_rows)]
        crow = (jnp.concatenate(rows, axis=1) >> OTHER_BITS) - start
        return lax.broadcasted_iota(jnp.int32, (WIN, SUB), 0) == crow

    def select(k, s, start):
        row = k * per + s * sub_rows
        hot = window_hot(k, s, start)
        tiles = [
            y_ref[pl.ds(pl.multiple_of((row + j) * 8, 8), 8), :] for j in range(sub_rows)
        ]
        ys = jnp.concatenate(tiles, axis=1)
        parts = [hot.astype(F32)]
        for m in range(8):
            parts.append(jnp.where(hot, ys[m : m + 1, :], 0.0))
        return jnp.concatenate(parts, axis=0).astype(BF16)

    def load_window(ref, start):
        return jnp.concatenate(
            [ref[m, pl.ds(start, WIN), :] for m in range(9)], axis=0
        ).astype(BF16)

    def add_window(ref, start, rows):
        for m in range(9):
            ref[m, pl.ds(start, WIN), :] += rows[m * WIN : (m + 1) * WIN, :]

    def sub_lanes(s):
        if isinstance(s, int):
            return slice(s * SUB, (s + 1) * SUB)
        return pl.ds(pl.multiple_of(s * SUB, SUB), SUB)

    def more_windows(k, body):
        @pl.when(most > 0)
        def _():
            def over(s, carry):
                start, more = window(k, s)

                def step(t, carry):
                    body(s, pl.multiple_of(start + t * WIN, 8))
                    return carry

                return lax.fori_loop(1, more + 1, step, carry)

            lax.fori_loop(0, subs, over, 0)

    def row_of(plane, k):
        return in_lanes(geo_ref[plane, k])

    def phase_a(k, carry):
        kt = key_ref[k]
        crow = in_lanes(kt >> OTHER_BITS)
        orow = in_lanes(kt & OTHER_MASK)
        hots = [one_hot(crow, 0, own)]
        for base in range(0, n_tab, LANES):
            hots.append(one_hot(orow, base, min(LANES, n_tab - base)))
        tiles = [
            basis_ref[pl.ds(pl.multiple_of((k * per + j) * n_basis, 8), n_basis), :]
            for j in range(per)
        ]
        basis = jnp.concatenate(tiles, axis=1)
        b_hi, b_lo = split(basis)
        hots.append(jnp.concatenate([b_hi, b_lo], axis=0).astype(BF16))
        hots.append(jnp.concatenate([b_hi, jnp.zeros_like(b_hi)], axis=0).astype(BF16))
        mixed = dot_nn(table_ref[...], jnp.concatenate(hots, axis=0)).astype(BF16)
        z1 = dot_nn(w1t_ref[...], mixed)
        sg = 0.5 + 0.5 * jnp.tanh(0.5 * z1)
        first = z1 * sg
        dsilu_ref[k] = (sg + first * (1.0 - sg)).astype(BF16)
        first = first.astype(BF16)
        first_ref[k] = first
        both = dot_nn(wevt_ref[...], first)
        ew = (both[0:chans] * row_of(6, k)).astype(BF16)
        ew_ref[k] = ew
        val_ref[k] = both[chans:].astype(BF16)
        for s in range(subs):
            start, _ = window(k, s)
            a = select(k, s, start)
            a_ref[k * subs + s] = a
            add_window(env_ref, start, dot_nt(a, ew[:, sub_lanes(s)]))

        def again(s, start):
            a = select(k, s, start)
            add_window(env_ref, start, dot_nt(a, ew_ref[k, :, sub_lanes(s)]))

        more_windows(k, again)
        return carry

    lax.fori_loop(0, n_chunks, phase_a, 0)

    def phase_b(k, carry):
        for s in range(subs):
            start, _ = window(k, s)
            big_ref[:, sub_lanes(s)] = dot_tn(load_window(env_ref, start), a_ref[k * subs + s])

        def again_total(s, start):
            big_ref[:, sub_lanes(s)] += dot_tn(load_window(env_ref, start), select(k, s, start))

        more_windows(k, again_total)
        total = 0.2 * big_ref[...]
        value = val_ref[k].astype(F32)
        scalar = (value * total).astype(BF16)
        z2 = dot_nn(w2t_ref[...], jnp.concatenate([first_ref[k], scalar], axis=0))
        sg = 0.5 + 0.5 * jnp.tanh(0.5 * z2)
        second = z2 * sg
        wcol = jnp.concatenate([wcol_ref[...]] * per, axis=1)
        ee = jnp.sum(second.astype(BF16).astype(F32) * wcol, axis=0, keepdims=True)
        envv = row_of(6, k)
        live = ee * row_of(7, k)
        for j in range(per):
            live_ref[k, j : j + 1, :] = live[:, j * LANES : (j + 1) * LANES]
        energy_ref[...] = ee * envv
        dz2 = ((wcol * envv) * (sg + second * (1.0 - sg))).astype(BF16)
        dj = dot_nn(w2_ref[...], dz2)
        dfa_ref[k] = dj[0:chans].astype(BF16)
        dscalar = dj[chans:]
        dt = (0.2 * value * dscalar).astype(BF16)
        dt_ref[k] = dt
        dv_ref[k] = (total * dscalar).astype(BF16)

        def add_energy(s, start):
            hot = window_hot(k, s, start)
            part = jnp.where(hot, energy_ref[:, sub_lanes(s)], 0.0)
            half = part[:, 0:LANES]
            for j in range(1, sub_rows):
                half = half + part[:, j * LANES : (j + 1) * LANES]
            ae_ref[pl.ds(start, WIN), :] += half

        for s in range(subs):
            start, _ = window(k, s)
            add_window(denv_ref, start, dot_nt(a_ref[k * subs + s], dt[:, sub_lanes(s)]))
            add_energy(s, start)

        def again(s, start):
            add_window(
                denv_ref, start, dot_nt(select(k, s, start), dt_ref[k, :, sub_lanes(s)])
            )
            add_energy(s, start)

        more_windows(k, again)
        return carry

    lax.fori_loop(0, n_chunks, phase_b, 0)

    def phase_c(k, carry):
        def env_terms(s, start, a, fresh):
            e_win = load_window(env_ref, start)
            d_win = load_window(denv_ref, start)
            dew = dot_tn(d_win, a)
            pair = jnp.concatenate(
                [dt_ref[k, :, sub_lanes(s)], ew_ref[k, :, sub_lanes(s)]], axis=0
            )
            prods = dot_nn(jnp.concatenate([e_win, d_win], axis=1), pair)
            hot = a[0:WIN].astype(F32)
            if fresh:
                big_ref[:, sub_lanes(s)] = dew
            else:
                big_ref[:, sub_lanes(s)] += dew
            for m in range(1, 9):
                row = jnp.sum(prods[m * WIN : (m + 1) * WIN] * hot, axis=0, keepdims=True)
                for j in range(sub_rows):
                    at = s * sub_rows + j
                    piece = row[:, j * LANES : (j + 1) * LANES]
                    if fresh:
                        dy_ref[m, pl.ds(at, 1), :] = piece
                    else:
                        dy_ref[m, pl.ds(at, 1), :] += piece

        for s in range(subs):
            start, _ = window(k, s)
            env_terms(s, start, a_ref[k * subs + s], True)
        more_windows(k, lambda s, start: env_terms(s, start, select(k, s, start), False))
        dew = big_ref[...]
        dpre = (dew * row_of(6, k)).astype(BF16)
        denv_row = jnp.sum(dew * ew_ref[k].astype(F32), axis=0, keepdims=True)
        for j in range(per):
            dy_ref[0, j : j + 1, :] = denv_row[:, j * LANES : (j + 1) * LANES]
        dfirst = dfa_ref[k].astype(F32) + dot_nn(
            wev_ref[...], jnp.concatenate([dpre, dv_ref[k]], axis=0)
        )
        dz1 = (dfirst * dsilu_ref[k].astype(F32)).astype(BF16)
        dboth = dot_nn(w1_ref[...], dz1)
        dmixed = dboth[0:chans].astype(BF16)
        dbasis = dboth[chans:]
        for j in range(per):
            db_ref[j * n_basis : (j + 1) * n_basis, :] = dbasis[
                0:n_basis, j * LANES : (j + 1) * LANES
            ]
        ux, uy, uz, dist, inv, q = [geo_ref[i, k] for i in range(6)]
        envelope = q * q
        g = envelope * inv
        denvelope = -(q * envelope) * dist
        dg = (denvelope - g) * inv
        sins, coss = waves(0.5 * dist, n_basis)
        denv_direct = live_ref[k] + dy_ref[0] / envelope
        ddist = denv_direct * denvelope
        for n in range(n_basis):
            db = db_ref[pl.ds(n, per, stride=n_basis), :]
            ddist = ddist + db * (coss[n] * ((n + 1) * math.pi / 2.0) * g + sins[n] * dg)
        y = [dy_ref[m] for m in range(9)]
        gx = y[1] + ROOT3 * (uy * y[4] + uz * y[6]) + (2.0 * 0.866) * ux * y[7]
        gy = y[2] + ROOT3 * (ux * y[4] + uz * y[5]) - (2.0 * 0.866) * uy * y[7]
        gz = y[3] + ROOT3 * (uy * y[5] + ux * y[6]) + 3.0 * uz * y[8]
        along = ddist - inv * (gx * ux + gy * uy + gz * uz)
        for i, (gu, u) in enumerate(((gx, ux), (gy, uy), (gz, uz))):
            hi, lo = split(inv * gu + along * u)
            dr_ref[pl.ds(i, per, stride=16), :] = hi
            dr_ref[pl.ds(3 + i, per, stride=16), :] = lo
        dr = jnp.concatenate([dr_ref[j * 16 : (j + 1) * 16, :] for j in range(per)], axis=1)
        kt = key_ref[k]
        crow = in_lanes(kt >> OTHER_BITS)
        orow = in_lanes(kt & OTHER_MASK)
        hots = [one_hot(crow, 0, own)]
        for base in range(0, n_tab, LANES):
            hots.append(one_hot(orow, base, min(LANES, n_tab - base)))
        sums = dot_nt(
            jnp.concatenate(hots, axis=0),
            jnp.concatenate([dmixed, dr.astype(BF16)], axis=0),
        )
        acc_ref[:, 0:chans] += sums[:, 0:chans]
        acc_ref[:, chans : chans + 16] += sums[:, chans:]
        return carry

    lax.fori_loop(0, n_chunks, phase_c, 0)

    own_ref[...] = acc_ref[0 : 2 * own, :]
    row = lax.broadcasted_iota(jnp.int32, (LANES, LANES), 0)
    group = lax.broadcasted_iota(jnp.int32, (LANES, LANES), 1) // GROUP
    both = ((group < 3) & ((row == group) | (row == group + 3))).astype(F32)
    places = dot_nn(acc_ref[2 * own :, LANES:], both, HIGH)
    found = {}
    at = 2 * own
    for off in OFFSETS:
        found[off] = at
        at += plan.live(off)
    for blocks, ref in zip(
        plan.groups[0] + [plan.held_rest], tuple(back_refs) + (rest_ref,)
    ):
        for off, row in plan.spans(blocks):
            live = plan.live(off)
            at = found[off]
            ref[row : row + live, :] = acc_ref[at : at + live, 0:chans]
            block = places[at - 2 * own : at - 2 * own + live, :]
            ref[row + live : row + live + 1, :] = jnp.sum(diagonal(block), axis=0, keepdims=True)


def own_kernel(ae_ref, own_ref, wa_ref, wb_ref, energy_ref, fg_ref, force_ref):
    chans = wa_ref.shape[1]
    own = force_ref.shape[1]
    energy_ref[...] = jnp.sum(ae_ref[0:own, :].T, axis=0, keepdims=True)
    fg_ref[...] = dot_nt(own_ref[0:own, 0:chans], wa_ref[...], HIGH) + dot_nt(
        own_ref[own:, 0:chans], wb_ref[...], HIGH
    )
    force = (own_ref[own:, LANES:] - own_ref[0:own, LANES:]).T
    force_ref[...] = force[0:3, :] + force[3:6, :]


def last_kernel(plan, sel_ref, fg_ref, force_ref, wb_ref, *refs):
    came, refs = plan.cut(refs, 0, 1, 2)
    out_force_ref, out_fg_ref, both_ref = refs
    both_ref[...] = jnp.zeros_like(both_ref)
    chans = fg_ref.shape[1]
    at = 0
    for blocks in plan.groups[2] + [plan.own_rest]:
        for off, row in plan.spans(blocks):
            live = plan.live(off)
            src, begin = plan.find(came, (2, 1, 0), None, [], off)
            here = slice(at + row, at + row + live)
            both_ref[here, 0:chans] = src[begin : begin + live, :]
            both_ref[here, chans:] = spread(src[begin + live : begin + live + 1, :], live)
        at += plan.total(blocks)
    sums = dot_exact(sel_ref[...].astype(BF16), both_ref[...], ((0,), (0,)))
    out_fg_ref[...] = fg_ref[...] + dot_nt(sums[:, 0:chans], wb_ref[...], HIGH)
    total = dot_nt(group_rows(8), sums[:, chans:], HIGH)
    out_force_ref[...] = -(force_ref[...] + total[0:3, :])


def stack(*arrays):
    dtype = arrays[0].dtype
    tile = 32 // dtype.itemsize
    starts = [0]
    for x in arrays:
        starts.append(starts[-1] + -(-x.shape[0] // tile) * tile)
    total = None
    for x, at in zip(arrays, starts):
        below = starts[-1] - at - x.shape[0]
        part = jnp.pad(x.astype(dtype), ((at, below), (0, LANES - x.shape[1])))
        total = part if total is None else total + part
    return total


def local(
    positions,
    atom_features,
    send_face,
    send_edge,
    send_corner,
    centre,
    other,
    edge_count,
    w_proj_a,
    w_proj_b,
    w_radial,
    w_first,
    w_env,
    w_value,
    w_second,
    w_out,
):
    own, chans = atom_features.shape
    edges = centre.shape[0]
    n_basis = w_radial.shape[0]
    plan = Plan(
        [send_face.shape[2], send_edge.shape[2], send_corner.shape[2]],
        [lax.axis_size(axis) for axis in AXES],
    )
    n_ghost = sum(len(c) * w for c, w in zip(CLASSES, plan.widths))
    n_sel = 2 * own + n_ghost
    n_send = sum(plan.total(blocks) for blocks in plan.groups[2]) + plan.total(plan.own_rest)
    n_table = n_sel + 4 * n_basis
    edges_up = -(-edges // CHUNK) * CHUNK
    n_rows = edges_up // LANES
    n_chunks = edges_up // CHUNK

    with jax.named_scope("prep"):
        rows = stack(
            atom_features,
            positions,
            send_face[0],
            jnp.transpose(send_edge[0]),
            jnp.transpose(send_corner[0]),
        )
        *sends, own_rows, sel = pl.pallas_call(
            lambda *refs: prep_kernel(plan, *refs),
            out_shape=plan.shapes(2, chans)
            + [shape(plan.total(plan.own_rest), chans), shape(n_send, own)],
            in_specs=[VMEM],
            out_specs=[VMEM] * (len(plan.groups[2]) + 2),
            scratch_shapes=[pltpu.VMEM((LANES, LANES), F32)],
            compiler_params=PARAMS,
        )(rows)

    came = {}
    with jax.named_scope("halo_z"):
        came[2] = plan.send(2, sends)

    with jax.named_scope("group_edges"):
        dead = (own - 1) * (OTHER_MASK + 1) + OTHER_MASK
        pad = [(0, edges_up - edges)]
        regs = max(sorted_size(edges_up) // (8 * LANES), 1)
        key, bounds = pl.pallas_call(
            lambda *refs: sort_kernel(dead, *refs),
            out_shape=[
                shape(n_chunks, CHUNK // LANES, LANES, dtype=jnp.int32),
                shape(2, LANES, dtype=jnp.int32),
            ],
            in_specs=[SMEM, VMEM, VMEM],
            out_specs=[VMEM] * 2,
            scratch_shapes=[pltpu.VMEM((16 * regs, LANES), F32)],
            compiler_params=PARAMS,
        )(
            edge_count,
            jnp.pad(centre, pad).reshape(n_rows, LANES),
            jnp.pad(other, pad).reshape(n_rows, LANES),
        )

    with jax.named_scope("halo_y"):
        came[2], key, bounds, w_first, w_env, w_value, w_second, w_out = lax.optimization_barrier(
            (came[2], key, bounds, w_first, w_env, w_value, w_second, w_out)
        )
        came[1] = plan.send(1, glue(plan, 1, (2,), plan.own_rest, own_rows, came))

    with jax.named_scope("weights"):
        wide = stack(w_proj_a, w_proj_b, w_radial)
        narrow = stack(w_first, w_env, w_value, w_second, w_out[None, :])
        half, *weights = pl.pallas_call(
            weight_kernel,
            out_shape=[
                shape(2 * own + 4 * n_basis, chans),
                shape(chans, chans, dtype=BF16),
                shape(2 * chans, chans, dtype=BF16),
                shape(chans, 2 * chans, dtype=BF16),
                shape(chans + 2 * n_basis, chans, dtype=BF16),
                shape(chans, 2 * chans, dtype=BF16),
                shape(2 * chans, chans, dtype=BF16),
                shape(chans, LANES),
            ],
            in_specs=[VMEM] * 3,
            out_specs=[VMEM] * 8,
            compiler_params=PARAMS,
        )(rows, wide, narrow)

    with jax.named_scope("halo_x"):
        came[1], half, weights = lax.optimization_barrier((came[1], half, weights))
        came[0] = plan.send(0, glue(plan, 0, (1, 2), plan.own_rest, own_rows, came))

    planes = (n_chunks, chans, CHUNK)
    scratch = [
        pltpu.VMEM((n_table, chans), F32),
        pltpu.VMEM((n_ghost, chans), F32),
        pltpu.VMEM((-(-n_ghost // LANES) * LANES, LANES), F32),
        pltpu.VMEM((chans, n_table), BF16),
        pltpu.VMEM((n_rows * 8, LANES), F32),
        pltpu.VMEM((n_rows * n_basis, LANES), F32),
        pltpu.VMEM((8, n_chunks, CHUNK // LANES, LANES), F32),
        pltpu.VMEM(planes, BF16),
        pltpu.VMEM(planes, BF16),
        pltpu.VMEM(planes, BF16),
        pltpu.VMEM(planes, BF16),
        pltpu.VMEM((edges_up // SUB, 9 * WIN, SUB), BF16),
        pltpu.VMEM((9, own + WIN, chans), F32),
        pltpu.VMEM((9, own + WIN, chans), F32),
        pltpu.VMEM((chans, CHUNK), F32),
        pltpu.VMEM(planes, BF16),
        pltpu.VMEM(planes, BF16),
        pltpu.VMEM(planes, BF16),
        pltpu.VMEM((n_chunks, CHUNK // LANES, LANES), F32),
        pltpu.VMEM((1, CHUNK), F32),
        pltpu.VMEM((9, CHUNK // LANES, LANES), F32),
        pltpu.VMEM((CHUNK // LANES * n_basis, LANES), F32),
        pltpu.VMEM((CHUNK // LANES * 16, LANES), F32),
        pltpu.VMEM((n_sel, 2 * LANES), F32),
    ]
    with jax.named_scope("layer"):
        given = [edge_count, bounds, key, positions, w_proj_b]
        given += [*came[0], *came[1], *came[2], half, *weights]
        atom_sums, own_sums, *back, held = pl.pallas_call(
            lambda *refs: main_kernel(plan, *refs),
            out_shape=[shape(own + WIN, LANES), shape(2 * own, 2 * LANES)]
            + plan.shapes(0, chans)
            + [shape(plan.total(plan.held_rest), chans)],
            in_specs=[SMEM, SMEM] + [VMEM] * (len(given) - 2),
            out_specs=[VMEM] * (3 + len(plan.groups[0])),
            scratch_shapes=scratch,
            compiler_params=PARAMS,
        )(*given)

    with jax.named_scope("halo_back"):
        home = {0: plan.send(0, back, back=True)}
        home[1] = plan.send(1, glue(plan, 1, (0,), plan.held_rest, held, home), back=True)
        home[2] = plan.send(2, glue(plan, 2, (1, 0), plan.held_rest, held, home), back=True)

    with jax.named_scope("own_part"):
        energy, fg, force = pl.pallas_call(
            own_kernel,
            out_shape=[shape(1, own), shape(own, chans), shape(3, own)],
            in_specs=[VMEM] * 4,
            out_specs=[VMEM] * 3,
            compiler_params=PARAMS,
        )(atom_sums, own_sums, w_proj_a, w_proj_b)

    with jax.named_scope("owner_sums"):
        given = [sel, fg, force, w_proj_b, *home[0], *home[1], *home[2]]
        forces, feature_grad = pl.pallas_call(
            lambda *refs: last_kernel(plan, *refs),
            out_shape=[shape(3, own), shape(own, chans)],
            in_specs=[VMEM] * len(given),
            out_specs=[VMEM] * 2,
            scratch_shapes=[pltpu.VMEM((n_send, chans + LANES), F32)],
            compiler_params=PARAMS,
        )(*given)
    return forces, energy.reshape(own), feature_grad


def solution(mesh):
    shard = P(AXES)
    return jax.shard_map(
        local,
        mesh=mesh,
        in_specs=(
            P(None, AXES),
            P(AXES, None),
            P(AXES, None, None),
            P(AXES, None, None),
            P(AXES, None, None),
            shard,
            shard,
            shard,
        )
        + (P(),) * 8,
        out_specs=(P(None, AXES), shard, P(AXES, None)),
        check_vma=False,
    )
```

```python
import math

import jax
import jax.numpy as jnp
from jax import lax
from jax.experimental import pallas as pl
from jax.experimental.pallas import tpu as pltpu
from jax.sharding import PartitionSpec as P

F32 = jnp.float32
BF16 = jnp.bfloat16
HIGH = lax.Precision.HIGHEST
AXES = ("gx", "gy", "gz")
CHUNK = 3072
SUB = 256
WIN = 16
OTHER_BITS = 9
OTHER_MASK = (1 << OTHER_BITS) - 1
LANES = 128
ROOT3 = 1.732


VMEM = pl.BlockSpec(memory_space=pltpu.VMEM)
SMEM = pl.BlockSpec(memory_space=pltpu.SMEM)
PARAMS = pltpu.CompilerParams(vmem_limit_bytes=52 * 2**20)


def shape(*dims, dtype=F32):
    return jax.ShapeDtypeStruct(dims, dtype)


def dot_nn(a, b, precision=None):
    return lax.dot_general(
        a, b, (((1,), (0,)), ((), ())), preferred_element_type=F32, precision=precision
    )


def dot_nt(a, b, precision=None):
    return lax.dot_general(
        a, b, (((1,), (1,)), ((), ())), preferred_element_type=F32, precision=precision
    )


def dot_tn(a, b, precision=None):
    return lax.dot_general(
        a, b, (((0,), (0,)), ((), ())), preferred_element_type=F32, precision=precision
    )


def offset_classes():
    classes = [[], [], []]
    for a in (-1, 0, 1):
        for b in (-1, 0, 1):
            for c in (-1, 0, 1):
                if (a, b, c) != (0, 0, 0):
                    classes[abs(a) + abs(b) + abs(c) - 1].append((a, b, c))
    return classes


CLASSES = offset_classes()


OFFSETS = [off for group in CLASSES for off in group]


def kind(off):
    return abs(off[0]) + abs(off[1]) + abs(off[2]) - 1


class Plan:
    def __init__(self, widths, sizes):
        self.widths = widths
        self.sizes = sizes
        self.groups = [self.group(a) for a in range(3)]
        self.own_rest = [off for off in OFFSETS if off[2] == 0]
        self.held_rest = [off for off in OFFSETS if off[0] == 0]

    def group(self, a):
        groups = {}
        for off in OFFSETS:
            if off[a] != 0:
                groups.setdefault(off[a] % self.sizes[a], []).append(off)
        return list(groups.values())

    def live(self, off):
        return self.widths[kind(off)]

    def rows(self, off):
        return self.live(off) + 1

    def total(self, blocks):
        return sum(self.rows(off) for off in blocks)

    def spans(self, blocks):
        at = 0
        for off in blocks:
            yield off, at
            at += self.rows(off)

    def place(self, a, off):
        for g, blocks in enumerate(self.groups[a]):
            if off in blocks:
                return g, dict(self.spans(blocks))[off]
        raise KeyError(off)

    def find(self, came, axes, rest_ref, rest, off):
        for a in axes:
            if off[a] != 0:
                g, begin = self.place(a, off)
                return came[a][g], begin
        return rest_ref, dict(self.spans(rest))[off]

    def cut(self, refs, *axes):
        came = {}
        for a in axes:
            n = len(self.groups[a])
            came[a], refs = refs[:n], refs[n:]
        return came, refs

    def shapes(self, a, chans):
        return [shape(self.total(blocks), chans) for blocks in self.groups[a]]

    def send(self, a, messages, back=False):
        n = self.sizes[a]
        got = []
        for blocks, message in zip(self.groups[a], messages):
            step = -blocks[0][a] if back else blocks[0][a]
            got.append(lax.ppermute(message, AXES[a], [(i, (i + step) % n) for i in range(n)]))
        return got


GROUP = 32


def group_rows(count):
    row = lax.broadcasted_iota(jnp.int32, (count, LANES), 0)
    group = lax.broadcasted_iota(jnp.int32, (count, LANES), 1) // GROUP
    return (row == group).astype(F32) * (group < 3).astype(F32)


def diagonal(x):
    row = lax.broadcasted_iota(jnp.int32, x.shape, 0)
    lane = lax.broadcasted_iota(jnp.int32, x.shape, 1)
    return jnp.where((lane & (GROUP - 1)) == row, x, 0.0)


def spread(row, live):
    return diagonal(jnp.broadcast_to(row, (live, LANES)))


def split(x):
    high = x.astype(BF16).astype(F32)
    return high, x - high


def dot_exact(hot, x, dims):
    high, low = split(x)
    both = jnp.concatenate([high, low], axis=1).astype(BF16)
    out = lax.dot_general(hot, both, (dims, ((), ())), preferred_element_type=F32)
    return out[:, 0 : x.shape[1]] + out[:, x.shape[1] :]


def prep_kernel(plan, rows_ref, *outs):
    n_z = len(plan.groups[2])
    sends, rest_ref, sel_ref, turn_ref = outs[:n_z], outs[n_z], outs[n_z + 1], outs[n_z + 2]
    own = sel_ref.shape[1]
    lane = lax.broadcasted_iota(jnp.int32, (1, own), 1).astype(F32)
    n_faces = len(CLASSES[0])
    turn_ref[...] = jnp.zeros_like(turn_ref)
    turn_ref[0:n_faces, :] = rows_ref[own + 8 : own + 8 + n_faces, :]
    columns = [turn_ref[...].T]
    at = own + 16
    for width in plan.widths[1:]:
        columns.append(rows_ref[at : at + width, :])
        at += -(-width // 8) * 8
    sel_ref[...] = jnp.zeros_like(sel_ref)
    messages = plan.groups[2] + [plan.own_rest]
    at = 0
    for blocks in messages:
        for off, begin in plan.spans(blocks):
            key = CLASSES[kind(off)].index(off)
            live = plan.live(off)
            column = columns[kind(off)][0:live, key : key + 1]
            sel_ref[at + begin : at + begin + live, :] = (column == lane).astype(F32)
        at += plan.total(blocks)
    pos = dot_tn(rows_ref[own : own + 3, :], group_rows(3), HIGH)
    sel = sel_ref[...]
    rows = dot_nn(sel, rows_ref[0:own, :], HIGH)
    places = dot_nn(sel, pos, HIGH)
    at = 0
    for blocks, send in zip(messages, tuple(sends) + (rest_ref,)):
        count = plan.total(blocks)
        send[...] = rows[at : at + count, :]
        for off, begin in plan.spans(blocks):
            live = plan.live(off)
            block = places[at + begin : at + begin + live, :]
            send[begin + live : begin + live + 1, :] = jnp.sum(
                diagonal(block), axis=0, keepdims=True
            )
        at += count


def glue_kernel(plan, a, axes, rest, *refs):
    rest_ref = refs[0]
    came, outs = plan.cut(refs[1:], *axes)
    for blocks, out in zip(plan.groups[a], outs):
        for off, row in plan.spans(blocks):
            src, begin = plan.find(came, axes, rest_ref, rest, off)
            out[row : row + plan.rows(off), :] = src[begin : begin + plan.rows(off), :]


def glue(plan, a, axes, rest, rest_rows, came):
    given = [rest_rows] + [message for axis in axes for message in came[axis]]
    outs = plan.shapes(a, rest_rows.shape[1])
    return pl.pallas_call(
        lambda *refs: glue_kernel(plan, a, axes, rest, *refs),
        out_shape=outs,
        in_specs=[VMEM] * len(given),
        out_specs=[VMEM] * len(outs),
        compiler_params=PARAMS,
    )(*given)


def sort_kernel(own, count_ref, centre_ref, other_ref, key_ref, bound_ref, turn_ref):
    dead = (own - 1) * (OTHER_MASK + 1) + OTHER_MASK
    rows = centre_ref.shape[0]
    regs = turn_ref.shape[0] // 16
    group = regs * 8
    row = lax.broadcasted_iota(jnp.int32, (rows, LANES), 0)
    lane = lax.broadcasted_iota(jnp.int32, (rows, LANES), 1)
    live = row * LANES + lane < count_ref[0]
    centre = centre_ref[...]
    key = jnp.where(live, (centre << OTHER_BITS) + other_ref[...], dead).astype(F32)
    x = [key[8 * v : 8 * v + 8, :] for v in range(rows // 8)]
    x += [jnp.full((8, LANES), float(dead), F32)] * (regs - len(x))
    n_windows = own // WIN
    free = regs - rows // 8
    if n_windows * SUB <= free * 8 * LANES:
        window = jnp.where(live, centre // WIN, -1)
        need = []
        used = jnp.zeros((1, 1), F32)
        for w in range(n_windows):
            hits = jnp.sum((window == w).astype(F32), axis=0, keepdims=True)
            hits = jnp.sum(hits, axis=1, keepdims=True)
            whole = jnp.floor((hits + (SUB - 1)) * (1.0 / SUB)) * SUB
            used = used + whole
            need.append(whole - hits)
        fits = used <= float(rows * LANES)
        slot = lax.broadcasted_iota(jnp.int32, (8, LANES), 0) * LANES
        slot = slot + lax.broadcasted_iota(jnp.int32, (8, LANES), 1)
        per_reg = 8 * LANES // SUB
        for w in range(n_windows):
            v = rows // 8 + w // per_reg
            at = slot - (w % per_reg) * SUB
            take = (at >= 0) & (at.astype(F32) < need[w]) & fits
            mark = float((w * WIN + WIN - 1) * (OTHER_MASK + 1) + OTHER_MASK)
            x[v] = jnp.where(take, mark, x[v])
    s = lax.broadcasted_iota(jnp.int32, (8, LANES), 0)
    ln = lax.broadcasted_iota(jnp.int32, (8, LANES), 1)
    base = ln * group + s * regs

    def sign(k, v):
        return jnp.where(((base + v) & k) == 0, 1.0, -1.0).astype(F32)

    last = [jnp.ones((8, LANES), F32)] * regs
    total = group * LANES
    k = 2
    while k <= total:
        signs = [sign(k, v) for v in range(regs)] if k < total else [1.0] * regs
        x = [x[v] * (last[v] * signs[v]) for v in range(regs)]
        last = signs
        j = k // 2
        while j >= 1:
            if j < regs:
                for v in range(regs):
                    if v & j == 0:
                        a, b = x[v], x[v | j]
                        x[v], x[v | j] = jnp.minimum(a, b), jnp.maximum(a, b)
            else:
                axis, step, size, ids = (
                    (0, j // regs, 8, s) if j < group else (1, j // group, LANES, ln)
                )
                low = (ids & step) == 0
                for v in range(regs):
                    up = pltpu.roll(x[v], size - step, axis)
                    if 2 * step == size:
                        mate = up
                    else:
                        mate = jnp.where(low, up, pltpu.roll(x[v], step, axis))
                    x[v] = jnp.where(low, jnp.minimum(x[v], mate), jnp.maximum(x[v], mate))
            j //= 2
        k *= 2
    least = x[0]
    most = jnp.where(x[0] == float(dead), -1.0, x[0])
    for v in range(1, regs):
        least = jnp.minimum(least, x[v])
        most = jnp.maximum(most, jnp.where(x[v] == float(dead), -1.0, x[v]))
    bound_ref[0:1, :] = jnp.min(least, axis=0, keepdims=True).astype(jnp.int32) >> OTHER_BITS
    bound_ref[1:2, :] = jnp.max(most, axis=0, keepdims=True).astype(jnp.int32) >> OTHER_BITS
    turned = jnp.concatenate(x + [jnp.zeros((LANES - group, LANES), F32)], axis=0).T
    turn_ref[...] = turned
    ratio = LANES // group
    parts = [
        turn_ref[pl.ds(i, rows, stride=ratio), 0:group] for i in range(ratio)
    ]
    done = jnp.concatenate(parts, axis=1).astype(jnp.int32)
    per = key_ref.shape[1]
    for c in range(key_ref.shape[0]):
        key_ref[c] = done[c * per : (c + 1) * per, :]


def weight_kernel(
    rows_ref,
    wide_ref,
    half_ref,
    tab_ref,
    w1t_ref,
    wevt_ref,
    w2t_ref,
    w1_ref,
    wev_ref,
    w2_ref,
    wcol_ref,
):
    chans = wide_ref.shape[1]
    rad_rows = wide_ref.shape[0] - 2 * chans
    own = (tab_ref.shape[0] - 4 * rad_rows) // 2
    wa, wb, rad = wide_ref[0:chans, :], wide_ref[chans : 2 * chans, :], wide_ref[2 * chans :, :]
    w1, wenv, wval = [half_ref[i * chans : (i + 1) * chans, :] for i in range(3)]
    w2 = half_ref[3 * chans : 5 * chans, :]

    def flip(w):
        return w.astype(F32).T.astype(BF16)

    down = dot_nn(rad, w1.astype(F32), HIGH)
    w1_ref[0:chans, :] = w1
    w1_ref[chans:, :] = jnp.concatenate([down, jnp.zeros_like(down)], axis=0).astype(BF16)
    w2_ref[...] = w2
    w1t_ref[...] = flip(w1)
    wevt_ref[0:chans, :] = flip(wenv)
    wevt_ref[chans:, :] = flip(wval)
    w2t_ref[:, 0:chans] = flip(w2[0:chans, :])
    w2t_ref[:, chans:] = flip(w2[chans:, :])
    wev_ref[:, 0:chans] = wenv
    wev_ref[:, chans:] = wval
    wout = half_ref[5 * chans : 5 * chans + 1, :].astype(F32)
    wcol_ref[...] = jnp.broadcast_to(wout, (LANES, chans)).T
    feat = rows_ref[0:own, :]
    tab_ref[0:own, :] = dot_nn(feat, wa, HIGH)
    tab_ref[own : 2 * own, :] = dot_nn(feat, wb, HIGH)
    rad_hi, rad_lo = split(rad)
    tab_ref[2 * own :, :] = jnp.concatenate([rad_hi, rad_hi, rad_lo, jnp.zeros_like(rad)], axis=0)


def harmonics(ux, uy, uz):
    return [
        ux,
        uy,
        uz,
        ROOT3 * ux * uy,
        ROOT3 * uy * uz,
        ROOT3 * ux * uz,
        0.866 * (ux * ux - uy * uy),
        0.5 * (3.0 * uz * uz - 1.0),
    ]


def trig(half):
    turns = jnp.round(half)
    x = math.pi * (half - turns)
    odd = turns - 2.0 * jnp.floor(0.5 * turns)
    sign = 1.0 - 2.0 * odd
    x2 = x * x
    s = jnp.full_like(x, -1.0 / 39916800)
    for coef in (1.0 / 362880, -1.0 / 5040, 1.0 / 120, -1.0 / 6, 1.0):
        s = s * x2 + coef
    c = jnp.full_like(x, 1.0 / 479001600)
    for coef in (-1.0 / 3628800, 1.0 / 40320, -1.0 / 720, 1.0 / 24, -0.5, 1.0):
        c = c * x2 + coef
    return sign * x * s, sign * c


def waves(half, count):
    s1, c1 = trig(half)
    sins, coss = [s1], [c1]
    s0, c0 = jnp.zeros_like(s1), jnp.ones_like(c1)
    for _ in range(count - 1):
        sn = 2.0 * c1 * sins[-1] - s0
        cn = 2.0 * c1 * coss[-1] - c0
        s0, c0 = sins[-1], coss[-1]
        sins.append(sn)
        coss.append(cn)
    return sins, coss


def look_up(table_row, index):
    low = index & (LANES - 1)
    high = index >> 7
    result = jnp.zeros(index.shape, F32)
    for block in range(table_row.shape[1] // LANES):
        part = jnp.broadcast_to(table_row[:, block * LANES : (block + 1) * LANES], index.shape)
        got = jnp.take_along_axis(part, low, axis=1)
        result = jnp.where(high == block, got, result)
    return result


def in_lanes(tile):
    return jnp.concatenate([tile[r : r + 1, :] for r in range(tile.shape[0])], axis=1)


def one_hot(row, base, count):
    near = jnp.clip(row - base, -1, LANES).astype(BF16)
    iota = lax.broadcasted_iota(jnp.int32, (count, row.shape[1]), 0).astype(BF16)
    return jnp.where(iota == near, jnp.ones((), BF16), jnp.zeros((), BF16))


def sorted_size(edges):
    return 1 << (edges - 1).bit_length()


def main_kernel(plan, *refs):
    bound_ref, key_ref, pos_ref, wb_ref = refs[:4]
    came, refs = plan.cut(refs[4:], 0, 1, 2)
    half_ref, w1t_ref, wevt_ref, w2t_ref, w1_ref, wev_ref, w2_ref, wcol_ref = refs[:8]
    ae_ref, own_ref = refs[8:10]
    n_x = len(plan.groups[0])
    back_refs, rest_ref = refs[10 : 10 + n_x], refs[10 + n_x]
    (
        tab_ref,
        ghost_ref,
        place_ref,
        table_ref,
        y_ref,
        basis_ref,
        geo_ref,
        first_ref,
        dsilu_ref,
        ew_ref,
        val_ref,
        a_ref,
        env_ref,
        denv_ref,
        big_ref,
        dt_ref,
        dv_ref,
        dfa_ref,
        live_ref,
        dy_ref,
        db_ref,
        dr_ref,
        acc_ref,
        cacc_ref,
    ) = refs[11 + n_x :]
    own = pos_ref.shape[1]
    chans = w1_ref.shape[1]
    n_basis = (w1_ref.shape[0] - chans) // 2
    rows_all = key_ref.shape[0] * key_ref.shape[1]
    per = CHUNK // LANES
    subs = CHUNK // SUB
    sub_rows = SUB // LANES
    n_ghost = sum(len(c) * w for c, w in zip(CLASSES, plan.widths))
    n_tab = own + n_ghost
    n_sel = own + n_tab

    place_ref[...] = jnp.zeros_like(place_ref)
    at = 0
    for off in OFFSETS:
        live = plan.live(off)
        message, begin = plan.find(came, (0, 1, 2), None, [], off)
        ghost_ref[at : at + live, :] = message[begin : begin + live, :]
        place_ref[at : at + live, :] = spread(message[begin + live : begin + live + 1, :], live)
        at += live
    ghost_pos = dot_nt(group_rows(8), place_ref[...], HIGH)
    pos_t = jnp.concatenate([pos_ref[...], ghost_pos[0:3, :]], axis=1)
    f_hi, f_lo = split(ghost_ref[...])
    w_hi, w_lo = split(wb_ref[...])
    tab_ref[0 : 2 * own, :] = half_ref[0 : 2 * own, :]
    tab_ref[2 * own : n_sel, :] = dot_nn(
        jnp.concatenate([f_hi, f_lo, f_hi], axis=1).astype(BF16),
        jnp.concatenate([w_hi, w_hi, w_lo], axis=0).astype(BF16),
    )
    tab_ref[n_sel:, :] = half_ref[2 * own :, :]
    table_ref[...] = tab_ref[...].T.astype(BF16)

    keys = key_ref[...].reshape(rows_all, LANES)
    centre = keys >> OTHER_BITS
    other = keys & OTHER_MASK
    valid = (other != OTHER_MASK).astype(F32)
    r = [
        look_up(pos_t[a : a + 1, :], other) - look_up(pos_t[a : a + 1, 0:LANES], centre)
        for a in range(3)
    ]
    d2 = r[0] * r[0] + r[1] * r[1] + r[2] * r[2] + 0.01
    dist = jnp.sqrt(d2)
    inv = 1.0 / dist
    q = 1.0 / (1.0 + 0.25 * d2)
    envelope = q * q
    unit = [x * inv for x in r]
    for m, comp in enumerate(harmonics(*unit)):
        y_ref[pl.ds(m, rows_all, stride=8), :] = comp
    sins, _ = waves(0.5 * dist, n_basis)
    scale = envelope * inv
    for n in range(n_basis):
        basis_ref[pl.ds(n, rows_all, stride=n_basis), :] = sins[n] * scale
    for i, plane in enumerate((unit[0], unit[1], unit[2], dist, inv, q, envelope * valid, valid)):
        geo_ref[i] = plane.reshape(geo_ref.shape[1:])

    env_ref[...] = jnp.zeros_like(env_ref)
    denv_ref[...] = jnp.zeros_like(denv_ref)
    ae_ref[...] = jnp.zeros_like(ae_ref)
    acc_ref[...] = jnp.zeros_like(acc_ref)
    cacc_ref[...] = jnp.zeros_like(cacc_ref)
    dr_ref[...] = jnp.zeros_like(dr_ref)

    groups = bound_ref.shape[1] * SUB // sorted_size(rows_all * LANES)

    def window(k, s):
        first = (k * subs + s) * groups
        low = bound_ref[0, first]
        high = low
        for g in range(groups):
            high = jnp.maximum(high, bound_ref[1, first + g])
        start = pl.multiple_of((low >> 3) << 3, 8)
        more = lax.div(high - start, jnp.int32(WIN))
        return start, more

    most = jnp.int32(0)
    n_chunks = jnp.int32(0)
    for s in range(rows_all // sub_rows):
        most = jnp.maximum(most, window(s // subs, s % subs)[1])
        for g in range(groups):
            any_live = bound_ref[1, s * groups + g] >= 0
            n_chunks = jnp.where(any_live, s // subs + 1, n_chunks)


    def lanes_of(s, n):
        if isinstance(s, int):
            return slice(s * SUB, (s + n) * SUB)
        return pl.ds(pl.multiple_of(s * SUB, SUB), n * SUB)

    def tile_of(load, s, n):
        if isinstance(s, int):
            return load(slice(s * sub_rows, (s + n) * sub_rows))
        return jnp.concatenate(
            [load(pl.ds(s * sub_rows + j, 1)) for j in range(n * sub_rows)], axis=0
        )

    def plane(i, k, s, n):
        return tile_of(lambda rows: geo_ref[i, k, rows, :], s, n)

    def keys_of(k, s, n):
        return tile_of(lambda rows: key_ref[k, rows, :], s, n)

    def stacked(ref, k, s, n, height):
        first = (k * subs + s) * sub_rows
        tiles = [
            ref[pl.ds(pl.multiple_of((first + j) * height, 8), height), :]
            for j in range(n * sub_rows)
        ]
        return jnp.concatenate(tiles, axis=1)

    def window_hot(k, s, start):
        crow = in_lanes(keys_of(k, s, 1) >> OTHER_BITS) - start
        return lax.broadcasted_iota(jnp.int32, (WIN, SUB), 0) == crow

    def select(k, s, start):
        hot = window_hot(k, s, start)
        ys = stacked(y_ref, k, s, 1, 8)
        parts = [hot.astype(F32)]
        for m in range(8):
            parts.append(jnp.where(hot, ys[m : m + 1, :], 0.0))
        return jnp.concatenate(parts, axis=0).astype(BF16)

    def load_window(ref, start):
        return jnp.concatenate(
            [ref[m, pl.ds(start, WIN), :] for m in range(9)], axis=0
        ).astype(BF16)

    def add_window(ref, start, rows):
        for m in range(9):
            ref[m, pl.ds(start, WIN), :] += rows[m * WIN : (m + 1) * WIN, :]

    def each_window(k, s, n, slow, body):
        for j in range(n):
            start, more = window(k, s + j)
            body(s + j, j, start, True)
            if slow:

                def step(i, carry, s=s, j=j, start=start):
                    body(s + j, j, pl.multiple_of(start + i * WIN, 8), False)
                    return carry

                lax.fori_loop(1, more + 1, step, 0)

    def kept(k, s, start, fresh):
        return a_ref[k * subs + s] if fresh else select(k, s, start)

    def table_hots(k, s, n):
        row = in_lanes(keys_of(k, s, n) & OTHER_MASK)
        return [one_hot(row, at, min(LANES, n_tab - at)) for at in range(0, n_tab, LANES)]

    def part(j):
        return slice(j * SUB, (j + 1) * SUB)

    def phase_a(k, s, n, slow):
        lanes = lanes_of(s, n)
        crow = in_lanes(keys_of(k, s, n) >> OTHER_BITS)
        hots = [one_hot(crow, 0, own)] + table_hots(k, s, n)
        basis = stacked(basis_ref, k, s, n, n_basis)
        b_hi, b_lo = split(basis)
        hots.append(jnp.concatenate([b_hi, b_lo], axis=0).astype(BF16))
        hots.append(jnp.concatenate([b_hi, jnp.zeros_like(b_hi)], axis=0).astype(BF16))
        mixed = dot_nn(table_ref[...], jnp.concatenate(hots, axis=0)).astype(BF16)
        z1 = dot_nn(w1t_ref[...], mixed)
        sg = 0.5 + 0.5 * jnp.tanh(0.5 * z1)
        first = z1 * sg
        dsilu_ref[k, :, lanes] = (sg + first * (1.0 - sg)).astype(BF16)
        first = first.astype(BF16)
        first_ref[k, :, lanes] = first
        both = dot_nn(wevt_ref[...], first)
        ew = (both[0:chans] * in_lanes(plane(6, k, s, n))).astype(BF16)
        ew_ref[k, :, lanes] = ew
        val_ref[k, :, lanes] = both[chans:].astype(BF16)

        def body(s, j, start, fresh):
            a = select(k, s, start)
            if fresh:
                a_ref[k * subs + s] = a
            add_window(env_ref, start, dot_nt(a, ew[:, part(j)]))

        each_window(k, s, n, slow, body)

    def phase_b(k, s, n, slow):
        lanes = lanes_of(s, n)

        def totals(s, j, start, fresh):
            value = dot_tn(load_window(env_ref, start), kept(k, s, start, fresh))
            if fresh:
                big_ref[:, part(j)] = value
            else:
                big_ref[:, part(j)] += value

        each_window(k, s, n, slow, totals)
        total = 0.2 * big_ref[:, 0 : n * SUB]
        value = val_ref[k, :, lanes].astype(F32)
        scalar = (value * total).astype(BF16)
        z2 = dot_nn(w2t_ref[...], jnp.concatenate([first_ref[k, :, lanes], scalar], axis=0))
        sg = 0.5 + 0.5 * jnp.tanh(0.5 * z2)
        second = z2 * sg
        wcol = jnp.concatenate([wcol_ref[...]] * (n * sub_rows), axis=1)
        ee = jnp.sum(second.astype(BF16).astype(F32) * wcol, axis=0, keepdims=True)
        envv = in_lanes(plane(6, k, s, n))
        live = ee * in_lanes(plane(7, k, s, n))
        first_row = s * sub_rows
        for j in range(n * sub_rows):
            live_ref[k, pl.ds(first_row + j, 1), :] = live[:, j * LANES : (j + 1) * LANES]
        energy = ee * envv
        dz2 = ((wcol * envv) * (sg + second * (1.0 - sg))).astype(BF16)
        dj = dot_nn(w2_ref[...], dz2)
        dfa_ref[k, :, lanes] = dj[0:chans].astype(BF16)
        dscalar = dj[chans:]
        dt = (0.2 * value * dscalar).astype(BF16)
        dt_ref[k, :, lanes] = dt
        dv_ref[k, :, lanes] = (total * dscalar).astype(BF16)

        def body(s, j, start, fresh):
            add_window(denv_ref, start, dot_nt(kept(k, s, start, fresh), dt[:, part(j)]))
            mine = jnp.where(window_hot(k, s, start), energy[:, part(j)], 0.0)
            half = mine[:, 0:LANES]
            for i in range(1, sub_rows):
                half = half + mine[:, i * LANES : (i + 1) * LANES]
            ae_ref[pl.ds(start, WIN), :] += half

        each_window(k, s, n, slow, body)

    def phase_c(k, s, n, slow):
        lanes = lanes_of(s, n)
        height = n * sub_rows

        def env_terms(s, j, start, fresh):
            a = kept(k, s, start, fresh)
            e_win = load_window(env_ref, start)
            d_win = load_window(denv_ref, start)
            dew = dot_tn(d_win, a)
            here = lanes_of(s, 1)
            pair = jnp.concatenate([dt_ref[k, :, here], ew_ref[k, :, here]], axis=0)
            prods = dot_nn(jnp.concatenate([e_win, d_win], axis=1), pair)
            hot = a[0:WIN].astype(F32)
            if fresh:
                big_ref[:, part(j)] = dew
            else:
                big_ref[:, part(j)] += dew
            for m in range(1, 9):
                row = jnp.sum(prods[m * WIN : (m + 1) * WIN] * hot, axis=0, keepdims=True)
                for i in range(sub_rows):
                    at = j * sub_rows + i
                    piece = row[:, i * LANES : (i + 1) * LANES]
                    if fresh:
                        dy_ref[m, at : at + 1, :] = piece
                    else:
                        dy_ref[m, at : at + 1, :] += piece

        each_window(k, s, n, slow, env_terms)
        dew = big_ref[:, 0 : n * SUB]
        dpre = (dew * in_lanes(plane(6, k, s, n))).astype(BF16)
        denv_row = jnp.sum(dew * ew_ref[k, :, lanes].astype(F32), axis=0, keepdims=True)
        for j in range(height):
            dy_ref[0, j : j + 1, :] = denv_row[:, j * LANES : (j + 1) * LANES]
        dfirst = dfa_ref[k, :, lanes].astype(F32) + dot_nn(
            wev_ref[...], jnp.concatenate([dpre, dv_ref[k, :, lanes]], axis=0)
        )
        dz1 = (dfirst * dsilu_ref[k, :, lanes].astype(F32)).astype(BF16)
        dboth = dot_nn(w1_ref[...], dz1)
        dmixed = dboth[0:chans].astype(BF16)
        dbasis = dboth[chans:]
        for j in range(height):
            db_ref[j * n_basis : (j + 1) * n_basis, :] = dbasis[
                0:n_basis, j * LANES : (j + 1) * LANES
            ]
        ux, uy, uz, dist, inv, q = [plane(i, k, s, n) for i in range(6)]
        envelope = q * q
        g = envelope * inv
        denvelope = -(q * envelope) * dist
        dg = (denvelope - g) * inv
        sins, coss = waves(0.5 * dist, n_basis)
        live = tile_of(lambda rows: live_ref[k, rows, :], s, n)
        y = [dy_ref[m, 0:height, :] for m in range(9)]
        ddist = (live + y[0] / envelope) * denvelope
        for i in range(n_basis):
            db = db_ref[pl.ds(i, height, stride=n_basis), :]
            ddist = ddist + db * (coss[i] * ((i + 1) * math.pi / 2.0) * g + sins[i] * dg)
        gx = y[1] + ROOT3 * (uy * y[4] + uz * y[6]) + (2.0 * 0.866) * ux * y[7]
        gy = y[2] + ROOT3 * (ux * y[4] + uz * y[5]) - (2.0 * 0.866) * uy * y[7]
        gz = y[3] + ROOT3 * (uy * y[5] + ux * y[6]) + 3.0 * uz * y[8]
        along = ddist - inv * (gx * ux + gy * uy + gz * uz)
        for i, (gu, u) in enumerate(((gx, ux), (gy, uy), (gz, uz))):
            hi, lo = split(inv * gu + along * u)
            dr_ref[pl.ds(i, height, stride=16), :] = hi
            dr_ref[pl.ds(3 + i, height, stride=16), :] = lo
        dr = jnp.concatenate([dr_ref[j * 16 : (j + 1) * 16, :] for j in range(height)], axis=1)
        moved = jnp.concatenate([dmixed, dr.astype(BF16)], axis=0)
        sums = dot_nt(jnp.concatenate(table_hots(k, s, n), axis=0), moved)
        acc_ref[:, 0:chans] += sums[:, 0:chans]
        acc_ref[:, chans : chans + 16] += sums[:, chans:]

        def body(s, j, start, fresh):
            hot = a_ref[k * subs + s, 0:WIN, :] if fresh else window_hot(k, s, start).astype(BF16)
            mine = dot_nt(hot, moved[:, part(j)])
            cacc_ref[pl.ds(start, WIN), 0:chans] += mine[:, 0:chans]
            cacc_ref[pl.ds(start, WIN), chans : chans + 16] += mine[:, chans:]

        each_window(k, s, n, slow, body)

    for phase in (phase_a, phase_b, phase_c):

        @pl.when(most == 0)
        def _(phase=phase):
            def chunk(k, carry):
                phase(k, 0, subs, False)
                return carry

            lax.fori_loop(0, n_chunks, chunk, 0)

        @pl.when(most != 0)
        def _(phase=phase):
            def sub(i, carry):
                phase(lax.div(i, subs), lax.rem(i, subs), 1, True)
                return carry

            lax.fori_loop(0, n_chunks * subs, sub, 0)

    own_ref[0:own, :] = cacc_ref[0:own, :]
    own_ref[own:, :] = acc_ref[0:own, :]
    row = lax.broadcasted_iota(jnp.int32, (LANES, LANES), 0)
    group = lax.broadcasted_iota(jnp.int32, (LANES, LANES), 1) // GROUP
    both = ((group < 3) & ((row == group) | (row == group + 3))).astype(F32)
    places = dot_nn(acc_ref[own:, LANES:], both, HIGH)
    found = {}
    at = own
    for off in OFFSETS:
        found[off] = at
        at += plan.live(off)
    for blocks, ref in zip(
        plan.groups[0] + [plan.held_rest], tuple(back_refs) + (rest_ref,)
    ):
        for off, row in plan.spans(blocks):
            live = plan.live(off)
            at = found[off]
            ref[row : row + live, :] = acc_ref[at : at + live, 0:chans]
            block = places[at - own : at - own + live, :]
            ref[row + live : row + live + 1, :] = jnp.sum(diagonal(block), axis=0, keepdims=True)


def own_kernel(ae_ref, own_ref, wa_ref, wb_ref, energy_ref, fg_ref, force_ref):
    chans = wa_ref.shape[1]
    own = force_ref.shape[1]
    energy_ref[...] = jnp.sum(ae_ref[0:own, :].T, axis=0, keepdims=True)
    fg_ref[...] = dot_nt(own_ref[0:own, 0:chans], wa_ref[...], HIGH) + dot_nt(
        own_ref[own:, 0:chans], wb_ref[...], HIGH
    )
    force = (own_ref[own:, LANES:] - own_ref[0:own, LANES:]).T
    force_ref[...] = force[0:3, :] + force[3:6, :]


def last_kernel(plan, sel_ref, fg_ref, force_ref, wb_ref, *refs):
    came, refs = plan.cut(refs, 0, 1, 2)
    out_force_ref, out_fg_ref, both_ref = refs
    both_ref[...] = jnp.zeros_like(both_ref)
    chans = fg_ref.shape[1]
    at = 0
    for blocks in plan.groups[2] + [plan.own_rest]:
        for off, row in plan.spans(blocks):
            live = plan.live(off)
            src, begin = plan.find(came, (2, 1, 0), None, [], off)
            here = slice(at + row, at + row + live)
            both_ref[here, 0:chans] = src[begin : begin + live, :]
            both_ref[here, chans:] = spread(src[begin + live : begin + live + 1, :], live)
        at += plan.total(blocks)
    sums = dot_exact(sel_ref[...].astype(BF16), both_ref[...], ((0,), (0,)))
    out_fg_ref[...] = fg_ref[...] + dot_nt(sums[:, 0:chans], wb_ref[...], HIGH)
    total = dot_nt(group_rows(8), sums[:, chans:], HIGH)
    out_force_ref[...] = -(force_ref[...] + total[0:3, :])


def stack(*arrays):
    dtype = arrays[0].dtype
    tile = 32 // dtype.itemsize
    starts = [0]
    for x in arrays:
        starts.append(starts[-1] + -(-x.shape[0] // tile) * tile)
    total = None
    for x, at in zip(arrays, starts):
        below = starts[-1] - at - x.shape[0]
        part = jnp.pad(x.astype(dtype), ((at, below), (0, LANES - x.shape[1])))
        total = part if total is None else total + part
    return total


def local(
    positions,
    atom_features,
    send_face,
    send_edge,
    send_corner,
    centre,
    other,
    edge_count,
    w_proj_a,
    w_proj_b,
    w_radial,
    w_first,
    w_env,
    w_value,
    w_second,
    w_out,
):
    own, chans = atom_features.shape
    edges = centre.shape[0]
    n_basis = w_radial.shape[0]
    plan = Plan(
        [send_face.shape[2], send_edge.shape[2], send_corner.shape[2]],
        [lax.axis_size(axis) for axis in AXES],
    )
    n_ghost = sum(len(c) * w for c, w in zip(CLASSES, plan.widths))
    n_sel = 2 * own + n_ghost
    n_send = sum(plan.total(blocks) for blocks in plan.groups[2]) + plan.total(plan.own_rest)
    n_table = n_sel + 4 * n_basis
    edges_up = -(-edges // CHUNK) * CHUNK
    n_rows = edges_up // LANES
    n_chunks = edges_up // CHUNK

    with jax.named_scope("prep"):
        rows = stack(
            atom_features,
            positions,
            send_face[0],
            jnp.transpose(send_edge[0]),
            jnp.transpose(send_corner[0]),
        )
        *sends, own_rows, sel = pl.pallas_call(
            lambda *refs: prep_kernel(plan, *refs),
            out_shape=plan.shapes(2, chans)
            + [shape(plan.total(plan.own_rest), chans), shape(n_send, own)],
            in_specs=[VMEM],
            out_specs=[VMEM] * (len(plan.groups[2]) + 2),
            scratch_shapes=[pltpu.VMEM((LANES, LANES), F32)],
            compiler_params=PARAMS,
        )(rows)

    came = {}
    with jax.named_scope("halo_z"):
        came[2] = plan.send(2, sends)

    with jax.named_scope("group_edges"):
        pad = [(0, edges_up - edges)]
        regs = max(sorted_size(edges_up) // (8 * LANES), 1)
        key, bounds = pl.pallas_call(
            lambda *refs: sort_kernel(own, *refs),
            out_shape=[
                shape(n_chunks, CHUNK // LANES, LANES, dtype=jnp.int32),
                shape(2, LANES, dtype=jnp.int32),
            ],
            in_specs=[SMEM, VMEM, VMEM],
            out_specs=[VMEM] * 2,
            scratch_shapes=[pltpu.VMEM((16 * regs, LANES), F32)],
            compiler_params=PARAMS,
        )(
            edge_count,
            jnp.pad(centre, pad).reshape(n_rows, LANES),
            jnp.pad(other, pad).reshape(n_rows, LANES),
        )

    with jax.named_scope("halo_y"):
        came[2], key, bounds, w_first, w_env, w_value, w_second, w_out = lax.optimization_barrier(
            (came[2], key, bounds, w_first, w_env, w_value, w_second, w_out)
        )
        came[1] = plan.send(1, glue(plan, 1, (2,), plan.own_rest, own_rows, came))

    with jax.named_scope("weights"):
        wide = stack(w_proj_a, w_proj_b, w_radial)
        narrow = stack(w_first, w_env, w_value, w_second, w_out[None, :])
        half, *weights = pl.pallas_call(
            weight_kernel,
            out_shape=[
                shape(2 * own + 4 * n_basis, chans),
                shape(chans, chans, dtype=BF16),
                shape(2 * chans, chans, dtype=BF16),
                shape(chans, 2 * chans, dtype=BF16),
                shape(chans + 2 * n_basis, chans, dtype=BF16),
                shape(chans, 2 * chans, dtype=BF16),
                shape(2 * chans, chans, dtype=BF16),
                shape(chans, LANES),
            ],
            in_specs=[VMEM] * 3,
            out_specs=[VMEM] * 8,
            compiler_params=PARAMS,
        )(rows, wide, narrow)

    with jax.named_scope("halo_x"):
        came[1], half, weights = lax.optimization_barrier((came[1], half, weights))
        came[0] = plan.send(0, glue(plan, 0, (1, 2), plan.own_rest, own_rows, came))

    planes = (n_chunks, chans, CHUNK)
    scratch = [
        pltpu.VMEM((n_table, chans), F32),
        pltpu.VMEM((n_ghost, chans), F32),
        pltpu.VMEM((-(-n_ghost // LANES) * LANES, LANES), F32),
        pltpu.VMEM((chans, n_table), BF16),
        pltpu.VMEM((n_rows * 8, LANES), F32),
        pltpu.VMEM((n_rows * n_basis, LANES), F32),
        pltpu.VMEM((8, n_chunks, CHUNK // LANES, LANES), F32),
        pltpu.VMEM(planes, BF16),
        pltpu.VMEM(planes, BF16),
        pltpu.VMEM(planes, BF16),
        pltpu.VMEM(planes, BF16),
        pltpu.VMEM((edges_up // SUB, 9 * WIN, SUB), BF16),
        pltpu.VMEM((9, own + WIN, chans), F32),
        pltpu.VMEM((9, own + WIN, chans), F32),
        pltpu.VMEM((chans, CHUNK), F32),
        pltpu.VMEM(planes, BF16),
        pltpu.VMEM(planes, BF16),
        pltpu.VMEM(planes, BF16),
        pltpu.VMEM((n_chunks, CHUNK // LANES, LANES), F32),
        pltpu.VMEM((9, CHUNK // LANES, LANES), F32),
        pltpu.VMEM((CHUNK // LANES * n_basis, LANES), F32),
        pltpu.VMEM((CHUNK // LANES * 16, LANES), F32),
        pltpu.VMEM((n_sel - own, 2 * LANES), F32),
        pltpu.VMEM((own + WIN, 2 * LANES), F32),
    ]
    with jax.named_scope("layer"):
        given = [bounds, key, positions, w_proj_b]
        given += [*came[0], *came[1], *came[2], half, *weights]
        atom_sums, own_sums, *back, held = pl.pallas_call(
            lambda *refs: main_kernel(plan, *refs),
            out_shape=[shape(own + WIN, LANES), shape(2 * own, 2 * LANES)]
            + plan.shapes(0, chans)
            + [shape(plan.total(plan.held_rest), chans)],
            in_specs=[SMEM] + [VMEM] * (len(given) - 1),
            out_specs=[VMEM] * (3 + len(plan.groups[0])),
            scratch_shapes=scratch,
            compiler_params=PARAMS,
        )(*given)

    with jax.named_scope("halo_back"):
        home = {0: plan.send(0, back, back=True)}
        home[1] = plan.send(1, glue(plan, 1, (0,), plan.held_rest, held, home), back=True)
        home[2] = plan.send(2, glue(plan, 2, (1, 0), plan.held_rest, held, home), back=True)

    with jax.named_scope("own_part"):
        energy, fg, force = pl.pallas_call(
            own_kernel,
            out_shape=[shape(1, own), shape(own, chans), shape(3, own)],
            in_specs=[VMEM] * 4,
            out_specs=[VMEM] * 3,
            compiler_params=PARAMS,
        )(atom_sums, own_sums, w_proj_a, w_proj_b)

    with jax.named_scope("owner_sums"):
        given = [sel, fg, force, w_proj_b, *home[0], *home[1], *home[2]]
        forces, feature_grad = pl.pallas_call(
            lambda *refs: last_kernel(plan, *refs),
            out_shape=[shape(3, own), shape(own, chans)],
            in_specs=[VMEM] * len(given),
            out_specs=[VMEM] * 2,
            scratch_shapes=[pltpu.VMEM((n_send, chans + LANES), F32)],
            compiler_params=PARAMS,
        )(*given)
    return forces, energy.reshape(own), feature_grad


def solution(mesh):
    shard = P(AXES)
    return jax.shard_map(
        local,
        mesh=mesh,
        in_specs=(
            P(None, AXES),
            P(AXES, None),
            P(AXES, None, None),
            P(AXES, None, None),
            P(AXES, None, None),
            shard,
            shard,
            shard,
        )
        + (P(),) * 8,
        out_specs=(P(None, AXES), shard, P(AXES, None)),
        check_vma=False,
    )
```

```python
import math

import jax
import jax.numpy as jnp
from jax import lax
from jax.experimental import pallas as pl
from jax.experimental.pallas import tpu as pltpu
from jax.sharding import PartitionSpec as P

F32 = jnp.float32
BF16 = jnp.bfloat16
HIGH = lax.Precision.HIGHEST
AXES = ("gx", "gy", "gz")
CHUNK = 512
SUB = 256
WIN = 16
OTHER_BITS = 9
OTHER_MASK = (1 << OTHER_BITS) - 1
LANES = 128
ROOT3 = 1.732


VMEM = pl.BlockSpec(memory_space=pltpu.VMEM)
SMEM = pl.BlockSpec(memory_space=pltpu.SMEM)
PARAMS = pltpu.CompilerParams(vmem_limit_bytes=52 * 2**20)


def shape(*dims, dtype=F32):
    return jax.ShapeDtypeStruct(dims, dtype)


def dot_nn(a, b, precision=None):
    return lax.dot_general(
        a, b, (((1,), (0,)), ((), ())), preferred_element_type=F32, precision=precision
    )


def dot_nt(a, b, precision=None):
    return lax.dot_general(
        a, b, (((1,), (1,)), ((), ())), preferred_element_type=F32, precision=precision
    )


def dot_tn(a, b, precision=None):
    return lax.dot_general(
        a, b, (((0,), (0,)), ((), ())), preferred_element_type=F32, precision=precision
    )


def offset_classes():
    classes = [[], [], []]
    for a in (-1, 0, 1):
        for b in (-1, 0, 1):
            for c in (-1, 0, 1):
                if (a, b, c) != (0, 0, 0):
                    classes[abs(a) + abs(b) + abs(c) - 1].append((a, b, c))
    return classes


CLASSES = offset_classes()


OFFSETS = [off for group in CLASSES for off in group]


def kind(off):
    return abs(off[0]) + abs(off[1]) + abs(off[2]) - 1


class Plan:
    def __init__(self, widths, sizes):
        self.widths = widths
        self.sizes = sizes
        self.groups = [self.group(a) for a in range(3)]
        self.own_rest = [off for off in OFFSETS if off[2] == 0]
        self.held_rest = [off for off in OFFSETS if off[0] == 0]

    def group(self, a):
        groups = {}
        for off in OFFSETS:
            if off[a] != 0:
                groups.setdefault(off[a] % self.sizes[a], []).append(off)
        return list(groups.values())

    def live(self, off):
        return self.widths[kind(off)]

    def rows(self, off):
        return self.live(off) + 1

    def total(self, blocks):
        return sum(self.rows(off) for off in blocks)

    def spans(self, blocks):
        at = 0
        for off in blocks:
            yield off, at
            at += self.rows(off)

    def place(self, a, off):
        for g, blocks in enumerate(self.groups[a]):
            if off in blocks:
                return g, dict(self.spans(blocks))[off]
        raise KeyError(off)

    def find(self, came, axes, rest_ref, rest, off):
        for a in axes:
            if off[a] != 0:
                g, begin = self.place(a, off)
                return came[a][g], begin
        return rest_ref, dict(self.spans(rest))[off]

    def cut(self, refs, *axes):
        came = {}
        for a in axes:
            n = len(self.groups[a])
            came[a], refs = refs[:n], refs[n:]
        return came, refs

    def shapes(self, a, chans):
        return [shape(self.total(blocks), chans) for blocks in self.groups[a]]

    def send(self, a, messages, back=False):
        n = self.sizes[a]
        got = []
        for blocks, message in zip(self.groups[a], messages):
            step = -blocks[0][a] if back else blocks[0][a]
            got.append(lax.ppermute(message, AXES[a], [(i, (i + step) % n) for i in range(n)]))
        return got


GROUP = 32


def group_rows(count):
    row = lax.broadcasted_iota(jnp.int32, (count, LANES), 0)
    group = lax.broadcasted_iota(jnp.int32, (count, LANES), 1) // GROUP
    return (row == group).astype(F32) * (group < 3).astype(F32)


def diagonal(x):
    row = lax.broadcasted_iota(jnp.int32, x.shape, 0)
    lane = lax.broadcasted_iota(jnp.int32, x.shape, 1)
    return jnp.where((lane & (GROUP - 1)) == row, x, 0.0)


def spread(row, live):
    return diagonal(jnp.broadcast_to(row, (live, LANES)))


def split(x):
    high = x.astype(BF16).astype(F32)
    return high, x - high


def dot_exact(hot, x, dims):
    high, low = split(x)
    both = jnp.concatenate([high, low], axis=1).astype(BF16)
    out = lax.dot_general(hot, both, (dims, ((), ())), preferred_element_type=F32)
    return out[:, 0 : x.shape[1]] + out[:, x.shape[1] :]


def prep_kernel(plan, rows_ref, *outs):
    n_z = len(plan.groups[2])
    sends, rest_ref, sel_ref, turn_ref = outs[:n_z], outs[n_z], outs[n_z + 1], outs[n_z + 2]
    own = sel_ref.shape[1]
    lane = lax.broadcasted_iota(jnp.int32, (1, own), 1).astype(F32)
    n_faces = len(CLASSES[0])
    turn_ref[...] = jnp.zeros_like(turn_ref)
    turn_ref[0:n_faces, :] = rows_ref[own + 8 : own + 8 + n_faces, :]
    columns = [turn_ref[...].T]
    at = own + 16
    for width in plan.widths[1:]:
        columns.append(rows_ref[at : at + width, :])
        at += -(-width // 8) * 8
    sel_ref[...] = jnp.zeros_like(sel_ref)
    messages = plan.groups[2] + [plan.own_rest]
    at = 0
    for blocks in messages:
        for off, begin in plan.spans(blocks):
            key = CLASSES[kind(off)].index(off)
            live = plan.live(off)
            column = columns[kind(off)][0:live, key : key + 1]
            sel_ref[at + begin : at + begin + live, :] = (column == lane).astype(F32)
        at += plan.total(blocks)
    pos = dot_tn(rows_ref[own : own + 3, :], group_rows(3), HIGH)
    sel = sel_ref[...]
    rows = dot_nn(sel, rows_ref[0:own, :], HIGH)
    places = dot_nn(sel, pos, HIGH)
    at = 0
    for blocks, send in zip(messages, tuple(sends) + (rest_ref,)):
        count = plan.total(blocks)
        send[...] = rows[at : at + count, :]
        for off, begin in plan.spans(blocks):
            live = plan.live(off)
            block = places[at + begin : at + begin + live, :]
            send[begin + live : begin + live + 1, :] = jnp.sum(
                diagonal(block), axis=0, keepdims=True
            )
        at += count


def glue_kernel(plan, a, axes, rest, *refs):
    rest_ref = refs[0]
    came, outs = plan.cut(refs[1:], *axes)
    for blocks, out in zip(plan.groups[a], outs):
        for off, row in plan.spans(blocks):
            src, begin = plan.find(came, axes, rest_ref, rest, off)
            out[row : row + plan.rows(off), :] = src[begin : begin + plan.rows(off), :]


def glue(plan, a, axes, rest, rest_rows, came):
    given = [rest_rows] + [message for axis in axes for message in came[axis]]
    outs = plan.shapes(a, rest_rows.shape[1])
    return pl.pallas_call(
        lambda *refs: glue_kernel(plan, a, axes, rest, *refs),
        out_shape=outs,
        in_specs=[VMEM] * len(given),
        out_specs=[VMEM] * len(outs),
        compiler_params=PARAMS,
    )(*given)


def sort_kernel(own, count_ref, centre_ref, other_ref, key_ref, bound_ref, turn_ref):
    dead = (own - 1) * (OTHER_MASK + 1) + OTHER_MASK
    rows = centre_ref.shape[0]
    regs = turn_ref.shape[0] // 16
    group = regs * 8
    row = lax.broadcasted_iota(jnp.int32, (rows, LANES), 0)
    lane = lax.broadcasted_iota(jnp.int32, (rows, LANES), 1)
    live = row * LANES + lane < count_ref[...]
    centre = centre_ref[...]
    key = jnp.where(live, (centre << OTHER_BITS) + other_ref[...], dead).astype(F32)
    x = [key[8 * v : 8 * v + 8, :] for v in range(rows // 8)]
    x += [jnp.full((8, LANES), float(dead), F32)] * (regs - len(x))
    n_windows = own // WIN
    free = regs - rows // 8
    if n_windows * SUB <= free * 8 * LANES:
        window = jnp.where(live, centre // WIN, -1)
        need = []
        used = jnp.zeros((1, 1), F32)
        for w in range(n_windows):
            hits = jnp.sum((window == w).astype(F32), axis=0, keepdims=True)
            hits = jnp.sum(hits, axis=1, keepdims=True)
            whole = jnp.floor((hits + (SUB - 1)) * (1.0 / SUB)) * SUB
            used = used + whole
            need.append(whole - hits)
        fits = used <= float(rows * LANES)
        slot = lax.broadcasted_iota(jnp.int32, (8, LANES), 0) * LANES
        slot = slot + lax.broadcasted_iota(jnp.int32, (8, LANES), 1)
        per_reg = 8 * LANES // SUB
        for w in range(n_windows):
            v = rows // 8 + w // per_reg
            at = slot - (w % per_reg) * SUB
            take = (at >= 0) & (at.astype(F32) < need[w]) & fits
            mark = float((w * WIN + WIN - 1) * (OTHER_MASK + 1) + OTHER_MASK)
            x[v] = jnp.where(take, mark, x[v])
    s = lax.broadcasted_iota(jnp.int32, (8, LANES), 0)
    ln = lax.broadcasted_iota(jnp.int32, (8, LANES), 1)
    base = ln * group + s * regs

    def sign(k, v):
        return jnp.where(((base + v) & k) == 0, 1.0, -1.0).astype(F32)

    last = [jnp.ones((8, LANES), F32)] * regs
    total = group * LANES
    k = 2
    while k <= total:
        signs = [sign(k, v) for v in range(regs)] if k < total else [1.0] * regs
        x = [x[v] * (last[v] * signs[v]) for v in range(regs)]
        last = signs
        j = k // 2
        while j >= 1:
            if j < regs:
                for v in range(regs):
                    if v & j == 0:
                        a, b = x[v], x[v | j]
                        x[v], x[v | j] = jnp.minimum(a, b), jnp.maximum(a, b)
            else:
                axis, step, size, ids = (
                    (0, j // regs, 8, s) if j < group else (1, j // group, LANES, ln)
                )
                low = (ids & step) == 0
                for v in range(regs):
                    up = pltpu.roll(x[v], size - step, axis)
                    if 2 * step == size:
                        mate = up
                    else:
                        mate = jnp.where(low, up, pltpu.roll(x[v], step, axis))
                    x[v] = jnp.where(low, jnp.minimum(x[v], mate), jnp.maximum(x[v], mate))
            j //= 2
        k *= 2
    least = x[0]
    most = jnp.where(x[0] == float(dead), -1.0, x[0])
    for v in range(1, regs):
        least = jnp.minimum(least, x[v])
        most = jnp.maximum(most, jnp.where(x[v] == float(dead), -1.0, x[v]))
    bound_ref[0:1, :] = jnp.min(least, axis=0, keepdims=True).astype(jnp.int32) >> OTHER_BITS
    bound_ref[1:2, :] = jnp.max(most, axis=0, keepdims=True).astype(jnp.int32) >> OTHER_BITS
    turned = jnp.concatenate(x + [jnp.zeros((LANES - group, LANES), F32)], axis=0).T
    turn_ref[...] = turned
    ratio = LANES // group
    parts = [
        turn_ref[pl.ds(i, rows, stride=ratio), 0:group] for i in range(ratio)
    ]
    done = jnp.concatenate(parts, axis=1).astype(jnp.int32)
    per = key_ref.shape[1]
    for c in range(key_ref.shape[0] - 1):
        key_ref[c] = done[c * per : (c + 1) * per, :]
    key_ref[key_ref.shape[0] - 1] = jnp.full((per, LANES), dead, jnp.int32)


def weight_kernel(
    rows_ref,
    wide_ref,
    half_ref,
    tab_ref,
    w1t_ref,
    wevt_ref,
    w2t_ref,
    w1_ref,
    wev_ref,
    w2_ref,
    wcol_ref,
):
    chans = wide_ref.shape[1]
    rad_rows = wide_ref.shape[0] - 2 * chans
    own = (tab_ref.shape[0] - 4 * rad_rows) // 2
    wa, wb, rad = wide_ref[0:chans, :], wide_ref[chans : 2 * chans, :], wide_ref[2 * chans :, :]
    w1, wenv, wval = [half_ref[i * chans : (i + 1) * chans, :] for i in range(3)]
    w2 = half_ref[3 * chans : 5 * chans, :]

    def flip(w):
        return w.astype(F32).T.astype(BF16)

    down = dot_nn(rad, w1.astype(F32), HIGH)
    w1_ref[0:chans, :] = w1
    w1_ref[chans:, :] = jnp.concatenate([down, jnp.zeros_like(down)], axis=0).astype(BF16)
    w2_ref[...] = w2
    w1t_ref[...] = flip(w1)
    wevt_ref[0:chans, :] = flip(wenv)
    wevt_ref[chans:, :] = flip(wval)
    w2t_ref[:, 0:chans] = flip(w2[0:chans, :])
    w2t_ref[:, chans:] = flip(w2[chans:, :])
    wev_ref[:, 0:chans] = wenv
    wev_ref[:, chans:] = wval
    wout = half_ref[5 * chans : 5 * chans + 1, :].astype(F32)
    wcol_ref[...] = jnp.broadcast_to(wout, (LANES, chans)).T
    feat = rows_ref[0:own, :]
    tab_ref[0:own, :] = dot_nn(feat, wa, HIGH)
    tab_ref[own : 2 * own, :] = dot_nn(feat, wb, HIGH)
    rad_hi, rad_lo = split(rad)
    tab_ref[2 * own :, :] = jnp.concatenate([rad_hi, rad_hi, rad_lo, jnp.zeros_like(rad)], axis=0)


def harmonics(ux, uy, uz):
    return [
        ux,
        uy,
        uz,
        ROOT3 * ux * uy,
        ROOT3 * uy * uz,
        ROOT3 * ux * uz,
        0.866 * (ux * ux - uy * uy),
        0.5 * (3.0 * uz * uz - 1.0),
    ]


def trig(half):
    turns = jnp.round(half)
    x = math.pi * (half - turns)
    odd = turns - 2.0 * jnp.floor(0.5 * turns)
    sign = 1.0 - 2.0 * odd
    x2 = x * x
    s = jnp.full_like(x, -1.0 / 39916800)
    for coef in (1.0 / 362880, -1.0 / 5040, 1.0 / 120, -1.0 / 6, 1.0):
        s = s * x2 + coef
    c = jnp.full_like(x, 1.0 / 479001600)
    for coef in (-1.0 / 3628800, 1.0 / 40320, -1.0 / 720, 1.0 / 24, -0.5, 1.0):
        c = c * x2 + coef
    return sign * x * s, sign * c


def waves(half, count):
    s1, c1 = trig(half)
    sins, coss = [s1], [c1]
    s0, c0 = jnp.zeros_like(s1), jnp.ones_like(c1)
    for _ in range(count - 1):
        sn = 2.0 * c1 * sins[-1] - s0
        cn = 2.0 * c1 * coss[-1] - c0
        s0, c0 = sins[-1], coss[-1]
        sins.append(sn)
        coss.append(cn)
    return sins, coss


def look_up(table_row, index):
    low = index & (LANES - 1)
    high = index >> 7
    result = jnp.zeros(index.shape, F32)
    for block in range(table_row.shape[1] // LANES):
        part = jnp.broadcast_to(table_row[:, block * LANES : (block + 1) * LANES], index.shape)
        got = jnp.take_along_axis(part, low, axis=1)
        result = jnp.where(high == block, got, result)
    return result


def in_lanes(tile):
    return jnp.concatenate([tile[r : r + 1, :] for r in range(tile.shape[0])], axis=1)


def one_hot(row, base, count):
    near = jnp.clip(row - base, -1, LANES).astype(BF16)
    iota = lax.broadcasted_iota(jnp.int32, (count, row.shape[1]), 0).astype(BF16)
    return jnp.where(iota == near, jnp.ones((), BF16), jnp.zeros((), BF16))


def sorted_size(edges):
    return 1 << (edges - 1).bit_length()


def main_kernel(plan, *refs):
    bound_ref, key_ref, pos_ref, wb_ref = refs[:4]
    came, refs = plan.cut(refs[4:], 0, 1, 2)
    half_ref, w1t_ref, wevt_ref, w2t_ref, w1_ref, wev_ref, w2_ref, wcol_ref = refs[:8]
    ae_ref, own_ref = refs[8:10]
    n_x = len(plan.groups[0])
    back_refs, rest_ref = refs[10 : 10 + n_x], refs[10 + n_x]
    (
        tab_ref,
        ghost_ref,
        place_ref,
        table_ref,
        y_ref,
        basis_ref,
        geo_ref,
        first_ref,
        dsilu_ref,
        ew_ref,
        val_ref,
        a_ref,
        env_ref,
        denv_ref,
        big_ref,
        mix_ref,
        scal_ref,
        dz2_ref,
        dpre_ref,
        dz1_ref,
        dt_ref,
        dv_ref,
        dfa_ref,
        tot_ref,
        dmix_ref,
        live_ref,
        dy_ref,
        db_ref,
        dr_ref,
        acc_ref,
        cacc_ref,
    ) = refs[11 + n_x :]
    own = pos_ref.shape[1]
    chans = w1_ref.shape[1]
    n_basis = (w1_ref.shape[0] - chans) // 2
    rows_all = key_ref.shape[0] * key_ref.shape[1]
    per = CHUNK // LANES
    subs = CHUNK // SUB
    sub_rows = SUB // LANES
    n_ghost = sum(len(c) * w for c, w in zip(CLASSES, plan.widths))
    n_tab = own + n_ghost
    n_sel = own + n_tab

    place_ref[...] = jnp.zeros_like(place_ref)
    at = 0
    for off in OFFSETS:
        live = plan.live(off)
        message, begin = plan.find(came, (0, 1, 2), None, [], off)
        ghost_ref[at : at + live, :] = message[begin : begin + live, :]
        place_ref[at : at + live, :] = spread(message[begin + live : begin + live + 1, :], live)
        at += live
    ghost_pos = dot_nt(group_rows(8), place_ref[...], HIGH)
    pos_t = jnp.concatenate([pos_ref[...], ghost_pos[0:3, :]], axis=1)
    f_hi, f_lo = split(ghost_ref[...])
    w_hi, w_lo = split(wb_ref[...])
    tab_ref[0 : 2 * own, :] = half_ref[0 : 2 * own, :]
    tab_ref[2 * own : n_sel, :] = dot_nn(
        jnp.concatenate([f_hi, f_lo, f_hi], axis=1).astype(BF16),
        jnp.concatenate([w_hi, w_hi, w_lo], axis=0).astype(BF16),
    )
    tab_ref[n_sel:, :] = half_ref[2 * own :, :]
    table_ref[...] = tab_ref[...].T.astype(BF16)

    keys = key_ref[...].reshape(rows_all, LANES)
    centre = keys >> OTHER_BITS
    other = keys & OTHER_MASK
    valid = (other != OTHER_MASK).astype(F32)
    r = [
        look_up(pos_t[a : a + 1, :], other) - look_up(pos_t[a : a + 1, 0:LANES], centre)
        for a in range(3)
    ]
    d2 = r[0] * r[0] + r[1] * r[1] + r[2] * r[2] + 0.01
    dist = jnp.sqrt(d2)
    inv = 1.0 / dist
    q = 1.0 / (1.0 + 0.25 * d2)
    envelope = q * q
    unit = [x * inv for x in r]
    for m, comp in enumerate(harmonics(*unit)):
        y_ref[pl.ds(m, rows_all, stride=8), :] = comp
    sins, _ = waves(0.5 * dist, n_basis)
    scale = envelope * inv
    for n in range(n_basis):
        basis_ref[pl.ds(n, rows_all, stride=n_basis), :] = sins[n] * scale
    for i, plane in enumerate((unit[0], unit[1], unit[2], dist, inv, q, envelope * valid, valid)):
        geo_ref[i] = plane.reshape(geo_ref.shape[1:])

    env_ref[...] = jnp.zeros_like(env_ref)
    denv_ref[...] = jnp.zeros_like(denv_ref)
    ae_ref[...] = jnp.zeros_like(ae_ref)
    acc_ref[...] = jnp.zeros_like(acc_ref)
    cacc_ref[...] = jnp.zeros_like(cacc_ref)
    dr_ref[...] = jnp.zeros_like(dr_ref)

    groups = bound_ref.shape[1] * SUB // sorted_size((rows_all - per) * LANES)

    def window(k, s):
        first = jnp.minimum((k * subs + s) * groups, bound_ref.shape[1] - groups)
        low = bound_ref[0, first]
        high = low
        for g in range(groups):
            high = jnp.maximum(high, bound_ref[1, first + g])
        start = pl.multiple_of((low >> 3) << 3, 8)
        more = lax.div(high - start, jnp.int32(WIN))
        return start, more

    most = jnp.int32(0)
    n_chunks = jnp.int32(0)
    for s in range((rows_all - per) // sub_rows):
        most = jnp.maximum(most, window(s // subs, s % subs)[1])
        for g in range(groups):
            any_live = bound_ref[1, s * groups + g] >= 0
            n_chunks = jnp.where(any_live, s // subs + 1, n_chunks)


    def lanes_of(s, n):
        if isinstance(s, int):
            return slice(s * SUB, (s + n) * SUB)
        return pl.ds(pl.multiple_of(s * SUB, SUB), n * SUB)

    def tile_of(load, s, n):
        if isinstance(s, int):
            return load(slice(s * sub_rows, (s + n) * sub_rows))
        return jnp.concatenate(
            [load(pl.ds(s * sub_rows + j, 1)) for j in range(n * sub_rows)], axis=0
        )

    def plane(i, k, s, n):
        return tile_of(lambda rows: geo_ref[i, k, rows, :], s, n)

    def keys_of(k, s, n):
        return tile_of(lambda rows: key_ref[k, rows, :], s, n)

    def put_row(ref, index, s, row):
        for j in range(row.shape[1] // LANES):
            at = pl.ds(s * sub_rows + j, 1)
            ref[index + (at, slice(None))] = row[:, j * LANES : (j + 1) * LANES]

    def stacked(ref, k, s, n, height):
        first = (k * subs + s) * sub_rows
        tiles = [
            ref[pl.ds(pl.multiple_of((first + j) * height, 8), height), :]
            for j in range(n * sub_rows)
        ]
        return jnp.concatenate(tiles, axis=1)

    def window_hot(k, s, start):
        crow = in_lanes(keys_of(k, s, 1) >> OTHER_BITS) - start
        return lax.broadcasted_iota(jnp.int32, (WIN, SUB), 0) == crow

    def select(k, s, start):
        hot = window_hot(k, s, start)
        ys = stacked(y_ref, k, s, 1, 8)
        parts = [hot.astype(F32)]
        for m in range(8):
            parts.append(jnp.where(hot, ys[m : m + 1, :], 0.0))
        return jnp.concatenate(parts, axis=0).astype(BF16)

    def load_window(ref, start):
        return jnp.concatenate(
            [ref[m, pl.ds(start, WIN), :] for m in range(9)], axis=0
        ).astype(BF16)

    def add_window(ref, start, rows):
        for m in range(9):
            ref[m, pl.ds(start, WIN), :] += rows[m * WIN : (m + 1) * WIN, :]

    def each_window(k, s, n, slow, body):
        for j in range(n):
            start, more = window(k, s + j)
            body(s + j, j, start, True)
            if slow:

                def step(i, carry, s=s, j=j, start=start):
                    body(s + j, j, pl.multiple_of(start + i * WIN, 8), False)
                    return carry

                lax.fori_loop(1, more + 1, step, 0)

    def sum_windows(k, s, n, slow, value):
        if not slow:
            return jnp.concatenate([value(s + j, window(k, s + j)[0], True) for j in range(n)], axis=1)

        def body(s, j, start, fresh):
            if fresh:
                big_ref[:, part(j)] = value(s, start, fresh)
            else:
                big_ref[:, part(j)] += value(s, start, fresh)

        each_window(k, s, n, slow, body)
        return big_ref[:, 0 : n * SUB]

    def kept(k, s, start, fresh):
        return a_ref[k * subs + s] if fresh else select(k, s, start)

    def table_hots(k, s, n):
        row = in_lanes(keys_of(k, s, n) & OTHER_MASK)
        return [one_hot(row, at, min(LANES, n_tab - at)) for at in range(0, n_tab, LANES)]

    def part(j):
        return slice(j * SUB, (j + 1) * SUB)

    def width(n):
        return slice(0, n * SUB)

    def mix(k, s, n, slow):
        crow = in_lanes(keys_of(k, s, n) >> OTHER_BITS)
        hots = [one_hot(crow, 0, own)] + table_hots(k, s, n)
        basis = stacked(basis_ref, k, s, n, n_basis)
        b_hi, b_lo = split(basis)
        hots.append(jnp.concatenate([b_hi, b_lo], axis=0).astype(BF16))
        hots.append(jnp.concatenate([b_hi, jnp.zeros_like(b_hi)], axis=0).astype(BF16))
        mixed = dot_nn(table_ref[...], jnp.concatenate(hots, axis=0))
        mix_ref[:, width(n)] = mixed.astype(BF16)

    def first_layer(k, s, n, slow):
        lanes = lanes_of(s, n)
        z1 = dot_nn(w1t_ref[...], mix_ref[:, width(n)])
        sg = 0.5 + 0.5 * jnp.tanh(0.5 * z1)
        first = z1 * sg
        dsilu_ref[k, :, lanes] = (sg + first * (1.0 - sg)).astype(BF16)
        first_ref[k, :, lanes] = first.astype(BF16)

    def tracks(k, s, n, slow):
        lanes = lanes_of(s, n)
        both = dot_nn(wevt_ref[...], first_ref[k, :, lanes])
        ew_ref[k, :, lanes] = (both[0:chans] * in_lanes(plane(6, k, s, n))).astype(BF16)
        val_ref[k, :, lanes] = both[chans:].astype(BF16)

    def env_sums(k, s, n, slow):
        def body(s, j, start, fresh):
            a = select(k, s, start)
            if fresh:
                a_ref[k * subs + s] = a
            add_window(env_ref, start, dot_nt(a, ew_ref[k, :, lanes_of(s, 1)]))

        each_window(k, s, n, slow, body)

    def tensor(k, s, n, slow):
        lanes = lanes_of(s, n)

        def value(s, start, fresh):
            return dot_tn(load_window(env_ref, start), kept(k, s, start, fresh))

        total = 0.2 * sum_windows(k, s, n, slow, value)
        tot_ref[k, :, lanes] = total
        scal_ref[:, width(n)] = (val_ref[k, :, lanes].astype(F32) * total).astype(BF16)

    def second_layer(k, s, n, slow):
        lanes = lanes_of(s, n)
        joined = jnp.concatenate([first_ref[k, :, lanes], scal_ref[:, width(n)]], axis=0)
        z2 = dot_nn(w2t_ref[...], joined)
        sg = 0.5 + 0.5 * jnp.tanh(0.5 * z2)
        second = z2 * sg
        wcol = jnp.concatenate([wcol_ref[...]] * (n * sub_rows), axis=1)
        ee = jnp.sum(second.astype(BF16).astype(F32) * wcol, axis=0, keepdims=True)
        envv = in_lanes(plane(6, k, s, n))
        put_row(live_ref, (k,), s, ee * in_lanes(plane(7, k, s, n)))
        energy = ee * envv
        dz2_ref[:, width(n)] = ((wcol * envv) * (sg + second * (1.0 - sg))).astype(BF16)

        def body(s, j, start, fresh):
            mine = jnp.where(window_hot(k, s, start), energy[:, part(j)], 0.0)
            half = mine[:, 0:LANES]
            for i in range(1, sub_rows):
                half = half + mine[:, i * LANES : (i + 1) * LANES]
            ae_ref[pl.ds(start, WIN), :] += half

        each_window(k, s, n, slow, body)

    def second_back(k, s, n, slow):
        lanes = lanes_of(s, n)
        dj = dot_nn(w2_ref[...], dz2_ref[:, width(n)])
        dfa_ref[k, :, lanes] = dj[0:chans].astype(BF16)
        dscalar = dj[chans:]
        dt_ref[k, :, lanes] = (0.2 * val_ref[k, :, lanes].astype(F32) * dscalar).astype(BF16)
        dv_ref[k, :, lanes] = (tot_ref[k, :, lanes] * dscalar).astype(BF16)

    def env_back(k, s, n, slow):
        def body(s, j, start, fresh):
            a = kept(k, s, start, fresh)
            add_window(denv_ref, start, dot_nt(a, dt_ref[k, :, lanes_of(s, 1)]))

        each_window(k, s, n, slow, body)

    def track_back(k, s, n, slow):
        lanes = lanes_of(s, n)

        def value(s, start, fresh):
            a = kept(k, s, start, fresh)
            e_win = load_window(env_ref, start)
            d_win = load_window(denv_ref, start)
            here = lanes_of(s, 1)
            pair = jnp.concatenate([dt_ref[k, :, here], ew_ref[k, :, here]], axis=0)
            prods = dot_nn(jnp.concatenate([e_win, d_win], axis=1), pair)
            hot = a[0:WIN].astype(F32)
            for m in range(1, 9):
                row = jnp.sum(prods[m * WIN : (m + 1) * WIN] * hot, axis=0, keepdims=True)
                if not fresh:
                    row = row + in_lanes(tile_of(lambda rows: dy_ref[k, m, rows, :], s, 1))
                put_row(dy_ref, (k, m), s, row)
            return dot_tn(d_win, a)

        dew = sum_windows(k, s, n, slow, value)
        dpre_ref[:, width(n)] = (dew * in_lanes(plane(6, k, s, n))).astype(BF16)
        denv_row = jnp.sum(dew * ew_ref[k, :, lanes].astype(F32), axis=0, keepdims=True)
        put_row(dy_ref, (k, 0), s, denv_row)

    def first_back(k, s, n, slow):
        lanes = lanes_of(s, n)
        joined = jnp.concatenate([dpre_ref[:, width(n)], dv_ref[k, :, lanes]], axis=0)
        dfirst = dfa_ref[k, :, lanes].astype(F32) + dot_nn(wev_ref[...], joined)
        dz1_ref[:, width(n)] = (dfirst * dsilu_ref[k, :, lanes].astype(F32)).astype(BF16)

    def mix_back(k, s, n, slow):
        dboth = dot_nn(w1_ref[...], dz1_ref[:, width(n)])
        dmix_ref[k, :, lanes_of(s, n)] = dboth[0:chans].astype(BF16)
        for j in range(n * sub_rows):
            db_ref[j * n_basis : (j + 1) * n_basis, :] = dboth[
                chans : chans + n_basis, j * LANES : (j + 1) * LANES
            ]

    def geometry_back(k, s, n, slow):
        height = n * sub_rows
        ux, uy, uz, dist, inv, q = [plane(i, k, s, n) for i in range(6)]
        envelope = q * q
        g = envelope * inv
        denvelope = -(q * envelope) * dist
        dg = (denvelope - g) * inv
        sins, coss = waves(0.5 * dist, n_basis)
        live = tile_of(lambda rows: live_ref[k, rows, :], s, n)
        y = [tile_of(lambda rows, m=m: dy_ref[k, m, rows, :], s, n) for m in range(9)]
        ddist = (live + y[0] / envelope) * denvelope
        for i in range(n_basis):
            db = db_ref[pl.ds(i, height, stride=n_basis), :]
            ddist = ddist + db * (coss[i] * ((i + 1) * math.pi / 2.0) * g + sins[i] * dg)
        gx = y[1] + ROOT3 * (uy * y[4] + uz * y[6]) + (2.0 * 0.866) * ux * y[7]
        gy = y[2] + ROOT3 * (ux * y[4] + uz * y[5]) - (2.0 * 0.866) * uy * y[7]
        gz = y[3] + ROOT3 * (uy * y[5] + ux * y[6]) + 3.0 * uz * y[8]
        along = ddist - inv * (gx * ux + gy * uy + gz * uz)
        for i, (gu, u) in enumerate(((gx, ux), (gy, uy), (gz, uz))):
            hi, lo = split(inv * gu + along * u)
            dr_ref[pl.ds(i, height, stride=16), :] = hi
            dr_ref[pl.ds(3 + i, height, stride=16), :] = lo

    def scatter(k, s, n, slow):
        dr = jnp.concatenate(
            [dr_ref[j * 16 : (j + 1) * 16, :] for j in range(n * sub_rows)], axis=1
        )
        moved = jnp.concatenate([dmix_ref[k, :, lanes_of(s, n)], dr.astype(BF16)], axis=0)
        sums = dot_nt(jnp.concatenate(table_hots(k, s, n), axis=0), moved)
        acc_ref[:, 0:chans] += sums[:, 0:chans]
        acc_ref[:, chans : chans + 16] += sums[:, chans:]

        def body(s, j, start, fresh):
            hot = a_ref[k * subs + s, 0:WIN, :] if fresh else window_hot(k, s, start).astype(BF16)
            mine = dot_nt(hot, moved[:, part(j)])
            cacc_ref[pl.ds(start, WIN), 0:chans] += mine[:, 0:chans]
            cacc_ref[pl.ds(start, WIN), chans : chans + 16] += mine[:, chans:]

        each_window(k, s, n, slow, body)

    phases = (
        (mix, first_layer, tracks, env_sums),
        (tensor, second_layer, second_back, env_back),
        (track_back, first_back, mix_back, geometry_back, scatter),
    )
    dummy = key_ref.shape[0] - 1
    for ref in (mix_ref, scal_ref, dz2_ref, dpre_ref, dz1_ref, db_ref, dr_ref):
        ref[...] = jnp.zeros_like(ref)
    for ref in (first_ref, dsilu_ref, ew_ref, val_ref, dt_ref, dv_ref, dfa_ref, tot_ref):
        ref[dummy] = jnp.zeros(ref.shape[1:], ref.dtype)
    for ref in (dmix_ref, live_ref, dy_ref):
        ref[dummy] = jnp.zeros(ref.shape[1:], ref.dtype)
    for s in range(subs):
        a_ref[dummy * subs + s] = jnp.zeros(a_ref.shape[1:], BF16)
    for stages in phases:

        @pl.when(most == 0)
        def _(stages=stages):
            def step(i, carry):
                for j in reversed(range(len(stages))):
                    k = i - j
                    k = jnp.where((k >= 0) & (k < n_chunks), k, dummy)
                    stages[j](k, 0, subs, False)
                return carry

            lax.fori_loop(0, n_chunks + (len(stages) - 1), step, 0)

        @pl.when(most != 0)
        def _(stages=stages):
            def sub(i, carry):
                for stage in stages:
                    stage(lax.div(i, subs), lax.rem(i, subs), 1, True)
                return carry

            lax.fori_loop(0, n_chunks * subs, sub, 0)

    own_ref[0:own, :] = cacc_ref[0:own, :]
    own_ref[own:, :] = acc_ref[0:own, :]
    row = lax.broadcasted_iota(jnp.int32, (LANES, LANES), 0)
    group = lax.broadcasted_iota(jnp.int32, (LANES, LANES), 1) // GROUP
    both = ((group < 3) & ((row == group) | (row == group + 3))).astype(F32)
    places = dot_nn(acc_ref[own:, LANES:], both, HIGH)
    found = {}
    at = own
    for off in OFFSETS:
        found[off] = at
        at += plan.live(off)
    for blocks, ref in zip(
        plan.groups[0] + [plan.held_rest], tuple(back_refs) + (rest_ref,)
    ):
        for off, row in plan.spans(blocks):
            live = plan.live(off)
            at = found[off]
            ref[row : row + live, :] = acc_ref[at : at + live, 0:chans]
            block = places[at - own : at - own + live, :]
            ref[row + live : row + live + 1, :] = jnp.sum(diagonal(block), axis=0, keepdims=True)


def own_kernel(ae_ref, own_ref, wa_ref, wb_ref, energy_ref, fg_ref, force_ref):
    chans = wa_ref.shape[1]
    own = force_ref.shape[1]
    energy_ref[...] = jnp.sum(ae_ref[0:own, :].T, axis=0, keepdims=True)
    fg_ref[...] = dot_nt(own_ref[0:own, 0:chans], wa_ref[...], HIGH) + dot_nt(
        own_ref[own:, 0:chans], wb_ref[...], HIGH
    )
    force = (own_ref[own:, LANES:] - own_ref[0:own, LANES:]).T
    force_ref[...] = force[0:3, :] + force[3:6, :]


def last_kernel(plan, sel_ref, fg_ref, force_ref, wb_ref, *refs):
    came, refs = plan.cut(refs, 0, 1, 2)
    out_force_ref, out_fg_ref, both_ref = refs
    both_ref[...] = jnp.zeros_like(both_ref)
    chans = fg_ref.shape[1]
    at = 0
    for blocks in plan.groups[2] + [plan.own_rest]:
        for off, row in plan.spans(blocks):
            live = plan.live(off)
            src, begin = plan.find(came, (2, 1, 0), None, [], off)
            here = slice(at + row, at + row + live)
            both_ref[here, 0:chans] = src[begin : begin + live, :]
            both_ref[here, chans:] = spread(src[begin + live : begin + live + 1, :], live)
        at += plan.total(blocks)
    sums = dot_exact(sel_ref[...].astype(BF16), both_ref[...], ((0,), (0,)))
    out_fg_ref[...] = fg_ref[...] + dot_nt(sums[:, 0:chans], wb_ref[...], HIGH)
    total = dot_nt(group_rows(8), sums[:, chans:], HIGH)
    out_force_ref[...] = -(force_ref[...] + total[0:3, :])


def stack(*arrays):
    dtype = arrays[0].dtype
    tile = 32 // dtype.itemsize
    starts = [0]
    for x in arrays:
        starts.append(starts[-1] + -(-x.shape[0] // tile) * tile)
    total = None
    for x, at in zip(arrays, starts):
        below = starts[-1] - at - x.shape[0]
        part = jnp.pad(x.astype(dtype), ((at, below), (0, LANES - x.shape[1])))
        total = part if total is None else total + part
    return total


def local(
    positions,
    atom_features,
    send_face,
    send_edge,
    send_corner,
    centre,
    other,
    edge_count,
    w_proj_a,
    w_proj_b,
    w_radial,
    w_first,
    w_env,
    w_value,
    w_second,
    w_out,
):
    own, chans = atom_features.shape
    edges = centre.shape[0]
    n_basis = w_radial.shape[0]
    plan = Plan(
        [send_face.shape[2], send_edge.shape[2], send_corner.shape[2]],
        [lax.axis_size(axis) for axis in AXES],
    )
    n_ghost = sum(len(c) * w for c, w in zip(CLASSES, plan.widths))
    n_sel = 2 * own + n_ghost
    n_send = sum(plan.total(blocks) for blocks in plan.groups[2]) + plan.total(plan.own_rest)
    n_table = n_sel + 4 * n_basis
    edges_up = -(-edges // CHUNK) * CHUNK
    n_rows = edges_up // LANES
    n_chunks = edges_up // CHUNK

    with jax.named_scope("prep"):
        rows = stack(
            atom_features,
            positions,
            send_face[0],
            jnp.transpose(send_edge[0]),
            jnp.transpose(send_corner[0]),
        )
        *sends, own_rows, sel = pl.pallas_call(
            lambda *refs: prep_kernel(plan, *refs),
            out_shape=plan.shapes(2, chans)
            + [shape(plan.total(plan.own_rest), chans), shape(n_send, own)],
            in_specs=[VMEM],
            out_specs=[VMEM] * (len(plan.groups[2]) + 2),
            scratch_shapes=[pltpu.VMEM((LANES, LANES), F32)],
            compiler_params=PARAMS,
        )(rows)

    came = {}
    with jax.named_scope("halo_z"):
        came[2] = plan.send(2, sends)

    with jax.named_scope("group_edges"):
        pad = [(0, edges_up - edges)]
        regs = max(sorted_size(edges_up) // (8 * LANES), 1)
        key, bounds = pl.pallas_call(
            lambda *refs: sort_kernel(own, *refs),
            out_shape=[
                shape(n_chunks + 1, CHUNK // LANES, LANES, dtype=jnp.int32),
                shape(2, LANES, dtype=jnp.int32),
            ],
            in_specs=[VMEM] * 3,
            out_specs=[VMEM] * 2,
            scratch_shapes=[pltpu.VMEM((16 * regs, LANES), F32)],
            compiler_params=PARAMS,
        )(
            edge_count.reshape(1, 1),
            jnp.pad(centre, pad).reshape(n_rows, LANES),
            jnp.pad(other, pad).reshape(n_rows, LANES),
        )

    with jax.named_scope("halo_y"):
        came[2], key, bounds, w_first, w_env, w_value, w_second, w_out = lax.optimization_barrier(
            (came[2], key, bounds, w_first, w_env, w_value, w_second, w_out)
        )
        came[1] = plan.send(1, glue(plan, 1, (2,), plan.own_rest, own_rows, came))

    with jax.named_scope("weights"):
        wide = stack(w_proj_a, w_proj_b, w_radial)
        narrow = stack(w_first, w_env, w_value, w_second, w_out[None, :])
        half, *weights = pl.pallas_call(
            weight_kernel,
            out_shape=[
                shape(2 * own + 4 * n_basis, chans),
                shape(chans, chans, dtype=BF16),
                shape(2 * chans, chans, dtype=BF16),
                shape(chans, 2 * chans, dtype=BF16),
                shape(chans + 2 * n_basis, chans, dtype=BF16),
                shape(chans, 2 * chans, dtype=BF16),
                shape(2 * chans, chans, dtype=BF16),
                shape(chans, LANES),
            ],
            in_specs=[VMEM] * 3,
            out_specs=[VMEM] * 8,
            compiler_params=PARAMS,
        )(rows, wide, narrow)

    with jax.named_scope("halo_x"):
        came[1], half, weights = lax.optimization_barrier((came[1], half, weights))
        came[0] = plan.send(0, glue(plan, 0, (1, 2), plan.own_rest, own_rows, came))

    blocks = n_chunks + 1
    per = CHUNK // LANES
    planes = pltpu.VMEM((blocks, chans, CHUNK), BF16)
    buffer = pltpu.VMEM((chans, CHUNK), BF16)
    env = pltpu.VMEM((9, own + WIN, chans), F32)
    scratch = [
        pltpu.VMEM((n_table, chans), F32),
        pltpu.VMEM((n_ghost, chans), F32),
        pltpu.VMEM((-(-n_ghost // LANES) * LANES, LANES), F32),
        pltpu.VMEM((chans, n_table), BF16),
        pltpu.VMEM((blocks * per * 8, LANES), F32),
        pltpu.VMEM((blocks * per * n_basis, LANES), F32),
        pltpu.VMEM((8, blocks, per, LANES), F32),
        planes,
        planes,
        planes,
        planes,
        pltpu.VMEM((blocks * CHUNK // SUB, 9 * WIN, SUB), BF16),
        env,
        env,
        pltpu.VMEM((chans, SUB), F32),
        buffer,
        buffer,
        buffer,
        buffer,
        buffer,
        planes,
        planes,
        planes,
        pltpu.VMEM((blocks, chans, CHUNK), F32),
        planes,
        pltpu.VMEM((blocks, per, LANES), F32),
        pltpu.VMEM((blocks, 9, per, LANES), F32),
        pltpu.VMEM((per * n_basis, LANES), F32),
        pltpu.VMEM((per * 16, LANES), F32),
        pltpu.VMEM((n_sel - own, 2 * LANES), F32),
        pltpu.VMEM((own + WIN, 2 * LANES), F32),
    ]
    with jax.named_scope("layer"):
        given = [bounds, key, positions, w_proj_b]
        given += [*came[0], *came[1], *came[2], half, *weights]
        atom_sums, own_sums, *back, held = pl.pallas_call(
            lambda *refs: main_kernel(plan, *refs),
            out_shape=[shape(own + WIN, LANES), shape(2 * own, 2 * LANES)]
            + plan.shapes(0, chans)
            + [shape(plan.total(plan.held_rest), chans)],
            in_specs=[SMEM] + [VMEM] * (len(given) - 1),
            out_specs=[VMEM] * (3 + len(plan.groups[0])),
            scratch_shapes=scratch,
            compiler_params=PARAMS,
        )(*given)

    with jax.named_scope("halo_back"):
        home = {0: plan.send(0, back, back=True)}
        home[1] = plan.send(1, glue(plan, 1, (0,), plan.held_rest, held, home), back=True)
        home[2] = plan.send(2, glue(plan, 2, (1, 0), plan.held_rest, held, home), back=True)

    with jax.named_scope("own_part"):
        energy, fg, force = pl.pallas_call(
            own_kernel,
            out_shape=[shape(1, own), shape(own, chans), shape(3, own)],
            in_specs=[VMEM] * 4,
            out_specs=[VMEM] * 3,
            compiler_params=PARAMS,
        )(atom_sums, own_sums, w_proj_a, w_proj_b)

    with jax.named_scope("owner_sums"):
        given = [sel, fg, force, w_proj_b, *home[0], *home[1], *home[2]]
        forces, feature_grad = pl.pallas_call(
            lambda *refs: last_kernel(plan, *refs),
            out_shape=[shape(3, own), shape(own, chans)],
            in_specs=[VMEM] * len(given),
            out_specs=[VMEM] * 2,
            scratch_shapes=[pltpu.VMEM((n_send, chans + LANES), F32)],
            compiler_params=PARAMS,
        )(*given)
    return forces, energy.reshape(own), feature_grad


def solution(mesh):
    shard = P(AXES)
    return jax.shard_map(
        local,
        mesh=mesh,
        in_specs=(
            P(None, AXES),
            P(AXES, None),
            P(AXES, None, None),
            P(AXES, None, None),
            P(AXES, None, None),
            shard,
            shard,
            shard,
        )
        + (P(),) * 8,
        out_specs=(P(None, AXES), shard, P(AXES, None)),
        check_vma=False,
    )
```

```python
import math

import jax
import jax.numpy as jnp
from jax import lax
from jax.experimental import pallas as pl
from jax.experimental.pallas import tpu as pltpu
from jax.sharding import PartitionSpec as P

F32 = jnp.float32
BF16 = jnp.bfloat16
HIGH = lax.Precision.HIGHEST
AXES = ("gx", "gy", "gz")
CHUNK = 3072
SUB = 256
WIN = 16
OTHER_BITS = 9
OTHER_MASK = (1 << OTHER_BITS) - 1
LANES = 128
ROOT3 = 1.732


VMEM = pl.BlockSpec(memory_space=pltpu.VMEM)
SMEM = pl.BlockSpec(memory_space=pltpu.SMEM)
PARAMS = pltpu.CompilerParams(vmem_limit_bytes=52 * 2**20)


def shape(*dims, dtype=F32):
    return jax.ShapeDtypeStruct(dims, dtype)


def dot_nn(a, b, precision=None):
    return lax.dot_general(
        a, b, (((1,), (0,)), ((), ())), preferred_element_type=F32, precision=precision
    )


def dot_nt(a, b, precision=None):
    return lax.dot_general(
        a, b, (((1,), (1,)), ((), ())), preferred_element_type=F32, precision=precision
    )


def dot_tn(a, b, precision=None):
    return lax.dot_general(
        a, b, (((0,), (0,)), ((), ())), preferred_element_type=F32, precision=precision
    )


def offset_classes():
    classes = [[], [], []]
    for a in (-1, 0, 1):
        for b in (-1, 0, 1):
            for c in (-1, 0, 1):
                if (a, b, c) != (0, 0, 0):
                    classes[abs(a) + abs(b) + abs(c) - 1].append((a, b, c))
    return classes


CLASSES = offset_classes()


OFFSETS = [off for group in CLASSES for off in group]


def kind(off):
    return abs(off[0]) + abs(off[1]) + abs(off[2]) - 1


class Plan:
    def __init__(self, widths, sizes):
        self.widths = widths
        self.sizes = sizes
        self.groups = [self.group(a) for a in range(3)]
        self.own_rest = [off for off in OFFSETS if off[2] == 0]
        self.held_rest = [off for off in OFFSETS if off[0] == 0]

    def group(self, a):
        groups = {}
        for off in OFFSETS:
            if off[a] != 0:
                groups.setdefault(off[a] % self.sizes[a], []).append(off)
        return list(groups.values())

    def live(self, off):
        return self.widths[kind(off)]

    def rows(self, off):
        return self.live(off) + 1

    def total(self, blocks):
        return sum(self.rows(off) for off in blocks)

    def spans(self, blocks):
        at = 0
        for off in blocks:
            yield off, at
            at += self.rows(off)

    def place(self, a, off):
        for g, blocks in enumerate(self.groups[a]):
            if off in blocks:
                return g, dict(self.spans(blocks))[off]
        raise KeyError(off)

    def find(self, came, axes, rest_ref, rest, off):
        for a in axes:
            if off[a] != 0:
                g, begin = self.place(a, off)
                return came[a][g], begin
        return rest_ref, dict(self.spans(rest))[off]

    def cut(self, refs, *axes):
        came = {}
        for a in axes:
            n = len(self.groups[a])
            came[a], refs = refs[:n], refs[n:]
        return came, refs

    def shapes(self, a, chans):
        return [shape(self.total(blocks), chans) for blocks in self.groups[a]]

    def send(self, a, messages, back=False):
        n = self.sizes[a]
        got = []
        for blocks, message in zip(self.groups[a], messages):
            step = -blocks[0][a] if back else blocks[0][a]
            got.append(lax.ppermute(message, AXES[a], [(i, (i + step) % n) for i in range(n)]))
        return got


GROUP = 32


def group_rows(count):
    row = lax.broadcasted_iota(jnp.int32, (count, LANES), 0)
    group = lax.broadcasted_iota(jnp.int32, (count, LANES), 1) // GROUP
    return (row == group).astype(F32) * (group < 3).astype(F32)


def diagonal(x):
    row = lax.broadcasted_iota(jnp.int32, x.shape, 0)
    lane = lax.broadcasted_iota(jnp.int32, x.shape, 1)
    return jnp.where((lane & (GROUP - 1)) == row, x, 0.0)


def spread(row, live):
    return diagonal(jnp.broadcast_to(row, (live, LANES)))


def split(x):
    high = x.astype(BF16).astype(F32)
    return high, x - high


def dot_exact(hot, x, dims):
    high, low = split(x)
    both = jnp.concatenate([high, low], axis=1).astype(BF16)
    out = lax.dot_general(hot, both, (dims, ((), ())), preferred_element_type=F32)
    return out[:, 0 : x.shape[1]] + out[:, x.shape[1] :]


def prep_kernel(plan, rows_ref, pos_ref, corner_ref, *outs):
    n_z = len(plan.groups[2])
    sends, rest_ref, sel_ref, turn_ref = outs[:n_z], outs[n_z], outs[n_z + 1], outs[n_z + 2]
    own = sel_ref.shape[1]
    lane = lax.broadcasted_iota(jnp.int32, (1, own), 1).astype(F32)
    n_faces = len(CLASSES[0])
    turn_ref[...] = jnp.zeros_like(turn_ref)
    turn_ref[0:n_faces, :] = rows_ref[own : own + n_faces, :]
    columns = [
        turn_ref[...].T,
        rows_ref[own + 8 : own + 8 + plan.widths[1], :],
        corner_ref[0].astype(F32),
    ]
    sel_ref[...] = jnp.zeros_like(sel_ref)
    messages = plan.groups[2] + [plan.own_rest]
    at = 0
    for blocks in messages:
        for off, begin in plan.spans(blocks):
            key = CLASSES[kind(off)].index(off)
            live = plan.live(off)
            column = columns[kind(off)][0:live, key : key + 1]
            sel_ref[at + begin : at + begin + live, :] = (column == lane).astype(F32)
        at += plan.total(blocks)
    pos = dot_tn(pos_ref[...], group_rows(3), HIGH)
    sel = sel_ref[...]
    rows = dot_nn(sel, rows_ref[0:own, :], HIGH)
    places = dot_nn(sel, pos, HIGH)
    at = 0
    for blocks, send in zip(messages, tuple(sends) + (rest_ref,)):
        count = plan.total(blocks)
        send[...] = rows[at : at + count, :]
        for off, begin in plan.spans(blocks):
            live = plan.live(off)
            block = places[at + begin : at + begin + live, :]
            send[begin + live : begin + live + 1, :] = jnp.sum(
                diagonal(block), axis=0, keepdims=True
            )
        at += count


def glue_kernel(plan, a, axes, rest, *refs):
    rest_ref = refs[0]
    came, outs = plan.cut(refs[1:], *axes)
    for blocks, out in zip(plan.groups[a], outs):
        for off, row in plan.spans(blocks):
            src, begin = plan.find(came, axes, rest_ref, rest, off)
            out[row : row + plan.rows(off), :] = src[begin : begin + plan.rows(off), :]


def glue(plan, a, axes, rest, rest_rows, came):
    given = [rest_rows] + [message for axis in axes for message in came[axis]]
    outs = plan.shapes(a, rest_rows.shape[1])
    return pl.pallas_call(
        lambda *refs: glue_kernel(plan, a, axes, rest, *refs),
        out_shape=outs,
        in_specs=[VMEM] * len(given),
        out_specs=[VMEM] * len(outs),
        compiler_params=PARAMS,
    )(*given)


def sort_kernel(own, count_ref, centre_ref, other_ref, key_ref, bound_ref, turn_ref):
    dead = (own - 1) * (OTHER_MASK + 1) + OTHER_MASK
    rows = centre_ref.shape[0]
    regs = turn_ref.shape[0] // 16
    group = regs * 8
    row = lax.broadcasted_iota(jnp.int32, (rows, LANES), 0)
    lane = lax.broadcasted_iota(jnp.int32, (rows, LANES), 1)
    count = count_ref[count_ref.shape[0] - 8 : count_ref.shape[0] - 7, 0:1].astype(jnp.int32)
    live = row * LANES + lane < count
    centre = centre_ref[...]
    key = jnp.where(live, (centre << OTHER_BITS) + other_ref[...], dead).astype(F32)
    x = [key[8 * v : 8 * v + 8, :] for v in range(rows // 8)]
    x += [jnp.full((8, LANES), float(dead), F32)] * (regs - len(x))
    n_windows = own // WIN
    free = regs - rows // 8
    if n_windows * SUB <= free * 8 * LANES:
        window = jnp.where(live, centre // WIN, -1)
        need = []
        used = jnp.zeros((1, 1), F32)
        for w in range(n_windows):
            hits = jnp.sum((window == w).astype(F32), axis=0, keepdims=True)
            hits = jnp.sum(hits, axis=1, keepdims=True)
            whole = jnp.floor((hits + (SUB - 1)) * (1.0 / SUB)) * SUB
            used = used + whole
            need.append(whole - hits)
        fits = used <= float(rows * LANES)
        slot = lax.broadcasted_iota(jnp.int32, (8, LANES), 0) * LANES
        slot = slot + lax.broadcasted_iota(jnp.int32, (8, LANES), 1)
        per_reg = 8 * LANES // SUB
        for w in range(n_windows):
            v = rows // 8 + w // per_reg
            at = slot - (w % per_reg) * SUB
            take = (at >= 0) & (at.astype(F32) < need[w]) & fits
            mark = float((w * WIN + WIN - 1) * (OTHER_MASK + 1) + OTHER_MASK)
            x[v] = jnp.where(take, mark, x[v])
    s = lax.broadcasted_iota(jnp.int32, (8, LANES), 0)
    ln = lax.broadcasted_iota(jnp.int32, (8, LANES), 1)
    base = ln * group + s * regs

    def sign(k, v):
        return jnp.where(((base + v) & k) == 0, 1.0, -1.0).astype(F32)

    last = [jnp.ones((8, LANES), F32)] * regs
    total = group * LANES
    k = 2
    while k <= total:
        signs = [sign(k, v) for v in range(regs)] if k < total else [1.0] * regs
        x = [x[v] * (last[v] * signs[v]) for v in range(regs)]
        last = signs
        j = k // 2
        while j >= 1:
            if j < regs:
                for v in range(regs):
                    if v & j == 0:
                        a, b = x[v], x[v | j]
                        x[v], x[v | j] = jnp.minimum(a, b), jnp.maximum(a, b)
            else:
                axis, step, size, ids = (
                    (0, j // regs, 8, s) if j < group else (1, j // group, LANES, ln)
                )
                low = (ids & step) == 0
                for v in range(regs):
                    up = pltpu.roll(x[v], size - step, axis)
                    if 2 * step == size:
                        mate = up
                    else:
                        mate = jnp.where(low, up, pltpu.roll(x[v], step, axis))
                    x[v] = jnp.where(low, jnp.minimum(x[v], mate), jnp.maximum(x[v], mate))
            j //= 2
        k *= 2
    least = x[0]
    most = jnp.where(x[0] == float(dead), -1.0, x[0])
    for v in range(1, regs):
        least = jnp.minimum(least, x[v])
        most = jnp.maximum(most, jnp.where(x[v] == float(dead), -1.0, x[v]))
    bound_ref[0:1, :] = jnp.min(least, axis=0, keepdims=True).astype(jnp.int32) >> OTHER_BITS
    bound_ref[1:2, :] = jnp.max(most, axis=0, keepdims=True).astype(jnp.int32) >> OTHER_BITS
    turned = jnp.concatenate(x + [jnp.zeros((LANES - group, LANES), F32)], axis=0).T
    turn_ref[...] = turned
    ratio = LANES // group
    parts = [
        turn_ref[pl.ds(i, rows, stride=ratio), 0:group] for i in range(ratio)
    ]
    done = jnp.concatenate(parts, axis=1).astype(jnp.int32)
    per = key_ref.shape[1]
    for c in range(key_ref.shape[0]):
        key_ref[c] = done[c * per : (c + 1) * per, :]


def weight_kernel(
    rows_ref,
    wide_ref,
    half_ref,
    tab_ref,
    w1t_ref,
    wevt_ref,
    w2t_ref,
    w1_ref,
    wev_ref,
    w2_ref,
    wcol_ref,
):
    chans = wide_ref.shape[1]
    rad_rows = wide_ref.shape[0] - 2 * chans
    own = (tab_ref.shape[0] - 4 * rad_rows) // 2
    wa, wb, rad = wide_ref[0:chans, :], wide_ref[chans : 2 * chans, :], wide_ref[2 * chans :, :]
    w1, wenv, wval = [half_ref[i * chans : (i + 1) * chans, :] for i in range(3)]
    w2 = half_ref[3 * chans : 5 * chans, :]

    def flip(w):
        return w.astype(F32).T.astype(BF16)

    down = dot_nn(rad, w1.astype(F32), HIGH)
    w1_ref[0:chans, :] = w1
    w1_ref[chans:, :] = jnp.concatenate([down, jnp.zeros_like(down)], axis=0).astype(BF16)
    w2_ref[...] = w2
    w1t_ref[...] = flip(w1)
    wevt_ref[0:chans, :] = flip(wenv)
    wevt_ref[chans:, :] = flip(wval)
    w2t_ref[:, 0:chans] = flip(w2[0:chans, :])
    w2t_ref[:, chans:] = flip(w2[chans:, :])
    wev_ref[:, 0:chans] = wenv
    wev_ref[:, chans:] = wval
    wout = half_ref[5 * chans : 5 * chans + 1, :].astype(F32)
    wcol_ref[...] = jnp.broadcast_to(wout, (LANES, chans)).T
    feat = rows_ref[0:own, :]
    tab_ref[0:own, :] = dot_nn(feat, wa, HIGH)
    tab_ref[own : 2 * own, :] = dot_nn(feat, wb, HIGH)
    rad_hi, rad_lo = split(rad)
    tab_ref[2 * own :, :] = jnp.concatenate([rad_hi, rad_hi, rad_lo, jnp.zeros_like(rad)], axis=0)


def harmonics(ux, uy, uz):
    return [
        ux,
        uy,
        uz,
        ROOT3 * ux * uy,
        ROOT3 * uy * uz,
        ROOT3 * ux * uz,
        0.866 * (ux * ux - uy * uy),
        0.5 * (3.0 * uz * uz - 1.0),
    ]


def trig(half):
    turns = jnp.round(half)
    x = math.pi * (half - turns)
    odd = turns - 2.0 * jnp.floor(0.5 * turns)
    sign = 1.0 - 2.0 * odd
    x2 = x * x
    s = jnp.full_like(x, -1.0 / 39916800)
    for coef in (1.0 / 362880, -1.0 / 5040, 1.0 / 120, -1.0 / 6, 1.0):
        s = s * x2 + coef
    c = jnp.full_like(x, 1.0 / 479001600)
    for coef in (-1.0 / 3628800, 1.0 / 40320, -1.0 / 720, 1.0 / 24, -0.5, 1.0):
        c = c * x2 + coef
    return sign * x * s, sign * c


def waves(half, count):
    s1, c1 = trig(half)
    sins, coss = [s1], [c1]
    s0, c0 = jnp.zeros_like(s1), jnp.ones_like(c1)
    for _ in range(count - 1):
        sn = 2.0 * c1 * sins[-1] - s0
        cn = 2.0 * c1 * coss[-1] - c0
        s0, c0 = sins[-1], coss[-1]
        sins.append(sn)
        coss.append(cn)
    return sins, coss


def look_up(table_row, index):
    low = index & (LANES - 1)
    high = index >> 7
    result = jnp.zeros(index.shape, F32)
    for block in range(table_row.shape[1] // LANES):
        part = jnp.broadcast_to(table_row[:, block * LANES : (block + 1) * LANES], index.shape)
        got = jnp.take_along_axis(part, low, axis=1)
        result = jnp.where(high == block, got, result)
    return result


def in_lanes(tile):
    return jnp.concatenate([tile[r : r + 1, :] for r in range(tile.shape[0])], axis=1)


def one_hot(row, base, count):
    near = jnp.clip(row - base, -1, LANES).astype(BF16)
    iota = lax.broadcasted_iota(jnp.int32, (count, row.shape[1]), 0).astype(BF16)
    return jnp.where(iota == near, jnp.ones((), BF16), jnp.zeros((), BF16))


def sorted_size(edges):
    return 1 << (edges - 1).bit_length()


def main_kernel(plan, *refs):
    bound_ref, key_ref, pos_ref, wide_ref = refs[:4]
    came, refs = plan.cut(refs[4:], 0, 1, 2)
    half_ref, w1t_ref, wevt_ref, w2t_ref, w1_ref, wev_ref, w2_ref, wcol_ref = refs[:8]
    ae_ref, own_ref = refs[8:10]
    n_x = len(plan.groups[0])
    back_refs, rest_ref = refs[10 : 10 + n_x], refs[10 + n_x]
    (
        tab_ref,
        ghost_ref,
        place_ref,
        table_ref,
        y_ref,
        basis_ref,
        geo_ref,
        first_ref,
        dsilu_ref,
        ew_ref,
        val_ref,
        a_ref,
        env_ref,
        denv_ref,
        big_ref,
        dt_ref,
        dv_ref,
        dfa_ref,
        live_ref,
        dy_ref,
        db_ref,
        dr_ref,
        acc_ref,
        cacc_ref,
    ) = refs[11 + n_x :]
    own = pos_ref.shape[1]
    chans = w1_ref.shape[1]
    n_basis = (w1_ref.shape[0] - chans) // 2
    rows_all = key_ref.shape[0] * key_ref.shape[1]
    per = CHUNK // LANES
    subs = CHUNK // SUB
    sub_rows = SUB // LANES
    n_ghost = sum(len(c) * w for c, w in zip(CLASSES, plan.widths))
    n_tab = own + n_ghost
    n_sel = own + n_tab

    place_ref[...] = jnp.zeros_like(place_ref)
    at = 0
    for off in OFFSETS:
        live = plan.live(off)
        message, begin = plan.find(came, (0, 1, 2), None, [], off)
        ghost_ref[at : at + live, :] = message[begin : begin + live, :]
        place_ref[at : at + live, :] = spread(message[begin + live : begin + live + 1, :], live)
        at += live
    ghost_pos = dot_nt(group_rows(8), place_ref[...], HIGH)
    pos_t = jnp.concatenate([pos_ref[...], ghost_pos[0:3, :]], axis=1)
    f_hi, f_lo = split(ghost_ref[...])
    w_hi, w_lo = split(wide_ref[chans : 2 * chans, :])
    tab_ref[0 : 2 * own, :] = half_ref[0 : 2 * own, :]
    tab_ref[2 * own : n_sel, :] = dot_nn(
        jnp.concatenate([f_hi, f_lo, f_hi], axis=1).astype(BF16),
        jnp.concatenate([w_hi, w_hi, w_lo], axis=0).astype(BF16),
    )
    tab_ref[n_sel:, :] = half_ref[2 * own :, :]
    table_ref[...] = tab_ref[...].T.astype(BF16)

    keys = key_ref[...].reshape(rows_all, LANES)
    centre = keys >> OTHER_BITS
    other = keys & OTHER_MASK
    valid = (other != OTHER_MASK).astype(F32)
    r = [
        look_up(pos_t[a : a + 1, :], other) - look_up(pos_t[a : a + 1, 0:LANES], centre)
        for a in range(3)
    ]
    d2 = r[0] * r[0] + r[1] * r[1] + r[2] * r[2] + 0.01
    dist = jnp.sqrt(d2)
    inv = 1.0 / dist
    q = 1.0 / (1.0 + 0.25 * d2)
    envelope = q * q
    unit = [x * inv for x in r]
    for m, comp in enumerate(harmonics(*unit)):
        y_ref[pl.ds(m, rows_all, stride=8), :] = comp
    sins, _ = waves(0.5 * dist, n_basis)
    scale = envelope * inv
    for n in range(n_basis):
        basis_ref[pl.ds(n, rows_all, stride=n_basis), :] = sins[n] * scale
    for i, plane in enumerate((unit[0], unit[1], unit[2], dist, inv, q, envelope * valid, valid)):
        geo_ref[i] = plane.reshape(geo_ref.shape[1:])

    env_ref[...] = jnp.zeros_like(env_ref)
    denv_ref[...] = jnp.zeros_like(denv_ref)
    ae_ref[...] = jnp.zeros_like(ae_ref)
    acc_ref[...] = jnp.zeros_like(acc_ref)
    cacc_ref[...] = jnp.zeros_like(cacc_ref)
    dr_ref[...] = jnp.zeros_like(dr_ref)

    groups = bound_ref.shape[1] * SUB // sorted_size(rows_all * LANES)

    def window(k, s):
        first = (k * subs + s) * groups
        low = bound_ref[0, first]
        high = low
        for g in range(groups):
            high = jnp.maximum(high, bound_ref[1, first + g])
        start = pl.multiple_of((low >> 3) << 3, 8)
        more = lax.div(high - start, jnp.int32(WIN))
        return start, more

    most = jnp.int32(0)
    n_chunks = jnp.int32(0)
    for s in range(rows_all // sub_rows):
        most = jnp.maximum(most, window(s // subs, s % subs)[1])
        for g in range(groups):
            any_live = bound_ref[1, s * groups + g] >= 0
            n_chunks = jnp.where(any_live, s // subs + 1, n_chunks)


    def lanes_of(s, n):
        if isinstance(s, int):
            return slice(s * SUB, (s + n) * SUB)
        return pl.ds(pl.multiple_of(s * SUB, SUB), n * SUB)

    def tile_of(load, s, n):
        if isinstance(s, int):
            return load(slice(s * sub_rows, (s + n) * sub_rows))
        return jnp.concatenate(
            [load(pl.ds(s * sub_rows + j, 1)) for j in range(n * sub_rows)], axis=0
        )

    def plane(i, k, s, n):
        return tile_of(lambda rows: geo_ref[i, k, rows, :], s, n)

    def keys_of(k, s, n):
        return tile_of(lambda rows: key_ref[k, rows, :], s, n)

    def stacked(ref, k, s, n, height):
        first = (k * subs + s) * sub_rows
        tiles = [
            ref[pl.ds(pl.multiple_of((first + j) * height, 8), height), :]
            for j in range(n * sub_rows)
        ]
        return jnp.concatenate(tiles, axis=1)

    def window_hot(k, s, start):
        crow = in_lanes(keys_of(k, s, 1) >> OTHER_BITS) - start
        return lax.broadcasted_iota(jnp.int32, (WIN, SUB), 0) == crow

    def select(k, s, start):
        hot = window_hot(k, s, start)
        ys = stacked(y_ref, k, s, 1, 8)
        parts = [hot.astype(F32)]
        for m in range(8):
            parts.append(jnp.where(hot, ys[m : m + 1, :], 0.0))
        return jnp.concatenate(parts, axis=0).astype(BF16)

    def load_window(ref, start):
        return jnp.concatenate(
            [ref[m, pl.ds(start, WIN), :] for m in range(9)], axis=0
        ).astype(BF16)

    def add_window(ref, start, rows):
        for m in range(9):
            ref[m, pl.ds(start, WIN), :] += rows[m * WIN : (m + 1) * WIN, :]

    def each_window(k, s, n, slow, body):
        for j in range(n):
            start, more = window(k, s + j)
            body(s + j, j, start, True)
            if slow:

                def step(i, carry, s=s, j=j, start=start):
                    body(s + j, j, pl.multiple_of(start + i * WIN, 8), False)
                    return carry

                lax.fori_loop(1, more + 1, step, 0)

    def kept(k, s, start, fresh):
        return a_ref[k * subs + s] if fresh else select(k, s, start)

    def table_hots(k, s, n):
        row = in_lanes(keys_of(k, s, n) & OTHER_MASK)
        return [one_hot(row, at, min(LANES, n_tab - at)) for at in range(0, n_tab, LANES)]

    def part(j):
        return slice(j * SUB, (j + 1) * SUB)

    def phase_a(k, s, n, slow):
        lanes = lanes_of(s, n)
        crow = in_lanes(keys_of(k, s, n) >> OTHER_BITS)
        hots = [one_hot(crow, 0, own)] + table_hots(k, s, n)
        basis = stacked(basis_ref, k, s, n, n_basis)
        b_hi, b_lo = split(basis)
        hots.append(jnp.concatenate([b_hi, b_lo], axis=0).astype(BF16))
        hots.append(jnp.concatenate([b_hi, jnp.zeros_like(b_hi)], axis=0).astype(BF16))
        mixed = dot_nn(table_ref[...], jnp.concatenate(hots, axis=0)).astype(BF16)
        z1 = dot_nn(w1t_ref[...], mixed)
        sg = 0.5 + 0.5 * jnp.tanh(0.5 * z1)
        first = z1 * sg
        dsilu_ref[k, :, lanes] = (sg + first * (1.0 - sg)).astype(BF16)
        first = first.astype(BF16)
        first_ref[k, :, lanes] = first
        both = dot_nn(wevt_ref[...], first)
        ew = (both[0:chans] * in_lanes(plane(6, k, s, n))).astype(BF16)
        ew_ref[k, :, lanes] = ew
        val_ref[k, :, lanes] = both[chans:].astype(BF16)

        def body(s, j, start, fresh):
            a = select(k, s, start)
            if fresh:
                a_ref[k * subs + s] = a
            add_window(env_ref, start, dot_nt(a, ew[:, part(j)]))

        each_window(k, s, n, slow, body)

    def phase_b(k, s, n, slow):
        lanes = lanes_of(s, n)

        def totals(s, j, start, fresh):
            value = dot_tn(load_window(env_ref, start), kept(k, s, start, fresh))
            if fresh:
                big_ref[:, part(j)] = value
            else:
                big_ref[:, part(j)] += value

        each_window(k, s, n, slow, totals)
        total = 0.2 * big_ref[:, 0 : n * SUB]
        value = val_ref[k, :, lanes].astype(F32)
        scalar = (value * total).astype(BF16)
        z2 = dot_nn(w2t_ref[...], jnp.concatenate([first_ref[k, :, lanes], scalar], axis=0))
        sg = 0.5 + 0.5 * jnp.tanh(0.5 * z2)
        second = z2 * sg
        wcol = jnp.concatenate([wcol_ref[...]] * (n * sub_rows), axis=1)
        ee = jnp.sum(second.astype(BF16).astype(F32) * wcol, axis=0, keepdims=True)
        envv = in_lanes(plane(6, k, s, n))
        live = ee * in_lanes(plane(7, k, s, n))
        first_row = s * sub_rows
        for j in range(n * sub_rows):
            live_ref[k, pl.ds(first_row + j, 1), :] = live[:, j * LANES : (j + 1) * LANES]
        energy = ee * envv
        dz2 = ((wcol * envv) * (sg + second * (1.0 - sg))).astype(BF16)
        dj = dot_nn(w2_ref[...], dz2)
        dfa_ref[k, :, lanes] = dj[0:chans].astype(BF16)
        dscalar = dj[chans:]
        dt = (0.2 * value * dscalar).astype(BF16)
        dt_ref[k, :, lanes] = dt
        dv_ref[k, :, lanes] = (total * dscalar).astype(BF16)

        def body(s, j, start, fresh):
            add_window(denv_ref, start, dot_nt(kept(k, s, start, fresh), dt[:, part(j)]))
            mine = jnp.where(window_hot(k, s, start), energy[:, part(j)], 0.0)
            half = mine[:, 0:LANES]
            for i in range(1, sub_rows):
                half = half + mine[:, i * LANES : (i + 1) * LANES]
            ae_ref[pl.ds(start, WIN), :] += half

        each_window(k, s, n, slow, body)

    def phase_c(k, s, n, slow):
        lanes = lanes_of(s, n)
        height = n * sub_rows

        def env_terms(s, j, start, fresh):
            a = kept(k, s, start, fresh)
            e_win = load_window(env_ref, start)
            d_win = load_window(denv_ref, start)
            dew = dot_tn(d_win, a)
            here = lanes_of(s, 1)
            pair = jnp.concatenate([dt_ref[k, :, here], ew_ref[k, :, here]], axis=0)
            prods = dot_nn(jnp.concatenate([e_win, d_win], axis=1), pair)
            hot = a[0:WIN].astype(F32)
            if fresh:
                big_ref[:, part(j)] = dew
            else:
                big_ref[:, part(j)] += dew
            for m in range(1, 9):
                row = jnp.sum(prods[m * WIN : (m + 1) * WIN] * hot, axis=0, keepdims=True)
                for i in range(sub_rows):
                    at = j * sub_rows + i
                    piece = row[:, i * LANES : (i + 1) * LANES]
                    if fresh:
                        dy_ref[m, at : at + 1, :] = piece
                    else:
                        dy_ref[m, at : at + 1, :] += piece

        each_window(k, s, n, slow, env_terms)
        dew = big_ref[:, 0 : n * SUB]
        dpre = (dew * in_lanes(plane(6, k, s, n))).astype(BF16)
        denv_row = jnp.sum(dew * ew_ref[k, :, lanes].astype(F32), axis=0, keepdims=True)
        for j in range(height):
            dy_ref[0, j : j + 1, :] = denv_row[:, j * LANES : (j + 1) * LANES]
        dfirst = dfa_ref[k, :, lanes].astype(F32) + dot_nn(
            wev_ref[...], jnp.concatenate([dpre, dv_ref[k, :, lanes]], axis=0)
        )
        dz1 = (dfirst * dsilu_ref[k, :, lanes].astype(F32)).astype(BF16)
        dboth = dot_nn(w1_ref[...], dz1)
        dmixed = dboth[0:chans].astype(BF16)
        dbasis = dboth[chans:]
        for j in range(height):
            db_ref[j * n_basis : (j + 1) * n_basis, :] = dbasis[
                0:n_basis, j * LANES : (j + 1) * LANES
            ]
        ux, uy, uz, dist, inv, q = [plane(i, k, s, n) for i in range(6)]
        envelope = q * q
        g = envelope * inv
        denvelope = -(q * envelope) * dist
        dg = (denvelope - g) * inv
        sins, coss = waves(0.5 * dist, n_basis)
        live = tile_of(lambda rows: live_ref[k, rows, :], s, n)
        y = [dy_ref[m, 0:height, :] for m in range(9)]
        ddist = (live + y[0] / envelope) * denvelope
        for i in range(n_basis):
            db = db_ref[pl.ds(i, height, stride=n_basis), :]
            ddist = ddist + db * (coss[i] * ((i + 1) * math.pi / 2.0) * g + sins[i] * dg)
        gx = y[1] + ROOT3 * (uy * y[4] + uz * y[6]) + (2.0 * 0.866) * ux * y[7]
        gy = y[2] + ROOT3 * (ux * y[4] + uz * y[5]) - (2.0 * 0.866) * uy * y[7]
        gz = y[3] + ROOT3 * (uy * y[5] + ux * y[6]) + 3.0 * uz * y[8]
        along = ddist - inv * (gx * ux + gy * uy + gz * uz)
        for i, (gu, u) in enumerate(((gx, ux), (gy, uy), (gz, uz))):
            hi, lo = split(inv * gu + along * u)
            dr_ref[pl.ds(i, height, stride=16), :] = hi
            dr_ref[pl.ds(3 + i, height, stride=16), :] = lo
        dr = jnp.concatenate([dr_ref[j * 16 : (j + 1) * 16, :] for j in range(height)], axis=1)
        moved = jnp.concatenate([dmixed, dr.astype(BF16)], axis=0)
        sums = dot_nt(jnp.concatenate(table_hots(k, s, n), axis=0), moved)
        acc_ref[:, 0:chans] += sums[:, 0:chans]
        acc_ref[:, chans : chans + 16] += sums[:, chans:]

        def body(s, j, start, fresh):
            hot = a_ref[k * subs + s, 0:WIN, :] if fresh else window_hot(k, s, start).astype(BF16)
            mine = dot_nt(hot, moved[:, part(j)])
            cacc_ref[pl.ds(start, WIN), 0:chans] += mine[:, 0:chans]
            cacc_ref[pl.ds(start, WIN), chans : chans + 16] += mine[:, chans:]

        each_window(k, s, n, slow, body)

    for phase in (phase_a, phase_b, phase_c):

        @pl.when(most == 0)
        def _(phase=phase):
            def chunk(k, carry):
                phase(k, 0, subs, False)
                return carry

            lax.fori_loop(0, n_chunks, chunk, 0)

        @pl.when(most != 0)
        def _(phase=phase):
            def sub(i, carry):
                phase(lax.div(i, subs), lax.rem(i, subs), 1, True)
                return carry

            lax.fori_loop(0, n_chunks * subs, sub, 0)

    own_ref[0:own, :] = cacc_ref[0:own, :]
    own_ref[own:, :] = acc_ref[0:own, :]
    row = lax.broadcasted_iota(jnp.int32, (LANES, LANES), 0)
    group = lax.broadcasted_iota(jnp.int32, (LANES, LANES), 1) // GROUP
    both = ((group < 3) & ((row == group) | (row == group + 3))).astype(F32)
    places = dot_nn(acc_ref[own:, LANES:], both, HIGH)
    found = {}
    at = own
    for off in OFFSETS:
        found[off] = at
        at += plan.live(off)
    for blocks, ref in zip(
        plan.groups[0] + [plan.held_rest], tuple(back_refs) + (rest_ref,)
    ):
        for off, row in plan.spans(blocks):
            live = plan.live(off)
            at = found[off]
            ref[row : row + live, :] = acc_ref[at : at + live, 0:chans]
            block = places[at - own : at - own + live, :]
            ref[row + live : row + live + 1, :] = jnp.sum(diagonal(block), axis=0, keepdims=True)


def returned_sums(plan, came, axes, messages, first, sel_ref, both_ref):
    chans = both_ref.shape[1] - LANES
    both_ref[...] = jnp.zeros_like(both_ref)
    at = 0
    for blocks in messages:
        for off, row in plan.spans(blocks):
            live = plan.live(off)
            src, begin = plan.find(came, axes, None, [], off)
            here = slice(at + row, at + row + live)
            both_ref[here, 0:chans] = src[begin : begin + live, :]
            both_ref[here, chans:] = spread(src[begin + live : begin + live + 1, :], live)
        at += plan.total(blocks)
    hot = sel_ref[first : first + at, :].astype(BF16)
    return dot_exact(hot, both_ref[...], ((0,), (0,)))


def own_kernel(plan, ae_ref, own_ref, wide_ref, sel_ref, *refs):
    came, refs = plan.cut(refs, 0, 1)
    energy_ref, fg_ref, force_ref, both_ref = refs
    chans = fg_ref.shape[1]
    own = force_ref.shape[1]
    first = sum(plan.total(blocks) for blocks in plan.groups[2])
    sums = returned_sums(plan, came, (1, 0), [plan.own_rest], first, sel_ref, both_ref)
    energy_ref[...] = jnp.sum(ae_ref[0:own, :].T, axis=0, keepdims=True)
    fg_ref[...] = dot_nt(own_ref[0:own, 0:chans], wide_ref[0:chans, :], HIGH) + dot_nt(
        own_ref[own:, 0:chans] + sums[:, 0:chans], wide_ref[chans : 2 * chans, :], HIGH
    )
    force = (own_ref[own:, LANES:] - own_ref[0:own, LANES:]).T
    total = dot_nt(group_rows(8), sums[:, chans:], HIGH)
    force_ref[...] = force[0:3, :] + force[3:6, :] + total[0:3, :]


def last_kernel(plan, sel_ref, fg_ref, force_ref, wide_ref, *refs):
    came, refs = plan.cut(refs, 2)
    out_force_ref, out_fg_ref, both_ref = refs
    chans = fg_ref.shape[1]
    sums = returned_sums(plan, came, (2,), plan.groups[2], 0, sel_ref, both_ref)
    s_hi, s_lo = split(sums[:, 0:chans])
    w_hi, w_lo = split(wide_ref[chans : 2 * chans, :])
    out_fg_ref[...] = fg_ref[...] + dot_nt(
        jnp.concatenate([s_hi, s_lo, s_hi], axis=1).astype(BF16),
        jnp.concatenate([w_hi, w_hi, w_lo], axis=1).astype(BF16),
    )
    total = dot_nt(group_rows(8), sums[:, chans:], HIGH)
    out_force_ref[...] = -(force_ref[...] + total[0:3, :])


def stack(*arrays):
    dtype = arrays[0].dtype
    tile = 32 // dtype.itemsize
    starts = [0]
    for x in arrays:
        starts.append(starts[-1] + -(-x.shape[0] // tile) * tile)
    total = None
    for x, at in zip(arrays, starts):
        below = starts[-1] - at - x.shape[0]
        part = jnp.pad(x.astype(dtype), ((at, below), (0, LANES - x.shape[1])))
        total = part if total is None else total + part
    return total


def local(
    positions,
    atom_features,
    send_face,
    send_edge,
    send_corner,
    centre,
    other,
    edge_count,
    w_proj_a,
    w_proj_b,
    w_radial,
    w_first,
    w_env,
    w_value,
    w_second,
    w_out,
):
    own, chans = atom_features.shape
    edges = centre.shape[0]
    n_basis = w_radial.shape[0]
    plan = Plan(
        [send_face.shape[2], send_edge.shape[2], send_corner.shape[2]],
        [lax.axis_size(axis) for axis in AXES],
    )
    n_ghost = sum(len(c) * w for c, w in zip(CLASSES, plan.widths))
    n_sel = 2 * own + n_ghost
    n_send = sum(plan.total(blocks) for blocks in plan.groups[2]) + plan.total(plan.own_rest)
    n_table = n_sel + 4 * n_basis
    edges_up = -(-edges // CHUNK) * CHUNK
    n_rows = edges_up // LANES
    n_chunks = edges_up // CHUNK

    with jax.named_scope("prep"):
        rows = stack(
            atom_features, send_face[0], jnp.transpose(send_edge[0]), edge_count.reshape(1, 1)
        )
        *sends, own_rows, sel = pl.pallas_call(
            lambda *refs: prep_kernel(plan, *refs),
            out_shape=plan.shapes(2, chans)
            + [shape(plan.total(plan.own_rest), chans), shape(n_send, own)],
            in_specs=[VMEM] * 3,
            out_specs=[VMEM] * (len(plan.groups[2]) + 2),
            scratch_shapes=[pltpu.VMEM((LANES, LANES), F32)],
            compiler_params=PARAMS,
        )(rows, positions, jnp.transpose(send_corner, (0, 2, 1)))

    came = {}
    with jax.named_scope("halo_z"):
        came[2] = plan.send(2, sends)

    with jax.named_scope("group_edges"):
        pad = [(0, edges_up - edges)]
        regs = max(sorted_size(edges_up) // (8 * LANES), 1)
        key, bounds = pl.pallas_call(
            lambda *refs: sort_kernel(own, *refs),
            out_shape=[
                shape(n_chunks, CHUNK // LANES, LANES, dtype=jnp.int32),
                shape(2, LANES, dtype=jnp.int32),
            ],
            in_specs=[VMEM] * 3,
            out_specs=[VMEM] * 2,
            scratch_shapes=[pltpu.VMEM((16 * regs, LANES), F32)],
            compiler_params=PARAMS,
        )(
            rows,
            jnp.pad(centre, pad).reshape(n_rows, LANES),
            jnp.pad(other, pad).reshape(n_rows, LANES),
        )

    with jax.named_scope("halo_y"):
        came[2], key, bounds, w_first, w_env, w_value, w_second, w_out = lax.optimization_barrier(
            (came[2], key, bounds, w_first, w_env, w_value, w_second, w_out)
        )
        came[1] = plan.send(1, glue(plan, 1, (2,), plan.own_rest, own_rows, came))

    with jax.named_scope("weights"):
        wide = stack(w_proj_a, w_proj_b, w_radial)
        narrow = stack(w_first, w_env, w_value, w_second, w_out[None, :])
        half, *weights = pl.pallas_call(
            weight_kernel,
            out_shape=[
                shape(2 * own + 4 * n_basis, chans),
                shape(chans, chans, dtype=BF16),
                shape(2 * chans, chans, dtype=BF16),
                shape(chans, 2 * chans, dtype=BF16),
                shape(chans + 2 * n_basis, chans, dtype=BF16),
                shape(chans, 2 * chans, dtype=BF16),
                shape(2 * chans, chans, dtype=BF16),
                shape(chans, LANES),
            ],
            in_specs=[VMEM] * 3,
            out_specs=[VMEM] * 8,
            compiler_params=PARAMS,
        )(rows, wide, narrow)

    with jax.named_scope("halo_x"):
        came[1], half, weights = lax.optimization_barrier((came[1], half, weights))
        came[0] = plan.send(0, glue(plan, 0, (1, 2), plan.own_rest, own_rows, came))

    planes = (n_chunks, chans, CHUNK)
    scratch = [
        pltpu.VMEM((n_table, chans), F32),
        pltpu.VMEM((n_ghost, chans), F32),
        pltpu.VMEM((-(-n_ghost // LANES) * LANES, LANES), F32),
        pltpu.VMEM((chans, n_table), BF16),
        pltpu.VMEM((n_rows * 8, LANES), F32),
        pltpu.VMEM((n_rows * n_basis, LANES), F32),
        pltpu.VMEM((8, n_chunks, CHUNK // LANES, LANES), F32),
        pltpu.VMEM(planes, BF16),
        pltpu.VMEM(planes, BF16),
        pltpu.VMEM(planes, BF16),
        pltpu.VMEM(planes, BF16),
        pltpu.VMEM((edges_up // SUB, 9 * WIN, SUB), BF16),
        pltpu.VMEM((9, own + WIN, chans), F32),
        pltpu.VMEM((9, own + WIN, chans), F32),
        pltpu.VMEM((chans, CHUNK), F32),
        pltpu.VMEM(planes, BF16),
        pltpu.VMEM(planes, BF16),
        pltpu.VMEM(planes, BF16),
        pltpu.VMEM((n_chunks, CHUNK // LANES, LANES), F32),
        pltpu.VMEM((9, CHUNK // LANES, LANES), F32),
        pltpu.VMEM((CHUNK // LANES * n_basis, LANES), F32),
        pltpu.VMEM((CHUNK // LANES * 16, LANES), F32),
        pltpu.VMEM((n_sel - own, 2 * LANES), F32),
        pltpu.VMEM((own + WIN, 2 * LANES), F32),
    ]
    with jax.named_scope("layer"):
        given = [bounds, key, positions, wide]
        given += [*came[0], *came[1], *came[2], half, *weights]
        atom_sums, own_sums, *back, held = pl.pallas_call(
            lambda *refs: main_kernel(plan, *refs),
            out_shape=[shape(own + WIN, LANES), shape(2 * own, 2 * LANES)]
            + plan.shapes(0, chans)
            + [shape(plan.total(plan.held_rest), chans)],
            in_specs=[SMEM] + [VMEM] * (len(given) - 1),
            out_specs=[VMEM] * (3 + len(plan.groups[0])),
            scratch_shapes=scratch,
            compiler_params=PARAMS,
        )(*given)

    with jax.named_scope("halo_back"):
        home = {0: plan.send(0, back, back=True)}
        home[1] = plan.send(1, glue(plan, 1, (0,), plan.held_rest, held, home), back=True)
        home[2] = plan.send(2, glue(plan, 2, (1, 0), plan.held_rest, held, home), back=True)

    with jax.named_scope("own_part"):
        given = [atom_sums, own_sums, wide, sel, *home[0], *home[1]]
        energy, fg, force = pl.pallas_call(
            lambda *refs: own_kernel(plan, *refs),
            out_shape=[shape(1, own), shape(own, chans), shape(3, own)],
            in_specs=[VMEM] * len(given),
            out_specs=[VMEM] * 3,
            scratch_shapes=[pltpu.VMEM((plan.total(plan.own_rest), chans + LANES), F32)],
            compiler_params=PARAMS,
        )(*given)

    with jax.named_scope("owner_sums"):
        given = [sel, fg, force, wide, *home[2]]
        n_z = n_send - plan.total(plan.own_rest)
        forces, feature_grad = pl.pallas_call(
            lambda *refs: last_kernel(plan, *refs),
            out_shape=[shape(3, own), shape(own, chans)],
            in_specs=[VMEM] * len(given),
            out_specs=[VMEM] * 2,
            scratch_shapes=[pltpu.VMEM((n_z, chans + LANES), F32)],
            compiler_params=PARAMS,
        )(*given)
    return forces, energy.reshape(own), feature_grad


def solution(mesh):
    shard = P(AXES)
    return jax.shard_map(
        local,
        mesh=mesh,
        in_specs=(
            P(None, AXES),
            P(AXES, None),
            P(AXES, None, None),
            P(AXES, None, None),
            P(AXES, None, None),
            shard,
            shard,
            shard,
        )
        + (P(),) * 8,
        out_specs=(P(None, AXES), shard, P(AXES, None)),
        check_vma=False,
    )
```

```python
import math

import jax
import jax.numpy as jnp
from jax import lax
from jax.experimental import pallas as pl
from jax.experimental.pallas import tpu as pltpu
from jax.sharding import PartitionSpec as P

F32 = jnp.float32
BF16 = jnp.bfloat16
HIGH = lax.Precision.HIGHEST
AXES = ("gx", "gy", "gz")
CHUNK = 3072
SUB = 256
WIN = 16
OTHER_BITS = 9
OTHER_MASK = (1 << OTHER_BITS) - 1
LANES = 128
ROOT3 = 1.732


VMEM = pl.BlockSpec(memory_space=pltpu.VMEM)
SMEM = pl.BlockSpec(memory_space=pltpu.SMEM)
PARAMS = pltpu.CompilerParams(vmem_limit_bytes=52 * 2**20)


def shape(*dims, dtype=F32):
    return jax.ShapeDtypeStruct(dims, dtype)


def dot_nn(a, b, precision=None):
    return lax.dot_general(
        a, b, (((1,), (0,)), ((), ())), preferred_element_type=F32, precision=precision
    )


def dot_nt(a, b, precision=None):
    return lax.dot_general(
        a, b, (((1,), (1,)), ((), ())), preferred_element_type=F32, precision=precision
    )


def dot_tn(a, b, precision=None):
    return lax.dot_general(
        a, b, (((0,), (0,)), ((), ())), preferred_element_type=F32, precision=precision
    )


def offset_classes():
    classes = [[], [], []]
    for a in (-1, 0, 1):
        for b in (-1, 0, 1):
            for c in (-1, 0, 1):
                if (a, b, c) != (0, 0, 0):
                    classes[abs(a) + abs(b) + abs(c) - 1].append((a, b, c))
    return classes


CLASSES = offset_classes()


OFFSETS = [off for group in CLASSES for off in group]


def kind(off):
    return abs(off[0]) + abs(off[1]) + abs(off[2]) - 1


class Plan:
    def __init__(self, widths, sizes):
        self.widths = widths
        self.sizes = sizes
        self.groups = [self.group(a) for a in range(3)]
        self.own_rest = [off for off in OFFSETS if off[2] == 0]
        self.held_rest = [off for off in OFFSETS if off[0] == 0]

    def group(self, a):
        groups = {}
        for off in OFFSETS:
            if off[a] != 0:
                groups.setdefault(off[a] % self.sizes[a], []).append(off)
        return list(groups.values())

    def live(self, off):
        return self.widths[kind(off)]

    def rows(self, off):
        return self.live(off) + 1

    def total(self, blocks):
        return sum(self.rows(off) for off in blocks)

    def spans(self, blocks):
        at = 0
        for off in blocks:
            yield off, at
            at += self.rows(off)

    def place(self, a, off):
        for g, blocks in enumerate(self.groups[a]):
            if off in blocks:
                return g, dict(self.spans(blocks))[off]
        raise KeyError(off)

    def find(self, came, axes, rest_ref, rest, off):
        for a in axes:
            if off[a] != 0:
                g, begin = self.place(a, off)
                return came[a][g], begin
        return rest_ref, dict(self.spans(rest))[off]

    def cut(self, refs, *axes):
        came = {}
        for a in axes:
            n = len(self.groups[a])
            came[a], refs = refs[:n], refs[n:]
        return came, refs

    def shapes(self, a, chans):
        return [shape(self.total(blocks), chans) for blocks in self.groups[a]]

    def send(self, a, messages, back=False):
        n = self.sizes[a]
        steps = [-blocks[0][a] if back else blocks[0][a] for blocks in self.groups[a]]
        if n % 2 or n == 2:
            return [
                lax.ppermute(message, AXES[a], [(i, (i + step) % n) for i in range(n)])
                for step, message in zip(steps, messages)
            ]
        up, down = steps.index(1), steps.index(-1)
        even = lax.axis_index(AXES[a]) % 2 == 0
        ahead = [(i, i + 1 - 2 * (i % 2)) for i in range(n)]
        behind = [(i, (i - 1 + 2 * (i % 2)) % n) for i in range(n)]
        first = lax.ppermute(jnp.where(even, messages[up], messages[down]), AXES[a], ahead)
        second = lax.ppermute(jnp.where(even, messages[down], messages[up]), AXES[a], behind)
        got = [None, None]
        got[up] = jnp.where(even, second, first)
        got[down] = jnp.where(even, first, second)
        return got


GROUP = 32


def group_rows(count):
    row = lax.broadcasted_iota(jnp.int32, (count, LANES), 0)
    group = lax.broadcasted_iota(jnp.int32, (count, LANES), 1) // GROUP
    return (row == group).astype(F32) * (group < 3).astype(F32)


def diagonal(x):
    row = lax.broadcasted_iota(jnp.int32, x.shape, 0)
    lane = lax.broadcasted_iota(jnp.int32, x.shape, 1)
    return jnp.where((lane & (GROUP - 1)) == row, x, 0.0)


def spread(row, live):
    return diagonal(jnp.broadcast_to(row, (live, LANES)))


def split(x):
    high = x.astype(BF16).astype(F32)
    return high, x - high


def dot_exact(hot, x, dims):
    high, low = split(x)
    both = jnp.concatenate([high, low], axis=1).astype(BF16)
    out = lax.dot_general(hot, both, (dims, ((), ())), preferred_element_type=F32)
    return out[:, 0 : x.shape[1]] + out[:, x.shape[1] :]


def prep_kernel(plan, rows_ref, pos_ref, corner_ref, *outs):
    n_z = len(plan.groups[2])
    sends, rest_ref, sel_ref, turn_ref = outs[:n_z], outs[n_z], outs[n_z + 1], outs[n_z + 2]
    own = sel_ref.shape[1]
    lane = lax.broadcasted_iota(jnp.int32, (1, own), 1).astype(F32)
    n_faces = len(CLASSES[0])
    turn_ref[...] = jnp.zeros_like(turn_ref)
    turn_ref[0:n_faces, :] = rows_ref[own : own + n_faces, :]
    columns = [
        turn_ref[...].T,
        rows_ref[own + 8 : own + 8 + plan.widths[1], :],
        corner_ref[0].astype(F32),
    ]
    sel_ref[...] = jnp.zeros_like(sel_ref)
    messages = plan.groups[2] + [plan.own_rest]
    at = 0
    for blocks in messages:
        for off, begin in plan.spans(blocks):
            key = CLASSES[kind(off)].index(off)
            live = plan.live(off)
            column = columns[kind(off)][0:live, key : key + 1]
            sel_ref[at + begin : at + begin + live, :] = (column == lane).astype(F32)
        at += plan.total(blocks)
    pos = dot_tn(pos_ref[...], group_rows(3), HIGH)
    sel = sel_ref[...]
    rows = dot_nn(sel, rows_ref[0:own, :], HIGH)
    places = dot_nn(sel, pos, HIGH)
    at = 0
    for blocks, send in zip(messages, tuple(sends) + (rest_ref,)):
        count = plan.total(blocks)
        send[...] = rows[at : at + count, :]
        for off, begin in plan.spans(blocks):
            live = plan.live(off)
            block = places[at + begin : at + begin + live, :]
            send[begin + live : begin + live + 1, :] = jnp.sum(
                diagonal(block), axis=0, keepdims=True
            )
        at += count


def glue_kernel(plan, a, axes, rest, *refs):
    rest_ref = refs[0]
    came, outs = plan.cut(refs[1:], *axes)
    for blocks, out in zip(plan.groups[a], outs):
        for off, row in plan.spans(blocks):
            src, begin = plan.find(came, axes, rest_ref, rest, off)
            out[row : row + plan.rows(off), :] = src[begin : begin + plan.rows(off), :]


def glue(plan, a, axes, rest, rest_rows, came):
    given = [rest_rows] + [message for axis in axes for message in came[axis]]
    outs = plan.shapes(a, rest_rows.shape[1])
    return pl.pallas_call(
        lambda *refs: glue_kernel(plan, a, axes, rest, *refs),
        out_shape=outs,
        in_specs=[VMEM] * len(given),
        out_specs=[VMEM] * len(outs),
        compiler_params=PARAMS,
    )(*given)


def sort_kernel(own, count_ref, centre_ref, other_ref, key_ref, bound_ref, turn_ref):
    dead = (own - 1) * (OTHER_MASK + 1) + OTHER_MASK
    rows = centre_ref.shape[0]
    regs = turn_ref.shape[0] // 16
    group = regs * 8
    row = lax.broadcasted_iota(jnp.int32, (rows, LANES), 0)
    lane = lax.broadcasted_iota(jnp.int32, (rows, LANES), 1)
    count = count_ref[count_ref.shape[0] - 8 : count_ref.shape[0] - 7, 0:1].astype(jnp.int32)
    live = row * LANES + lane < count
    centre = centre_ref[...]
    key = jnp.where(live, (centre << OTHER_BITS) + other_ref[...], dead).astype(F32)
    x = [key[8 * v : 8 * v + 8, :] for v in range(rows // 8)]
    x += [jnp.full((8, LANES), float(dead), F32)] * (regs - len(x))
    n_windows = own // WIN
    free = regs - rows // 8
    if n_windows * SUB <= free * 8 * LANES:
        window = jnp.where(live, centre // WIN, -1)
        need = []
        used = jnp.zeros((1, 1), F32)
        for w in range(n_windows):
            hits = jnp.sum((window == w).astype(F32), axis=0, keepdims=True)
            hits = jnp.sum(hits, axis=1, keepdims=True)
            whole = jnp.floor((hits + (SUB - 1)) * (1.0 / SUB)) * SUB
            used = used + whole
            need.append(whole - hits)
        fits = used <= float(rows * LANES)
        slot = lax.broadcasted_iota(jnp.int32, (8, LANES), 0) * LANES
        slot = slot + lax.broadcasted_iota(jnp.int32, (8, LANES), 1)
        per_reg = 8 * LANES // SUB
        for w in range(n_windows):
            v = rows // 8 + w // per_reg
            at = slot - (w % per_reg) * SUB
            take = (at >= 0) & (at.astype(F32) < need[w]) & fits
            mark = float((w * WIN + WIN - 1) * (OTHER_MASK + 1) + OTHER_MASK)
            x[v] = jnp.where(take, mark, x[v])
    s = lax.broadcasted_iota(jnp.int32, (8, LANES), 0)
    ln = lax.broadcasted_iota(jnp.int32, (8, LANES), 1)
    base = ln * group + s * regs

    def sign(k, v):
        return jnp.where(((base + v) & k) == 0, 1.0, -1.0).astype(F32)

    last = [jnp.ones((8, LANES), F32)] * regs
    total = group * LANES
    k = 2
    while k <= total:
        signs = [sign(k, v) for v in range(regs)] if k < total else [1.0] * regs
        x = [x[v] * (last[v] * signs[v]) for v in range(regs)]
        last = signs
        j = k // 2
        while j >= 1:
            if j < regs:
                for v in range(regs):
                    if v & j == 0:
                        a, b = x[v], x[v | j]
                        x[v], x[v | j] = jnp.minimum(a, b), jnp.maximum(a, b)
            else:
                axis, step, size, ids = (
                    (0, j // regs, 8, s) if j < group else (1, j // group, LANES, ln)
                )
                low = (ids & step) == 0
                for v in range(regs):
                    up = pltpu.roll(x[v], size - step, axis)
                    if 2 * step == size:
                        mate = up
                    else:
                        mate = jnp.where(low, up, pltpu.roll(x[v], step, axis))
                    x[v] = jnp.where(low, jnp.minimum(x[v], mate), jnp.maximum(x[v], mate))
            j //= 2
        k *= 2
    least = x[0]
    most = jnp.where(x[0] == float(dead), -1.0, x[0])
    for v in range(1, regs):
        least = jnp.minimum(least, x[v])
        most = jnp.maximum(most, jnp.where(x[v] == float(dead), -1.0, x[v]))
    bound_ref[0:1, :] = jnp.min(least, axis=0, keepdims=True).astype(jnp.int32) >> OTHER_BITS
    bound_ref[1:2, :] = jnp.max(most, axis=0, keepdims=True).astype(jnp.int32) >> OTHER_BITS
    turned = jnp.concatenate(x + [jnp.zeros((LANES - group, LANES), F32)], axis=0).T
    turn_ref[...] = turned
    ratio = LANES // group
    parts = [
        turn_ref[pl.ds(i, rows, stride=ratio), 0:group] for i in range(ratio)
    ]
    done = jnp.concatenate(parts, axis=1).astype(jnp.int32)
    per = key_ref.shape[1]
    for c in range(key_ref.shape[0]):
        key_ref[c] = done[c * per : (c + 1) * per, :]


def weight_kernel(
    rows_ref,
    wide_ref,
    half_ref,
    tab_ref,
    w1t_ref,
    wevt_ref,
    w2t_ref,
    w1_ref,
    wev_ref,
    w2_ref,
    wcol_ref,
):
    chans = wide_ref.shape[1]
    rad_rows = wide_ref.shape[0] - 2 * chans
    own = (tab_ref.shape[0] - 4 * rad_rows) // 2
    wa, wb, rad = wide_ref[0:chans, :], wide_ref[chans : 2 * chans, :], wide_ref[2 * chans :, :]
    w1, wenv, wval = [half_ref[i * chans : (i + 1) * chans, :] for i in range(3)]
    w2 = half_ref[3 * chans : 5 * chans, :]

    def flip(w):
        return w.astype(F32).T.astype(BF16)

    down = dot_nn(rad, w1.astype(F32), HIGH)
    w1_ref[0:chans, :] = w1
    w1_ref[chans:, :] = jnp.concatenate([down, jnp.zeros_like(down)], axis=0).astype(BF16)
    w2_ref[...] = w2
    w1t_ref[...] = flip(w1)
    wevt_ref[0:chans, :] = flip(wenv)
    wevt_ref[chans:, :] = flip(wval)
    w2t_ref[:, 0:chans] = flip(w2[0:chans, :])
    w2t_ref[:, chans:] = flip(w2[chans:, :])
    wev_ref[:, 0:chans] = wenv
    wev_ref[:, chans:] = wval
    wout = half_ref[5 * chans : 5 * chans + 1, :].astype(F32)
    wcol_ref[...] = jnp.broadcast_to(wout, (LANES, chans)).T
    feat = rows_ref[0:own, :]
    tab_ref[0:own, :] = dot_nn(feat, wa, HIGH)
    tab_ref[own : 2 * own, :] = dot_nn(feat, wb, HIGH)
    rad_hi, rad_lo = split(rad)
    tab_ref[2 * own :, :] = jnp.concatenate([rad_hi, rad_hi, rad_lo, jnp.zeros_like(rad)], axis=0)


def harmonics(ux, uy, uz):
    return [
        ux,
        uy,
        uz,
        ROOT3 * ux * uy,
        ROOT3 * uy * uz,
        ROOT3 * ux * uz,
        0.866 * (ux * ux - uy * uy),
        0.5 * (3.0 * uz * uz - 1.0),
    ]


def trig(half):
    turns = jnp.round(half)
    x = math.pi * (half - turns)
    odd = turns - 2.0 * jnp.floor(0.5 * turns)
    sign = 1.0 - 2.0 * odd
    x2 = x * x
    s = jnp.full_like(x, -1.0 / 39916800)
    for coef in (1.0 / 362880, -1.0 / 5040, 1.0 / 120, -1.0 / 6, 1.0):
        s = s * x2 + coef
    c = jnp.full_like(x, 1.0 / 479001600)
    for coef in (-1.0 / 3628800, 1.0 / 40320, -1.0 / 720, 1.0 / 24, -0.5, 1.0):
        c = c * x2 + coef
    return sign * x * s, sign * c


def waves(half, count):
    s1, c1 = trig(half)
    sins, coss = [s1], [c1]
    s0, c0 = jnp.zeros_like(s1), jnp.ones_like(c1)
    for _ in range(count - 1):
        sn = 2.0 * c1 * sins[-1] - s0
        cn = 2.0 * c1 * coss[-1] - c0
        s0, c0 = sins[-1], coss[-1]
        sins.append(sn)
        coss.append(cn)
    return sins, coss


def look_up(table_row, index):
    low = index & (LANES - 1)
    high = index >> 7
    result = jnp.zeros(index.shape, F32)
    for block in range(table_row.shape[1] // LANES):
        part = jnp.broadcast_to(table_row[:, block * LANES : (block + 1) * LANES], index.shape)
        got = jnp.take_along_axis(part, low, axis=1)
        result = jnp.where(high == block, got, result)
    return result


def in_lanes(tile):
    return jnp.concatenate([tile[r : r + 1, :] for r in range(tile.shape[0])], axis=1)


def one_hot(row, base, count):
    near = jnp.clip(row - base, -1, LANES).astype(BF16)
    iota = lax.broadcasted_iota(jnp.int32, (count, row.shape[1]), 0).astype(BF16)
    return jnp.where(iota == near, jnp.ones((), BF16), jnp.zeros((), BF16))


def sorted_size(edges):
    return 1 << (edges - 1).bit_length()


def main_kernel(plan, *refs):
    bound_ref, key_ref, pos_ref, wide_ref = refs[:4]
    came, refs = plan.cut(refs[4:], 0, 1, 2)
    half_ref, w1t_ref, wevt_ref, w2t_ref, w1_ref, wev_ref, w2_ref, wcol_ref = refs[:8]
    ae_ref, own_ref = refs[8:10]
    n_x = len(plan.groups[0])
    back_refs, rest_ref = refs[10 : 10 + n_x], refs[10 + n_x]
    (
        tab_ref,
        ghost_ref,
        place_ref,
        table_ref,
        y_ref,
        basis_ref,
        geo_ref,
        first_ref,
        dsilu_ref,
        ew_ref,
        val_ref,
        a_ref,
        env_ref,
        denv_ref,
        big_ref,
        dt_ref,
        dv_ref,
        dfa_ref,
        live_ref,
        dy_ref,
        db_ref,
        dr_ref,
        acc_ref,
        cacc_ref,
    ) = refs[11 + n_x :]
    own = pos_ref.shape[1]
    chans = w1_ref.shape[1]
    n_basis = (w1_ref.shape[0] - chans) // 2
    rows_all = key_ref.shape[0] * key_ref.shape[1]
    per = CHUNK // LANES
    subs = CHUNK // SUB
    sub_rows = SUB // LANES
    n_ghost = sum(len(c) * w for c, w in zip(CLASSES, plan.widths))
    n_tab = own + n_ghost
    n_sel = own + n_tab

    place_ref[...] = jnp.zeros_like(place_ref)
    at = 0
    for off in OFFSETS:
        live = plan.live(off)
        message, begin = plan.find(came, (0, 1, 2), None, [], off)
        ghost_ref[at : at + live, :] = message[begin : begin + live, :]
        place_ref[at : at + live, :] = spread(message[begin + live : begin + live + 1, :], live)
        at += live
    ghost_pos = dot_nt(group_rows(8), place_ref[...], HIGH)
    pos_t = jnp.concatenate([pos_ref[...], ghost_pos[0:3, :]], axis=1)
    f_hi, f_lo = split(ghost_ref[...])
    w_hi, w_lo = split(wide_ref[chans : 2 * chans, :])
    tab_ref[0 : 2 * own, :] = half_ref[0 : 2 * own, :]
    tab_ref[2 * own : n_sel, :] = dot_nn(
        jnp.concatenate([f_hi, f_lo, f_hi], axis=1).astype(BF16),
        jnp.concatenate([w_hi, w_hi, w_lo], axis=0).astype(BF16),
    )
    tab_ref[n_sel:, :] = half_ref[2 * own :, :]
    table_ref[...] = tab_ref[...].T.astype(BF16)

    keys = key_ref[...].reshape(rows_all, LANES)
    centre = keys >> OTHER_BITS
    other = keys & OTHER_MASK
    valid = (other != OTHER_MASK).astype(F32)
    r = [
        look_up(pos_t[a : a + 1, :], other) - look_up(pos_t[a : a + 1, 0:LANES], centre)
        for a in range(3)
    ]
    d2 = r[0] * r[0] + r[1] * r[1] + r[2] * r[2] + 0.01
    dist = jnp.sqrt(d2)
    inv = 1.0 / dist
    q = 1.0 / (1.0 + 0.25 * d2)
    envelope = q * q
    unit = [x * inv for x in r]
    for m, comp in enumerate(harmonics(*unit)):
        y_ref[pl.ds(m, rows_all, stride=8), :] = comp
    sins, _ = waves(0.5 * dist, n_basis)
    scale = envelope * inv
    for n in range(n_basis):
        basis_ref[pl.ds(n, rows_all, stride=n_basis), :] = sins[n] * scale
    for i, plane in enumerate((unit[0], unit[1], unit[2], dist, inv, q, envelope * valid, valid)):
        geo_ref[i] = plane.reshape(geo_ref.shape[1:])

    env_ref[...] = jnp.zeros_like(env_ref)
    denv_ref[...] = jnp.zeros_like(denv_ref)
    ae_ref[...] = jnp.zeros_like(ae_ref)
    acc_ref[...] = jnp.zeros_like(acc_ref)
    cacc_ref[...] = jnp.zeros_like(cacc_ref)
    dr_ref[...] = jnp.zeros_like(dr_ref)

    groups = bound_ref.shape[1] * SUB // sorted_size(rows_all * LANES)

    def window(k, s):
        first = (k * subs + s) * groups
        low = bound_ref[0, first]
        high = low
        for g in range(groups):
            high = jnp.maximum(high, bound_ref[1, first + g])
        start = pl.multiple_of((low >> 3) << 3, 8)
        more = lax.div(high - start, jnp.int32(WIN))
        return start, more

    most = jnp.int32(0)
    n_chunks = jnp.int32(0)
    for s in range(rows_all // sub_rows):
        most = jnp.maximum(most, window(s // subs, s % subs)[1])
        for g in range(groups):
            any_live = bound_ref[1, s * groups + g] >= 0
            n_chunks = jnp.where(any_live, s // subs + 1, n_chunks)


    def lanes_of(s, n):
        if isinstance(s, int):
            return slice(s * SUB, (s + n) * SUB)
        return pl.ds(pl.multiple_of(s * SUB, SUB), n * SUB)

    def tile_of(load, s, n):
        if isinstance(s, int):
            return load(slice(s * sub_rows, (s + n) * sub_rows))
        return jnp.concatenate(
            [load(pl.ds(s * sub_rows + j, 1)) for j in range(n * sub_rows)], axis=0
        )

    def plane(i, k, s, n):
        return tile_of(lambda rows: geo_ref[i, k, rows, :], s, n)

    def keys_of(k, s, n):
        return tile_of(lambda rows: key_ref[k, rows, :], s, n)

    def stacked(ref, k, s, n, height):
        first = (k * subs + s) * sub_rows
        tiles = [
            ref[pl.ds(pl.multiple_of((first + j) * height, 8), height), :]
            for j in range(n * sub_rows)
        ]
        return jnp.concatenate(tiles, axis=1)

    def window_hot(k, s, start):
        crow = in_lanes(keys_of(k, s, 1) >> OTHER_BITS) - start
        return lax.broadcasted_iota(jnp.int32, (WIN, SUB), 0) == crow

    def select(k, s, start):
        hot = window_hot(k, s, start)
        ys = stacked(y_ref, k, s, 1, 8)
        parts = [hot.astype(F32)]
        for m in range(8):
            parts.append(jnp.where(hot, ys[m : m + 1, :], 0.0))
        return jnp.concatenate(parts, axis=0).astype(BF16)

    def load_window(ref, start):
        return jnp.concatenate(
            [ref[m, pl.ds(start, WIN), :] for m in range(9)], axis=0
        ).astype(BF16)

    def add_window(ref, start, rows):
        for m in range(9):
            ref[m, pl.ds(start, WIN), :] += rows[m * WIN : (m + 1) * WIN, :]

    def each_window(k, s, n, slow, body):
        for j in range(n):
            start, more = window(k, s + j)
            body(s + j, j, start, True)
            if slow:

                def step(i, carry, s=s, j=j, start=start):
                    body(s + j, j, pl.multiple_of(start + i * WIN, 8), False)
                    return carry

                lax.fori_loop(1, more + 1, step, 0)

    def kept(k, s, start, fresh):
        return a_ref[k * subs + s] if fresh else select(k, s, start)

    def table_hots(k, s, n):
        row = in_lanes(keys_of(k, s, n) & OTHER_MASK)
        return [one_hot(row, at, min(LANES, n_tab - at)) for at in range(0, n_tab, LANES)]

    def part(j):
        return slice(j * SUB, (j + 1) * SUB)

    def phase_a(k, s, n, slow):
        lanes = lanes_of(s, n)
        crow = in_lanes(keys_of(k, s, n) >> OTHER_BITS)
        hots = [one_hot(crow, 0, own)] + table_hots(k, s, n)
        basis = stacked(basis_ref, k, s, n, n_basis)
        b_hi, b_lo = split(basis)
        hots.append(jnp.concatenate([b_hi, b_lo], axis=0).astype(BF16))
        hots.append(jnp.concatenate([b_hi, jnp.zeros_like(b_hi)], axis=0).astype(BF16))
        mixed = dot_nn(table_ref[...], jnp.concatenate(hots, axis=0)).astype(BF16)
        z1 = dot_nn(w1t_ref[...], mixed)
        sg = 0.5 + 0.5 * jnp.tanh(0.5 * z1)
        first = z1 * sg
        dsilu_ref[k, :, lanes] = (sg + first * (1.0 - sg)).astype(BF16)
        first = first.astype(BF16)
        first_ref[k, :, lanes] = first
        both = dot_nn(wevt_ref[...], first)
        ew = (both[0:chans] * in_lanes(plane(6, k, s, n))).astype(BF16)
        ew_ref[k, :, lanes] = ew
        val_ref[k, :, lanes] = both[chans:].astype(BF16)

        def body(s, j, start, fresh):
            a = select(k, s, start)
            if fresh:
                a_ref[k * subs + s] = a
            add_window(env_ref, start, dot_nt(a, ew[:, part(j)]))

        each_window(k, s, n, slow, body)

    def phase_b(k, s, n, slow):
        lanes = lanes_of(s, n)

        def totals(s, j, start, fresh):
            value = dot_tn(load_window(env_ref, start), kept(k, s, start, fresh))
            if fresh:
                big_ref[:, part(j)] = value
            else:
                big_ref[:, part(j)] += value

        each_window(k, s, n, slow, totals)
        total = 0.2 * big_ref[:, 0 : n * SUB]
        value = val_ref[k, :, lanes].astype(F32)
        scalar = (value * total).astype(BF16)
        z2 = dot_nn(w2t_ref[...], jnp.concatenate([first_ref[k, :, lanes], scalar], axis=0))
        sg = 0.5 + 0.5 * jnp.tanh(0.5 * z2)
        second = z2 * sg
        wcol = jnp.concatenate([wcol_ref[...]] * (n * sub_rows), axis=1)
        ee = jnp.sum(second.astype(BF16).astype(F32) * wcol, axis=0, keepdims=True)
        envv = in_lanes(plane(6, k, s, n))
        live = ee * in_lanes(plane(7, k, s, n))
        first_row = s * sub_rows
        for j in range(n * sub_rows):
            live_ref[k, pl.ds(first_row + j, 1), :] = live[:, j * LANES : (j + 1) * LANES]
        energy = ee * envv
        dz2 = ((wcol * envv) * (sg + second * (1.0 - sg))).astype(BF16)
        dj = dot_nn(w2_ref[...], dz2)
        dfa_ref[k, :, lanes] = dj[0:chans].astype(BF16)
        dscalar = dj[chans:]
        dt = (0.2 * value * dscalar).astype(BF16)
        dt_ref[k, :, lanes] = dt
        dv_ref[k, :, lanes] = (total * dscalar).astype(BF16)

        def body(s, j, start, fresh):
            add_window(denv_ref, start, dot_nt(kept(k, s, start, fresh), dt[:, part(j)]))
            mine = jnp.where(window_hot(k, s, start), energy[:, part(j)], 0.0)
            half = mine[:, 0:LANES]
            for i in range(1, sub_rows):
                half = half + mine[:, i * LANES : (i + 1) * LANES]
            ae_ref[pl.ds(start, WIN), :] += half

        each_window(k, s, n, slow, body)

    def phase_c(k, s, n, slow):
        lanes = lanes_of(s, n)
        height = n * sub_rows

        def env_terms(s, j, start, fresh):
            a = kept(k, s, start, fresh)
            e_win = load_window(env_ref, start)
            d_win = load_window(denv_ref, start)
            dew = dot_tn(d_win, a)
            here = lanes_of(s, 1)
            pair = jnp.concatenate([dt_ref[k, :, here], ew_ref[k, :, here]], axis=0)
            prods = dot_nn(jnp.concatenate([e_win, d_win], axis=1), pair)
            hot = a[0:WIN].astype(F32)
            if fresh:
                big_ref[:, part(j)] = dew
            else:
                big_ref[:, part(j)] += dew
            for m in range(1, 9):
                row = jnp.sum(prods[m * WIN : (m + 1) * WIN] * hot, axis=0, keepdims=True)
                for i in range(sub_rows):
                    at = j * sub_rows + i
                    piece = row[:, i * LANES : (i + 1) * LANES]
                    if fresh:
                        dy_ref[m, at : at + 1, :] = piece
                    else:
                        dy_ref[m, at : at + 1, :] += piece

        each_window(k, s, n, slow, env_terms)
        dew = big_ref[:, 0 : n * SUB]
        dpre = (dew * in_lanes(plane(6, k, s, n))).astype(BF16)
        denv_row = jnp.sum(dew * ew_ref[k, :, lanes].astype(F32), axis=0, keepdims=True)
        for j in range(height):
            dy_ref[0, j : j + 1, :] = denv_row[:, j * LANES : (j + 1) * LANES]
        dfirst = dfa_ref[k, :, lanes].astype(F32) + dot_nn(
            wev_ref[...], jnp.concatenate([dpre, dv_ref[k, :, lanes]], axis=0)
        )
        dz1 = (dfirst * dsilu_ref[k, :, lanes].astype(F32)).astype(BF16)
        dboth = dot_nn(w1_ref[...], dz1)
        dmixed = dboth[0:chans].astype(BF16)
        dbasis = dboth[chans:]
        for j in range(height):
            db_ref[j * n_basis : (j + 1) * n_basis, :] = dbasis[
                0:n_basis, j * LANES : (j + 1) * LANES
            ]
        ux, uy, uz, dist, inv, q = [plane(i, k, s, n) for i in range(6)]
        envelope = q * q
        g = envelope * inv
        denvelope = -(q * envelope) * dist
        dg = (denvelope - g) * inv
        sins, coss = waves(0.5 * dist, n_basis)
        live = tile_of(lambda rows: live_ref[k, rows, :], s, n)
        y = [dy_ref[m, 0:height, :] for m in range(9)]
        ddist = (live + y[0] / envelope) * denvelope
        for i in range(n_basis):
            db = db_ref[pl.ds(i, height, stride=n_basis), :]
            ddist = ddist + db * (coss[i] * ((i + 1) * math.pi / 2.0) * g + sins[i] * dg)
        gx = y[1] + ROOT3 * (uy * y[4] + uz * y[6]) + (2.0 * 0.866) * ux * y[7]
        gy = y[2] + ROOT3 * (ux * y[4] + uz * y[5]) - (2.0 * 0.866) * uy * y[7]
        gz = y[3] + ROOT3 * (uy * y[5] + ux * y[6]) + 3.0 * uz * y[8]
        along = ddist - inv * (gx * ux + gy * uy + gz * uz)
        for i, (gu, u) in enumerate(((gx, ux), (gy, uy), (gz, uz))):
            hi, lo = split(inv * gu + along * u)
            dr_ref[pl.ds(i, height, stride=16), :] = hi
            dr_ref[pl.ds(3 + i, height, stride=16), :] = lo
        dr = jnp.concatenate([dr_ref[j * 16 : (j + 1) * 16, :] for j in range(height)], axis=1)
        moved = jnp.concatenate([dmixed, dr.astype(BF16)], axis=0)
        sums = dot_nt(jnp.concatenate(table_hots(k, s, n), axis=0), moved)
        acc_ref[:, 0:chans] += sums[:, 0:chans]
        acc_ref[:, chans : chans + 16] += sums[:, chans:]

        def body(s, j, start, fresh):
            hot = a_ref[k * subs + s, 0:WIN, :] if fresh else window_hot(k, s, start).astype(BF16)
            mine = dot_nt(hot, moved[:, part(j)])
            cacc_ref[pl.ds(start, WIN), 0:chans] += mine[:, 0:chans]
            cacc_ref[pl.ds(start, WIN), chans : chans + 16] += mine[:, chans:]

        each_window(k, s, n, slow, body)

    for phase in (phase_a, phase_b, phase_c):

        @pl.when(most == 0)
        def _(phase=phase):
            def chunk(k, carry):
                phase(k, 0, subs, False)
                return carry

            lax.fori_loop(0, n_chunks, chunk, 0)

        @pl.when(most != 0)
        def _(phase=phase):
            def sub(i, carry):
                phase(lax.div(i, subs), lax.rem(i, subs), 1, True)
                return carry

            lax.fori_loop(0, n_chunks * subs, sub, 0)

    own_ref[0:own, :] = cacc_ref[0:own, :]
    own_ref[own:, :] = acc_ref[0:own, :]
    row = lax.broadcasted_iota(jnp.int32, (LANES, LANES), 0)
    group = lax.broadcasted_iota(jnp.int32, (LANES, LANES), 1) // GROUP
    both = ((group < 3) & ((row == group) | (row == group + 3))).astype(F32)
    places = dot_nn(acc_ref[own:, LANES:], both, HIGH)
    found = {}
    at = own
    for off in OFFSETS:
        found[off] = at
        at += plan.live(off)
    for blocks, ref in zip(
        plan.groups[0] + [plan.held_rest], tuple(back_refs) + (rest_ref,)
    ):
        for off, row in plan.spans(blocks):
            live = plan.live(off)
            at = found[off]
            ref[row : row + live, :] = acc_ref[at : at + live, 0:chans]
            block = places[at - own : at - own + live, :]
            ref[row + live : row + live + 1, :] = jnp.sum(diagonal(block), axis=0, keepdims=True)


def returned_sums(plan, came, axes, messages, first, sel_ref, both_ref):
    chans = both_ref.shape[1] - LANES
    both_ref[...] = jnp.zeros_like(both_ref)
    at = 0
    for blocks in messages:
        for off, row in plan.spans(blocks):
            live = plan.live(off)
            src, begin = plan.find(came, axes, None, [], off)
            here = slice(at + row, at + row + live)
            both_ref[here, 0:chans] = src[begin : begin + live, :]
            both_ref[here, chans:] = spread(src[begin + live : begin + live + 1, :], live)
        at += plan.total(blocks)
    hot = sel_ref[first : first + at, :].astype(BF16)
    return dot_exact(hot, both_ref[...], ((0,), (0,)))


def own_kernel(plan, ae_ref, own_ref, wide_ref, sel_ref, *refs):
    came, refs = plan.cut(refs, 0, 1)
    energy_ref, fg_ref, force_ref, both_ref = refs
    chans = fg_ref.shape[1]
    own = force_ref.shape[1]
    first = sum(plan.total(blocks) for blocks in plan.groups[2])
    sums = returned_sums(plan, came, (1, 0), [plan.own_rest], first, sel_ref, both_ref)
    energy_ref[...] = jnp.sum(ae_ref[0:own, :].T, axis=0, keepdims=True)
    fg_ref[...] = dot_nt(own_ref[0:own, 0:chans], wide_ref[0:chans, :], HIGH) + dot_nt(
        own_ref[own:, 0:chans] + sums[:, 0:chans], wide_ref[chans : 2 * chans, :], HIGH
    )
    force = (own_ref[own:, LANES:] - own_ref[0:own, LANES:]).T
    total = dot_nt(group_rows(8), sums[:, chans:], HIGH)
    force_ref[...] = force[0:3, :] + force[3:6, :] + total[0:3, :]


def last_kernel(plan, sel_ref, fg_ref, force_ref, wide_ref, *refs):
    came, refs = plan.cut(refs, 2)
    out_force_ref, out_fg_ref, both_ref = refs
    chans = fg_ref.shape[1]
    sums = returned_sums(plan, came, (2,), plan.groups[2], 0, sel_ref, both_ref)
    s_hi, s_lo = split(sums[:, 0:chans])
    w_hi, w_lo = split(wide_ref[chans : 2 * chans, :])
    out_fg_ref[...] = fg_ref[...] + dot_nt(
        jnp.concatenate([s_hi, s_lo, s_hi], axis=1).astype(BF16),
        jnp.concatenate([w_hi, w_hi, w_lo], axis=1).astype(BF16),
    )
    total = dot_nt(group_rows(8), sums[:, chans:], HIGH)
    out_force_ref[...] = -(force_ref[...] + total[0:3, :])


def stack(*arrays):
    dtype = arrays[0].dtype
    tile = 32 // dtype.itemsize
    starts = [0]
    for x in arrays:
        starts.append(starts[-1] + -(-x.shape[0] // tile) * tile)
    total = None
    for x, at in zip(arrays, starts):
        below = starts[-1] - at - x.shape[0]
        part = jnp.pad(x.astype(dtype), ((at, below), (0, LANES - x.shape[1])))
        total = part if total is None else total + part
    return total


def local(
    positions,
    atom_features,
    send_face,
    send_edge,
    send_corner,
    centre,
    other,
    edge_count,
    w_proj_a,
    w_proj_b,
    w_radial,
    w_first,
    w_env,
    w_value,
    w_second,
    w_out,
):
    own, chans = atom_features.shape
    edges = centre.shape[0]
    n_basis = w_radial.shape[0]
    plan = Plan(
        [send_face.shape[2], send_edge.shape[2], send_corner.shape[2]],
        [lax.axis_size(axis) for axis in AXES],
    )
    n_ghost = sum(len(c) * w for c, w in zip(CLASSES, plan.widths))
    n_sel = 2 * own + n_ghost
    n_send = sum(plan.total(blocks) for blocks in plan.groups[2]) + plan.total(plan.own_rest)
    n_table = n_sel + 4 * n_basis
    edges_up = -(-edges // CHUNK) * CHUNK
    n_rows = edges_up // LANES
    n_chunks = edges_up // CHUNK

    with jax.named_scope("prep"):
        rows = stack(
            atom_features, send_face[0], jnp.transpose(send_edge[0]), edge_count.reshape(1, 1)
        )
        *sends, own_rows, sel = pl.pallas_call(
            lambda *refs: prep_kernel(plan, *refs),
            out_shape=plan.shapes(2, chans)
            + [shape(plan.total(plan.own_rest), chans), shape(n_send, own)],
            in_specs=[VMEM] * 3,
            out_specs=[VMEM] * (len(plan.groups[2]) + 2),
            scratch_shapes=[pltpu.VMEM((LANES, LANES), F32)],
            compiler_params=PARAMS,
        )(rows, positions, jnp.transpose(send_corner, (0, 2, 1)))

    came = {}
    with jax.named_scope("halo_z"):
        came[2] = plan.send(2, sends)

    with jax.named_scope("group_edges"):
        pad = [(0, edges_up - edges)]
        regs = max(sorted_size(edges_up) // (8 * LANES), 1)
        key, bounds = pl.pallas_call(
            lambda *refs: sort_kernel(own, *refs),
            out_shape=[
                shape(n_chunks, CHUNK // LANES, LANES, dtype=jnp.int32),
                shape(2, LANES, dtype=jnp.int32),
            ],
            in_specs=[VMEM] * 3,
            out_specs=[VMEM] * 2,
            scratch_shapes=[pltpu.VMEM((16 * regs, LANES), F32)],
            compiler_params=PARAMS,
        )(
            rows,
            jnp.pad(centre, pad).reshape(n_rows, LANES),
            jnp.pad(other, pad).reshape(n_rows, LANES),
        )

    with jax.named_scope("halo_y"):
        came[2], key, bounds, w_first, w_env, w_value, w_second, w_out = lax.optimization_barrier(
            (came[2], key, bounds, w_first, w_env, w_value, w_second, w_out)
        )
        came[1] = plan.send(1, glue(plan, 1, (2,), plan.own_rest, own_rows, came))

    with jax.named_scope("weights"):
        wide = stack(w_proj_a, w_proj_b, w_radial)
        narrow = stack(w_first, w_env, w_value, w_second, w_out[None, :])
        half, *weights = pl.pallas_call(
            weight_kernel,
            out_shape=[
                shape(2 * own + 4 * n_basis, chans),
                shape(chans, chans, dtype=BF16),
                shape(2 * chans, chans, dtype=BF16),
                shape(chans, 2 * chans, dtype=BF16),
                shape(chans + 2 * n_basis, chans, dtype=BF16),
                shape(chans, 2 * chans, dtype=BF16),
                shape(2 * chans, chans, dtype=BF16),
                shape(chans, LANES),
            ],
            in_specs=[VMEM] * 3,
            out_specs=[VMEM] * 8,
            compiler_params=PARAMS,
        )(rows, wide, narrow)

    with jax.named_scope("halo_x"):
        came[1], half, weights = lax.optimization_barrier((came[1], half, weights))
        came[0] = plan.send(0, glue(plan, 0, (1, 2), plan.own_rest, own_rows, came))

    planes = (n_chunks, chans, CHUNK)
    scratch = [
        pltpu.VMEM((n_table, chans), F32),
        pltpu.VMEM((n_ghost, chans), F32),
        pltpu.VMEM((-(-n_ghost // LANES) * LANES, LANES), F32),
        pltpu.VMEM((chans, n_table), BF16),
        pltpu.VMEM((n_rows * 8, LANES), F32),
        pltpu.VMEM((n_rows * n_basis, LANES), F32),
        pltpu.VMEM((8, n_chunks, CHUNK // LANES, LANES), F32),
        pltpu.VMEM(planes, BF16),
        pltpu.VMEM(planes, BF16),
        pltpu.VMEM(planes, BF16),
        pltpu.VMEM(planes, BF16),
        pltpu.VMEM((edges_up // SUB, 9 * WIN, SUB), BF16),
        pltpu.VMEM((9, own + WIN, chans), F32),
        pltpu.VMEM((9, own + WIN, chans), F32),
        pltpu.VMEM((chans, CHUNK), F32),
        pltpu.VMEM(planes, BF16),
        pltpu.VMEM(planes, BF16),
        pltpu.VMEM(planes, BF16),
        pltpu.VMEM((n_chunks, CHUNK // LANES, LANES), F32),
        pltpu.VMEM((9, CHUNK // LANES, LANES), F32),
        pltpu.VMEM((CHUNK // LANES * n_basis, LANES), F32),
        pltpu.VMEM((CHUNK // LANES * 16, LANES), F32),
        pltpu.VMEM((n_sel - own, 2 * LANES), F32),
        pltpu.VMEM((own + WIN, 2 * LANES), F32),
    ]
    with jax.named_scope("layer"):
        given = [bounds, key, positions, wide]
        given += [*came[0], *came[1], *came[2], half, *weights]
        atom_sums, own_sums, *back, held = pl.pallas_call(
            lambda *refs: main_kernel(plan, *refs),
            out_shape=[shape(own + WIN, LANES), shape(2 * own, 2 * LANES)]
            + plan.shapes(0, chans)
            + [shape(plan.total(plan.held_rest), chans)],
            in_specs=[SMEM] + [VMEM] * (len(given) - 1),
            out_specs=[VMEM] * (3 + len(plan.groups[0])),
            scratch_shapes=scratch,
            compiler_params=PARAMS,
        )(*given)

    with jax.named_scope("halo_back"):
        home = {0: plan.send(0, back, back=True)}
        home[1] = plan.send(1, glue(plan, 1, (0,), plan.held_rest, held, home), back=True)
        home[2] = plan.send(2, glue(plan, 2, (1, 0), plan.held_rest, held, home), back=True)

    with jax.named_scope("own_part"):
        given = [atom_sums, own_sums, wide, sel, *home[0], *home[1]]
        energy, fg, force = pl.pallas_call(
            lambda *refs: own_kernel(plan, *refs),
            out_shape=[shape(1, own), shape(own, chans), shape(3, own)],
            in_specs=[VMEM] * len(given),
            out_specs=[VMEM] * 3,
            scratch_shapes=[pltpu.VMEM((plan.total(plan.own_rest), chans + LANES), F32)],
            compiler_params=PARAMS,
        )(*given)

    with jax.named_scope("owner_sums"):
        given = [sel, fg, force, wide, *home[2]]
        n_z = n_send - plan.total(plan.own_rest)
        forces, feature_grad = pl.pallas_call(
            lambda *refs: last_kernel(plan, *refs),
            out_shape=[shape(3, own), shape(own, chans)],
            in_specs=[VMEM] * len(given),
            out_specs=[VMEM] * 2,
            scratch_shapes=[pltpu.VMEM((n_z, chans + LANES), F32)],
            compiler_params=PARAMS,
        )(*given)
    return forces, energy.reshape(own), feature_grad


def solution(mesh):
    shard = P(AXES)
    return jax.shard_map(
        local,
        mesh=mesh,
        in_specs=(
            P(None, AXES),
            P(AXES, None),
            P(AXES, None, None),
            P(AXES, None, None),
            P(AXES, None, None),
            shard,
            shard,
            shard,
        )
        + (P(),) * 8,
        out_specs=(P(None, AXES), shard, P(AXES, None)),
        check_vma=False,
    )
```

```python
import math

import jax
import jax.numpy as jnp
from jax import lax
from jax.experimental import pallas as pl
from jax.experimental.pallas import tpu as pltpu
from jax.sharding import PartitionSpec as P

F32 = jnp.float32
BF16 = jnp.bfloat16
HIGH = lax.Precision.HIGHEST
AXES = ("gx", "gy", "gz")
CHUNK = 2048
SUB = 256
WIN = 16
OTHER_BITS = 9
OTHER_MASK = (1 << OTHER_BITS) - 1
LANES = 128
ROOT3 = 1.732


VMEM = pl.BlockSpec(memory_space=pltpu.VMEM)
SMEM = pl.BlockSpec(memory_space=pltpu.SMEM)
PARAMS = pltpu.CompilerParams(vmem_limit_bytes=52 * 2**20)


def shape(*dims, dtype=F32):
    return jax.ShapeDtypeStruct(dims, dtype)


def dot_nn(a, b, precision=None):
    return lax.dot_general(
        a, b, (((1,), (0,)), ((), ())), preferred_element_type=F32, precision=precision
    )


def dot_nt(a, b, precision=None):
    return lax.dot_general(
        a, b, (((1,), (1,)), ((), ())), preferred_element_type=F32, precision=precision
    )


def dot_tn(a, b, precision=None):
    return lax.dot_general(
        a, b, (((0,), (0,)), ((), ())), preferred_element_type=F32, precision=precision
    )


def offset_classes():
    classes = [[], [], []]
    for a in (-1, 0, 1):
        for b in (-1, 0, 1):
            for c in (-1, 0, 1):
                if (a, b, c) != (0, 0, 0):
                    classes[abs(a) + abs(b) + abs(c) - 1].append((a, b, c))
    return classes


CLASSES = offset_classes()


OFFSETS = [off for group in CLASSES for off in group]


def kind(off):
    return abs(off[0]) + abs(off[1]) + abs(off[2]) - 1


class Plan:
    def __init__(self, widths, sizes):
        self.widths = widths
        self.sizes = sizes
        self.groups = [self.group(a) for a in range(3)]
        self.even = [lax.axis_index(axis) % 2 == 0 for axis in AXES]
        self.own_rest = [off for off in OFFSETS if off[2] == 0]
        self.held_rest = [off for off in OFFSETS if off[0] == 0]

    def group(self, a):
        groups = {}
        for off in OFFSETS:
            if off[a] != 0:
                groups.setdefault(off[a] % self.sizes[a], []).append(off)
        return list(groups.values())

    def live(self, off):
        return self.widths[kind(off)]

    def rows(self, off):
        return self.live(off) + 1

    def total(self, blocks):
        return sum(self.rows(off) for off in blocks)

    def spans(self, blocks):
        at = 0
        for off in blocks:
            yield off, at
            at += self.rows(off)

    def place(self, a, off):
        for g, blocks in enumerate(self.groups[a]):
            if off in blocks:
                return g, dict(self.spans(blocks))[off]
        raise KeyError(off)

    def find(self, came, axes, rest_ref, rest, off):
        for a in axes:
            if off[a] != 0:
                g, begin = self.place(a, off)
                return came[a][g], begin
        return rest_ref, dict(self.spans(rest))[off]

    def cut(self, refs, *axes):
        came = {}
        for a in axes:
            n = len(self.groups[a])
            came[a], refs = refs[:n], refs[n:]
        return came, refs

    def shapes(self, a, chans):
        return [shape(self.total(blocks), chans) for blocks in self.groups[a]]

    def send(self, a, messages, back=False):
        n = self.sizes[a]
        steps = [-blocks[0][a] if back else blocks[0][a] for blocks in self.groups[a]]
        if n % 2 or n == 2:
            return [
                lax.ppermute(message, AXES[a], [(i, (i + step) % n) for i in range(n)])
                for step, message in zip(steps, messages)
            ]
        up, down = steps.index(1), steps.index(-1)
        even = self.even[a]
        ahead = [(i, i + 1 - 2 * (i % 2)) for i in range(n)]
        behind = [(i, (i - 1 + 2 * (i % 2)) % n) for i in range(n)]
        first = lax.ppermute(jnp.where(even, messages[up], messages[down]), AXES[a], ahead)
        second = lax.ppermute(jnp.where(even, messages[down], messages[up]), AXES[a], behind)
        got = [None, None]
        got[up] = jnp.where(even, second, first)
        got[down] = jnp.where(even, first, second)
        return got


GROUP = 32


def group_rows(count):
    row = lax.broadcasted_iota(jnp.int32, (count, LANES), 0)
    group = lax.broadcasted_iota(jnp.int32, (count, LANES), 1) // GROUP
    return (row == group).astype(F32) * (group < 3).astype(F32)


def diagonal(x):
    row = lax.broadcasted_iota(jnp.int32, x.shape, 0)
    lane = lax.broadcasted_iota(jnp.int32, x.shape, 1)
    return jnp.where((lane & (GROUP - 1)) == row, x, 0.0)


def spread(row, live):
    return diagonal(jnp.broadcast_to(row, (live, LANES)))


def split(x):
    high = x.astype(BF16).astype(F32)
    return high, x - high


def dot_exact(hot, x, dims):
    high, low = split(x)
    both = jnp.concatenate([high, low], axis=1).astype(BF16)
    out = lax.dot_general(hot, both, (dims, ((), ())), preferred_element_type=F32)
    return out[:, 0 : x.shape[1]] + out[:, x.shape[1] :]


def prep_kernel(plan, rows_ref, pos_ref, face_ref, *outs):
    n_z = len(plan.groups[2])
    sends, rest_ref, sel_ref, turn_ref = outs[:n_z], outs[n_z], outs[n_z + 1], outs[n_z + 2]
    own = sel_ref.shape[1]
    lane = lax.broadcasted_iota(jnp.int32, (1, own), 1).astype(F32)
    turn_ref[...] = jnp.zeros_like(turn_ref)
    for key in range(face_ref.shape[0]):
        turn_ref[key : key + 1, 0 : face_ref.shape[2]] = face_ref[key].astype(F32)
    columns = [turn_ref[...].T]
    at = own
    for width in plan.widths[1:]:
        columns.append(rows_ref[at : at + width, :])
        at += -(-width // 8) * 8
    sel_ref[...] = jnp.zeros_like(sel_ref)
    messages = plan.groups[2] + [plan.own_rest]
    at = 0
    for blocks in messages:
        for off, begin in plan.spans(blocks):
            key = CLASSES[kind(off)].index(off)
            live = plan.live(off)
            column = columns[kind(off)][0:live, key : key + 1]
            sel_ref[at + begin : at + begin + live, :] = (column == lane).astype(F32)
        at += plan.total(blocks)
    pos = dot_tn(pos_ref[...], group_rows(3), HIGH)
    sel = sel_ref[...]
    rows = dot_nn(sel, rows_ref[0:own, :], HIGH)
    places = dot_nn(sel, pos, HIGH)
    at = 0
    for blocks, send in zip(messages, tuple(sends) + (rest_ref,)):
        count = plan.total(blocks)
        send[...] = rows[at : at + count, :]
        for off, begin in plan.spans(blocks):
            live = plan.live(off)
            block = places[at + begin : at + begin + live, :]
            send[begin + live : begin + live + 1, :] = jnp.sum(
                diagonal(block), axis=0, keepdims=True
            )
        at += count


def glue_kernel(plan, a, axes, rest, *refs):
    rest_ref = refs[0]
    came, outs = plan.cut(refs[1:], *axes)
    for blocks, out in zip(plan.groups[a], outs):
        for off, row in plan.spans(blocks):
            src, begin = plan.find(came, axes, rest_ref, rest, off)
            out[row : row + plan.rows(off), :] = src[begin : begin + plan.rows(off), :]


def glue(plan, a, axes, rest, rest_rows, came):
    given = [rest_rows] + [message for axis in axes for message in came[axis]]
    outs = plan.shapes(a, rest_rows.shape[1])
    return pl.pallas_call(
        lambda *refs: glue_kernel(plan, a, axes, rest, *refs),
        out_shape=outs,
        in_specs=[VMEM] * len(given),
        out_specs=[VMEM] * len(outs),
        compiler_params=PARAMS,
    )(*given)


def sort_kernel(own, count_ref, centre_ref, other_ref, key_ref, bound_ref, turn_ref):
    dead = (own - 1) * (OTHER_MASK + 1) + OTHER_MASK
    rows = centre_ref.shape[0]
    regs = turn_ref.shape[0] // 16
    group = regs * 8
    row = lax.broadcasted_iota(jnp.int32, (rows, LANES), 0)
    lane = lax.broadcasted_iota(jnp.int32, (rows, LANES), 1)
    count = count_ref[count_ref.shape[0] - 8 : count_ref.shape[0] - 7, 0:1].astype(jnp.int32)
    live = row * LANES + lane < count
    centre = centre_ref[...]
    key = jnp.where(live, (centre << OTHER_BITS) + other_ref[...], dead).astype(F32)
    x = [key[8 * v : 8 * v + 8, :] for v in range(rows // 8)]
    x += [jnp.full((8, LANES), float(dead), F32)] * (regs - len(x))
    n_windows = own // WIN
    free = regs - rows // 8
    if n_windows * SUB <= free * 8 * LANES:
        window = jnp.where(live, centre // WIN, -1)
        need = []
        used = jnp.zeros((1, 1), F32)
        for w in range(n_windows):
            hits = jnp.sum((window == w).astype(F32), axis=0, keepdims=True)
            hits = jnp.sum(hits, axis=1, keepdims=True)
            whole = jnp.floor((hits + (SUB - 1)) * (1.0 / SUB)) * SUB
            used = used + whole
            need.append(whole - hits)
        fits = used <= float(rows * LANES)
        slot = lax.broadcasted_iota(jnp.int32, (8, LANES), 0) * LANES
        slot = slot + lax.broadcasted_iota(jnp.int32, (8, LANES), 1)
        per_reg = 8 * LANES // SUB
        for w in range(n_windows):
            v = rows // 8 + w // per_reg
            at = slot - (w % per_reg) * SUB
            take = (at >= 0) & (at.astype(F32) < need[w]) & fits
            mark = float((w * WIN + WIN - 1) * (OTHER_MASK + 1) + OTHER_MASK)
            x[v] = jnp.where(take, mark, x[v])
    s = lax.broadcasted_iota(jnp.int32, (8, LANES), 0)
    ln = lax.broadcasted_iota(jnp.int32, (8, LANES), 1)
    base = ln * group + s * regs

    def sign(k, v):
        return jnp.where(((base + v) & k) == 0, 1.0, -1.0).astype(F32)

    last = [jnp.ones((8, LANES), F32)] * regs
    total = group * LANES
    k = 2
    while k <= total:
        signs = [sign(k, v) for v in range(regs)] if k < total else [1.0] * regs
        x = [x[v] * (last[v] * signs[v]) for v in range(regs)]
        last = signs
        j = k // 2
        while j >= 1:
            if j < regs:
                for v in range(regs):
                    if v & j == 0:
                        a, b = x[v], x[v | j]
                        x[v], x[v | j] = jnp.minimum(a, b), jnp.maximum(a, b)
            else:
                axis, step, size, ids = (
                    (0, j // regs, 8, s) if j < group else (1, j // group, LANES, ln)
                )
                low = (ids & step) == 0
                for v in range(regs):
                    up = pltpu.roll(x[v], size - step, axis)
                    if 2 * step == size:
                        mate = up
                    else:
                        mate = jnp.where(low, up, pltpu.roll(x[v], step, axis))
                    x[v] = jnp.where(low, jnp.minimum(x[v], mate), jnp.maximum(x[v], mate))
            j //= 2
        k *= 2
    least = x[0]
    most = jnp.where(x[0] == float(dead), -1.0, x[0])
    for v in range(1, regs):
        least = jnp.minimum(least, x[v])
        most = jnp.maximum(most, jnp.where(x[v] == float(dead), -1.0, x[v]))
    bound_ref[0:1, :] = jnp.min(least, axis=0, keepdims=True).astype(jnp.int32) >> OTHER_BITS
    bound_ref[1:2, :] = jnp.max(most, axis=0, keepdims=True).astype(jnp.int32) >> OTHER_BITS
    turned = jnp.concatenate(x + [jnp.zeros((LANES - group, LANES), F32)], axis=0).T
    turn_ref[...] = turned
    ratio = LANES // group
    parts = [
        turn_ref[pl.ds(i, rows, stride=ratio), 0:group] for i in range(ratio)
    ]
    done = jnp.concatenate(parts, axis=1).astype(jnp.int32)
    per = key_ref.shape[1]
    for c in range(key_ref.shape[0]):
        key_ref[c] = done[c * per : (c + 1) * per, :]


def weight_kernel(
    rows_ref,
    wide_ref,
    half_ref,
    tab_ref,
    w1t_ref,
    wevt_ref,
    w2t_ref,
    w1_ref,
    wev_ref,
    w2_ref,
    wcol_ref,
):
    chans = wide_ref.shape[1]
    rad_rows = wide_ref.shape[0] - 2 * chans
    own = (tab_ref.shape[0] - 4 * rad_rows) // 2
    wa, wb, rad = wide_ref[0:chans, :], wide_ref[chans : 2 * chans, :], wide_ref[2 * chans :, :]
    w1, wenv, wval = [half_ref[i * chans : (i + 1) * chans, :] for i in range(3)]
    w2 = half_ref[3 * chans : 5 * chans, :]

    def flip(w):
        return w.astype(F32).T.astype(BF16)

    down = dot_nn(rad, w1.astype(F32), HIGH)
    w1_ref[0:chans, :] = w1
    w1_ref[chans:, :] = jnp.concatenate([down, jnp.zeros_like(down)], axis=0).astype(BF16)
    w2_ref[...] = w2
    w1t_ref[...] = flip(w1)
    wevt_ref[0:chans, :] = flip(wenv)
    wevt_ref[chans:, :] = flip(wval)
    w2t_ref[:, 0:chans] = flip(w2[0:chans, :])
    w2t_ref[:, chans:] = flip(w2[chans:, :])
    wev_ref[:, 0:chans] = wenv
    wev_ref[:, chans:] = wval
    wout = half_ref[5 * chans : 5 * chans + 1, :].astype(F32)
    wcol_ref[...] = jnp.broadcast_to(wout, (LANES, chans)).T
    feat = rows_ref[0:own, :]
    tab_ref[0:own, :] = dot_nn(feat, wa, HIGH)
    tab_ref[own : 2 * own, :] = dot_nn(feat, wb, HIGH)
    rad_hi, rad_lo = split(rad)
    tab_ref[2 * own :, :] = jnp.concatenate([rad_hi, rad_hi, rad_lo, jnp.zeros_like(rad)], axis=0)


def harmonics(ux, uy, uz):
    return [
        ux,
        uy,
        uz,
        ROOT3 * ux * uy,
        ROOT3 * uy * uz,
        ROOT3 * ux * uz,
        0.866 * (ux * ux - uy * uy),
        0.5 * (3.0 * uz * uz - 1.0),
    ]


def trig(half):
    turns = jnp.round(half)
    x = math.pi * (half - turns)
    odd = turns - 2.0 * jnp.floor(0.5 * turns)
    sign = 1.0 - 2.0 * odd
    x2 = x * x
    s = jnp.full_like(x, -1.0 / 39916800)
    for coef in (1.0 / 362880, -1.0 / 5040, 1.0 / 120, -1.0 / 6, 1.0):
        s = s * x2 + coef
    c = jnp.full_like(x, 1.0 / 479001600)
    for coef in (-1.0 / 3628800, 1.0 / 40320, -1.0 / 720, 1.0 / 24, -0.5, 1.0):
        c = c * x2 + coef
    return sign * x * s, sign * c


def waves(half, count):
    s1, c1 = trig(half)
    sins, coss = [s1], [c1]
    s0, c0 = jnp.zeros_like(s1), jnp.ones_like(c1)
    for _ in range(count - 1):
        sn = 2.0 * c1 * sins[-1] - s0
        cn = 2.0 * c1 * coss[-1] - c0
        s0, c0 = sins[-1], coss[-1]
        sins.append(sn)
        coss.append(cn)
    return sins, coss


def look_up(table_row, index):
    low = index & (LANES - 1)
    high = index >> 7
    result = jnp.zeros(index.shape, F32)
    for block in range(table_row.shape[1] // LANES):
        part = jnp.broadcast_to(table_row[:, block * LANES : (block + 1) * LANES], index.shape)
        got = jnp.take_along_axis(part, low, axis=1)
        result = jnp.where(high == block, got, result)
    return result


def in_lanes(tile):
    return jnp.concatenate([tile[r : r + 1, :] for r in range(tile.shape[0])], axis=1)


def one_hot(row, base, count):
    near = jnp.clip(row - base, -1, LANES).astype(BF16)
    iota = lax.broadcasted_iota(jnp.int32, (count, row.shape[1]), 0).astype(BF16)
    return jnp.where(iota == near, jnp.ones((), BF16), jnp.zeros((), BF16))


def sorted_size(edges):
    return 1 << (edges - 1).bit_length()


def main_kernel(plan, *refs):
    bound_ref, key_ref, pos_ref, wide_ref = refs[:4]
    came, refs = plan.cut(refs[4:], 0, 1, 2)
    half_ref, w1t_ref, wevt_ref, w2t_ref, w1_ref, wev_ref, w2_ref, wcol_ref = refs[:8]
    ae_ref, own_ref = refs[8:10]
    n_x = len(plan.groups[0])
    back_refs, rest_ref = refs[10 : 10 + n_x], refs[10 + n_x]
    (
        tab_ref,
        ghost_ref,
        place_ref,
        table_ref,
        y_ref,
        basis_ref,
        geo_ref,
        first_ref,
        dsilu_ref,
        ew_ref,
        val_ref,
        a_ref,
        env_ref,
        denv_ref,
        big_ref,
        dt_ref,
        dv_ref,
        dfa_ref,
        live_ref,
        dy_ref,
        db_ref,
        dr_ref,
        acc_ref,
        cacc_ref,
    ) = refs[11 + n_x :]
    own = pos_ref.shape[1]
    chans = w1_ref.shape[1]
    n_basis = (w1_ref.shape[0] - chans) // 2
    rows_all = key_ref.shape[0] * key_ref.shape[1]
    per = CHUNK // LANES
    subs = CHUNK // SUB
    sub_rows = SUB // LANES
    n_ghost = sum(len(c) * w for c, w in zip(CLASSES, plan.widths))
    n_tab = own + n_ghost
    n_sel = own + n_tab

    place_ref[...] = jnp.zeros_like(place_ref)
    at = 0
    for off in OFFSETS:
        live = plan.live(off)
        message, begin = plan.find(came, (0, 1, 2), None, [], off)
        ghost_ref[at : at + live, :] = message[begin : begin + live, :]
        place_ref[at : at + live, :] = spread(message[begin + live : begin + live + 1, :], live)
        at += live
    ghost_pos = dot_nt(group_rows(8), place_ref[...], HIGH)
    pos_t = jnp.concatenate([pos_ref[...], ghost_pos[0:3, :]], axis=1)
    f_hi, f_lo = split(ghost_ref[...])
    w_hi, w_lo = split(wide_ref[chans : 2 * chans, :])
    tab_ref[0 : 2 * own, :] = half_ref[0 : 2 * own, :]
    tab_ref[2 * own : n_sel, :] = dot_nn(
        jnp.concatenate([f_hi, f_lo, f_hi], axis=1).astype(BF16),
        jnp.concatenate([w_hi, w_hi, w_lo], axis=0).astype(BF16),
    )
    tab_ref[n_sel:, :] = half_ref[2 * own :, :]
    table_ref[...] = tab_ref[...].T.astype(BF16)

    keys = key_ref[...].reshape(rows_all, LANES)
    centre = keys >> OTHER_BITS
    other = keys & OTHER_MASK
    valid = (other != OTHER_MASK).astype(F32)
    r = [
        look_up(pos_t[a : a + 1, :], other) - look_up(pos_t[a : a + 1, 0:LANES], centre)
        for a in range(3)
    ]
    d2 = r[0] * r[0] + r[1] * r[1] + r[2] * r[2] + 0.01
    dist = jnp.sqrt(d2)
    inv = 1.0 / dist
    q = 1.0 / (1.0 + 0.25 * d2)
    envelope = q * q
    unit = [x * inv for x in r]
    for m, comp in enumerate(harmonics(*unit)):
        y_ref[pl.ds(m, rows_all, stride=8), :] = comp
    sins, _ = waves(0.5 * dist, n_basis)
    scale = envelope * inv
    for n in range(n_basis):
        basis_ref[pl.ds(n, rows_all, stride=n_basis), :] = sins[n] * scale
    for i, plane in enumerate((unit[0], unit[1], unit[2], dist, inv, q, envelope * valid, valid)):
        geo_ref[i] = plane.reshape(geo_ref.shape[1:])

    env_ref[...] = jnp.zeros_like(env_ref)
    denv_ref[...] = jnp.zeros_like(denv_ref)
    ae_ref[...] = jnp.zeros_like(ae_ref)
    acc_ref[...] = jnp.zeros_like(acc_ref)
    cacc_ref[...] = jnp.zeros_like(cacc_ref)
    dr_ref[...] = jnp.zeros_like(dr_ref)

    groups = bound_ref.shape[1] * SUB // sorted_size(rows_all * LANES)

    def window(k, s):
        first = (k * subs + s) * groups
        low = bound_ref[0, first]
        high = low
        for g in range(groups):
            high = jnp.maximum(high, bound_ref[1, first + g])
        start = pl.multiple_of((low >> 3) << 3, 8)
        more = lax.div(high - start, jnp.int32(WIN))
        return start, more

    most = jnp.int32(0)
    n_chunks = jnp.int32(0)
    for s in range(rows_all // sub_rows):
        most = jnp.maximum(most, window(s // subs, s % subs)[1])
        for g in range(groups):
            any_live = bound_ref[1, s * groups + g] >= 0
            n_chunks = jnp.where(any_live, s // subs + 1, n_chunks)


    def lanes_of(s, n):
        if isinstance(s, int):
            return slice(s * SUB, (s + n) * SUB)
        return pl.ds(pl.multiple_of(s * SUB, SUB), n * SUB)

    def tile_of(load, s, n):
        if isinstance(s, int):
            return load(slice(s * sub_rows, (s + n) * sub_rows))
        return jnp.concatenate(
            [load(pl.ds(s * sub_rows + j, 1)) for j in range(n * sub_rows)], axis=0
        )

    def plane(i, k, s, n):
        return tile_of(lambda rows: geo_ref[i, k, rows, :], s, n)

    def keys_of(k, s, n):
        return tile_of(lambda rows: key_ref[k, rows, :], s, n)

    def stacked(ref, k, s, n, height):
        first = (k * subs + s) * sub_rows
        tiles = [
            ref[pl.ds(pl.multiple_of((first + j) * height, 8), height), :]
            for j in range(n * sub_rows)
        ]
        return jnp.concatenate(tiles, axis=1)

    def window_hot(k, s, start):
        crow = in_lanes(keys_of(k, s, 1) >> OTHER_BITS) - start
        return lax.broadcasted_iota(jnp.int32, (WIN, SUB), 0) == crow

    def select(k, s, start):
        hot = window_hot(k, s, start)
        ys = stacked(y_ref, k, s, 1, 8)
        parts = [hot.astype(F32)]
        for m in range(8):
            parts.append(jnp.where(hot, ys[m : m + 1, :], 0.0))
        return jnp.concatenate(parts, axis=0).astype(BF16)

    def load_window(ref, start):
        return jnp.concatenate(
            [ref[m, pl.ds(start, WIN), :] for m in range(9)], axis=0
        ).astype(BF16)

    def add_window(ref, start, rows):
        for m in range(9):
            ref[m, pl.ds(start, WIN), :] += rows[m * WIN : (m + 1) * WIN, :]

    def each_window(k, s, n, slow, body):
        for j in range(n):
            start, more = window(k, s + j)
            body(s + j, j, start, True)
            if slow:

                def step(i, carry, s=s, j=j, start=start):
                    body(s + j, j, pl.multiple_of(start + i * WIN, 8), False)
                    return carry

                lax.fori_loop(1, more + 1, step, 0)

    def kept(k, s, start, fresh):
        return a_ref[k * subs + s] if fresh else select(k, s, start)

    def table_hots(k, s, n):
        row = in_lanes(keys_of(k, s, n) & OTHER_MASK)
        return [one_hot(row, at, min(LANES, n_tab - at)) for at in range(0, n_tab, LANES)]

    def part(j):
        return slice(j * SUB, (j + 1) * SUB)

    def phase_a(k, s, n, slow):
        lanes = lanes_of(s, n)
        crow = in_lanes(keys_of(k, s, n) >> OTHER_BITS)
        hots = [one_hot(crow, 0, own)] + table_hots(k, s, n)
        basis = stacked(basis_ref, k, s, n, n_basis)
        b_hi, b_lo = split(basis)
        hots.append(jnp.concatenate([b_hi, b_lo], axis=0).astype(BF16))
        hots.append(jnp.concatenate([b_hi, jnp.zeros_like(b_hi)], axis=0).astype(BF16))
        mixed = dot_nn(table_ref[...], jnp.concatenate(hots, axis=0)).astype(BF16)
        z1 = dot_nn(w1t_ref[...], mixed)
        sg = 0.5 + 0.5 * jnp.tanh(0.5 * z1)
        first = z1 * sg
        dsilu_ref[k, :, lanes] = (sg + first * (1.0 - sg)).astype(BF16)
        first = first.astype(BF16)
        first_ref[k, :, lanes] = first
        both = dot_nn(wevt_ref[...], first)
        ew = (both[0:chans] * in_lanes(plane(6, k, s, n))).astype(BF16)
        ew_ref[k, :, lanes] = ew
        val_ref[k, :, lanes] = both[chans:].astype(BF16)

        def body(s, j, start, fresh):
            a = select(k, s, start)
            if fresh:
                a_ref[k * subs + s] = a
            add_window(env_ref, start, dot_nt(a, ew[:, part(j)]))

        each_window(k, s, n, slow, body)

    def phase_b(k, s, n, slow):
        lanes = lanes_of(s, n)

        def totals(s, j, start, fresh):
            value = dot_tn(load_window(env_ref, start), kept(k, s, start, fresh))
            if fresh:
                big_ref[:, part(j)] = value
            else:
                big_ref[:, part(j)] += value

        each_window(k, s, n, slow, totals)
        total = 0.2 * big_ref[:, 0 : n * SUB]
        value = val_ref[k, :, lanes].astype(F32)
        scalar = (value * total).astype(BF16)
        z2 = dot_nn(w2t_ref[...], jnp.concatenate([first_ref[k, :, lanes], scalar], axis=0))
        sg = 0.5 + 0.5 * jnp.tanh(0.5 * z2)
        second = z2 * sg
        wcol = jnp.concatenate([wcol_ref[...]] * (n * sub_rows), axis=1)
        ee = jnp.sum(second.astype(BF16).astype(F32) * wcol, axis=0, keepdims=True)
        envv = in_lanes(plane(6, k, s, n))
        live = ee * in_lanes(plane(7, k, s, n))
        first_row = s * sub_rows
        for j in range(n * sub_rows):
            live_ref[k, pl.ds(first_row + j, 1), :] = live[:, j * LANES : (j + 1) * LANES]
        energy = ee * envv
        dz2 = ((wcol * envv) * (sg + second * (1.0 - sg))).astype(BF16)
        dj = dot_nn(w2_ref[...], dz2)
        dfa_ref[k, :, lanes] = dj[0:chans].astype(BF16)
        dscalar = dj[chans:]
        dt = (0.2 * value * dscalar).astype(BF16)
        dt_ref[k, :, lanes] = dt
        dv_ref[k, :, lanes] = (total * dscalar).astype(BF16)

        def body(s, j, start, fresh):
            add_window(denv_ref, start, dot_nt(kept(k, s, start, fresh), dt[:, part(j)]))
            mine = jnp.where(window_hot(k, s, start), energy[:, part(j)], 0.0)
            half = mine[:, 0:LANES]
            for i in range(1, sub_rows):
                half = half + mine[:, i * LANES : (i + 1) * LANES]
            ae_ref[pl.ds(start, WIN), :] += half

        each_window(k, s, n, slow, body)

    def phase_c(k, s, n, slow):
        lanes = lanes_of(s, n)
        height = n * sub_rows

        def env_terms(s, j, start, fresh):
            a = kept(k, s, start, fresh)
            e_win = load_window(env_ref, start)
            d_win = load_window(denv_ref, start)
            dew = dot_tn(d_win, a)
            here = lanes_of(s, 1)
            pair = jnp.concatenate([dt_ref[k, :, here], ew_ref[k, :, here]], axis=0)
            prods = dot_nn(jnp.concatenate([e_win, d_win], axis=1)[WIN:], pair)
            hot = a[0:WIN].astype(F32)
            if fresh:
                big_ref[:, part(j)] = dew
            else:
                big_ref[:, part(j)] += dew
            for m in range(1, 9):
                row = jnp.sum(prods[(m - 1) * WIN : m * WIN] * hot, axis=0, keepdims=True)
                for i in range(sub_rows):
                    at = j * sub_rows + i
                    piece = row[:, i * LANES : (i + 1) * LANES]
                    if fresh:
                        dy_ref[m, at : at + 1, :] = piece
                    else:
                        dy_ref[m, at : at + 1, :] += piece

        each_window(k, s, n, slow, env_terms)
        dew = big_ref[:, 0 : n * SUB]
        dpre = (dew * in_lanes(plane(6, k, s, n))).astype(BF16)
        denv_row = jnp.sum(dew * ew_ref[k, :, lanes].astype(F32), axis=0, keepdims=True)
        for j in range(height):
            dy_ref[0, j : j + 1, :] = denv_row[:, j * LANES : (j + 1) * LANES]
        dfirst = dfa_ref[k, :, lanes].astype(F32) + dot_nn(
            wev_ref[...], jnp.concatenate([dpre, dv_ref[k, :, lanes]], axis=0)
        )
        dz1 = (dfirst * dsilu_ref[k, :, lanes].astype(F32)).astype(BF16)
        dboth = dot_nn(w1_ref[...], dz1)
        dmixed = dboth[0:chans].astype(BF16)
        dbasis = dboth[chans:]
        for j in range(height):
            db_ref[j * n_basis : (j + 1) * n_basis, :] = dbasis[
                0:n_basis, j * LANES : (j + 1) * LANES
            ]
        ux, uy, uz, dist, inv, q = [plane(i, k, s, n) for i in range(6)]
        envelope = q * q
        g = envelope * inv
        denvelope = -(q * envelope) * dist
        dg = (denvelope - g) * inv
        sins, coss = waves(0.5 * dist, n_basis)
        live = tile_of(lambda rows: live_ref[k, rows, :], s, n)
        y = [dy_ref[m, 0:height, :] for m in range(9)]
        ddist = (live + y[0] / envelope) * denvelope
        for i in range(n_basis):
            db = db_ref[pl.ds(i, height, stride=n_basis), :]
            ddist = ddist + db * (coss[i] * ((i + 1) * math.pi / 2.0) * g + sins[i] * dg)
        gx = y[1] + ROOT3 * (uy * y[4] + uz * y[6]) + (2.0 * 0.866) * ux * y[7]
        gy = y[2] + ROOT3 * (ux * y[4] + uz * y[5]) - (2.0 * 0.866) * uy * y[7]
        gz = y[3] + ROOT3 * (uy * y[5] + ux * y[6]) + 3.0 * uz * y[8]
        along = ddist - inv * (gx * ux + gy * uy + gz * uz)
        for i, (gu, u) in enumerate(((gx, ux), (gy, uy), (gz, uz))):
            hi, lo = split(inv * gu + along * u)
            dr_ref[pl.ds(i, height, stride=16), :] = hi
            dr_ref[pl.ds(3 + i, height, stride=16), :] = lo
        dr = jnp.concatenate([dr_ref[j * 16 : (j + 1) * 16, :] for j in range(height)], axis=1)
        moved = jnp.concatenate([dmixed, dr.astype(BF16)], axis=0)
        sums = dot_nt(jnp.concatenate(table_hots(k, s, n), axis=0), moved)
        acc_ref[:, 0:chans] += sums[:, 0:chans]
        acc_ref[:, chans : chans + 16] += sums[:, chans:]

        def body(s, j, start, fresh):
            hot = a_ref[k * subs + s, 0:WIN, :] if fresh else window_hot(k, s, start).astype(BF16)
            mine = dot_nt(hot, moved[:, part(j)])
            cacc_ref[pl.ds(start, WIN), 0:chans] += mine[:, 0:chans]
            cacc_ref[pl.ds(start, WIN), chans : chans + 16] += mine[:, chans:]

        each_window(k, s, n, slow, body)

    for phase in (phase_a, phase_b, phase_c):

        @pl.when(most == 0)
        def _(phase=phase):
            def chunk(k, carry):
                phase(k, 0, subs, False)
                return carry

            lax.fori_loop(0, n_chunks, chunk, 0)

        @pl.when(most != 0)
        def _(phase=phase):
            def sub(i, carry):
                phase(lax.div(i, subs), lax.rem(i, subs), 1, True)
                return carry

            lax.fori_loop(0, n_chunks * subs, sub, 0)

    own_ref[0:own, :] = cacc_ref[0:own, :]
    own_ref[own:, :] = acc_ref[0:own, :]
    row = lax.broadcasted_iota(jnp.int32, (LANES, LANES), 0)
    group = lax.broadcasted_iota(jnp.int32, (LANES, LANES), 1) // GROUP
    both = ((group < 3) & ((row == group) | (row == group + 3))).astype(F32)
    places = dot_nn(acc_ref[own:, LANES:], both, HIGH)
    found = {}
    at = own
    for off in OFFSETS:
        found[off] = at
        at += plan.live(off)
    for blocks, ref in zip(
        plan.groups[0] + [plan.held_rest], tuple(back_refs) + (rest_ref,)
    ):
        for off, row in plan.spans(blocks):
            live = plan.live(off)
            at = found[off]
            ref[row : row + live, :] = acc_ref[at : at + live, 0:chans]
            block = places[at - own : at - own + live, :]
            ref[row + live : row + live + 1, :] = jnp.sum(diagonal(block), axis=0, keepdims=True)


def returned_sums(plan, came, axes, messages, first, sel_ref, both_ref):
    chans = both_ref.shape[1] - LANES
    both_ref[...] = jnp.zeros_like(both_ref)
    at = 0
    for blocks in messages:
        for off, row in plan.spans(blocks):
            live = plan.live(off)
            src, begin = plan.find(came, axes, None, [], off)
            here = slice(at + row, at + row + live)
            both_ref[here, 0:chans] = src[begin : begin + live, :]
            both_ref[here, chans:] = spread(src[begin + live : begin + live + 1, :], live)
        at += plan.total(blocks)
    hot = sel_ref[first : first + at, :].astype(BF16)
    return dot_exact(hot, both_ref[...], ((0,), (0,)))


def own_kernel(plan, ae_ref, own_ref, wide_ref, sel_ref, *refs):
    came, refs = plan.cut(refs, 0, 1)
    energy_ref, fg_ref, force_ref, both_ref = refs
    chans = fg_ref.shape[1]
    own = force_ref.shape[1]
    first = sum(plan.total(blocks) for blocks in plan.groups[2])
    sums = returned_sums(plan, came, (1, 0), [plan.own_rest], first, sel_ref, both_ref)
    energy_ref[...] = jnp.sum(ae_ref[0:own, :].T, axis=0, keepdims=True)
    fg_ref[...] = dot_nt(own_ref[0:own, 0:chans], wide_ref[0:chans, :], HIGH) + dot_nt(
        own_ref[own:, 0:chans] + sums[:, 0:chans], wide_ref[chans : 2 * chans, :], HIGH
    )
    force = (own_ref[own:, LANES:] - own_ref[0:own, LANES:]).T
    total = dot_nt(group_rows(8), sums[:, chans:], HIGH)
    force_ref[...] = force[0:3, :] + force[3:6, :] + total[0:3, :]


def last_kernel(plan, sel_ref, fg_ref, force_ref, wide_ref, *refs):
    came, refs = plan.cut(refs, 2)
    out_force_ref, out_fg_ref, both_ref = refs
    chans = fg_ref.shape[1]
    sums = returned_sums(plan, came, (2,), plan.groups[2], 0, sel_ref, both_ref)
    s_hi, s_lo = split(sums[:, 0:chans])
    w_hi, w_lo = split(wide_ref[chans : 2 * chans, :])
    out_fg_ref[...] = fg_ref[...] + dot_nt(
        jnp.concatenate([s_hi, s_lo, s_hi], axis=1).astype(BF16),
        jnp.concatenate([w_hi, w_hi, w_lo], axis=1).astype(BF16),
    )
    total = dot_nt(group_rows(8), sums[:, chans:], HIGH)
    out_force_ref[...] = -(force_ref[...] + total[0:3, :])


def stack(*arrays):
    dtype = arrays[0].dtype
    tile = 32 // dtype.itemsize
    starts = [0]
    for x in arrays:
        starts.append(starts[-1] + -(-x.shape[1] // tile) * tile)
    total = None
    for x, at in zip(arrays, starts):
        below = starts[-1] - at - x.shape[1]
        part = jnp.pad(x.astype(dtype), ((0, 0), (at, below), (0, LANES - x.shape[2])))
        total = part if total is None else total + part
    return total[0]


def local(
    positions,
    atom_features,
    send_face,
    send_edge,
    send_corner,
    centre,
    other,
    edge_count,
    w_proj_a,
    w_proj_b,
    w_radial,
    w_first,
    w_env,
    w_value,
    w_second,
    w_out,
):
    own, chans = atom_features.shape
    edges = centre.shape[0]
    n_basis = w_radial.shape[0]
    plan = Plan(
        [send_face.shape[2], send_edge.shape[2], send_corner.shape[2]],
        [lax.axis_size(axis) for axis in AXES],
    )
    n_ghost = sum(len(c) * w for c, w in zip(CLASSES, plan.widths))
    n_sel = 2 * own + n_ghost
    n_send = sum(plan.total(blocks) for blocks in plan.groups[2]) + plan.total(plan.own_rest)
    n_table = n_sel + 4 * n_basis
    edges_up = -(-edges // CHUNK) * CHUNK
    n_rows = edges_up // LANES
    n_chunks = edges_up // CHUNK

    with jax.named_scope("prep"):
        atom_features, plan.even = lax.optimization_barrier((atom_features, plan.even))
        rows = stack(
            atom_features[None],
            jnp.transpose(send_edge, (0, 2, 1)),
            jnp.transpose(send_corner, (0, 2, 1)),
            edge_count.reshape(1, 1, 1),
        )
        *sends, own_rows, sel = pl.pallas_call(
            lambda *refs: prep_kernel(plan, *refs),
            out_shape=plan.shapes(2, chans)
            + [shape(plan.total(plan.own_rest), chans), shape(n_send, own)],
            in_specs=[VMEM] * 3,
            out_specs=[VMEM] * (len(plan.groups[2]) + 2),
            scratch_shapes=[pltpu.VMEM((LANES, LANES), F32)],
            compiler_params=PARAMS,
        )(rows, positions, jnp.transpose(send_face, (1, 0, 2)))

    came = {}
    with jax.named_scope("halo_z"):
        came[2] = plan.send(2, sends)

    with jax.named_scope("group_edges"):
        pad = [(0, edges_up - edges)]
        regs = max(sorted_size(edges_up) // (8 * LANES), 1)
        key, bounds = pl.pallas_call(
            lambda *refs: sort_kernel(own, *refs),
            out_shape=[
                shape(n_chunks, CHUNK // LANES, LANES, dtype=jnp.int32),
                shape(2, LANES, dtype=jnp.int32),
            ],
            in_specs=[VMEM] * 3,
            out_specs=[VMEM] * 2,
            scratch_shapes=[pltpu.VMEM((16 * regs, LANES), F32)],
            compiler_params=PARAMS,
        )(
            rows,
            jnp.pad(centre, pad).reshape(n_rows, LANES),
            jnp.pad(other, pad).reshape(n_rows, LANES),
        )

    with jax.named_scope("halo_y"):
        came[2], key, bounds, w_first, w_env, w_value, w_second, w_out = lax.optimization_barrier(
            (came[2], key, bounds, w_first, w_env, w_value, w_second, w_out)
        )
        came[1] = plan.send(1, glue(plan, 1, (2,), plan.own_rest, own_rows, came))

    with jax.named_scope("weights"):
        wide = stack(w_proj_a[None], w_proj_b[None], w_radial[None])
        narrow = stack(
            w_first[None], w_env[None], w_value[None], w_second[None], w_out[None, None, :]
        )
        half, *weights = pl.pallas_call(
            weight_kernel,
            out_shape=[
                shape(2 * own + 4 * n_basis, chans),
                shape(chans, chans, dtype=BF16),
                shape(2 * chans, chans, dtype=BF16),
                shape(chans, 2 * chans, dtype=BF16),
                shape(chans + 2 * n_basis, chans, dtype=BF16),
                shape(chans, 2 * chans, dtype=BF16),
                shape(2 * chans, chans, dtype=BF16),
                shape(chans, LANES),
            ],
            in_specs=[VMEM] * 3,
            out_specs=[VMEM] * 8,
            compiler_params=PARAMS,
        )(rows, wide, narrow)

    with jax.named_scope("halo_x"):
        came[1], half, weights = lax.optimization_barrier((came[1], half, weights))
        came[0] = plan.send(0, glue(plan, 0, (1, 2), plan.own_rest, own_rows, came))

    planes = (n_chunks, chans, CHUNK)
    scratch = [
        pltpu.VMEM((n_table, chans), F32),
        pltpu.VMEM((n_ghost, chans), F32),
        pltpu.VMEM((-(-n_ghost // LANES) * LANES, LANES), F32),
        pltpu.VMEM((chans, n_table), BF16),
        pltpu.VMEM((n_rows * 8, LANES), F32),
        pltpu.VMEM((n_rows * n_basis, LANES), F32),
        pltpu.VMEM((8, n_chunks, CHUNK // LANES, LANES), F32),
        pltpu.VMEM(planes, BF16),
        pltpu.VMEM(planes, BF16),
        pltpu.VMEM(planes, BF16),
        pltpu.VMEM(planes, BF16),
        pltpu.VMEM((edges_up // SUB, 9 * WIN, SUB), BF16),
        pltpu.VMEM((9, own + WIN, chans), F32),
        pltpu.VMEM((9, own + WIN, chans), F32),
        pltpu.VMEM((chans, CHUNK), F32),
        pltpu.VMEM(planes, BF16),
        pltpu.VMEM(planes, BF16),
        pltpu.VMEM(planes, BF16),
        pltpu.VMEM((n_chunks, CHUNK // LANES, LANES), F32),
        pltpu.VMEM((9, CHUNK // LANES, LANES), F32),
        pltpu.VMEM((CHUNK // LANES * n_basis, LANES), F32),
        pltpu.VMEM((CHUNK // LANES * 16, LANES), F32),
        pltpu.VMEM((n_sel - own, 2 * LANES), F32),
        pltpu.VMEM((own + WIN, 2 * LANES), F32),
    ]
    with jax.named_scope("layer"):
        given = [bounds, key, positions, wide]
        given += [*came[0], *came[1], *came[2], half, *weights]
        atom_sums, own_sums, *back, held = pl.pallas_call(
            lambda *refs: main_kernel(plan, *refs),
            out_shape=[shape(own + WIN, LANES), shape(2 * own, 2 * LANES)]
            + plan.shapes(0, chans)
            + [shape(plan.total(plan.held_rest), chans)],
            in_specs=[SMEM] + [VMEM] * (len(given) - 1),
            out_specs=[VMEM] * (3 + len(plan.groups[0])),
            scratch_shapes=scratch,
            compiler_params=PARAMS,
        )(*given)

    with jax.named_scope("halo_back"):
        home = {0: plan.send(0, back, back=True)}
        home[1] = plan.send(1, glue(plan, 1, (0,), plan.held_rest, held, home), back=True)
        home[2] = plan.send(2, glue(plan, 2, (1, 0), plan.held_rest, held, home), back=True)

    with jax.named_scope("own_part"):
        given = [atom_sums, own_sums, wide, sel, *home[0], *home[1]]
        energy, fg, force = pl.pallas_call(
            lambda *refs: own_kernel(plan, *refs),
            out_shape=[shape(1, own), shape(own, chans), shape(3, own)],
            in_specs=[VMEM] * len(given),
            out_specs=[VMEM] * 3,
            scratch_shapes=[pltpu.VMEM((plan.total(plan.own_rest), chans + LANES), F32)],
            compiler_params=PARAMS,
        )(*given)

    with jax.named_scope("owner_sums"):
        given = [sel, fg, force, wide, *home[2]]
        n_z = n_send - plan.total(plan.own_rest)
        forces, feature_grad = pl.pallas_call(
            lambda *refs: last_kernel(plan, *refs),
            out_shape=[shape(3, own), shape(own, chans)],
            in_specs=[VMEM] * len(given),
            out_specs=[VMEM] * 2,
            scratch_shapes=[pltpu.VMEM((n_z, chans + LANES), F32)],
            compiler_params=PARAMS,
        )(*given)
    return forces, energy.reshape(own), feature_grad


def solution(mesh):
    shard = P(AXES)
    return jax.shard_map(
        local,
        mesh=mesh,
        in_specs=(
            P(None, AXES),
            P(AXES, None),
            P(AXES, None, None),
            P(AXES, None, None),
            P(AXES, None, None),
            shard,
            shard,
            shard,
        )
        + (P(),) * 8,
        out_specs=(P(None, AXES), shard, P(AXES, None)),
        check_vma=False,
    )
```

```python
import math

import jax
import jax.numpy as jnp
from jax import lax
from jax.experimental import pallas as pl
from jax.experimental.pallas import tpu as pltpu
from jax.sharding import PartitionSpec as P

F32 = jnp.float32
BF16 = jnp.bfloat16
HIGH = lax.Precision.HIGHEST
AXES = ("gx", "gy", "gz")
CHUNK = 3072
SUB = 256
WIN = 16
OTHER_BITS = 9
OTHER_MASK = (1 << OTHER_BITS) - 1
LANES = 128
ROOT3 = 1.732


VMEM = pl.BlockSpec(memory_space=pltpu.VMEM)
SMEM = pl.BlockSpec(memory_space=pltpu.SMEM)
PARAMS = pltpu.CompilerParams(vmem_limit_bytes=52 * 2**20)


def shape(*dims, dtype=F32):
    return jax.ShapeDtypeStruct(dims, dtype)


def dot_nn(a, b, precision=None):
    return lax.dot_general(
        a, b, (((1,), (0,)), ((), ())), preferred_element_type=F32, precision=precision
    )


def dot_nt(a, b, precision=None):
    return lax.dot_general(
        a, b, (((1,), (1,)), ((), ())), preferred_element_type=F32, precision=precision
    )


def dot_tn(a, b, precision=None):
    return lax.dot_general(
        a, b, (((0,), (0,)), ((), ())), preferred_element_type=F32, precision=precision
    )


def offset_classes():
    classes = [[], [], []]
    for a in (-1, 0, 1):
        for b in (-1, 0, 1):
            for c in (-1, 0, 1):
                if (a, b, c) != (0, 0, 0):
                    classes[abs(a) + abs(b) + abs(c) - 1].append((a, b, c))
    return classes


CLASSES = offset_classes()


OFFSETS = [off for group in CLASSES for off in group]


def kind(off):
    return abs(off[0]) + abs(off[1]) + abs(off[2]) - 1


class Plan:
    def __init__(self, widths, sizes):
        self.widths = widths
        self.sizes = sizes
        self.groups = [self.group(a) for a in range(3)]
        self.even = [lax.axis_index(axis) % 2 == 0 for axis in AXES]
        self.own_rest = [off for off in OFFSETS if off[2] == 0]
        self.held_rest = [off for off in OFFSETS if off[0] == 0]

    def group(self, a):
        groups = {}
        for off in OFFSETS:
            if off[a] != 0:
                groups.setdefault(off[a] % self.sizes[a], []).append(off)
        return list(groups.values())

    def live(self, off):
        return self.widths[kind(off)]

    def rows(self, off):
        return self.live(off) + 1

    def total(self, blocks):
        return sum(self.rows(off) for off in blocks)

    def spans(self, blocks):
        at = 0
        for off in blocks:
            yield off, at
            at += self.rows(off)

    def place(self, a, off):
        for g, blocks in enumerate(self.groups[a]):
            if off in blocks:
                return g, dict(self.spans(blocks))[off]
        raise KeyError(off)

    def find(self, came, axes, rest_ref, rest, off):
        for a in axes:
            if off[a] != 0:
                g, begin = self.place(a, off)
                return came[a][g], begin
        return rest_ref, dict(self.spans(rest))[off]

    def cut(self, refs, *axes):
        came = {}
        for a in axes:
            n = len(self.groups[a])
            came[a], refs = refs[:n], refs[n:]
        return came, refs

    def shapes(self, a, chans):
        return [shape(self.total(blocks), chans) for blocks in self.groups[a]]

    def send(self, a, messages, back=False):
        n = self.sizes[a]
        steps = [-blocks[0][a] if back else blocks[0][a] for blocks in self.groups[a]]
        if n % 2 or n == 2:
            return [
                lax.ppermute(message, AXES[a], [(i, (i + step) % n) for i in range(n)])
                for step, message in zip(steps, messages)
            ]
        up, down = steps.index(1), steps.index(-1)
        even = self.even[a]
        ahead = [(i, i + 1 - 2 * (i % 2)) for i in range(n)]
        behind = [(i, (i - 1 + 2 * (i % 2)) % n) for i in range(n)]
        first = lax.ppermute(jnp.where(even, messages[up], messages[down]), AXES[a], ahead)
        second = lax.ppermute(jnp.where(even, messages[down], messages[up]), AXES[a], behind)
        got = [None, None]
        got[up] = jnp.where(even, second, first)
        got[down] = jnp.where(even, first, second)
        return got


GROUP = 32


def group_rows(count):
    row = lax.broadcasted_iota(jnp.int32, (count, LANES), 0)
    group = lax.broadcasted_iota(jnp.int32, (count, LANES), 1) // GROUP
    return (row == group).astype(F32) * (group < 3).astype(F32)


def diagonal(x):
    row = lax.broadcasted_iota(jnp.int32, x.shape, 0)
    lane = lax.broadcasted_iota(jnp.int32, x.shape, 1)
    return jnp.where((lane & (GROUP - 1)) == row, x, 0.0)


def spread(row, live):
    return diagonal(jnp.broadcast_to(row, (live, LANES)))


def split(x):
    high = x.astype(BF16).astype(F32)
    return high, x - high


def dot_exact(hot, x, dims):
    high, low = split(x)
    both = jnp.concatenate([high, low], axis=1).astype(BF16)
    out = lax.dot_general(hot, both, (dims, ((), ())), preferred_element_type=F32)
    return out[:, 0 : x.shape[1]] + out[:, x.shape[1] :]


def prep_kernel(plan, rows_ref, pos_ref, face_ref, edge_ref, corner_ref, *outs):
    n_z = len(plan.groups[2])
    sends, rest_ref, sel_ref, turn_ref = outs[:n_z], outs[n_z], outs[n_z + 1], outs[n_z + 2]
    own = sel_ref.shape[1]
    lane = lax.broadcasted_iota(jnp.int32, (1, own), 1).astype(F32)
    turn_ref[...] = jnp.zeros_like(turn_ref)
    for key in range(face_ref.shape[0]):
        turn_ref[key : key + 1, 0 : face_ref.shape[2]] = face_ref[key].astype(F32)
    columns = [turn_ref[...].T, edge_ref[0].astype(F32), corner_ref[0].astype(F32)]
    sel_ref[...] = jnp.zeros_like(sel_ref)
    messages = plan.groups[2] + [plan.own_rest]
    at = 0
    for blocks in messages:
        for off, begin in plan.spans(blocks):
            key = CLASSES[kind(off)].index(off)
            live = plan.live(off)
            column = columns[kind(off)][0:live, key : key + 1]
            sel_ref[at + begin : at + begin + live, :] = (column == lane).astype(F32)
        at += plan.total(blocks)
    pos = dot_tn(pos_ref[...], group_rows(3), HIGH)
    sel = sel_ref[...]
    rows = dot_nn(sel, rows_ref[0:own, :], HIGH)
    places = dot_nn(sel, pos, HIGH)
    at = 0
    for blocks, send in zip(messages, tuple(sends) + (rest_ref,)):
        count = plan.total(blocks)
        send[...] = rows[at : at + count, :]
        for off, begin in plan.spans(blocks):
            live = plan.live(off)
            block = places[at + begin : at + begin + live, :]
            send[begin + live : begin + live + 1, :] = jnp.sum(
                diagonal(block), axis=0, keepdims=True
            )
        at += count


def glue_kernel(plan, a, axes, rest, *refs):
    rest_ref = refs[0]
    came, outs = plan.cut(refs[1:], *axes)
    for blocks, out in zip(plan.groups[a], outs):
        for off, row in plan.spans(blocks):
            src, begin = plan.find(came, axes, rest_ref, rest, off)
            out[row : row + plan.rows(off), :] = src[begin : begin + plan.rows(off), :]


def glue(plan, a, axes, rest, rest_rows, came):
    given = [rest_rows] + [message for axis in axes for message in came[axis]]
    outs = plan.shapes(a, rest_rows.shape[1])
    return pl.pallas_call(
        lambda *refs: glue_kernel(plan, a, axes, rest, *refs),
        out_shape=outs,
        in_specs=[VMEM] * len(given),
        out_specs=[VMEM] * len(outs),
        compiler_params=PARAMS,
    )(*given)


def sort_kernel(own, count_ref, centre_ref, other_ref, key_ref, bound_ref, turn_ref):
    dead = (own - 1) * (OTHER_MASK + 1) + OTHER_MASK
    rows = centre_ref.shape[0]
    regs = turn_ref.shape[0] // 16
    group = regs * 8
    row = lax.broadcasted_iota(jnp.int32, (rows, LANES), 0)
    lane = lax.broadcasted_iota(jnp.int32, (rows, LANES), 1)
    count = count_ref[count_ref.shape[0] - 8 : count_ref.shape[0] - 7, 0:1].astype(jnp.int32)
    live = row * LANES + lane < count
    centre = centre_ref[...]
    key = jnp.where(live, (centre << OTHER_BITS) + other_ref[...], dead).astype(F32)
    x = [key[8 * v : 8 * v + 8, :] for v in range(rows // 8)]
    x += [jnp.full((8, LANES), float(dead), F32)] * (regs - len(x))
    n_windows = own // WIN
    free = regs - rows // 8
    if n_windows * SUB <= free * 8 * LANES:
        window = jnp.where(live, centre // WIN, -1)
        need = []
        used = jnp.zeros((1, 1), F32)
        for w in range(n_windows):
            hits = jnp.sum((window == w).astype(F32), axis=0, keepdims=True)
            hits = jnp.sum(hits, axis=1, keepdims=True)
            whole = jnp.floor((hits + (SUB - 1)) * (1.0 / SUB)) * SUB
            used = used + whole
            need.append(whole - hits)
        fits = used <= float(rows * LANES)
        slot = lax.broadcasted_iota(jnp.int32, (8, LANES), 0) * LANES
        slot = slot + lax.broadcasted_iota(jnp.int32, (8, LANES), 1)
        per_reg = 8 * LANES // SUB
        for w in range(n_windows):
            v = rows // 8 + w // per_reg
            at = slot - (w % per_reg) * SUB
            take = (at >= 0) & (at.astype(F32) < need[w]) & fits
            mark = float((w * WIN + WIN - 1) * (OTHER_MASK + 1) + OTHER_MASK)
            x[v] = jnp.where(take, mark, x[v])
    s = lax.broadcasted_iota(jnp.int32, (8, LANES), 0)
    ln = lax.broadcasted_iota(jnp.int32, (8, LANES), 1)
    base = ln * group + s * regs

    def sign(k, v):
        return jnp.where(((base + v) & k) == 0, 1.0, -1.0).astype(F32)

    last = [jnp.ones((8, LANES), F32)] * regs
    total = group * LANES
    k = 2
    while k <= total:
        signs = [sign(k, v) for v in range(regs)] if k < total else [1.0] * regs
        x = [x[v] * (last[v] * signs[v]) for v in range(regs)]
        last = signs
        j = k // 2
        while j >= 1:
            if j < regs:
                for v in range(regs):
                    if v & j == 0:
                        a, b = x[v], x[v | j]
                        x[v], x[v | j] = jnp.minimum(a, b), jnp.maximum(a, b)
            else:
                axis, step, size, ids = (
                    (0, j // regs, 8, s) if j < group else (1, j // group, LANES, ln)
                )
                low = (ids & step) == 0
                for v in range(regs):
                    up = pltpu.roll(x[v], size - step, axis)
                    if 2 * step == size:
                        mate = up
                    else:
                        mate = jnp.where(low, up, pltpu.roll(x[v], step, axis))
                    x[v] = jnp.where(low, jnp.minimum(x[v], mate), jnp.maximum(x[v], mate))
            j //= 2
        k *= 2
    least = x[0]
    most = jnp.where(x[0] == float(dead), -1.0, x[0])
    for v in range(1, regs):
        least = jnp.minimum(least, x[v])
        most = jnp.maximum(most, jnp.where(x[v] == float(dead), -1.0, x[v]))
    bound_ref[0:1, :] = jnp.min(least, axis=0, keepdims=True).astype(jnp.int32) >> OTHER_BITS
    bound_ref[1:2, :] = jnp.max(most, axis=0, keepdims=True).astype(jnp.int32) >> OTHER_BITS
    turned = jnp.concatenate(x + [jnp.zeros((LANES - group, LANES), F32)], axis=0).T
    turn_ref[...] = turned
    ratio = LANES // group
    parts = [
        turn_ref[pl.ds(i, rows, stride=ratio), 0:group] for i in range(ratio)
    ]
    done = jnp.concatenate(parts, axis=1).astype(jnp.int32)
    per = key_ref.shape[1]
    for c in range(key_ref.shape[0]):
        key_ref[c] = done[c * per : (c + 1) * per, :]


def weight_kernel(
    rows_ref,
    wide_ref,
    half_ref,
    tab_ref,
    w1t_ref,
    wevt_ref,
    w2t_ref,
    w1_ref,
    wev_ref,
    w2_ref,
    wcol_ref,
):
    chans = wide_ref.shape[1]
    rad_rows = wide_ref.shape[0] - 2 * chans
    own = (tab_ref.shape[0] - 4 * rad_rows) // 2
    wa, wb, rad = wide_ref[0:chans, :], wide_ref[chans : 2 * chans, :], wide_ref[2 * chans :, :]
    w1, wenv, wval = [half_ref[i * chans : (i + 1) * chans, :] for i in range(3)]
    w2 = half_ref[3 * chans : 5 * chans, :]

    def flip(w):
        return w.astype(F32).T.astype(BF16)

    w1, w2 = (0.5 * w1.astype(F32)).astype(BF16), (0.5 * w2.astype(F32)).astype(BF16)
    down = dot_nn(rad, w1.astype(F32), HIGH)
    w1_ref[0:chans, :] = w1
    w1_ref[chans:, :] = jnp.concatenate([down, jnp.zeros_like(down)], axis=0).astype(BF16)
    w2_ref[...] = w2
    w1t_ref[...] = flip(w1)
    wevt_ref[0:chans, :] = flip(wenv)
    wevt_ref[chans:, :] = flip(wval)
    w2t_ref[:, 0:chans] = flip(w2[0:chans, :])
    w2t_ref[:, chans:] = flip(w2[chans:, :])
    wev_ref[:, 0:chans] = wenv
    wev_ref[:, chans:] = wval
    wout = half_ref[5 * chans : 5 * chans + 1, :].astype(F32)
    wcol_ref[...] = jnp.broadcast_to(wout, (LANES, chans)).T
    feat = rows_ref[0:own, :]
    tab_ref[0:own, :] = dot_nn(feat, wa, HIGH)
    tab_ref[own : 2 * own, :] = dot_nn(feat, wb, HIGH)
    rad_hi, rad_lo = split(rad)
    tab_ref[2 * own :, :] = jnp.concatenate([rad_hi, rad_hi, rad_lo, jnp.zeros_like(rad)], axis=0)


def harmonics(ux, uy, uz):
    return [
        ux,
        uy,
        uz,
        ROOT3 * ux * uy,
        ROOT3 * uy * uz,
        ROOT3 * ux * uz,
        0.866 * (ux * ux - uy * uy),
        0.5 * (3.0 * uz * uz - 1.0),
    ]


def trig(half):
    turns = jnp.round(half)
    x = math.pi * (half - turns)
    odd = turns - 2.0 * jnp.floor(0.5 * turns)
    sign = 1.0 - 2.0 * odd
    x2 = x * x
    s = jnp.full_like(x, -1.0 / 39916800)
    for coef in (1.0 / 362880, -1.0 / 5040, 1.0 / 120, -1.0 / 6, 1.0):
        s = s * x2 + coef
    c = jnp.full_like(x, 1.0 / 479001600)
    for coef in (-1.0 / 3628800, 1.0 / 40320, -1.0 / 720, 1.0 / 24, -0.5, 1.0):
        c = c * x2 + coef
    return sign * x * s, sign * c


def waves(half, count):
    s1, c1 = trig(half)
    sins, coss = [s1], [c1]
    s0, c0 = jnp.zeros_like(s1), jnp.ones_like(c1)
    for _ in range(count - 1):
        sn = 2.0 * c1 * sins[-1] - s0
        cn = 2.0 * c1 * coss[-1] - c0
        s0, c0 = sins[-1], coss[-1]
        sins.append(sn)
        coss.append(cn)
    return sins, coss


def look_up(table_row, index):
    low = index & (LANES - 1)
    high = index >> 7
    result = jnp.zeros(index.shape, F32)
    for block in range(table_row.shape[1] // LANES):
        part = jnp.broadcast_to(table_row[:, block * LANES : (block + 1) * LANES], index.shape)
        got = jnp.take_along_axis(part, low, axis=1)
        result = jnp.where(high == block, got, result)
    return result


def in_lanes(tile):
    return jnp.concatenate([tile[r : r + 1, :] for r in range(tile.shape[0])], axis=1)


def one_hot(row, base, count):
    near = jnp.clip(row - base, -1, LANES).astype(BF16)
    iota = lax.broadcasted_iota(jnp.int32, (count, row.shape[1]), 0).astype(BF16)
    return jnp.where(iota == near, jnp.ones((), BF16), jnp.zeros((), BF16))


def sorted_size(edges):
    return 1 << (edges - 1).bit_length()


def main_kernel(plan, *refs):
    bound_ref, key_ref, pos_ref, wide_ref = refs[:4]
    came, refs = plan.cut(refs[4:], 0, 1, 2)
    half_ref, w1t_ref, wevt_ref, w2t_ref, w1_ref, wev_ref, w2_ref, wcol_ref = refs[:8]
    ae_ref, own_ref = refs[8:10]
    n_x = len(plan.groups[0])
    back_refs, rest_ref = refs[10 : 10 + n_x], refs[10 + n_x]
    (
        tab_ref,
        ghost_ref,
        place_ref,
        table_ref,
        y_ref,
        basis_ref,
        geo_ref,
        first_ref,
        dsilu_ref,
        ew_ref,
        val_ref,
        a_ref,
        env_ref,
        denv_ref,
        big_ref,
        dt_ref,
        dv_ref,
        dfa_ref,
        live_ref,
        dy_ref,
        db_ref,
        dr_ref,
        acc_ref,
        cacc_ref,
    ) = refs[11 + n_x :]
    own = pos_ref.shape[1]
    chans = w1_ref.shape[1]
    n_basis = (w1_ref.shape[0] - chans) // 2
    rows_all = key_ref.shape[0] * key_ref.shape[1]
    per = CHUNK // LANES
    subs = CHUNK // SUB
    sub_rows = SUB // LANES
    n_ghost = sum(len(c) * w for c, w in zip(CLASSES, plan.widths))
    n_tab = own + n_ghost
    n_sel = own + n_tab

    place_ref[...] = jnp.zeros_like(place_ref)
    at = 0
    for off in OFFSETS:
        live = plan.live(off)
        message, begin = plan.find(came, (0, 1, 2), None, [], off)
        ghost_ref[at : at + live, :] = message[begin : begin + live, :]
        place_ref[at : at + live, :] = spread(message[begin + live : begin + live + 1, :], live)
        at += live
    ghost_pos = dot_nt(group_rows(8), place_ref[...], HIGH)
    pos_t = jnp.concatenate([pos_ref[...], ghost_pos[0:3, :]], axis=1)
    f_hi, f_lo = split(ghost_ref[...])
    w_hi, w_lo = split(wide_ref[chans : 2 * chans, :])
    tab_ref[0 : 2 * own, :] = half_ref[0 : 2 * own, :]
    tab_ref[2 * own : n_sel, :] = dot_nn(
        jnp.concatenate([f_hi, f_lo, f_hi], axis=1).astype(BF16),
        jnp.concatenate([w_hi, w_hi, w_lo], axis=0).astype(BF16),
    )
    tab_ref[n_sel:, :] = half_ref[2 * own :, :]
    table_ref[...] = tab_ref[...].T.astype(BF16)

    keys = key_ref[...].reshape(rows_all, LANES)
    centre = keys >> OTHER_BITS
    other = keys & OTHER_MASK
    valid = (other != OTHER_MASK).astype(F32)
    r = [
        look_up(pos_t[a : a + 1, :], other) - look_up(pos_t[a : a + 1, 0:LANES], centre)
        for a in range(3)
    ]
    d2 = r[0] * r[0] + r[1] * r[1] + r[2] * r[2] + 0.01
    dist = jnp.sqrt(d2)
    inv = 1.0 / dist
    q = 1.0 / (1.0 + 0.25 * d2)
    envelope = q * q
    unit = [x * inv for x in r]
    for m, comp in enumerate(harmonics(*unit)):
        y_ref[pl.ds(m, rows_all, stride=8), :] = comp
    sins, _ = waves(0.5 * dist, n_basis)
    scale = envelope * inv
    for n in range(n_basis):
        basis_ref[pl.ds(n, rows_all, stride=n_basis), :] = sins[n] * scale
    for i, plane in enumerate((unit[0], unit[1], unit[2], dist, inv, q, envelope * valid, valid)):
        geo_ref[i] = plane.reshape(geo_ref.shape[1:])

    env_ref[...] = jnp.zeros_like(env_ref)
    denv_ref[...] = jnp.zeros_like(denv_ref)
    ae_ref[...] = jnp.zeros_like(ae_ref)
    acc_ref[...] = jnp.zeros_like(acc_ref)
    cacc_ref[...] = jnp.zeros_like(cacc_ref)
    dr_ref[...] = jnp.zeros_like(dr_ref)

    groups = bound_ref.shape[1] * SUB // sorted_size(rows_all * LANES)

    def window(k, s):
        first = (k * subs + s) * groups
        low = bound_ref[0, first]
        high = low
        for g in range(groups):
            high = jnp.maximum(high, bound_ref[1, first + g])
        start = pl.multiple_of((low >> 3) << 3, 8)
        more = lax.div(high - start, jnp.int32(WIN))
        return start, more

    most = jnp.int32(0)
    n_chunks = jnp.int32(0)
    for s in range(rows_all // sub_rows):
        most = jnp.maximum(most, window(s // subs, s % subs)[1])
        for g in range(groups):
            any_live = bound_ref[1, s * groups + g] >= 0
            n_chunks = jnp.where(any_live, s // subs + 1, n_chunks)


    def lanes_of(s, n):
        if isinstance(s, int):
            return slice(s * SUB, (s + n) * SUB)
        return pl.ds(pl.multiple_of(s * SUB, SUB), n * SUB)

    def tile_of(load, s, n):
        if isinstance(s, int):
            return load(slice(s * sub_rows, (s + n) * sub_rows))
        return jnp.concatenate(
            [load(pl.ds(s * sub_rows + j, 1)) for j in range(n * sub_rows)], axis=0
        )

    def plane(i, k, s, n):
        return tile_of(lambda rows: geo_ref[i, k, rows, :], s, n)

    def keys_of(k, s, n):
        return tile_of(lambda rows: key_ref[k, rows, :], s, n)

    def stacked(ref, k, s, n, height):
        first = (k * subs + s) * sub_rows
        tiles = [
            ref[pl.ds(pl.multiple_of((first + j) * height, 8), height), :]
            for j in range(n * sub_rows)
        ]
        return jnp.concatenate(tiles, axis=1)

    def window_hot(k, s, start):
        crow = in_lanes(keys_of(k, s, 1) >> OTHER_BITS) - start
        return lax.broadcasted_iota(jnp.int32, (WIN, SUB), 0) == crow

    def select(k, s, start):
        hot = window_hot(k, s, start)
        ys = stacked(y_ref, k, s, 1, 8)
        parts = [hot.astype(F32)]
        for m in range(8):
            parts.append(jnp.where(hot, ys[m : m + 1, :], 0.0))
        return jnp.concatenate(parts, axis=0).astype(BF16)

    def load_window(ref, start):
        return jnp.concatenate(
            [ref[m, pl.ds(start, WIN), :] for m in range(9)], axis=0
        ).astype(BF16)

    def add_window(ref, start, rows):
        for m in range(9):
            ref[m, pl.ds(start, WIN), :] += rows[m * WIN : (m + 1) * WIN, :]

    def each_window(k, s, n, slow, body):
        for j in range(n):
            start, more = window(k, s + j)
            body(s + j, j, start, True)
            if slow:

                def step(i, carry, s=s, j=j, start=start):
                    body(s + j, j, pl.multiple_of(start + i * WIN, 8), False)
                    return carry

                lax.fori_loop(1, more + 1, step, 0)

    def kept(k, s, start, fresh):
        return a_ref[k * subs + s] if fresh else select(k, s, start)

    def table_hots(k, s, n):
        row = in_lanes(keys_of(k, s, n) & OTHER_MASK)
        return [one_hot(row, at, min(LANES, n_tab - at)) for at in range(0, n_tab, LANES)]

    def part(j):
        return slice(j * SUB, (j + 1) * SUB)

    def phase_a(k, s, n, slow):
        lanes = lanes_of(s, n)
        crow = in_lanes(keys_of(k, s, n) >> OTHER_BITS)
        hots = [one_hot(crow, 0, own)] + table_hots(k, s, n)
        basis = stacked(basis_ref, k, s, n, n_basis)
        b_hi, b_lo = split(basis)
        hots.append(jnp.concatenate([b_hi, b_lo], axis=0).astype(BF16))
        hots.append(jnp.concatenate([b_hi, jnp.zeros_like(b_hi)], axis=0).astype(BF16))
        mixed = dot_nn(table_ref[...], jnp.concatenate(hots, axis=0)).astype(BF16)
        half = dot_nn(w1t_ref[...], mixed)
        up = 1.0 + jnp.tanh(half)
        first = half * up
        dsilu_ref[k, :, lanes] = (up + first * (2.0 - up)).astype(BF16)
        first = first.astype(BF16)
        first_ref[k, :, lanes] = first
        both = dot_nn(wevt_ref[...], first)
        ew = (both[0:chans] * in_lanes(plane(6, k, s, n))).astype(BF16)
        ew_ref[k, :, lanes] = ew
        val_ref[k, :, lanes] = both[chans:].astype(BF16)

        def body(s, j, start, fresh):
            a = select(k, s, start)
            if fresh:
                a_ref[k * subs + s] = a
            add_window(env_ref, start, dot_nt(a, ew[:, part(j)]))

        each_window(k, s, n, slow, body)

    def phase_b(k, s, n, slow):
        lanes = lanes_of(s, n)

        def totals(s, j, start, fresh):
            value = dot_tn(load_window(env_ref, start), kept(k, s, start, fresh))
            if fresh:
                big_ref[:, part(j)] = value
            else:
                big_ref[:, part(j)] += value

        each_window(k, s, n, slow, totals)
        total = 0.2 * big_ref[:, 0 : n * SUB]
        value = val_ref[k, :, lanes].astype(F32)
        scalar = (value * total).astype(BF16)
        half = dot_nn(w2t_ref[...], jnp.concatenate([first_ref[k, :, lanes], scalar], axis=0))
        up = 1.0 + jnp.tanh(half)
        second = half * up
        wcol = jnp.concatenate([wcol_ref[...]] * (n * sub_rows), axis=1)
        ee = jnp.sum(second.astype(BF16).astype(F32) * wcol, axis=0, keepdims=True)
        envv = in_lanes(plane(6, k, s, n))
        live = ee * in_lanes(plane(7, k, s, n))
        first_row = s * sub_rows
        for j in range(n * sub_rows):
            live_ref[k, pl.ds(first_row + j, 1), :] = live[:, j * LANES : (j + 1) * LANES]
        energy = ee * envv
        dz2 = ((wcol * envv) * (up + second * (2.0 - up))).astype(BF16)
        dj = dot_nn(w2_ref[...], dz2)
        dfa_ref[k, :, lanes] = dj[0:chans].astype(BF16)
        dscalar = dj[chans:]
        dt = (0.2 * value * dscalar).astype(BF16)
        dt_ref[k, :, lanes] = dt
        dv_ref[k, :, lanes] = (total * dscalar).astype(BF16)

        def body(s, j, start, fresh):
            add_window(denv_ref, start, dot_nt(kept(k, s, start, fresh), dt[:, part(j)]))
            mine = jnp.where(window_hot(k, s, start), energy[:, part(j)], 0.0)
            half = mine[:, 0:LANES]
            for i in range(1, sub_rows):
                half = half + mine[:, i * LANES : (i + 1) * LANES]
            ae_ref[pl.ds(start, WIN), :] += half

        each_window(k, s, n, slow, body)

    def phase_c(k, s, n, slow):
        lanes = lanes_of(s, n)
        height = n * sub_rows

        def env_terms(s, j, start, fresh):
            a = kept(k, s, start, fresh)
            e_win = load_window(env_ref, start)
            d_win = load_window(denv_ref, start)
            dew = dot_tn(d_win, a)
            here = lanes_of(s, 1)
            pair = jnp.concatenate([dt_ref[k, :, here], ew_ref[k, :, here]], axis=0)
            prods = dot_nn(jnp.concatenate([e_win, d_win], axis=1)[WIN:], pair)
            hot = a[0:WIN].astype(F32)
            if fresh:
                big_ref[:, part(j)] = dew
            else:
                big_ref[:, part(j)] += dew
            for m in range(1, 9):
                row = jnp.sum(prods[(m - 1) * WIN : m * WIN] * hot, axis=0, keepdims=True)
                for i in range(sub_rows):
                    at = j * sub_rows + i
                    piece = row[:, i * LANES : (i + 1) * LANES]
                    if fresh:
                        dy_ref[m, at : at + 1, :] = piece
                    else:
                        dy_ref[m, at : at + 1, :] += piece

        each_window(k, s, n, slow, env_terms)
        dew = big_ref[:, 0 : n * SUB]
        dpre = (dew * in_lanes(plane(6, k, s, n))).astype(BF16)
        denv_row = jnp.sum(dew * ew_ref[k, :, lanes].astype(F32), axis=0, keepdims=True)
        for j in range(height):
            dy_ref[0, j : j + 1, :] = denv_row[:, j * LANES : (j + 1) * LANES]
        dfirst = dfa_ref[k, :, lanes].astype(F32) + dot_nn(
            wev_ref[...], jnp.concatenate([dpre, dv_ref[k, :, lanes]], axis=0)
        )
        dz1 = (dfirst * dsilu_ref[k, :, lanes].astype(F32)).astype(BF16)
        dboth = dot_nn(w1_ref[...], dz1)
        dmixed = dboth[0:chans].astype(BF16)
        dbasis = dboth[chans:]
        for j in range(height):
            db_ref[j * n_basis : (j + 1) * n_basis, :] = dbasis[
                0:n_basis, j * LANES : (j + 1) * LANES
            ]
        ux, uy, uz, dist, inv, q = [plane(i, k, s, n) for i in range(6)]
        envelope = q * q
        g = envelope * inv
        denvelope = -(q * envelope) * dist
        dg = (denvelope - g) * inv
        sins, coss = waves(0.5 * dist, n_basis)
        live = tile_of(lambda rows: live_ref[k, rows, :], s, n)
        y = [dy_ref[m, 0:height, :] for m in range(9)]
        ddist = (live + y[0] / envelope) * denvelope
        for i in range(n_basis):
            db = db_ref[pl.ds(i, height, stride=n_basis), :]
            ddist = ddist + db * (coss[i] * ((i + 1) * math.pi / 2.0) * g + sins[i] * dg)
        gx = y[1] + ROOT3 * (uy * y[4] + uz * y[6]) + (2.0 * 0.866) * ux * y[7]
        gy = y[2] + ROOT3 * (ux * y[4] + uz * y[5]) - (2.0 * 0.866) * uy * y[7]
        gz = y[3] + ROOT3 * (uy * y[5] + ux * y[6]) + 3.0 * uz * y[8]
        along = ddist - inv * (gx * ux + gy * uy + gz * uz)
        for i, (gu, u) in enumerate(((gx, ux), (gy, uy), (gz, uz))):
            hi, lo = split(inv * gu + along * u)
            dr_ref[pl.ds(i, height, stride=16), :] = hi
            dr_ref[pl.ds(3 + i, height, stride=16), :] = lo
        dr = jnp.concatenate([dr_ref[j * 16 : (j + 1) * 16, :] for j in range(height)], axis=1)
        moved = jnp.concatenate([dmixed, dr.astype(BF16)], axis=0)
        sums = dot_nt(jnp.concatenate(table_hots(k, s, n), axis=0), moved)
        acc_ref[:, 0:chans] += sums[:, 0:chans]
        acc_ref[:, chans : chans + 16] += sums[:, chans:]

        def body(s, j, start, fresh):
            hot = a_ref[k * subs + s, 0:WIN, :] if fresh else window_hot(k, s, start).astype(BF16)
            mine = dot_nt(hot, moved[:, part(j)])
            cacc_ref[pl.ds(start, WIN), 0:chans] += mine[:, 0:chans]
            cacc_ref[pl.ds(start, WIN), chans : chans + 16] += mine[:, chans:]

        each_window(k, s, n, slow, body)

    for phase in (phase_a, phase_b, phase_c):

        @pl.when(most == 0)
        def _(phase=phase):
            def chunk(k, carry):
                phase(k, 0, subs, False)
                return carry

            lax.fori_loop(0, n_chunks, chunk, 0)

        @pl.when(most != 0)
        def _(phase=phase):
            def sub(i, carry):
                phase(lax.div(i, subs), lax.rem(i, subs), 1, True)
                return carry

            lax.fori_loop(0, n_chunks * subs, sub, 0)

    own_ref[0:own, :] = cacc_ref[0:own, :]
    own_ref[own:, :] = acc_ref[0:own, :]
    row = lax.broadcasted_iota(jnp.int32, (LANES, LANES), 0)
    group = lax.broadcasted_iota(jnp.int32, (LANES, LANES), 1) // GROUP
    both = ((group < 3) & ((row == group) | (row == group + 3))).astype(F32)
    places = dot_nn(acc_ref[own:, LANES:], both, HIGH)
    found = {}
    at = own
    for off in OFFSETS:
        found[off] = at
        at += plan.live(off)
    for blocks, ref in zip(
        plan.groups[0] + [plan.held_rest], tuple(back_refs) + (rest_ref,)
    ):
        for off, row in plan.spans(blocks):
            live = plan.live(off)
            at = found[off]
            ref[row : row + live, :] = acc_ref[at : at + live, 0:chans]
            block = places[at - own : at - own + live, :]
            ref[row + live : row + live + 1, :] = jnp.sum(diagonal(block), axis=0, keepdims=True)


def returned_sums(plan, came, axes, messages, first, sel_ref, both_ref):
    chans = both_ref.shape[1] - LANES
    both_ref[...] = jnp.zeros_like(both_ref)
    at = 0
    for blocks in messages:
        for off, row in plan.spans(blocks):
            live = plan.live(off)
            src, begin = plan.find(came, axes, None, [], off)
            here = slice(at + row, at + row + live)
            both_ref[here, 0:chans] = src[begin : begin + live, :]
            both_ref[here, chans:] = spread(src[begin + live : begin + live + 1, :], live)
        at += plan.total(blocks)
    hot = sel_ref[first : first + at, :].astype(BF16)
    return dot_exact(hot, both_ref[...], ((0,), (0,)))


def own_kernel(plan, ae_ref, own_ref, wide_ref, sel_ref, *refs):
    came, refs = plan.cut(refs, 0, 1)
    energy_ref, fg_ref, force_ref, both_ref = refs
    chans = fg_ref.shape[1]
    own = force_ref.shape[1]
    first = sum(plan.total(blocks) for blocks in plan.groups[2])
    sums = returned_sums(plan, came, (1, 0), [plan.own_rest], first, sel_ref, both_ref)
    energy_ref[...] = jnp.sum(ae_ref[0:own, :].T, axis=0, keepdims=True)
    fg_ref[...] = dot_nt(own_ref[0:own, 0:chans], wide_ref[0:chans, :], HIGH) + dot_nt(
        own_ref[own:, 0:chans] + sums[:, 0:chans], wide_ref[chans : 2 * chans, :], HIGH
    )
    force = (own_ref[own:, LANES:] - own_ref[0:own, LANES:]).T
    total = dot_nt(group_rows(8), sums[:, chans:], HIGH)
    force_ref[...] = force[0:3, :] + force[3:6, :] + total[0:3, :]


def last_kernel(plan, sel_ref, fg_ref, force_ref, wide_ref, *refs):
    came, refs = plan.cut(refs, 2)
    out_force_ref, out_fg_ref, both_ref = refs
    chans = fg_ref.shape[1]
    sums = returned_sums(plan, came, (2,), plan.groups[2], 0, sel_ref, both_ref)
    s_hi, s_lo = split(sums[:, 0:chans])
    w_hi, w_lo = split(wide_ref[chans : 2 * chans, :])
    out_fg_ref[...] = fg_ref[...] + dot_nt(
        jnp.concatenate([s_hi, s_lo, s_hi], axis=1).astype(BF16),
        jnp.concatenate([w_hi, w_hi, w_lo], axis=1).astype(BF16),
    )
    total = dot_nt(group_rows(8), sums[:, chans:], HIGH)
    out_force_ref[...] = -(force_ref[...] + total[0:3, :])


def stack(*arrays):
    dtype = arrays[0].dtype
    tile = 32 // dtype.itemsize
    starts = [0]
    for x in arrays:
        starts.append(starts[-1] + -(-x.shape[1] // tile) * tile)
    total = None
    for x, at in zip(arrays, starts):
        below = starts[-1] - at - x.shape[1]
        part = jnp.pad(x.astype(dtype), ((0, 0), (at, below), (0, LANES - x.shape[2])))
        total = part if total is None else total + part
    return total[0]


def local(
    positions,
    atom_features,
    send_face,
    send_edge,
    send_corner,
    centre,
    other,
    edge_count,
    w_proj_a,
    w_proj_b,
    w_radial,
    w_first,
    w_env,
    w_value,
    w_second,
    w_out,
):
    own, chans = atom_features.shape
    edges = centre.shape[0]
    n_basis = w_radial.shape[0]
    plan = Plan(
        [send_face.shape[2], send_edge.shape[2], send_corner.shape[2]],
        [lax.axis_size(axis) for axis in AXES],
    )
    n_ghost = sum(len(c) * w for c, w in zip(CLASSES, plan.widths))
    n_sel = 2 * own + n_ghost
    n_send = sum(plan.total(blocks) for blocks in plan.groups[2]) + plan.total(plan.own_rest)
    n_table = n_sel + 4 * n_basis
    edges_up = -(-edges // CHUNK) * CHUNK
    n_rows = edges_up // LANES
    n_chunks = edges_up // CHUNK

    with jax.named_scope("prep"):
        atom_features, plan.even = lax.optimization_barrier((atom_features, plan.even))
        rows = stack(atom_features[None], edge_count.reshape(1, 1, 1))
        *sends, own_rows, sel = pl.pallas_call(
            lambda *refs: prep_kernel(plan, *refs),
            out_shape=plan.shapes(2, chans)
            + [shape(plan.total(plan.own_rest), chans), shape(n_send, own)],
            in_specs=[VMEM] * 5,
            out_specs=[VMEM] * (len(plan.groups[2]) + 2),
            scratch_shapes=[pltpu.VMEM((LANES, LANES), F32)],
            compiler_params=PARAMS,
        )(
            rows,
            positions,
            jnp.transpose(send_face, (1, 0, 2)),
            jnp.transpose(send_edge, (0, 2, 1)),
            jnp.transpose(send_corner, (0, 2, 1)),
        )

    came = {}
    with jax.named_scope("halo_z"):
        came[2] = plan.send(2, sends)

    with jax.named_scope("group_edges"):
        pad = [(0, edges_up - edges)]
        regs = max(sorted_size(edges_up) // (8 * LANES), 1)
        key, bounds = pl.pallas_call(
            lambda *refs: sort_kernel(own, *refs),
            out_shape=[
                shape(n_chunks, CHUNK // LANES, LANES, dtype=jnp.int32),
                shape(2, LANES, dtype=jnp.int32),
            ],
            in_specs=[VMEM] * 3,
            out_specs=[VMEM] * 2,
            scratch_shapes=[pltpu.VMEM((16 * regs, LANES), F32)],
            compiler_params=PARAMS,
        )(
            rows,
            jnp.pad(centre, pad).reshape(n_rows, LANES),
            jnp.pad(other, pad).reshape(n_rows, LANES),
        )

    with jax.named_scope("halo_y"):
        came[2], key, bounds, w_first, w_env, w_value, w_second, w_out = lax.optimization_barrier(
            (came[2], key, bounds, w_first, w_env, w_value, w_second, w_out)
        )
        came[1] = plan.send(1, glue(plan, 1, (2,), plan.own_rest, own_rows, came))

    with jax.named_scope("weights"):
        wide = stack(w_proj_a[None], w_proj_b[None], w_radial[None])
        narrow = stack(
            w_first[None], w_env[None], w_value[None], w_second[None], w_out[None, None, :]
        )
        half, *weights = pl.pallas_call(
            weight_kernel,
            out_shape=[
                shape(2 * own + 4 * n_basis, chans),
                shape(chans, chans, dtype=BF16),
                shape(2 * chans, chans, dtype=BF16),
                shape(chans, 2 * chans, dtype=BF16),
                shape(chans + 2 * n_basis, chans, dtype=BF16),
                shape(chans, 2 * chans, dtype=BF16),
                shape(2 * chans, chans, dtype=BF16),
                shape(chans, LANES),
            ],
            in_specs=[VMEM] * 3,
            out_specs=[VMEM] * 8,
            compiler_params=PARAMS,
        )(rows, wide, narrow)

    with jax.named_scope("halo_x"):
        came[1], half, weights = lax.optimization_barrier((came[1], half, weights))
        came[0] = plan.send(0, glue(plan, 0, (1, 2), plan.own_rest, own_rows, came))

    planes = (n_chunks, chans, CHUNK)
    scratch = [
        pltpu.VMEM((n_table, chans), F32),
        pltpu.VMEM((n_ghost, chans), F32),
        pltpu.VMEM((-(-n_ghost // LANES) * LANES, LANES), F32),
        pltpu.VMEM((chans, n_table), BF16),
        pltpu.VMEM((n_rows * 8, LANES), F32),
        pltpu.VMEM((n_rows * n_basis, LANES), F32),
        pltpu.VMEM((8, n_chunks, CHUNK // LANES, LANES), F32),
        pltpu.VMEM(planes, BF16),
        pltpu.VMEM(planes, BF16),
        pltpu.VMEM(planes, BF16),
        pltpu.VMEM(planes, BF16),
        pltpu.VMEM((edges_up // SUB, 9 * WIN, SUB), BF16),
        pltpu.VMEM((9, own + WIN, chans), F32),
        pltpu.VMEM((9, own + WIN, chans), F32),
        pltpu.VMEM((chans, CHUNK), F32),
        pltpu.VMEM(planes, BF16),
        pltpu.VMEM(planes, BF16),
        pltpu.VMEM(planes, BF16),
        pltpu.VMEM((n_chunks, CHUNK // LANES, LANES), F32),
        pltpu.VMEM((9, CHUNK // LANES, LANES), F32),
        pltpu.VMEM((CHUNK // LANES * n_basis, LANES), F32),
        pltpu.VMEM((CHUNK // LANES * 16, LANES), F32),
        pltpu.VMEM((n_sel - own, 2 * LANES), F32),
        pltpu.VMEM((own + WIN, 2 * LANES), F32),
    ]
    with jax.named_scope("layer"):
        given = [bounds, key, positions, wide]
        given += [*came[0], *came[1], *came[2], half, *weights]
        atom_sums, own_sums, *back, held = pl.pallas_call(
            lambda *refs: main_kernel(plan, *refs),
            out_shape=[shape(own + WIN, LANES), shape(2 * own, 2 * LANES)]
            + plan.shapes(0, chans)
            + [shape(plan.total(plan.held_rest), chans)],
            in_specs=[SMEM] + [VMEM] * (len(given) - 1),
            out_specs=[VMEM] * (3 + len(plan.groups[0])),
            scratch_shapes=scratch,
            compiler_params=PARAMS,
        )(*given)

    with jax.named_scope("halo_back"):
        home = {0: plan.send(0, back, back=True)}
        home[1] = plan.send(1, glue(plan, 1, (0,), plan.held_rest, held, home), back=True)
        home[2] = plan.send(2, glue(plan, 2, (1, 0), plan.held_rest, held, home), back=True)

    with jax.named_scope("own_part"):
        given = [atom_sums, own_sums, wide, sel, *home[0], *home[1]]
        energy, fg, force = pl.pallas_call(
            lambda *refs: own_kernel(plan, *refs),
            out_shape=[shape(1, own), shape(own, chans), shape(3, own)],
            in_specs=[VMEM] * len(given),
            out_specs=[VMEM] * 3,
            scratch_shapes=[pltpu.VMEM((plan.total(plan.own_rest), chans + LANES), F32)],
            compiler_params=PARAMS,
        )(*given)

    with jax.named_scope("owner_sums"):
        given = [sel, fg, force, wide, *home[2]]
        n_z = n_send - plan.total(plan.own_rest)
        forces, feature_grad = pl.pallas_call(
            lambda *refs: last_kernel(plan, *refs),
            out_shape=[shape(3, own), shape(own, chans)],
            in_specs=[VMEM] * len(given),
            out_specs=[VMEM] * 2,
            scratch_shapes=[pltpu.VMEM((n_z, chans + LANES), F32)],
            compiler_params=PARAMS,
        )(*given)
    return forces, energy.reshape(own), feature_grad


def solution(mesh):
    shard = P(AXES)
    return jax.shard_map(
        local,
        mesh=mesh,
        in_specs=(
            P(None, AXES),
            P(AXES, None),
            P(AXES, None, None),
            P(AXES, None, None),
            P(AXES, None, None),
            shard,
            shard,
            shard,
        )
        + (P(),) * 8,
        out_specs=(P(None, AXES), shard, P(AXES, None)),
        check_vma=False,
    )
```

```python
import math

import jax
import jax.numpy as jnp
from jax import lax
from jax.experimental import pallas as pl
from jax.experimental.pallas import tpu as pltpu
from jax.sharding import PartitionSpec as P

F32 = jnp.float32
BF16 = jnp.bfloat16
HIGH = lax.Precision.HIGHEST
AXES = ("gx", "gy", "gz")
CHUNK = 3072
SUB = 256
WIN = 16
OTHER_BITS = 9
OTHER_MASK = (1 << OTHER_BITS) - 1
LANES = 128
ROOT3 = 1.732


VMEM = pl.BlockSpec(memory_space=pltpu.VMEM)
SMEM = pl.BlockSpec(memory_space=pltpu.SMEM)
PARAMS = pltpu.CompilerParams(vmem_limit_bytes=52 * 2**20)


def shape(*dims, dtype=F32):
    return jax.ShapeDtypeStruct(dims, dtype)


def dot_nn(a, b, precision=None):
    return lax.dot_general(
        a, b, (((1,), (0,)), ((), ())), preferred_element_type=F32, precision=precision
    )


def dot_nt(a, b, precision=None):
    return lax.dot_general(
        a, b, (((1,), (1,)), ((), ())), preferred_element_type=F32, precision=precision
    )


def dot_tn(a, b, precision=None):
    return lax.dot_general(
        a, b, (((0,), (0,)), ((), ())), preferred_element_type=F32, precision=precision
    )


def offset_classes():
    classes = [[], [], []]
    for a in (-1, 0, 1):
        for b in (-1, 0, 1):
            for c in (-1, 0, 1):
                if (a, b, c) != (0, 0, 0):
                    classes[abs(a) + abs(b) + abs(c) - 1].append((a, b, c))
    return classes


CLASSES = offset_classes()


OFFSETS = [off for group in CLASSES for off in group]


def kind(off):
    return abs(off[0]) + abs(off[1]) + abs(off[2]) - 1


class Plan:
    def __init__(self, widths, sizes):
        self.widths = widths
        self.sizes = sizes
        self.groups = [self.group(a) for a in range(3)]
        self.even = [lax.axis_index(axis) % 2 == 0 for axis in AXES]
        self.own_rest = [off for off in OFFSETS if off[2] == 0]
        self.held_rest = [off for off in OFFSETS if off[0] == 0]

    def group(self, a):
        groups = {}
        for off in OFFSETS:
            if off[a] != 0:
                groups.setdefault(off[a] % self.sizes[a], []).append(off)
        return list(groups.values())

    def live(self, off):
        return self.widths[kind(off)]

    def rows(self, off):
        return self.live(off) + 1

    def total(self, blocks):
        return sum(self.rows(off) for off in blocks)

    def spans(self, blocks):
        at = 0
        for off in blocks:
            yield off, at
            at += self.rows(off)

    def place(self, a, off):
        for g, blocks in enumerate(self.groups[a]):
            if off in blocks:
                return g, dict(self.spans(blocks))[off]
        raise KeyError(off)

    def find(self, came, axes, rest_ref, rest, off):
        for a in axes:
            if off[a] != 0:
                g, begin = self.place(a, off)
                return came[a][g], begin
        return rest_ref, dict(self.spans(rest))[off]

    def cut(self, refs, *axes):
        came = {}
        for a in axes:
            n = len(self.groups[a])
            came[a], refs = refs[:n], refs[n:]
        return came, refs

    def shapes(self, a, chans):
        return [shape(self.total(blocks), chans) for blocks in self.groups[a]]

    def send(self, a, messages, back=False):
        n = self.sizes[a]
        steps = [-blocks[0][a] if back else blocks[0][a] for blocks in self.groups[a]]
        if n % 2 or n == 2:
            return [
                lax.ppermute(message, AXES[a], [(i, (i + step) % n) for i in range(n)])
                for step, message in zip(steps, messages)
            ]
        up, down = steps.index(1), steps.index(-1)
        even = self.even[a]
        ahead = [(i, i + 1 - 2 * (i % 2)) for i in range(n)]
        behind = [(i, (i - 1 + 2 * (i % 2)) % n) for i in range(n)]
        first = lax.ppermute(jnp.where(even, messages[up], messages[down]), AXES[a], ahead)
        second = lax.ppermute(jnp.where(even, messages[down], messages[up]), AXES[a], behind)
        got = [None, None]
        got[up] = jnp.where(even, second, first)
        got[down] = jnp.where(even, first, second)
        return got


GROUP = 32


def group_rows(count):
    row = lax.broadcasted_iota(jnp.int32, (count, LANES), 0)
    group = lax.broadcasted_iota(jnp.int32, (count, LANES), 1) // GROUP
    return (row == group).astype(F32) * (group < 3).astype(F32)


def diagonal(x):
    row = lax.broadcasted_iota(jnp.int32, x.shape, 0)
    lane = lax.broadcasted_iota(jnp.int32, x.shape, 1)
    return jnp.where((lane & (GROUP - 1)) == row, x, 0.0)


def spread(row, live):
    return diagonal(jnp.broadcast_to(row, (live, LANES)))


def split(x):
    high = x.astype(BF16).astype(F32)
    return high, x - high


def dot_exact(hot, x, dims):
    high, low = split(x)
    both = jnp.concatenate([high, low], axis=1).astype(BF16)
    out = lax.dot_general(hot, both, (dims, ((), ())), preferred_element_type=F32)
    return out[:, 0 : x.shape[1]] + out[:, x.shape[1] :]


def prep_kernel(plan, rows_ref, pos_ref, face_ref, edge_ref, corner_ref, *outs):
    n_z = len(plan.groups[2])
    sends, rest_ref, sel_ref, turn_ref = outs[:n_z], outs[n_z], outs[n_z + 1], outs[n_z + 2]
    own = sel_ref.shape[1]
    lane = lax.broadcasted_iota(jnp.int32, (1, own), 1).astype(F32)
    turn_ref[...] = jnp.zeros_like(turn_ref)
    for key in range(face_ref.shape[0]):
        turn_ref[key : key + 1, 0 : face_ref.shape[2]] = face_ref[key].astype(F32)
    columns = [turn_ref[...].T, edge_ref[0].astype(F32), corner_ref[0].astype(F32)]
    sel_ref[...] = jnp.zeros_like(sel_ref)
    messages = plan.groups[2] + [plan.own_rest]
    at = 0
    for blocks in messages:
        for off, begin in plan.spans(blocks):
            key = CLASSES[kind(off)].index(off)
            live = plan.live(off)
            column = columns[kind(off)][0:live, key : key + 1]
            sel_ref[at + begin : at + begin + live, :] = (column == lane).astype(F32)
        at += plan.total(blocks)
    pos = dot_tn(pos_ref[...], group_rows(3), HIGH)
    sel = sel_ref[...]
    rows = dot_nn(sel, rows_ref[0:own, :], HIGH)
    places = dot_nn(sel, pos, HIGH)
    at = 0
    for blocks, send in zip(messages, tuple(sends) + (rest_ref,)):
        count = plan.total(blocks)
        send[...] = rows[at : at + count, :]
        for off, begin in plan.spans(blocks):
            live = plan.live(off)
            block = places[at + begin : at + begin + live, :]
            send[begin + live : begin + live + 1, :] = jnp.sum(
                diagonal(block), axis=0, keepdims=True
            )
        at += count


def glue_kernel(plan, a, axes, rest, *refs):
    rest_ref = refs[0]
    came, outs = plan.cut(refs[1:], *axes)
    for blocks, out in zip(plan.groups[a], outs):
        for off, row in plan.spans(blocks):
            src, begin = plan.find(came, axes, rest_ref, rest, off)
            out[row : row + plan.rows(off), :] = src[begin : begin + plan.rows(off), :]


def glue(plan, a, axes, rest, rest_rows, came):
    given = [rest_rows] + [message for axis in axes for message in came[axis]]
    outs = plan.shapes(a, rest_rows.shape[1])
    return pl.pallas_call(
        lambda *refs: glue_kernel(plan, a, axes, rest, *refs),
        out_shape=outs,
        in_specs=[VMEM] * len(given),
        out_specs=[VMEM] * len(outs),
        compiler_params=PARAMS,
    )(*given)


def sort_kernel(own, count_ref, centre_ref, other_ref, key_ref, bound_ref, turn_ref):
    dead = (own - 1) * (OTHER_MASK + 1) + OTHER_MASK
    rows = centre_ref.shape[0]
    regs = turn_ref.shape[0] // 16
    group = regs * 8
    row = lax.broadcasted_iota(jnp.int32, (rows, LANES), 0)
    lane = lax.broadcasted_iota(jnp.int32, (rows, LANES), 1)
    count = count_ref[count_ref.shape[0] - 8 : count_ref.shape[0] - 7, 0:1].astype(jnp.int32)
    live = row * LANES + lane < count
    centre = centre_ref[...]
    key = jnp.where(live, (centre << OTHER_BITS) + other_ref[...], dead).astype(F32)
    x = [key[8 * v : 8 * v + 8, :] for v in range(rows // 8)]
    x += [jnp.full((8, LANES), float(dead), F32)] * (regs - len(x))
    n_windows = own // WIN
    free = regs - rows // 8
    if n_windows * SUB <= free * 8 * LANES:
        window = jnp.where(live, centre // WIN, -1)
        need = []
        used = jnp.zeros((1, 1), F32)
        for w in range(n_windows):
            hits = jnp.sum((window == w).astype(F32), axis=0, keepdims=True)
            hits = jnp.sum(hits, axis=1, keepdims=True)
            whole = jnp.floor((hits + (SUB - 1)) * (1.0 / SUB)) * SUB
            used = used + whole
            need.append(whole - hits)
        fits = used <= float(rows * LANES)
        slot = lax.broadcasted_iota(jnp.int32, (8, LANES), 0) * LANES
        slot = slot + lax.broadcasted_iota(jnp.int32, (8, LANES), 1)
        per_reg = 8 * LANES // SUB
        for w in range(n_windows):
            v = rows // 8 + w // per_reg
            at = slot - (w % per_reg) * SUB
            take = (at >= 0) & (at.astype(F32) < need[w]) & fits
            mark = float((w * WIN + WIN - 1) * (OTHER_MASK + 1) + OTHER_MASK)
            x[v] = jnp.where(take, mark, x[v])
    s = lax.broadcasted_iota(jnp.int32, (8, LANES), 0)
    ln = lax.broadcasted_iota(jnp.int32, (8, LANES), 1)
    base = ln * group + s * regs

    def sign(k, v):
        return jnp.where(((base + v) & k) == 0, 1.0, -1.0).astype(F32)

    last = [jnp.ones((8, LANES), F32)] * regs
    total = group * LANES
    k = 2
    while k <= total:
        signs = [sign(k, v) for v in range(regs)] if k < total else [1.0] * regs
        x = [x[v] * (last[v] * signs[v]) for v in range(regs)]
        last = signs
        j = k // 2
        while j >= 1:
            if j < regs:
                for v in range(regs):
                    if v & j == 0:
                        a, b = x[v], x[v | j]
                        x[v], x[v | j] = jnp.minimum(a, b), jnp.maximum(a, b)
            else:
                axis, step, size, ids = (
                    (0, j // regs, 8, s) if j < group else (1, j // group, LANES, ln)
                )
                low = (ids & step) == 0
                for v in range(regs):
                    up = pltpu.roll(x[v], size - step, axis)
                    if 2 * step == size:
                        mate = up
                    else:
                        mate = jnp.where(low, up, pltpu.roll(x[v], step, axis))
                    x[v] = jnp.where(low, jnp.minimum(x[v], mate), jnp.maximum(x[v], mate))
            j //= 2
        k *= 2
    least = x[0]
    most = jnp.where(x[0] == float(dead), -1.0, x[0])
    for v in range(1, regs):
        least = jnp.minimum(least, x[v])
        most = jnp.maximum(most, jnp.where(x[v] == float(dead), -1.0, x[v]))
    bound_ref[0:1, :] = jnp.min(least, axis=0, keepdims=True).astype(jnp.int32) >> OTHER_BITS
    bound_ref[1:2, :] = jnp.max(most, axis=0, keepdims=True).astype(jnp.int32) >> OTHER_BITS
    turned = jnp.concatenate(x + [jnp.zeros((LANES - group, LANES), F32)], axis=0).T
    turn_ref[...] = turned
    ratio = LANES // group
    parts = [
        turn_ref[pl.ds(i, rows, stride=ratio), 0:group] for i in range(ratio)
    ]
    done = jnp.concatenate(parts, axis=1).astype(jnp.int32)
    per = key_ref.shape[1]
    for c in range(key_ref.shape[0]):
        key_ref[c] = done[c * per : (c + 1) * per, :]


def weight_kernel(
    rows_ref,
    wide_ref,
    half_ref,
    tab_ref,
    w1t_ref,
    wevt_ref,
    w2t_ref,
    w1_ref,
    wev_ref,
    w2_ref,
    wcol_ref,
):
    chans = wide_ref.shape[1]
    rad_rows = wide_ref.shape[0] - 2 * chans
    own = (tab_ref.shape[0] - 4 * rad_rows) // 2
    wa, wb, rad = wide_ref[0:chans, :], wide_ref[chans : 2 * chans, :], wide_ref[2 * chans :, :]
    w1, wenv, wval = [half_ref[i * chans : (i + 1) * chans, :] for i in range(3)]
    w2 = half_ref[3 * chans : 5 * chans, :]

    def flip(w):
        return w.astype(F32).T.astype(BF16)

    w1 = (0.5 * w1.astype(F32)).astype(BF16)
    wout = half_ref[5 * chans : 5 * chans + 1, :].astype(F32)
    w2 = (0.5 * w2.astype(F32)).astype(BF16)
    w2_out = (w2.astype(F32) * wout).astype(BF16)
    wval = (0.2 * wval.astype(F32)).astype(BF16)
    down = dot_nn(rad, w1.astype(F32), HIGH)
    w1_ref[0:chans, :] = w1
    w1_ref[chans:, :] = jnp.concatenate([down, jnp.zeros_like(down)], axis=0).astype(BF16)
    w2_ref[...] = w2_out[chans:, :]
    w1t_ref[...] = flip(w1)
    wevt_ref[0:chans, :] = flip(wenv)
    wevt_ref[chans:, :] = flip(wval)
    w2t_ref[:, 0:chans] = flip(w2[0:chans, :])
    w2t_ref[:, chans:] = flip(w2[chans:, :])
    wev_ref[:, 0:chans] = wenv
    wev_ref[:, chans : 2 * chans] = wval
    wev_ref[:, 2 * chans :] = w2_out[0:chans, :]
    wcol_ref[...] = jnp.broadcast_to(wout, (LANES, chans)).T
    feat = rows_ref[0:own, :]
    tab_ref[0:own, :] = dot_nn(feat, wa, HIGH)
    tab_ref[own : 2 * own, :] = dot_nn(feat, wb, HIGH)
    rad_hi, rad_lo = split(rad)
    tab_ref[2 * own :, :] = jnp.concatenate([rad_hi, rad_hi, rad_lo, jnp.zeros_like(rad)], axis=0)


def harmonics(ux, uy, uz):
    return [
        ux,
        uy,
        uz,
        ROOT3 * ux * uy,
        ROOT3 * uy * uz,
        ROOT3 * ux * uz,
        0.866 * (ux * ux - uy * uy),
        0.5 * (3.0 * uz * uz - 1.0),
    ]


def trig(half):
    turns = jnp.round(half)
    x = math.pi * (half - turns)
    odd = turns - 2.0 * jnp.floor(0.5 * turns)
    sign = 1.0 - 2.0 * odd
    x2 = x * x
    s = jnp.full_like(x, -1.0 / 39916800)
    for coef in (1.0 / 362880, -1.0 / 5040, 1.0 / 120, -1.0 / 6, 1.0):
        s = s * x2 + coef
    c = jnp.full_like(x, 1.0 / 479001600)
    for coef in (-1.0 / 3628800, 1.0 / 40320, -1.0 / 720, 1.0 / 24, -0.5, 1.0):
        c = c * x2 + coef
    return sign * x * s, sign * c


def waves(half, count):
    s1, c1 = trig(half)
    sins, coss = [s1], [c1]
    s0, c0 = jnp.zeros_like(s1), jnp.ones_like(c1)
    for _ in range(count - 1):
        sn = 2.0 * c1 * sins[-1] - s0
        cn = 2.0 * c1 * coss[-1] - c0
        s0, c0 = sins[-1], coss[-1]
        sins.append(sn)
        coss.append(cn)
    return sins, coss


def look_up(table_row, index):
    low = index & (LANES - 1)
    high = index >> 7
    result = jnp.zeros(index.shape, F32)
    for block in range(table_row.shape[1] // LANES):
        part = jnp.broadcast_to(table_row[:, block * LANES : (block + 1) * LANES], index.shape)
        got = jnp.take_along_axis(part, low, axis=1)
        result = jnp.where(high == block, got, result)
    return result


def in_lanes(tile):
    return jnp.concatenate([tile[r : r + 1, :] for r in range(tile.shape[0])], axis=1)


def one_hot(row, base, count):
    near = jnp.clip(row - base, -1, LANES).astype(BF16)
    iota = lax.broadcasted_iota(jnp.int32, (count, row.shape[1]), 0).astype(BF16)
    return jnp.where(iota == near, jnp.ones((), BF16), jnp.zeros((), BF16))


def sorted_size(edges):
    return 1 << (edges - 1).bit_length()


def main_kernel(plan, *refs):
    bound_ref, key_ref, pos_ref, wide_ref = refs[:4]
    came, refs = plan.cut(refs[4:], 0, 1, 2)
    half_ref, w1t_ref, wevt_ref, w2t_ref, w1_ref, wev_ref, w2_ref, wcol_ref = refs[:8]
    ae_ref, own_ref = refs[8:10]
    n_x = len(plan.groups[0])
    back_refs, rest_ref = refs[10 : 10 + n_x], refs[10 + n_x]
    (
        tab_ref,
        ghost_ref,
        place_ref,
        table_ref,
        y_ref,
        basis_ref,
        geo_ref,
        first_ref,
        dsilu_ref,
        ew_ref,
        val_ref,
        a_ref,
        env_ref,
        denv_ref,
        big_ref,
        dt_ref,
        dv_ref,
        dz2_ref,
        hots_ref,
        live_ref,
        dy_ref,
        db_ref,
        dr_ref,
        acc_ref,
        cacc_ref,
    ) = refs[11 + n_x :]
    own = pos_ref.shape[1]
    chans = w1_ref.shape[1]
    n_basis = (w1_ref.shape[0] - chans) // 2
    rows_all = key_ref.shape[0] * key_ref.shape[1]
    per = CHUNK // LANES
    subs = CHUNK // SUB
    sub_rows = SUB // LANES
    n_ghost = sum(len(c) * w for c, w in zip(CLASSES, plan.widths))
    n_tab = own + n_ghost
    n_sel = own + n_tab

    place_ref[...] = jnp.zeros_like(place_ref)
    at = 0
    for off in OFFSETS:
        live = plan.live(off)
        message, begin = plan.find(came, (0, 1, 2), None, [], off)
        ghost_ref[at : at + live, :] = message[begin : begin + live, :]
        place_ref[at : at + live, :] = spread(message[begin + live : begin + live + 1, :], live)
        at += live
    ghost_pos = dot_nt(group_rows(8), place_ref[...], HIGH)
    pos_t = jnp.concatenate([pos_ref[...], ghost_pos[0:3, :]], axis=1)
    f_hi, f_lo = split(ghost_ref[...])
    w_hi, w_lo = split(wide_ref[chans : 2 * chans, :])
    tab_ref[0 : 2 * own, :] = half_ref[0 : 2 * own, :]
    tab_ref[2 * own : n_sel, :] = dot_nn(
        jnp.concatenate([f_hi, f_lo, f_hi], axis=1).astype(BF16),
        jnp.concatenate([w_hi, w_hi, w_lo], axis=0).astype(BF16),
    )
    tab_ref[n_sel:, :] = half_ref[2 * own :, :]
    table_ref[...] = tab_ref[...].T.astype(BF16)

    keys = key_ref[...].reshape(rows_all, LANES)
    centre = keys >> OTHER_BITS
    other = keys & OTHER_MASK
    valid = (other != OTHER_MASK).astype(F32)
    r = [
        look_up(pos_t[a : a + 1, :], other) - look_up(pos_t[a : a + 1, 0:LANES], centre)
        for a in range(3)
    ]
    d2 = r[0] * r[0] + r[1] * r[1] + r[2] * r[2] + 0.01
    dist = jnp.sqrt(d2)
    inv = 1.0 / dist
    q = 1.0 / (1.0 + 0.25 * d2)
    envelope = q * q
    unit = [x * inv for x in r]
    for m, comp in enumerate(harmonics(*unit)):
        y_ref[pl.ds(m, rows_all, stride=8), :] = comp
    sins, _ = waves(0.5 * dist, n_basis)
    scale = envelope * inv
    for n in range(n_basis):
        basis_ref[pl.ds(n, rows_all, stride=n_basis), :] = sins[n] * scale
    for i, plane in enumerate((unit[0], unit[1], unit[2], dist, inv, q, envelope * valid, valid)):
        geo_ref[i] = plane.reshape(geo_ref.shape[1:])

    env_ref[...] = jnp.zeros_like(env_ref)
    denv_ref[...] = jnp.zeros_like(denv_ref)
    ae_ref[...] = jnp.zeros_like(ae_ref)
    acc_ref[...] = jnp.zeros_like(acc_ref)
    cacc_ref[...] = jnp.zeros_like(cacc_ref)
    dr_ref[...] = jnp.zeros_like(dr_ref)

    groups = bound_ref.shape[1] * SUB // sorted_size(rows_all * LANES)

    def window(k, s):
        first = (k * subs + s) * groups
        low = bound_ref[0, first]
        high = low
        for g in range(groups):
            high = jnp.maximum(high, bound_ref[1, first + g])
        start = pl.multiple_of((low >> 3) << 3, 8)
        more = lax.div(high - start, jnp.int32(WIN))
        return start, more

    most = jnp.int32(0)
    n_chunks = jnp.int32(0)
    for s in range(rows_all // sub_rows):
        most = jnp.maximum(most, window(s // subs, s % subs)[1])
        for g in range(groups):
            any_live = bound_ref[1, s * groups + g] >= 0
            n_chunks = jnp.where(any_live, s // subs + 1, n_chunks)


    def lanes_of(s, n):
        if isinstance(s, int):
            return slice(s * SUB, (s + n) * SUB)
        return pl.ds(pl.multiple_of(s * SUB, SUB), n * SUB)

    def tile_of(load, s, n):
        if isinstance(s, int):
            return load(slice(s * sub_rows, (s + n) * sub_rows))
        return jnp.concatenate(
            [load(pl.ds(s * sub_rows + j, 1)) for j in range(n * sub_rows)], axis=0
        )

    def plane(i, k, s, n):
        return tile_of(lambda rows: geo_ref[i, k, rows, :], s, n)

    def keys_of(k, s, n):
        return tile_of(lambda rows: key_ref[k, rows, :], s, n)

    def stacked(ref, k, s, n, height):
        first = (k * subs + s) * sub_rows
        tiles = [
            ref[pl.ds(pl.multiple_of((first + j) * height, 8), height), :]
            for j in range(n * sub_rows)
        ]
        return jnp.concatenate(tiles, axis=1)

    def window_hot(k, s, start):
        crow = in_lanes(keys_of(k, s, 1) >> OTHER_BITS) - start
        return lax.broadcasted_iota(jnp.int32, (WIN, SUB), 0) == crow

    def select(k, s, start):
        near = jnp.clip(in_lanes(keys_of(k, s, 1) >> OTHER_BITS) - start, -1, WIN).astype(BF16)
        hot = lax.broadcasted_iota(jnp.int32, (WIN, SUB), 0).astype(BF16) == near
        ys = stacked(y_ref, k, s, 1, 8)
        none = jnp.zeros((), BF16)
        parts = [jnp.where(hot, jnp.ones((), BF16), none)]
        for m in range(8):
            parts.append(jnp.where(hot, ys[m : m + 1, :].astype(BF16), none))
        return jnp.concatenate(parts, axis=0)

    def load_window(ref, start):
        return jnp.concatenate(
            [ref[m, pl.ds(start, WIN), :] for m in range(9)], axis=0
        ).astype(BF16)

    def add_window(ref, start, rows):
        for m in range(9):
            ref[m, pl.ds(start, WIN), :] += rows[m * WIN : (m + 1) * WIN, :]

    def each_window(k, s, n, slow, body):
        for j in range(n):
            start, more = window(k, s + j)
            body(s + j, j, start, True)
            if slow:

                def step(i, carry, s=s, j=j, start=start):
                    body(s + j, j, pl.multiple_of(start + i * WIN, 8), False)
                    return carry

                lax.fori_loop(1, more + 1, step, 0)

    def kept(k, s, start, fresh):
        return a_ref[k * subs + s] if fresh else select(k, s, start)

    def table_hots(k, s, n):
        row = in_lanes(keys_of(k, s, n) & OTHER_MASK)
        return [one_hot(row, at, min(LANES, n_tab - at)) for at in range(0, n_tab, LANES)]

    def part(j):
        return slice(j * SUB, (j + 1) * SUB)

    def phase_a(k, s, n, slow):
        lanes = lanes_of(s, n)
        crow = in_lanes(keys_of(k, s, n) >> OTHER_BITS)
        table = jnp.concatenate(table_hots(k, s, n), axis=0)
        hots_ref[k, :, lanes] = table
        hots = [one_hot(crow, 0, own), table]
        basis = stacked(basis_ref, k, s, n, n_basis)
        b_hi, b_lo = split(basis)
        hots.append(jnp.concatenate([b_hi, b_lo], axis=0).astype(BF16))
        hots.append(jnp.concatenate([b_hi, jnp.zeros_like(b_hi)], axis=0).astype(BF16))
        mixed = dot_nn(table_ref[...], jnp.concatenate(hots, axis=0)).astype(BF16)
        half = dot_nn(w1t_ref[...], mixed)
        up = 1.0 + jnp.tanh(half)
        first = half * up
        dsilu_ref[k, :, lanes] = (up + first * (2.0 - up)).astype(BF16)
        first = first.astype(BF16)
        first_ref[k, :, lanes] = first
        both = dot_nn(wevt_ref[...], first)
        ew = (both[0:chans] * in_lanes(plane(6, k, s, n))).astype(BF16)
        ew_ref[k, :, lanes] = ew
        val_ref[k, :, lanes] = both[chans:].astype(BF16)

        def body(s, j, start, fresh):
            a = select(k, s, start)
            if fresh:
                a_ref[k * subs + s] = a
            add_window(env_ref, start, dot_nt(a, ew[:, part(j)]))

        each_window(k, s, n, slow, body)

    def phase_b(k, s, n, slow):
        lanes = lanes_of(s, n)

        def totals(s, j, start, fresh):
            value = dot_tn(load_window(env_ref, start), kept(k, s, start, fresh))
            if fresh:
                big_ref[:, part(j)] = value
            else:
                big_ref[:, part(j)] += value

        each_window(k, s, n, slow, totals)
        total = big_ref[:, 0 : n * SUB]
        value = val_ref[k, :, lanes].astype(F32)
        scalar = (value * total).astype(BF16)
        half = dot_nn(w2t_ref[...], jnp.concatenate([first_ref[k, :, lanes], scalar], axis=0))
        up = 1.0 + jnp.tanh(half)
        second = half * up
        wcol = jnp.concatenate([wcol_ref[...]] * (n * sub_rows), axis=1)
        ee = jnp.sum(second * wcol, axis=0, keepdims=True)
        envv = in_lanes(plane(6, k, s, n))
        live = ee * in_lanes(plane(7, k, s, n))
        first_row = s * sub_rows
        for j in range(n * sub_rows):
            live_ref[k, pl.ds(first_row + j, 1), :] = live[:, j * LANES : (j + 1) * LANES]
        energy = ee * envv
        dz2 = (envv * (up + second * (2.0 - up))).astype(BF16)
        dz2_ref[k, :, lanes] = dz2
        dscalar = dot_nn(w2_ref[...], dz2)
        dt = (value * dscalar).astype(BF16)
        dt_ref[k, :, lanes] = dt
        dv_ref[k, :, lanes] = (total * dscalar).astype(BF16)

        def body(s, j, start, fresh):
            add_window(denv_ref, start, dot_nt(kept(k, s, start, fresh), dt[:, part(j)]))
            mine = jnp.where(window_hot(k, s, start), energy[:, part(j)], 0.0)
            half = mine[:, 0:LANES]
            for i in range(1, sub_rows):
                half = half + mine[:, i * LANES : (i + 1) * LANES]
            ae_ref[pl.ds(start, WIN), :] += half

        each_window(k, s, n, slow, body)

    def phase_c(k, s, n, slow):
        lanes = lanes_of(s, n)
        height = n * sub_rows

        def env_terms(s, j, start, fresh):
            a = kept(k, s, start, fresh)
            e_win = load_window(env_ref, start)
            d_win = load_window(denv_ref, start)
            dew = dot_tn(d_win, a)
            here = lanes_of(s, 1)
            pair = jnp.concatenate([dt_ref[k, :, here], ew_ref[k, :, here]], axis=0)
            prods = dot_nn(jnp.concatenate([e_win, d_win], axis=1)[WIN:], pair)
            hot = a[0:WIN].astype(F32)
            if fresh:
                big_ref[:, part(j)] = dew
            else:
                big_ref[:, part(j)] += dew
            for m in range(1, 9):
                row = jnp.sum(prods[(m - 1) * WIN : m * WIN] * hot, axis=0, keepdims=True)
                for i in range(sub_rows):
                    at = j * sub_rows + i
                    piece = row[:, i * LANES : (i + 1) * LANES]
                    if fresh:
                        dy_ref[m, at : at + 1, :] = piece
                    else:
                        dy_ref[m, at : at + 1, :] += piece

        each_window(k, s, n, slow, env_terms)
        dew = big_ref[:, 0 : n * SUB]
        dpre = (dew * in_lanes(plane(6, k, s, n))).astype(BF16)
        denv_row = jnp.sum(dew * ew_ref[k, :, lanes].astype(F32), axis=0, keepdims=True)
        for j in range(height):
            dy_ref[0, j : j + 1, :] = denv_row[:, j * LANES : (j + 1) * LANES]
        joined = jnp.concatenate([dpre, dv_ref[k, :, lanes], dz2_ref[k, :, lanes]], axis=0)
        dfirst = dot_nn(wev_ref[...], joined)
        dz1 = (dfirst * dsilu_ref[k, :, lanes].astype(F32)).astype(BF16)
        dboth = dot_nn(w1_ref[...], dz1)
        dmixed = dboth[0:chans].astype(BF16)
        dbasis = dboth[chans:]
        for j in range(height):
            db_ref[j * n_basis : (j + 1) * n_basis, :] = dbasis[
                0:n_basis, j * LANES : (j + 1) * LANES
            ]
        ux, uy, uz, dist, inv, q = [plane(i, k, s, n) for i in range(6)]
        envelope = q * q
        g = envelope * inv
        denvelope = -(q * envelope) * dist
        dg = (denvelope - g) * inv
        sins, coss = waves(0.5 * dist, n_basis)
        live = tile_of(lambda rows: live_ref[k, rows, :], s, n)
        y = [dy_ref[m, 0:height, :] for m in range(9)]
        ddist = (live + y[0] / envelope) * denvelope
        for i in range(n_basis):
            db = db_ref[pl.ds(i, height, stride=n_basis), :]
            ddist = ddist + db * (coss[i] * ((i + 1) * math.pi / 2.0) * g + sins[i] * dg)
        gx = y[1] + ROOT3 * (uy * y[4] + uz * y[6]) + (2.0 * 0.866) * ux * y[7]
        gy = y[2] + ROOT3 * (ux * y[4] + uz * y[5]) - (2.0 * 0.866) * uy * y[7]
        gz = y[3] + ROOT3 * (uy * y[5] + ux * y[6]) + 3.0 * uz * y[8]
        along = ddist - inv * (gx * ux + gy * uy + gz * uz)
        for i, (gu, u) in enumerate(((gx, ux), (gy, uy), (gz, uz))):
            hi, lo = split(inv * gu + along * u)
            dr_ref[pl.ds(i, height, stride=16), :] = hi
            dr_ref[pl.ds(3 + i, height, stride=16), :] = lo
        dr = jnp.concatenate([dr_ref[j * 16 : (j + 1) * 16, :] for j in range(height)], axis=1)
        moved = jnp.concatenate([dmixed, dr.astype(BF16)], axis=0)
        sums = dot_nt(hots_ref[k, :, lanes], moved)
        acc_ref[:, 0:chans] += sums[:, 0:chans]
        acc_ref[:, chans : chans + 16] += sums[:, chans:]

        def body(s, j, start, fresh):
            hot = a_ref[k * subs + s, 0:WIN, :] if fresh else window_hot(k, s, start).astype(BF16)
            mine = dot_nt(hot, moved[:, part(j)])
            cacc_ref[pl.ds(start, WIN), 0:chans] += mine[:, 0:chans]
            cacc_ref[pl.ds(start, WIN), chans : chans + 16] += mine[:, chans:]

        each_window(k, s, n, slow, body)

    for phase in (phase_a, phase_b, phase_c):

        @pl.when(most == 0)
        def _(phase=phase):
            def chunk(k, carry):
                phase(k, 0, subs, False)
                return carry

            lax.fori_loop(0, n_chunks, chunk, 0)

        @pl.when(most != 0)
        def _(phase=phase):
            def sub(i, carry):
                phase(lax.div(i, subs), lax.rem(i, subs), 1, True)
                return carry

            lax.fori_loop(0, n_chunks * subs, sub, 0)

    own_ref[0:own, :] = cacc_ref[0:own, :]
    own_ref[own:, :] = acc_ref[0:own, :]
    row = lax.broadcasted_iota(jnp.int32, (LANES, LANES), 0)
    group = lax.broadcasted_iota(jnp.int32, (LANES, LANES), 1) // GROUP
    both = ((group < 3) & ((row == group) | (row == group + 3))).astype(F32)
    places = dot_nn(acc_ref[own:, LANES:], both, HIGH)
    found = {}
    at = own
    for off in OFFSETS:
        found[off] = at
        at += plan.live(off)
    for blocks, ref in zip(
        plan.groups[0] + [plan.held_rest], tuple(back_refs) + (rest_ref,)
    ):
        for off, row in plan.spans(blocks):
            live = plan.live(off)
            at = found[off]
            ref[row : row + live, :] = acc_ref[at : at + live, 0:chans]
            block = places[at - own : at - own + live, :]
            ref[row + live : row + live + 1, :] = jnp.sum(diagonal(block), axis=0, keepdims=True)


def returned_sums(plan, came, axes, messages, first, sel_ref, both_ref):
    chans = both_ref.shape[1] - LANES
    both_ref[...] = jnp.zeros_like(both_ref)
    at = 0
    for blocks in messages:
        for off, row in plan.spans(blocks):
            live = plan.live(off)
            src, begin = plan.find(came, axes, None, [], off)
            here = slice(at + row, at + row + live)
            both_ref[here, 0:chans] = src[begin : begin + live, :]
            both_ref[here, chans:] = spread(src[begin + live : begin + live + 1, :], live)
        at += plan.total(blocks)
    hot = sel_ref[first : first + at, :].astype(BF16)
    return dot_exact(hot, both_ref[...], ((0,), (0,)))


def own_kernel(plan, ae_ref, own_ref, wide_ref, sel_ref, *refs):
    came, refs = plan.cut(refs, 0, 1)
    energy_ref, fg_ref, force_ref, both_ref = refs
    chans = fg_ref.shape[1]
    own = force_ref.shape[1]
    first = sum(plan.total(blocks) for blocks in plan.groups[2])
    sums = returned_sums(plan, came, (1, 0), [plan.own_rest], first, sel_ref, both_ref)
    energy_ref[...] = jnp.sum(ae_ref[0:own, :].T, axis=0, keepdims=True)
    fg_ref[...] = dot_nt(own_ref[0:own, 0:chans], wide_ref[0:chans, :], HIGH) + dot_nt(
        own_ref[own:, 0:chans] + sums[:, 0:chans], wide_ref[chans : 2 * chans, :], HIGH
    )
    force = (own_ref[own:, LANES:] - own_ref[0:own, LANES:]).T
    total = dot_nt(group_rows(8), sums[:, chans:], HIGH)
    force_ref[...] = force[0:3, :] + force[3:6, :] + total[0:3, :]


def last_kernel(plan, sel_ref, fg_ref, force_ref, wide_ref, *refs):
    came, refs = plan.cut(refs, 2)
    out_force_ref, out_fg_ref, both_ref = refs
    chans = fg_ref.shape[1]
    sums = returned_sums(plan, came, (2,), plan.groups[2], 0, sel_ref, both_ref)
    s_hi, s_lo = split(sums[:, 0:chans])
    w_hi, w_lo = split(wide_ref[chans : 2 * chans, :])
    out_fg_ref[...] = fg_ref[...] + dot_nt(
        jnp.concatenate([s_hi, s_lo, s_hi], axis=1).astype(BF16),
        jnp.concatenate([w_hi, w_hi, w_lo], axis=1).astype(BF16),
    )
    total = dot_nt(group_rows(8), sums[:, chans:], HIGH)
    out_force_ref[...] = -(force_ref[...] + total[0:3, :])


def stack(*arrays):
    dtype = arrays[0].dtype
    tile = 32 // dtype.itemsize
    starts = [0]
    for x in arrays:
        starts.append(starts[-1] + -(-x.shape[1] // tile) * tile)
    total = None
    for x, at in zip(arrays, starts):
        below = starts[-1] - at - x.shape[1]
        part = jnp.pad(x.astype(dtype), ((0, 0), (at, below), (0, LANES - x.shape[2])))
        total = part if total is None else total + part
    return total[0]


def local(
    positions,
    atom_features,
    send_face,
    send_edge,
    send_corner,
    centre,
    other,
    edge_count,
    w_proj_a,
    w_proj_b,
    w_radial,
    w_first,
    w_env,
    w_value,
    w_second,
    w_out,
):
    own, chans = atom_features.shape
    edges = centre.shape[0]
    n_basis = w_radial.shape[0]
    plan = Plan(
        [send_face.shape[2], send_edge.shape[2], send_corner.shape[2]],
        [lax.axis_size(axis) for axis in AXES],
    )
    n_ghost = sum(len(c) * w for c, w in zip(CLASSES, plan.widths))
    n_sel = 2 * own + n_ghost
    n_send = sum(plan.total(blocks) for blocks in plan.groups[2]) + plan.total(plan.own_rest)
    n_table = n_sel + 4 * n_basis
    edges_up = -(-edges // CHUNK) * CHUNK
    n_rows = edges_up // LANES
    n_chunks = edges_up // CHUNK

    with jax.named_scope("prep"):
        atom_features, plan.even = lax.optimization_barrier((atom_features, plan.even))
        rows = stack(atom_features[None], edge_count.reshape(1, 1, 1))
        *sends, own_rows, sel = pl.pallas_call(
            lambda *refs: prep_kernel(plan, *refs),
            out_shape=plan.shapes(2, chans)
            + [shape(plan.total(plan.own_rest), chans), shape(n_send, own)],
            in_specs=[VMEM] * 5,
            out_specs=[VMEM] * (len(plan.groups[2]) + 2),
            scratch_shapes=[pltpu.VMEM((LANES, LANES), F32)],
            compiler_params=PARAMS,
        )(
            rows,
            positions,
            jnp.transpose(send_face, (1, 0, 2)),
            jnp.transpose(send_edge, (0, 2, 1)),
            jnp.transpose(send_corner, (0, 2, 1)),
        )

    came = {}
    with jax.named_scope("halo_z"):
        came[2] = plan.send(2, sends)

    with jax.named_scope("group_edges"):
        pad = [(0, edges_up - edges)]
        regs = max(sorted_size(edges_up) // (8 * LANES), 1)
        key, bounds = pl.pallas_call(
            lambda *refs: sort_kernel(own, *refs),
            out_shape=[
                shape(n_chunks, CHUNK // LANES, LANES, dtype=jnp.int32),
                shape(2, LANES, dtype=jnp.int32),
            ],
            in_specs=[VMEM] * 3,
            out_specs=[VMEM] * 2,
            scratch_shapes=[pltpu.VMEM((16 * regs, LANES), F32)],
            compiler_params=PARAMS,
        )(
            rows,
            jnp.pad(centre, pad).reshape(n_rows, LANES),
            jnp.pad(other, pad).reshape(n_rows, LANES),
        )

    with jax.named_scope("halo_y"):
        given = (w_proj_a, w_proj_b, w_radial, w_first, w_env, w_value, w_second, w_out)
        came[2], key, bounds, given = lax.optimization_barrier((came[2], key, bounds, given))
        w_proj_a, w_proj_b, w_radial, w_first, w_env, w_value, w_second, w_out = given
        came[1] = plan.send(1, glue(plan, 1, (2,), plan.own_rest, own_rows, came))

    with jax.named_scope("weights"):
        wide = stack(w_proj_a[None], w_proj_b[None], w_radial[None])
        narrow = stack(
            w_first[None], w_env[None], w_value[None], w_second[None], w_out[None, None, :]
        )
        half, *weights = pl.pallas_call(
            weight_kernel,
            out_shape=[
                shape(2 * own + 4 * n_basis, chans),
                shape(chans, chans, dtype=BF16),
                shape(2 * chans, chans, dtype=BF16),
                shape(chans, 2 * chans, dtype=BF16),
                shape(chans + 2 * n_basis, chans, dtype=BF16),
                shape(chans, 3 * chans, dtype=BF16),
                shape(chans, chans, dtype=BF16),
                shape(chans, LANES),
            ],
            in_specs=[VMEM] * 3,
            out_specs=[VMEM] * 8,
            compiler_params=PARAMS,
        )(rows, wide, narrow)

    with jax.named_scope("halo_x"):
        came[1], half, weights = lax.optimization_barrier((came[1], half, weights))
        came[0] = plan.send(0, glue(plan, 0, (1, 2), plan.own_rest, own_rows, came))

    planes = (n_chunks, chans, CHUNK)
    scratch = [
        pltpu.VMEM((n_table, chans), F32),
        pltpu.VMEM((n_ghost, chans), F32),
        pltpu.VMEM((-(-n_ghost // LANES) * LANES, LANES), F32),
        pltpu.VMEM((chans, n_table), BF16),
        pltpu.VMEM((n_rows * 8, LANES), F32),
        pltpu.VMEM((n_rows * n_basis, LANES), F32),
        pltpu.VMEM((8, n_chunks, CHUNK // LANES, LANES), F32),
        pltpu.VMEM(planes, BF16),
        pltpu.VMEM(planes, BF16),
        pltpu.VMEM(planes, BF16),
        pltpu.VMEM(planes, BF16),
        pltpu.VMEM((edges_up // SUB, 9 * WIN, SUB), BF16),
        pltpu.VMEM((9, own + WIN, chans), F32),
        pltpu.VMEM((9, own + WIN, chans), F32),
        pltpu.VMEM((chans, CHUNK), F32),
        pltpu.VMEM(planes, BF16),
        pltpu.VMEM(planes, BF16),
        pltpu.VMEM(planes, BF16),
        pltpu.VMEM((n_chunks, n_sel - own, CHUNK), BF16),
        pltpu.VMEM((n_chunks, CHUNK // LANES, LANES), F32),
        pltpu.VMEM((9, CHUNK // LANES, LANES), F32),
        pltpu.VMEM((CHUNK // LANES * n_basis, LANES), F32),
        pltpu.VMEM((CHUNK // LANES * 16, LANES), F32),
        pltpu.VMEM((n_sel - own, 2 * LANES), F32),
        pltpu.VMEM((own + WIN, 2 * LANES), F32),
    ]
    with jax.named_scope("layer"):
        given = [bounds, key, positions, wide]
        given += [*came[0], *came[1], *came[2], half, *weights]
        atom_sums, own_sums, *back, held = pl.pallas_call(
            lambda *refs: main_kernel(plan, *refs),
            out_shape=[shape(own + WIN, LANES), shape(2 * own, 2 * LANES)]
            + plan.shapes(0, chans)
            + [shape(plan.total(plan.held_rest), chans)],
            in_specs=[SMEM] + [VMEM] * (len(given) - 1),
            out_specs=[VMEM] * (3 + len(plan.groups[0])),
            scratch_shapes=scratch,
            compiler_params=PARAMS,
        )(*given)

    with jax.named_scope("halo_back"):
        home = {0: plan.send(0, back, back=True)}
        home[1] = plan.send(1, glue(plan, 1, (0,), plan.held_rest, held, home), back=True)
        home[2] = plan.send(2, glue(plan, 2, (1, 0), plan.held_rest, held, home), back=True)

    with jax.named_scope("own_part"):
        given = [atom_sums, own_sums, wide, sel, *home[0], *home[1]]
        energy, fg, force = pl.pallas_call(
            lambda *refs: own_kernel(plan, *refs),
            out_shape=[shape(1, own), shape(own, chans), shape(3, own)],
            in_specs=[VMEM] * len(given),
            out_specs=[VMEM] * 3,
            scratch_shapes=[pltpu.VMEM((plan.total(plan.own_rest), chans + LANES), F32)],
            compiler_params=PARAMS,
        )(*given)

    with jax.named_scope("owner_sums"):
        given = [sel, fg, force, wide, *home[2]]
        n_z = n_send - plan.total(plan.own_rest)
        forces, feature_grad = pl.pallas_call(
            lambda *refs: last_kernel(plan, *refs),
            out_shape=[shape(3, own), shape(own, chans)],
            in_specs=[VMEM] * len(given),
            out_specs=[VMEM] * 2,
            scratch_shapes=[pltpu.VMEM((n_z, chans + LANES), F32)],
            compiler_params=PARAMS,
        )(*given)
    return forces, energy.reshape(own), feature_grad


def solution(mesh):
    shard = P(AXES)
    return jax.shard_map(
        local,
        mesh=mesh,
        in_specs=(
            P(None, AXES),
            P(AXES, None),
            P(AXES, None, None),
            P(AXES, None, None),
            P(AXES, None, None),
            shard,
            shard,
            shard,
        )
        + (P(),) * 8,
        out_specs=(P(None, AXES), shard, P(AXES, None)),
        check_vma=False,
    )
```

```python
import math

import jax
import jax.numpy as jnp
from jax import lax
from jax.experimental import pallas as pl
from jax.experimental.pallas import tpu as pltpu
from jax.sharding import PartitionSpec as P

F32 = jnp.float32
BF16 = jnp.bfloat16
HIGH = lax.Precision.HIGHEST
AXES = ("gx", "gy", "gz")
CHUNK = 3072
SUB = 256
WIN = 16
OTHER_BITS = 9
OTHER_MASK = (1 << OTHER_BITS) - 1
LANES = 128
ROOT3 = 1.732


VMEM = pl.BlockSpec(memory_space=pltpu.VMEM)
SMEM = pl.BlockSpec(memory_space=pltpu.SMEM)
PARAMS = pltpu.CompilerParams(vmem_limit_bytes=52 * 2**20)


def shape(*dims, dtype=F32):
    return jax.ShapeDtypeStruct(dims, dtype)


def dot_nn(a, b, precision=None):
    return lax.dot_general(
        a, b, (((1,), (0,)), ((), ())), preferred_element_type=F32, precision=precision
    )


def dot_nt(a, b, precision=None):
    return lax.dot_general(
        a, b, (((1,), (1,)), ((), ())), preferred_element_type=F32, precision=precision
    )


def dot_tn(a, b, precision=None):
    return lax.dot_general(
        a, b, (((0,), (0,)), ((), ())), preferred_element_type=F32, precision=precision
    )


def offset_classes():
    classes = [[], [], []]
    for a in (-1, 0, 1):
        for b in (-1, 0, 1):
            for c in (-1, 0, 1):
                if (a, b, c) != (0, 0, 0):
                    classes[abs(a) + abs(b) + abs(c) - 1].append((a, b, c))
    return classes


CLASSES = offset_classes()


OFFSETS = [off for group in CLASSES for off in group]


def kind(off):
    return abs(off[0]) + abs(off[1]) + abs(off[2]) - 1


class Plan:
    def __init__(self, widths, sizes):
        self.widths = widths
        self.sizes = sizes
        self.groups = [self.group(a) for a in range(3)]
        self.even = [lax.axis_index(axis) % 2 == 0 for axis in AXES]
        self.own_rest = [off for off in OFFSETS if off[2] == 0]
        self.held_rest = [off for off in OFFSETS if off[0] == 0]

    def group(self, a):
        groups = {}
        for off in OFFSETS:
            if off[a] != 0:
                groups.setdefault(off[a] % self.sizes[a], []).append(off)
        return list(groups.values())

    def live(self, off):
        return self.widths[kind(off)]

    def rows(self, off):
        return self.live(off) + 1

    def total(self, blocks):
        return sum(self.rows(off) for off in blocks)

    def spans(self, blocks):
        at = 0
        for off in blocks:
            yield off, at
            at += self.rows(off)

    def place(self, a, off):
        for g, blocks in enumerate(self.groups[a]):
            if off in blocks:
                return g, dict(self.spans(blocks))[off]
        raise KeyError(off)

    def find(self, came, axes, rest_ref, rest, off):
        for a in axes:
            if off[a] != 0:
                g, begin = self.place(a, off)
                return came[a][g], begin
        return rest_ref, dict(self.spans(rest))[off]

    def cut(self, refs, *axes):
        came = {}
        for a in axes:
            n = len(self.groups[a])
            came[a], refs = refs[:n], refs[n:]
        return came, refs

    def shapes(self, a, chans):
        return [shape(self.total(blocks), chans) for blocks in self.groups[a]]

    def send(self, a, messages, back=False):
        n = self.sizes[a]
        steps = [-blocks[0][a] if back else blocks[0][a] for blocks in self.groups[a]]
        if n % 2 or n == 2:
            return [
                lax.ppermute(message, AXES[a], [(i, (i + step) % n) for i in range(n)])
                for step, message in zip(steps, messages)
            ]
        up, down = steps.index(1), steps.index(-1)
        even = self.even[a]
        ahead = [(i, i + 1 - 2 * (i % 2)) for i in range(n)]
        behind = [(i, (i - 1 + 2 * (i % 2)) % n) for i in range(n)]
        first = lax.ppermute(jnp.where(even, messages[up], messages[down]), AXES[a], ahead)
        second = lax.ppermute(jnp.where(even, messages[down], messages[up]), AXES[a], behind)
        got = [None, None]
        got[up] = jnp.where(even, second, first)
        got[down] = jnp.where(even, first, second)
        return got


GROUP = 32


def group_rows(count):
    row = lax.broadcasted_iota(jnp.int32, (count, LANES), 0)
    group = lax.broadcasted_iota(jnp.int32, (count, LANES), 1) // GROUP
    return (row == group).astype(F32) * (group < 3).astype(F32)


def diagonal(x):
    row = lax.broadcasted_iota(jnp.int32, x.shape, 0)
    lane = lax.broadcasted_iota(jnp.int32, x.shape, 1)
    return jnp.where((lane & (GROUP - 1)) == row, x, 0.0)


def spread(row, live):
    return diagonal(jnp.broadcast_to(row, (live, LANES)))


def split(x):
    high = x.astype(BF16).astype(F32)
    return high, x - high


def dot_exact(hot, x, dims):
    high, low = split(x)
    both = jnp.concatenate([high, low], axis=1).astype(BF16)
    out = lax.dot_general(hot, both, (dims, ((), ())), preferred_element_type=F32)
    return out[:, 0 : x.shape[1]] + out[:, x.shape[1] :]


def prep_kernel(plan, rows_ref, pos_ref, face_ref, edge_ref, corner_ref, *outs):
    n_z = len(plan.groups[2])
    sends, rest_ref, sel_ref, turn_ref = outs[:n_z], outs[n_z], outs[n_z + 1], outs[n_z + 2]
    own = sel_ref.shape[1]
    lane = lax.broadcasted_iota(jnp.int32, (1, own), 1).astype(F32)
    turn_ref[...] = jnp.zeros_like(turn_ref)
    for key in range(face_ref.shape[0]):
        turn_ref[key : key + 1, 0 : face_ref.shape[2]] = face_ref[key].astype(F32)
    columns = [turn_ref[...].T, edge_ref[0].astype(F32), corner_ref[0].astype(F32)]
    sel_ref[...] = jnp.zeros_like(sel_ref)
    messages = plan.groups[2] + [plan.own_rest]
    at = 0
    for blocks in messages:
        for off, begin in plan.spans(blocks):
            key = CLASSES[kind(off)].index(off)
            live = plan.live(off)
            column = columns[kind(off)][0:live, key : key + 1]
            sel_ref[at + begin : at + begin + live, :] = (column == lane).astype(F32)
        at += plan.total(blocks)
    pos = dot_tn(pos_ref[...], group_rows(3), HIGH)
    sel = sel_ref[...]
    rows = dot_nn(sel, rows_ref[0:own, :], HIGH)
    places = dot_nn(sel, pos, HIGH)
    at = 0
    for blocks, send in zip(messages, tuple(sends) + (rest_ref,)):
        count = plan.total(blocks)
        send[...] = rows[at : at + count, :]
        for off, begin in plan.spans(blocks):
            live = plan.live(off)
            block = places[at + begin : at + begin + live, :]
            send[begin + live : begin + live + 1, :] = jnp.sum(
                diagonal(block), axis=0, keepdims=True
            )
        at += count


def glue_kernel(plan, a, axes, rest, *refs):
    rest_ref = refs[0]
    came, outs = plan.cut(refs[1:], *axes)
    for blocks, out in zip(plan.groups[a], outs):
        for off, row in plan.spans(blocks):
            src, begin = plan.find(came, axes, rest_ref, rest, off)
            out[row : row + plan.rows(off), :] = src[begin : begin + plan.rows(off), :]


def glue(plan, a, axes, rest, rest_rows, came):
    given = [rest_rows] + [message for axis in axes for message in came[axis]]
    outs = plan.shapes(a, rest_rows.shape[1])
    return pl.pallas_call(
        lambda *refs: glue_kernel(plan, a, axes, rest, *refs),
        out_shape=outs,
        in_specs=[VMEM] * len(given),
        out_specs=[VMEM] * len(outs),
        compiler_params=PARAMS,
    )(*given)


def sort_kernel(own, count_ref, centre_ref, other_ref, key_ref, bound_ref, turn_ref):
    dead = (own - 1) * (OTHER_MASK + 1) + OTHER_MASK
    rows = centre_ref.shape[0]
    regs = turn_ref.shape[0] // 16
    group = regs * 8
    row = lax.broadcasted_iota(jnp.int32, (rows, LANES), 0)
    lane = lax.broadcasted_iota(jnp.int32, (rows, LANES), 1)
    count = count_ref[count_ref.shape[0] - 8 : count_ref.shape[0] - 7, 0:1].astype(jnp.int32)
    live = row * LANES + lane < count
    centre = centre_ref[...]
    key = jnp.where(live, (centre << OTHER_BITS) + other_ref[...], dead).astype(F32)
    x = [key[8 * v : 8 * v + 8, :] for v in range(rows // 8)]
    x += [jnp.full((8, LANES), float(dead), F32)] * (regs - len(x))
    n_windows = own // WIN
    free = regs - rows // 8
    if n_windows * SUB <= free * 8 * LANES:
        window = jnp.where(live, centre // WIN, -1)
        need = []
        used = jnp.zeros((1, 1), F32)
        for w in range(n_windows):
            hits = jnp.sum((window == w).astype(F32), axis=0, keepdims=True)
            hits = jnp.sum(hits, axis=1, keepdims=True)
            whole = jnp.floor((hits + (SUB - 1)) * (1.0 / SUB)) * SUB
            used = used + whole
            need.append(whole - hits)
        fits = used <= float(rows * LANES)
        slot = lax.broadcasted_iota(jnp.int32, (8, LANES), 0) * LANES
        slot = slot + lax.broadcasted_iota(jnp.int32, (8, LANES), 1)
        per_reg = 8 * LANES // SUB
        for w in range(n_windows):
            v = rows // 8 + w // per_reg
            at = slot - (w % per_reg) * SUB
            take = (at >= 0) & (at.astype(F32) < need[w]) & fits
            mark = float((w * WIN + WIN - 1) * (OTHER_MASK + 1) + OTHER_MASK)
            x[v] = jnp.where(take, mark, x[v])
    s = lax.broadcasted_iota(jnp.int32, (8, LANES), 0)
    ln = lax.broadcasted_iota(jnp.int32, (8, LANES), 1)
    base = ln * group + s * regs

    def sign(k, v):
        return jnp.where(((base + v) & k) == 0, 1.0, -1.0).astype(F32)

    last = [jnp.ones((8, LANES), F32)] * regs
    total = group * LANES
    k = 2
    while k <= total:
        signs = [sign(k, v) for v in range(regs)] if k < total else [1.0] * regs
        x = [x[v] * (last[v] * signs[v]) for v in range(regs)]
        last = signs
        j = k // 2
        while j >= 1:
            if j < regs:
                for v in range(regs):
                    if v & j == 0:
                        a, b = x[v], x[v | j]
                        x[v], x[v | j] = jnp.minimum(a, b), jnp.maximum(a, b)
            else:
                axis, step, size, ids = (
                    (0, j // regs, 8, s) if j < group else (1, j // group, LANES, ln)
                )
                low = (ids & step) == 0
                for v in range(regs):
                    up = pltpu.roll(x[v], size - step, axis)
                    if 2 * step == size:
                        mate = up
                    else:
                        mate = jnp.where(low, up, pltpu.roll(x[v], step, axis))
                    x[v] = jnp.where(low, jnp.minimum(x[v], mate), jnp.maximum(x[v], mate))
            j //= 2
        k *= 2
    least = x[0]
    most = jnp.where(x[0] == float(dead), -1.0, x[0])
    for v in range(1, regs):
        least = jnp.minimum(least, x[v])
        most = jnp.maximum(most, jnp.where(x[v] == float(dead), -1.0, x[v]))
    bound_ref[0:1, :] = jnp.min(least, axis=0, keepdims=True).astype(jnp.int32) >> OTHER_BITS
    bound_ref[1:2, :] = jnp.max(most, axis=0, keepdims=True).astype(jnp.int32) >> OTHER_BITS
    turned = jnp.concatenate(x + [jnp.zeros((LANES - group, LANES), F32)], axis=0).T
    turn_ref[...] = turned
    ratio = LANES // group
    parts = [
        turn_ref[pl.ds(i, rows, stride=ratio), 0:group] for i in range(ratio)
    ]
    done = jnp.concatenate(parts, axis=1).astype(jnp.int32)
    per = key_ref.shape[1]
    for c in range(key_ref.shape[0]):
        key_ref[c] = done[c * per : (c + 1) * per, :]


def weight_kernel(
    rows_ref,
    wide_ref,
    half_ref,
    tab_ref,
    w1t_ref,
    wevt_ref,
    w2t_ref,
    w1_ref,
    wev_ref,
    w2_ref,
    wcol_ref,
):
    chans = wide_ref.shape[1]
    rad_rows = wide_ref.shape[0] - 2 * chans
    own = (tab_ref.shape[0] - 4 * rad_rows) // 2
    wa, wb, rad = wide_ref[0:chans, :], wide_ref[chans : 2 * chans, :], wide_ref[2 * chans :, :]
    w1, wenv, wval = [half_ref[i * chans : (i + 1) * chans, :] for i in range(3)]
    w2 = half_ref[3 * chans : 5 * chans, :]

    def flip(w):
        return w.astype(F32).T.astype(BF16)

    w1 = (0.5 * w1.astype(F32)).astype(BF16)
    wout = half_ref[5 * chans : 5 * chans + 1, :].astype(F32)
    w2 = (0.5 * w2.astype(F32)).astype(BF16)
    w2_out = (w2.astype(F32) * wout).astype(BF16)
    wval = (0.2 * wval.astype(F32)).astype(BF16)
    down = dot_nn(rad, w1.astype(F32), HIGH)
    w1_ref[0:chans, :] = w1
    w1_ref[chans:, :] = jnp.concatenate([down, jnp.zeros_like(down)], axis=0).astype(BF16)
    w2_ref[...] = w2_out[chans:, :]
    w1t_ref[...] = flip(w1)
    wevt_ref[0:chans, :] = flip(wenv)
    wevt_ref[chans:, :] = flip(wval)
    w2t_ref[:, 0:chans] = flip(w2[0:chans, :])
    w2t_ref[:, chans:] = flip(w2[chans:, :])
    wev_ref[:, 0:chans] = wenv
    wev_ref[:, chans : 2 * chans] = wval
    wev_ref[:, 2 * chans :] = w2_out[0:chans, :]
    wcol_ref[...] = jnp.broadcast_to(wout, (LANES, chans)).T
    feat = rows_ref[0:own, :]
    tab_ref[0:own, :] = dot_nn(feat, wa, HIGH)
    tab_ref[own : 2 * own, :] = dot_nn(feat, wb, HIGH)
    rad_hi, rad_lo = split(rad)
    tab_ref[2 * own :, :] = jnp.concatenate([rad_hi, rad_hi, rad_lo, jnp.zeros_like(rad)], axis=0)


def harmonics(ux, uy, uz):
    return [
        ux,
        uy,
        uz,
        ROOT3 * ux * uy,
        ROOT3 * uy * uz,
        ROOT3 * ux * uz,
        0.866 * (ux * ux - uy * uy),
        0.5 * (3.0 * uz * uz - 1.0),
    ]


def trig(half):
    turns = jnp.round(half)
    x = math.pi * (half - turns)
    odd = turns - 2.0 * jnp.floor(0.5 * turns)
    sign = 1.0 - 2.0 * odd
    x2 = x * x
    s = jnp.full_like(x, -1.0 / 39916800)
    for coef in (1.0 / 362880, -1.0 / 5040, 1.0 / 120, -1.0 / 6, 1.0):
        s = s * x2 + coef
    c = jnp.full_like(x, 1.0 / 479001600)
    for coef in (-1.0 / 3628800, 1.0 / 40320, -1.0 / 720, 1.0 / 24, -0.5, 1.0):
        c = c * x2 + coef
    return sign * x * s, sign * c


def waves(half, count):
    s1, c1 = trig(half)
    sins, coss = [s1], [c1]
    s0, c0 = jnp.zeros_like(s1), jnp.ones_like(c1)
    for _ in range(count - 1):
        sn = 2.0 * c1 * sins[-1] - s0
        cn = 2.0 * c1 * coss[-1] - c0
        s0, c0 = sins[-1], coss[-1]
        sins.append(sn)
        coss.append(cn)
    return sins, coss


def look_up(table_row, index):
    low = index & (LANES - 1)
    high = index >> 7
    result = jnp.zeros(index.shape, F32)
    for block in range(table_row.shape[1] // LANES):
        part = jnp.broadcast_to(table_row[:, block * LANES : (block + 1) * LANES], index.shape)
        got = jnp.take_along_axis(part, low, axis=1)
        result = jnp.where(high == block, got, result)
    return result


def in_lanes(tile):
    return jnp.concatenate([tile[r : r + 1, :] for r in range(tile.shape[0])], axis=1)


def one_hot(row, base, count):
    near = jnp.clip(row - base, -1, LANES).astype(BF16)
    iota = lax.broadcasted_iota(jnp.int32, (count, row.shape[1]), 0).astype(BF16)
    return jnp.where(iota == near, jnp.ones((), BF16), jnp.zeros((), BF16))


def sorted_size(edges):
    return 1 << (edges - 1).bit_length()


def main_kernel(plan, *refs):
    bound_ref, key_ref, pos_ref, wide_ref = refs[:4]
    came, refs = plan.cut(refs[4:], 0, 1, 2)
    half_ref, w1t_ref, wevt_ref, w2t_ref, w1_ref, wev_ref, w2_ref, wcol_ref = refs[:8]
    ae_ref, own_ref = refs[8:10]
    n_x = len(plan.groups[0])
    back_refs, rest_ref = refs[10 : 10 + n_x], refs[10 + n_x]
    (
        tab_ref,
        ghost_ref,
        place_ref,
        table_ref,
        y_ref,
        basis_ref,
        geo_ref,
        first_ref,
        dsilu_ref,
        ew_ref,
        val_ref,
        a_ref,
        env_ref,
        denv_ref,
        big_ref,
        dt_ref,
        dv_ref,
        dz2_ref,
        hots_ref,
        live_ref,
        dy_ref,
        db_ref,
        dr_ref,
        acc_ref,
        cacc_ref,
    ) = refs[11 + n_x :]
    own = pos_ref.shape[1]
    chans = w1_ref.shape[1]
    n_basis = (w1_ref.shape[0] - chans) // 2
    rows_all = key_ref.shape[0] * key_ref.shape[1]
    per = CHUNK // LANES
    subs = CHUNK // SUB
    sub_rows = SUB // LANES
    n_ghost = sum(len(c) * w for c, w in zip(CLASSES, plan.widths))
    n_tab = own + n_ghost
    n_sel = own + n_tab

    place_ref[...] = jnp.zeros_like(place_ref)
    at = 0
    for off in OFFSETS:
        live = plan.live(off)
        message, begin = plan.find(came, (0, 1, 2), None, [], off)
        ghost_ref[at : at + live, :] = message[begin : begin + live, :]
        place_ref[at : at + live, :] = spread(message[begin + live : begin + live + 1, :], live)
        at += live
    ghost_pos = dot_nt(group_rows(8), place_ref[...], HIGH)
    pos_t = jnp.concatenate([pos_ref[...], ghost_pos[0:3, :]], axis=1)
    f_hi, f_lo = split(ghost_ref[...])
    w_hi, w_lo = split(wide_ref[chans : 2 * chans, :])
    tab_ref[0 : 2 * own, :] = half_ref[0 : 2 * own, :]
    tab_ref[2 * own : n_sel, :] = dot_nn(
        jnp.concatenate([f_hi, f_lo, f_hi], axis=1).astype(BF16),
        jnp.concatenate([w_hi, w_hi, w_lo], axis=0).astype(BF16),
    )
    tab_ref[n_sel:, :] = half_ref[2 * own :, :]
    table_ref[...] = tab_ref[...].T.astype(BF16)

    keys = key_ref[...].reshape(rows_all, LANES)
    centre = keys >> OTHER_BITS
    other = keys & OTHER_MASK
    valid = (other != OTHER_MASK).astype(F32)
    r = [
        look_up(pos_t[a : a + 1, :], other) - look_up(pos_t[a : a + 1, 0:LANES], centre)
        for a in range(3)
    ]
    d2 = r[0] * r[0] + r[1] * r[1] + r[2] * r[2] + 0.01
    dist = jnp.sqrt(d2)
    inv = 1.0 / dist
    q = 1.0 / (1.0 + 0.25 * d2)
    envelope = q * q
    unit = [x * inv for x in r]
    for m, comp in enumerate(harmonics(*unit)):
        y_ref[pl.ds(m, rows_all, stride=8), :] = comp
    sins, _ = waves(0.5 * dist, n_basis)
    scale = envelope * inv
    for n in range(n_basis):
        basis_ref[pl.ds(n, rows_all, stride=n_basis), :] = sins[n] * scale
    for i, plane in enumerate((unit[0], unit[1], unit[2], dist, inv, q, envelope * valid, valid)):
        geo_ref[i] = plane.reshape(geo_ref.shape[1:])

    env_ref[...] = jnp.zeros_like(env_ref)
    denv_ref[...] = jnp.zeros_like(denv_ref)
    ae_ref[...] = jnp.zeros_like(ae_ref)
    acc_ref[...] = jnp.zeros_like(acc_ref)
    cacc_ref[...] = jnp.zeros_like(cacc_ref)
    dr_ref[...] = jnp.zeros_like(dr_ref)

    groups = bound_ref.shape[1] * SUB // sorted_size(rows_all * LANES)

    def window(k, s):
        first = (k * subs + s) * groups
        low = bound_ref[0, first]
        high = low
        for g in range(groups):
            high = jnp.maximum(high, bound_ref[1, first + g])
        start = pl.multiple_of((low >> 3) << 3, 8)
        more = lax.div(high - start, jnp.int32(WIN))
        return start, more

    most = jnp.int32(0)
    n_chunks = jnp.int32(0)
    for s in range(rows_all // sub_rows):
        most = jnp.maximum(most, window(s // subs, s % subs)[1])
        for g in range(groups):
            any_live = bound_ref[1, s * groups + g] >= 0
            n_chunks = jnp.where(any_live, s // subs + 1, n_chunks)


    def lanes_of(s, n):
        if isinstance(s, int):
            return slice(s * SUB, (s + n) * SUB)
        return pl.ds(pl.multiple_of(s * SUB, SUB), n * SUB)

    def tile_of(load, s, n):
        if isinstance(s, int):
            return load(slice(s * sub_rows, (s + n) * sub_rows))
        return jnp.concatenate(
            [load(pl.ds(s * sub_rows + j, 1)) for j in range(n * sub_rows)], axis=0
        )

    def plane(i, k, s, n):
        return tile_of(lambda rows: geo_ref[i, k, rows, :], s, n)

    def keys_of(k, s, n):
        return tile_of(lambda rows: key_ref[k, rows, :], s, n)

    def stacked(ref, k, s, n, height):
        first = (k * subs + s) * sub_rows
        tiles = [
            ref[pl.ds(pl.multiple_of((first + j) * height, 8), height), :]
            for j in range(n * sub_rows)
        ]
        return jnp.concatenate(tiles, axis=1)

    def window_hot(k, s, start):
        crow = in_lanes(keys_of(k, s, 1) >> OTHER_BITS) - start
        return lax.broadcasted_iota(jnp.int32, (WIN, SUB), 0) == crow

    def select(k, s, start):
        near = jnp.clip(in_lanes(keys_of(k, s, 1) >> OTHER_BITS) - start, -1, WIN).astype(BF16)
        hot = lax.broadcasted_iota(jnp.int32, (WIN, SUB), 0).astype(BF16) == near
        ys = stacked(y_ref, k, s, 1, 8)
        none = jnp.zeros((), BF16)
        parts = [jnp.where(hot, jnp.ones((), BF16), none)]
        for m in range(8):
            parts.append(jnp.where(hot, ys[m : m + 1, :].astype(BF16), none))
        return jnp.concatenate(parts, axis=0)

    def load_window(ref, start):
        return jnp.concatenate(
            [ref[m, pl.ds(start, WIN), :] for m in range(9)], axis=0
        ).astype(BF16)

    def add_window(ref, start, rows):
        for m in range(9):
            ref[m, pl.ds(start, WIN), :] += rows[m * WIN : (m + 1) * WIN, :]

    def each_window(k, s, n, slow, body):
        for j in range(n):
            start, more = window(k, s + j)
            body(s + j, j, start, True)
            if slow:

                def step(i, carry, s=s, j=j, start=start):
                    body(s + j, j, pl.multiple_of(start + i * WIN, 8), False)
                    return carry

                lax.fori_loop(1, more + 1, step, 0)

    def kept(k, s, start, fresh):
        return a_ref[k * subs + s] if fresh else select(k, s, start)

    def table_hots(k, s, n):
        row = in_lanes(keys_of(k, s, n) & OTHER_MASK)
        return [one_hot(row, at, min(LANES, n_tab - at)) for at in range(0, n_tab, LANES)]

    def part(j):
        return slice(j * SUB, (j + 1) * SUB)

    def phase_a(k, s, n, slow):
        lanes = lanes_of(s, n)
        crow = in_lanes(keys_of(k, s, n) >> OTHER_BITS)
        table = jnp.concatenate(table_hots(k, s, n), axis=0)
        hots_ref[k, :, lanes] = table
        hots = [one_hot(crow, 0, own), table]
        basis = stacked(basis_ref, k, s, n, n_basis)
        b_hi, b_lo = split(basis)
        hots.append(jnp.concatenate([b_hi, b_lo], axis=0).astype(BF16))
        hots.append(jnp.concatenate([b_hi, jnp.zeros_like(b_hi)], axis=0).astype(BF16))
        mixed = dot_nn(table_ref[...], jnp.concatenate(hots, axis=0)).astype(BF16)
        half = dot_nn(w1t_ref[...], mixed).astype(BF16)
        up = 1.0 + jnp.tanh(half)
        first = half * up
        dsilu_ref[k, :, lanes] = up + first * (2.0 - up)
        first_ref[k, :, lanes] = first
        both = dot_nn(wevt_ref[...], first)
        ew = (both[0:chans] * in_lanes(plane(6, k, s, n))).astype(BF16)
        ew_ref[k, :, lanes] = ew
        val_ref[k, :, lanes] = both[chans:].astype(BF16)

        def body(s, j, start, fresh):
            a = select(k, s, start)
            if fresh:
                a_ref[k * subs + s] = a
            add_window(env_ref, start, dot_nt(a, ew[:, part(j)]))

        each_window(k, s, n, slow, body)

    def phase_b(k, s, n, slow):
        lanes = lanes_of(s, n)

        def totals(s, j, start, fresh):
            value = dot_tn(load_window(env_ref, start), kept(k, s, start, fresh))
            if fresh:
                big_ref[:, part(j)] = value
            else:
                big_ref[:, part(j)] += value

        each_window(k, s, n, slow, totals)
        total = big_ref[:, 0 : n * SUB]
        value = val_ref[k, :, lanes].astype(F32)
        scalar = (value * total).astype(BF16)
        half = dot_nn(w2t_ref[...], jnp.concatenate([first_ref[k, :, lanes], scalar], axis=0))
        half = half.astype(BF16)
        up = 1.0 + jnp.tanh(half)
        second = half * up
        wcol = jnp.concatenate([wcol_ref[...]] * (n * sub_rows), axis=1)
        ee = jnp.sum(second.astype(F32) * wcol, axis=0, keepdims=True)
        envv = in_lanes(plane(6, k, s, n))
        live = ee * in_lanes(plane(7, k, s, n))
        first_row = s * sub_rows
        for j in range(n * sub_rows):
            live_ref[k, pl.ds(first_row + j, 1), :] = live[:, j * LANES : (j + 1) * LANES]
        energy = ee * envv
        dz2 = envv.astype(BF16) * (up + second * (2.0 - up))
        dz2_ref[k, :, lanes] = dz2
        dscalar = dot_nn(w2_ref[...], dz2)
        dt = (value * dscalar).astype(BF16)
        dt_ref[k, :, lanes] = dt
        dv_ref[k, :, lanes] = (total * dscalar).astype(BF16)

        def body(s, j, start, fresh):
            add_window(denv_ref, start, dot_nt(kept(k, s, start, fresh), dt[:, part(j)]))
            mine = jnp.where(window_hot(k, s, start), energy[:, part(j)], 0.0)
            half = mine[:, 0:LANES]
            for i in range(1, sub_rows):
                half = half + mine[:, i * LANES : (i + 1) * LANES]
            ae_ref[pl.ds(start, WIN), :] += half

        each_window(k, s, n, slow, body)

    def phase_c(k, s, n, slow):
        lanes = lanes_of(s, n)
        height = n * sub_rows

        def env_terms(s, j, start, fresh):
            a = kept(k, s, start, fresh)
            e_win = load_window(env_ref, start)
            d_win = load_window(denv_ref, start)
            dew = dot_tn(d_win, a)
            here = lanes_of(s, 1)
            pair = jnp.concatenate([dt_ref[k, :, here], ew_ref[k, :, here]], axis=0)
            prods = dot_nn(jnp.concatenate([e_win, d_win], axis=1)[WIN:], pair)
            hot = a[0:WIN].astype(F32)
            if fresh:
                big_ref[:, part(j)] = dew
            else:
                big_ref[:, part(j)] += dew
            for m in range(1, 9):
                row = jnp.sum(prods[(m - 1) * WIN : m * WIN] * hot, axis=0, keepdims=True)
                for i in range(sub_rows):
                    at = j * sub_rows + i
                    piece = row[:, i * LANES : (i + 1) * LANES]
                    if fresh:
                        dy_ref[m, at : at + 1, :] = piece
                    else:
                        dy_ref[m, at : at + 1, :] += piece

        each_window(k, s, n, slow, env_terms)
        dew = big_ref[:, 0 : n * SUB]
        dpre = (dew * in_lanes(plane(6, k, s, n))).astype(BF16)
        denv_row = jnp.sum(dew * ew_ref[k, :, lanes].astype(F32), axis=0, keepdims=True)
        for j in range(height):
            dy_ref[0, j : j + 1, :] = denv_row[:, j * LANES : (j + 1) * LANES]
        joined = jnp.concatenate([dpre, dv_ref[k, :, lanes], dz2_ref[k, :, lanes]], axis=0)
        dfirst = dot_nn(wev_ref[...], joined)
        dz1 = (dfirst * dsilu_ref[k, :, lanes].astype(F32)).astype(BF16)
        dboth = dot_nn(w1_ref[...], dz1)
        dmixed = dboth[0:chans].astype(BF16)
        dbasis = dboth[chans:]
        for j in range(height):
            db_ref[j * n_basis : (j + 1) * n_basis, :] = dbasis[
                0:n_basis, j * LANES : (j + 1) * LANES
            ]
        ux, uy, uz, dist, inv, q = [plane(i, k, s, n) for i in range(6)]
        envelope = q * q
        g = envelope * inv
        denvelope = -(q * envelope) * dist
        dg = (denvelope - g) * inv
        sins, coss = waves(0.5 * dist, n_basis)
        live = tile_of(lambda rows: live_ref[k, rows, :], s, n)
        y = [dy_ref[m, 0:height, :] for m in range(9)]
        ddist = (live + y[0] / envelope) * denvelope
        for i in range(n_basis):
            db = db_ref[pl.ds(i, height, stride=n_basis), :]
            ddist = ddist + db * (coss[i] * ((i + 1) * math.pi / 2.0) * g + sins[i] * dg)
        gx = y[1] + ROOT3 * (uy * y[4] + uz * y[6]) + (2.0 * 0.866) * ux * y[7]
        gy = y[2] + ROOT3 * (ux * y[4] + uz * y[5]) - (2.0 * 0.866) * uy * y[7]
        gz = y[3] + ROOT3 * (uy * y[5] + ux * y[6]) + 3.0 * uz * y[8]
        along = ddist - inv * (gx * ux + gy * uy + gz * uz)
        for i, (gu, u) in enumerate(((gx, ux), (gy, uy), (gz, uz))):
            hi, lo = split(inv * gu + along * u)
            dr_ref[pl.ds(i, height, stride=16), :] = hi
            dr_ref[pl.ds(3 + i, height, stride=16), :] = lo
        dr = jnp.concatenate([dr_ref[j * 16 : (j + 1) * 16, :] for j in range(height)], axis=1)
        moved = jnp.concatenate([dmixed, dr.astype(BF16)], axis=0)
        sums = dot_nt(hots_ref[k, :, lanes], moved)
        acc_ref[:, 0:chans] += sums[:, 0:chans]
        acc_ref[:, chans : chans + 16] += sums[:, chans:]

        def body(s, j, start, fresh):
            hot = a_ref[k * subs + s, 0:WIN, :] if fresh else window_hot(k, s, start).astype(BF16)
            mine = dot_nt(hot, moved[:, part(j)])
            cacc_ref[pl.ds(start, WIN), 0:chans] += mine[:, 0:chans]
            cacc_ref[pl.ds(start, WIN), chans : chans + 16] += mine[:, chans:]

        each_window(k, s, n, slow, body)

    for phase in (phase_a, phase_b, phase_c):

        @pl.when(most == 0)
        def _(phase=phase):
            def chunk(k, carry):
                phase(k, 0, subs, False)
                return carry

            lax.fori_loop(0, n_chunks, chunk, 0)

        @pl.when(most != 0)
        def _(phase=phase):
            def sub(i, carry):
                phase(lax.div(i, subs), lax.rem(i, subs), 1, True)
                return carry

            lax.fori_loop(0, n_chunks * subs, sub, 0)

    own_ref[0:own, :] = cacc_ref[0:own, :]
    own_ref[own:, :] = acc_ref[0:own, :]
    row = lax.broadcasted_iota(jnp.int32, (LANES, LANES), 0)
    group = lax.broadcasted_iota(jnp.int32, (LANES, LANES), 1) // GROUP
    both = ((group < 3) & ((row == group) | (row == group + 3))).astype(F32)
    places = dot_nn(acc_ref[own:, LANES:], both, HIGH)
    found = {}
    at = own
    for off in OFFSETS:
        found[off] = at
        at += plan.live(off)
    for blocks, ref in zip(
        plan.groups[0] + [plan.held_rest], tuple(back_refs) + (rest_ref,)
    ):
        for off, row in plan.spans(blocks):
            live = plan.live(off)
            at = found[off]
            ref[row : row + live, :] = acc_ref[at : at + live, 0:chans]
            block = places[at - own : at - own + live, :]
            ref[row + live : row + live + 1, :] = jnp.sum(diagonal(block), axis=0, keepdims=True)


def returned_sums(plan, came, axes, messages, first, sel_ref, both_ref):
    chans = both_ref.shape[1] - LANES
    both_ref[...] = jnp.zeros_like(both_ref)
    at = 0
    for blocks in messages:
        for off, row in plan.spans(blocks):
            live = plan.live(off)
            src, begin = plan.find(came, axes, None, [], off)
            here = slice(at + row, at + row + live)
            both_ref[here, 0:chans] = src[begin : begin + live, :]
            both_ref[here, chans:] = spread(src[begin + live : begin + live + 1, :], live)
        at += plan.total(blocks)
    hot = sel_ref[first : first + at, :].astype(BF16)
    return dot_exact(hot, both_ref[...], ((0,), (0,)))


def own_kernel(plan, ae_ref, own_ref, wide_ref, sel_ref, *refs):
    came, refs = plan.cut(refs, 0, 1)
    energy_ref, fg_ref, force_ref, both_ref = refs
    chans = fg_ref.shape[1]
    own = force_ref.shape[1]
    first = sum(plan.total(blocks) for blocks in plan.groups[2])
    sums = returned_sums(plan, came, (1, 0), [plan.own_rest], first, sel_ref, both_ref)
    energy_ref[...] = jnp.sum(ae_ref[0:own, :].T, axis=0, keepdims=True)
    fg_ref[...] = dot_nt(own_ref[0:own, 0:chans], wide_ref[0:chans, :], HIGH) + dot_nt(
        own_ref[own:, 0:chans] + sums[:, 0:chans], wide_ref[chans : 2 * chans, :], HIGH
    )
    force = (own_ref[own:, LANES:] - own_ref[0:own, LANES:]).T
    total = dot_nt(group_rows(8), sums[:, chans:], HIGH)
    force_ref[...] = force[0:3, :] + force[3:6, :] + total[0:3, :]


def last_kernel(plan, sel_ref, fg_ref, force_ref, wide_ref, *refs):
    came, refs = plan.cut(refs, 2)
    out_force_ref, out_fg_ref, both_ref = refs
    chans = fg_ref.shape[1]
    sums = returned_sums(plan, came, (2,), plan.groups[2], 0, sel_ref, both_ref)
    s_hi, s_lo = split(sums[:, 0:chans])
    w_hi, w_lo = split(wide_ref[chans : 2 * chans, :])
    out_fg_ref[...] = fg_ref[...] + dot_nt(
        jnp.concatenate([s_hi, s_lo, s_hi], axis=1).astype(BF16),
        jnp.concatenate([w_hi, w_hi, w_lo], axis=1).astype(BF16),
    )
    total = dot_nt(group_rows(8), sums[:, chans:], HIGH)
    out_force_ref[...] = -(force_ref[...] + total[0:3, :])


def stack(*arrays):
    dtype = arrays[0].dtype
    tile = 32 // dtype.itemsize
    starts = [0]
    for x in arrays:
        starts.append(starts[-1] + -(-x.shape[1] // tile) * tile)
    total = None
    for x, at in zip(arrays, starts):
        below = starts[-1] - at - x.shape[1]
        part = jnp.pad(x.astype(dtype), ((0, 0), (at, below), (0, LANES - x.shape[2])))
        total = part if total is None else total + part
    return total[0]


def local(
    positions,
    atom_features,
    send_face,
    send_edge,
    send_corner,
    centre,
    other,
    edge_count,
    w_proj_a,
    w_proj_b,
    w_radial,
    w_first,
    w_env,
    w_value,
    w_second,
    w_out,
):
    own, chans = atom_features.shape
    edges = centre.shape[0]
    n_basis = w_radial.shape[0]
    plan = Plan(
        [send_face.shape[2], send_edge.shape[2], send_corner.shape[2]],
        [lax.axis_size(axis) for axis in AXES],
    )
    n_ghost = sum(len(c) * w for c, w in zip(CLASSES, plan.widths))
    n_sel = 2 * own + n_ghost
    n_send = sum(plan.total(blocks) for blocks in plan.groups[2]) + plan.total(plan.own_rest)
    n_table = n_sel + 4 * n_basis
    edges_up = -(-edges // CHUNK) * CHUNK
    n_rows = edges_up // LANES
    n_chunks = edges_up // CHUNK

    with jax.named_scope("prep"):
        atom_features, plan.even = lax.optimization_barrier((atom_features, plan.even))
        rows = stack(atom_features[None], edge_count.reshape(1, 1, 1))
        *sends, own_rows, sel = pl.pallas_call(
            lambda *refs: prep_kernel(plan, *refs),
            out_shape=plan.shapes(2, chans)
            + [shape(plan.total(plan.own_rest), chans), shape(n_send, own)],
            in_specs=[VMEM] * 5,
            out_specs=[VMEM] * (len(plan.groups[2]) + 2),
            scratch_shapes=[pltpu.VMEM((LANES, LANES), F32)],
            compiler_params=PARAMS,
        )(
            rows,
            positions,
            jnp.transpose(send_face, (1, 0, 2)),
            jnp.transpose(send_edge, (0, 2, 1)),
            jnp.transpose(send_corner, (0, 2, 1)),
        )

    came = {}
    with jax.named_scope("halo_z"):
        came[2] = plan.send(2, sends)

    with jax.named_scope("group_edges"):
        pad = [(0, edges_up - edges)]
        regs = max(sorted_size(edges_up) // (8 * LANES), 1)
        key, bounds = pl.pallas_call(
            lambda *refs: sort_kernel(own, *refs),
            out_shape=[
                shape(n_chunks, CHUNK // LANES, LANES, dtype=jnp.int32),
                shape(2, LANES, dtype=jnp.int32),
            ],
            in_specs=[VMEM] * 3,
            out_specs=[VMEM] * 2,
            scratch_shapes=[pltpu.VMEM((16 * regs, LANES), F32)],
            compiler_params=PARAMS,
        )(
            rows,
            jnp.pad(centre, pad).reshape(n_rows, LANES),
            jnp.pad(other, pad).reshape(n_rows, LANES),
        )

    with jax.named_scope("halo_y"):
        given = (w_proj_a, w_proj_b, w_radial, w_first, w_env, w_value, w_second, w_out)
        came[2], key, bounds, given = lax.optimization_barrier((came[2], key, bounds, given))
        w_proj_a, w_proj_b, w_radial, w_first, w_env, w_value, w_second, w_out = given
        came[1] = plan.send(1, glue(plan, 1, (2,), plan.own_rest, own_rows, came))

    with jax.named_scope("weights"):
        wide = stack(w_proj_a[None], w_proj_b[None], w_radial[None])
        narrow = stack(
            w_first[None], w_env[None], w_value[None], w_second[None], w_out[None, None, :]
        )
        half, *weights = pl.pallas_call(
            weight_kernel,
            out_shape=[
                shape(2 * own + 4 * n_basis, chans),
                shape(chans, chans, dtype=BF16),
                shape(2 * chans, chans, dtype=BF16),
                shape(chans, 2 * chans, dtype=BF16),
                shape(chans + 2 * n_basis, chans, dtype=BF16),
                shape(chans, 3 * chans, dtype=BF16),
                shape(chans, chans, dtype=BF16),
                shape(chans, LANES),
            ],
            in_specs=[VMEM] * 3,
            out_specs=[VMEM] * 8,
            compiler_params=PARAMS,
        )(rows, wide, narrow)

    with jax.named_scope("halo_x"):
        came[1], half, weights = lax.optimization_barrier((came[1], half, weights))
        came[0] = plan.send(0, glue(plan, 0, (1, 2), plan.own_rest, own_rows, came))

    planes = (n_chunks, chans, CHUNK)
    scratch = [
        pltpu.VMEM((n_table, chans), F32),
        pltpu.VMEM((n_ghost, chans), F32),
        pltpu.VMEM((-(-n_ghost // LANES) * LANES, LANES), F32),
        pltpu.VMEM((chans, n_table), BF16),
        pltpu.VMEM((n_rows * 8, LANES), F32),
        pltpu.VMEM((n_rows * n_basis, LANES), F32),
        pltpu.VMEM((8, n_chunks, CHUNK // LANES, LANES), F32),
        pltpu.VMEM(planes, BF16),
        pltpu.VMEM(planes, BF16),
        pltpu.VMEM(planes, BF16),
        pltpu.VMEM(planes, BF16),
        pltpu.VMEM((edges_up // SUB, 9 * WIN, SUB), BF16),
        pltpu.VMEM((9, own + WIN, chans), F32),
        pltpu.VMEM((9, own + WIN, chans), F32),
        pltpu.VMEM((chans, CHUNK), F32),
        pltpu.VMEM(planes, BF16),
        pltpu.VMEM(planes, BF16),
        pltpu.VMEM(planes, BF16),
        pltpu.VMEM((n_chunks, n_sel - own, CHUNK), BF16),
        pltpu.VMEM((n_chunks, CHUNK // LANES, LANES), F32),
        pltpu.VMEM((9, CHUNK // LANES, LANES), F32),
        pltpu.VMEM((CHUNK // LANES * n_basis, LANES), F32),
        pltpu.VMEM((CHUNK // LANES * 16, LANES), F32),
        pltpu.VMEM((n_sel - own, 2 * LANES), F32),
        pltpu.VMEM((own + WIN, 2 * LANES), F32),
    ]
    with jax.named_scope("layer"):
        given = [bounds, key, positions, wide]
        given += [*came[0], *came[1], *came[2], half, *weights]
        atom_sums, own_sums, *back, held = pl.pallas_call(
            lambda *refs: main_kernel(plan, *refs),
            out_shape=[shape(own + WIN, LANES), shape(2 * own, 2 * LANES)]
            + plan.shapes(0, chans)
            + [shape(plan.total(plan.held_rest), chans)],
            in_specs=[SMEM] + [VMEM] * (len(given) - 1),
            out_specs=[VMEM] * (3 + len(plan.groups[0])),
            scratch_shapes=scratch,
            compiler_params=PARAMS,
        )(*given)

    with jax.named_scope("halo_back"):
        home = {0: plan.send(0, back, back=True)}
        home[1] = plan.send(1, glue(plan, 1, (0,), plan.held_rest, held, home), back=True)
        home[2] = plan.send(2, glue(plan, 2, (1, 0), plan.held_rest, held, home), back=True)

    with jax.named_scope("own_part"):
        given = [atom_sums, own_sums, wide, sel, *home[0], *home[1]]
        energy, fg, force = pl.pallas_call(
            lambda *refs: own_kernel(plan, *refs),
            out_shape=[shape(1, own), shape(own, chans), shape(3, own)],
            in_specs=[VMEM] * len(given),
            out_specs=[VMEM] * 3,
            scratch_shapes=[pltpu.VMEM((plan.total(plan.own_rest), chans + LANES), F32)],
            compiler_params=PARAMS,
        )(*given)

    with jax.named_scope("owner_sums"):
        given = [sel, fg, force, wide, *home[2]]
        n_z = n_send - plan.total(plan.own_rest)
        forces, feature_grad = pl.pallas_call(
            lambda *refs: last_kernel(plan, *refs),
            out_shape=[shape(3, own), shape(own, chans)],
            in_specs=[VMEM] * len(given),
            out_specs=[VMEM] * 2,
            scratch_shapes=[pltpu.VMEM((n_z, chans + LANES), F32)],
            compiler_params=PARAMS,
        )(*given)
    return forces, energy.reshape(own), feature_grad


def solution(mesh):
    shard = P(AXES)
    return jax.shard_map(
        local,
        mesh=mesh,
        in_specs=(
            P(None, AXES),
            P(AXES, None),
            P(AXES, None, None),
            P(AXES, None, None),
            P(AXES, None, None),
            shard,
            shard,
            shard,
        )
        + (P(),) * 8,
        out_specs=(P(None, AXES), shard, P(AXES, None)),
        check_vma=False,
    )
```
